32 devices in a mesh: group: 2 (over y), angle: 4 (over z), slab: 2 (over x), col: 2 (over core).
Axes of the slice: x: 2, y: 2, z: 4, core: 2. Of those that a mesh axis runs over, the one named last changes fastest.
Arguments:
- projections: bfloat16 [32, 128, 8192], P(('group', 'angle'), 'slab', 'col'), parts along dimension 0, may hold values from -6 to 6
- filter_taps: bfloat16 [2048], replicated, may hold values from -0.125 to 0.125
- row_first: int32 [32, 2], P(('group', 'angle'), 'slab'), parts along dimension 0, may hold values from 0 to 64, as said below
- interp_index: int32 [32, 2, 256], P(('group', 'angle'), 'slab'), parts along dimension 0, may hold values from 0 to 94, as said below
- interp_frac: float32 [32, 2, 256], P(('group', 'angle'), 'slab'), parts along dimension 0, may hold values from 0 to 1
Outputs:
- volume: float32 [1024, 8192], P(('group', 'slab', 'angle'), 'col'), parts along dimension 0
The draws below stay inside these ranges and needn't reach their ends.
There are 2 independent parts, one for each index of `group`. The reference program is written for one: setup_inputs(seed, part) draws one part's arguments, and reference() takes and returns one part's arrays. A program takes and returns all parts, laid end to end along the dimension named above; an argument that names none is the same for every part. Nothing has to cross between parts.
Inputs may be any that keep to these rules, and one draw needn't show every extreme that they name: row_first[a, s] lies between s * 64 - 32 and s * 64, and equals 0 for s = 0. row_first[a, s] + interp_index[a, s, z] + 1 stays below (s + 1) * 64 + 32 and below 128.
All inputs are finite; a program needn't handle non-finite values.
Results may differ from the reference program's by a relative error of at most 0.0048.
Values may be sent and summed in bfloat16 or wider, within the bound.
No kernel may reach another device: no remote copies, remote signals or barrier semaphores. Data moves between devices by JAX's collectives and lax.ppermute only.
A program may use at most 64 MiB of HBM per device.

```python
import math
import jax
import jax.numpy as jnp
from jax import lax

DET = 8192
TAPS = 2048
ROWS_DEV = 64
ZSLAB = 256
HALO = 32
SLABS = 2
ANGLES = 16
DROWS = 128


def draw_row_first(key, part):
    key = jax.random.fold_in(key, 11)
    lower = jax.random.randint(key, (ANGLES, SLABS), 0, HALO + 1)
    angle_ids = jnp.arange(ANGLES)[:, None]
    slab_ids = jnp.arange(SLABS)[None, :]
    lower = jnp.where(angle_ids == 0, HALO, jnp.where(angle_ids == 1, 0, lower))
    lower = jnp.where(slab_ids == 0, 0, lower)
    return (slab_ids * ROWS_DEV - lower).astype(jnp.int32)


def draw_interp_index(key, part):
    key = jax.random.fold_in(key, 23)
    slab_ids = jnp.arange(SLABS)[None, :, None]
    counts = jnp.where(slab_ids == SLABS - 1, ROWS_DEV, ROWS_DEV + HALO)
    jitter = jax.random.randint(key, (ANGLES, SLABS, ZSLAB), 0, ZSLAB - 1)
    depth = jnp.arange(ZSLAB, dtype=jnp.int32)[None, None, :]
    return ((depth * (counts - 2) + jitter) // (ZSLAB - 1)).astype(jnp.int32)


def block_levels(stream_key, extent, cuts, smallest, top_value):
    gain, own = 1.0, jax.random.fold_in(stream_key, 6)
    for position, shards_of in cuts:
        draws = jnp.exp(jax.random.uniform(jax.random.fold_in(own, position), (shards_of,), jnp.float32, smallest / len(cuts), top_value / len(cuts)))
        gain = gain * jnp.repeat(draws, extent[position] // shards_of).reshape([-1 if axis == position else 1 for axis in range(len(extent))])
    return gain


def gaussian(own_key, shape, width, most, pieces=(), kind=jnp.bfloat16):
    gain = block_levels(own_key, shape, pieces, -0.22, 0.18) if pieces else 1.0
    entries = jax.random.normal(own_key, shape, jnp.float32) * width * gain
    return jnp.minimum(jnp.maximum(entries, -most), most).astype(kind)


def setup_inputs(seed: int = 0, part: int = 0) -> dict:
    streams_of = jax.random.split(jax.random.key(seed), 6)
    part_splits = jax.random.split(jax.random.fold_in(streams_of[5], part), 6)
    projections = gaussian(part_splits[0], (ANGLES, DROWS, DET), 1.0, 6.0, ((0, 4), (1, 2), (2, 2)))
    filter_taps = gaussian(streams_of[1], (TAPS,), TAPS ** -0.5, 0.125)
    row_first = draw_row_first(jax.random.fold_in(jax.random.fold_in(streams_of[5], part), 71), part)
    interp_index = draw_interp_index(jax.random.fold_in(jax.random.fold_in(streams_of[5], part), 71), part)
    interp_frac = jnp.clip(1.0 * jax.random.uniform(part_splits[4], (ANGLES, SLABS, ZSLAB), jnp.float32) ** block_levels(part_splits[4], (ANGLES, SLABS, ZSLAB), ((0, 4), (1, 2)), -0.2, 0.2), 0.0, 1.0)
    return dict(projections=projections, filter_taps=filter_taps, row_first=row_first, interp_index=interp_index, interp_frac=interp_frac)


def cosine_factor():
    row_ids = jnp.arange(DROWS).astype(jnp.float32) - DROWS / 2 + 0.5
    col_ids = jnp.arange(DET).astype(jnp.float32) - DET / 2 + 0.5
    distance = jnp.float32(DET)
    return distance / jnp.sqrt(distance * distance + col_ids[None, :] ** 2 + row_ids[:, None] ** 2)

def reference(projections, filter_taps, row_first, interp_index, interp_frac):
    factor = cosine_factor()
    length = DET + TAPS
    taps_wide = jnp.pad(filter_taps.astype(jnp.float32), (0, length - TAPS))
    spectrum = jnp.conj(jnp.fft.rfft(taps_wide))

    def filter_one(image):
        weighted = (image.astype(jnp.float32) * factor).astype(jnp.bfloat16)
        weighted = lax.optimization_barrier(weighted).astype(jnp.float32)
        padded = jnp.pad(weighted, ((0, 0), (TAPS // 2, length - DET - TAPS // 2)))
        result = jnp.fft.irfft(spectrum[None, :] * jnp.fft.rfft(padded, axis=1), n=length, axis=1)
        return result[:, :DET].astype(jnp.bfloat16)
    filtered = lax.map(filter_one, projections)
    low_weight = lax.optimization_barrier((1.0 - interp_frac).astype(jnp.bfloat16)).astype(jnp.float32)
    high_weight = lax.optimization_barrier(interp_frac.astype(jnp.bfloat16)).astype(jnp.float32)
    absolute = (row_first[:, :, None] + interp_index).astype(jnp.int32)

    def accumulate(total, inputs):
        image, row_ids, lower_w, upper_w = inputs
        lower = image[row_ids].astype(jnp.float32)
        upper = image[row_ids + 1].astype(jnp.float32)
        return (total + lower_w[:, :, None] * lower + upper_w[:, :, None] * upper, None)
    start = jnp.zeros((SLABS, ZSLAB, DET), jnp.float32)
    total, _ = lax.scan(accumulate, start, (filtered, absolute, low_weight, high_weight))
    return total.reshape(SLABS * ZSLAB, DET) * (math.pi / ANGLES)
```

```python
import math

import jax
import jax.numpy as jnp
from jax import lax
from jax.experimental import pallas as pl
from jax.experimental.pallas import tpu as pltpu
from jax.sharding import PartitionSpec as P

BLOCK = 256
TILE = 128
STACK = 4
VMEM_BYTES = 14 * 1024 * 1024
FIRST_VMEM_BYTES = 103 * 512 * 1024
LINE_ORDER = ((3, 2, 1, 0), (0, 2, 3, 1), (3, 1, 0, 2), (0, 1, 2, 3))

VMEM = pl.BlockSpec(memory_space=pltpu.VMEM)
HELD = pl.BlockSpec(memory_space=pltpu.HBM)
SMEM = pl.BlockSpec(memory_space=pltpu.SMEM)


def kernel_call(
    body, out_shape, args, flops, scratch=(), name=None, specs=None, grant=VMEM_BYTES
):
    specs = specs or [VMEM] * len(args)
    moved = sum(a.size * a.dtype.itemsize for a in (*args, *out_shape))
    return pl.pallas_call(
        body,
        out_shape=out_shape,
        in_specs=specs,
        out_specs=[VMEM] * len(out_shape),
        scratch_shapes=list(scratch),
        compiler_params=pltpu.CompilerParams(vmem_limit_bytes=grant),
        cost_estimate=pl.CostEstimate(flops=flops, bytes_accessed=moved, transcendentals=0),
        name=name,
    )(*args)


def build_band(taps_ref, band_ref):
    count = taps_ref.shape[0]
    steps, tiles = band_ref.shape[1] // TILE, band_ref.shape[0] // TILE
    zero = jnp.zeros((TILE, TILE), jnp.float32)
    ahead = lax.broadcasted_iota(jnp.int32, (TILE, TILE), 1) >= lax.broadcasted_iota(
        jnp.int32, (TILE, TILE), 0
    )
    taps = taps_ref[...].astype(jnp.float32)

    def shifted(d):
        if not 0 <= d < count:
            return zero
        row = jnp.broadcast_to(taps[d : d + 1, :], (TILE, TILE))
        return pltpu.roll(row, 0, 1, stride=1, stride_axis=0)

    before = zero
    for d in range(-(steps - 1), tiles):
        here = shifted(d)
        block = jnp.where(ahead, here, before).T.astype(jnp.bfloat16)
        before = here
        for c in range(steps):
            if 0 <= d + c < tiles:
                band_ref[(d + c) * TILE : (d + c + 1) * TILE, c * TILE : (c + 1) * TILE] = block


def weigh(proj_ref, weighted_ref, half, row_at, row_start, col_start, sizes, start, stop):
    angles = proj_ref.shape[0]
    total_rows, total_cols, count = sizes
    distance = jnp.float32(total_cols)
    v = lax.broadcasted_iota(jnp.int32, (count, 1), 0) + (row_start + row_at)
    v = v.astype(jnp.float32) - total_rows / 2 + 0.5
    step = BLOCK
    for c in range(start, stop, step):
        u = lax.broadcasted_iota(jnp.int32, (1, step), 1) + (col_start + c)
        u = u.astype(jnp.float32) - total_cols / 2 + 0.5
        factor = distance / jnp.sqrt(distance * distance + u * u + v * v)
        for a in range(angles):
            raw = proj_ref[a, pl.ds(row_at, count), c : c + step].astype(jnp.float32)
            at = (half * angles + a) * count
            weighted_ref[at : at + count, c : c + step] = (raw * factor).astype(jnp.bfloat16)


def filter_columns(columns, rows, weighted_ref, left_ref, right_ref, band_ref, out_ref, stack):
    cols = weighted_ref.shape[1]
    length = band_ref.shape[0]
    reach = (length - BLOCK) // 2
    count = rows.stop - rows.start

    def window(c):
        lo, hi = c - reach, c - reach + length
        pieces = []
        if lo < 0:
            pieces.append(left_ref[rows, reach + lo : reach + min(hi, 0)])
        if max(lo, 0) < min(hi, cols):
            pieces.append(weighted_ref[rows, max(lo, 0) : min(hi, cols)])
        if hi > cols:
            pieces.append(right_ref[rows, max(lo - cols, 0) : hi - cols])
        return pieces[0] if len(pieces) == 1 else jnp.concatenate(pieces, axis=1)

    starts = [c for start, width in columns for c in range(start, start + width, BLOCK)]
    for at in range(0, len(starts), stack):
        group = starts[at : at + stack]
        tall = jnp.concatenate([window(c) for c in group], axis=0)
        result = jnp.dot(tall, band_ref[...], preferred_element_type=jnp.float32)
        result = result.astype(jnp.bfloat16)
        for k in range(len(group)):
            out_ref[:, (at + k) * BLOCK : (at + k + 1) * BLOCK] = result[
                k * count : (k + 1) * count, :
            ]


def bf16(*shape):
    return jax.ShapeDtypeStruct(shape, jnp.bfloat16)


def f32(*shape):
    return jax.ShapeDtypeStruct(shape, jnp.float32)


def chunk_plan(cols, reach):
    assert cols >= 2 * reach + 4 * BLOCK
    cut = reach + (cols - 2 * reach) // 2 // BLOCK * BLOCK
    return [
        [(reach, cut - reach)],
        [(cut, cols - reach - cut)],
        [(0, reach), (cols - reach, reach)],
    ]


def on_device(projections, filter_taps, row_first, interp_index, interp_frac):
    angles, rows, cols = projections.shape
    depth = interp_index.shape[2]
    taps = filter_taps.shape[0]
    reach = taps // 2
    length = taps + BLOCK
    margin = rows // 2
    slabs, line, sides = (lax.axis_size(n) for n in ("slab", "angle", "col"))
    angle_index = lax.axis_index("angle")
    scale = math.pi / (angles * line)
    both = slabs == 2
    halos = 1 if both else 2
    quick = line == 4
    shard = depth // line
    order = LINE_ORDER if quick else (tuple(range(line)),) * line
    total_rows, total_cols = rows * slabs, cols * sides
    chunks = chunk_plan(cols, reach)
    widths = [sum(w for _, w in c) for c in chunks]
    part = angles * margin
    first_half, second_half = slice(0, part), slice(part, 2 * part)
    sizes = (total_rows, total_cols, margin)

    def half_rows(slab):
        if both:
            return jnp.where(slab == 0, margin, 0), jnp.where(slab == 0, 0, margin)
        return margin, 0

    def aligned(row):
        return row if isinstance(row, int) else pl.multiple_of(row, margin)

    ((start, width),) = chunks[0]
    assert start == reach
    window = width + 2 * reach
    early = halos

    def first_kernel(proj_ref, taps_ref, band_ref, edge_ref, *rest):
        outs, (raw_ref, weighted_ref, sem) = rest[:-3], rest[-3:]
        slab = lax.axis_index("slab")
        col = lax.axis_index("col")
        starts = [aligned(r) for r in half_rows(slab)][:early]
        copies = [
            pltpu.make_async_copy(
                proj_ref.at[a, pl.ds(r, margin), pl.ds(0, window)],
                raw_ref.at[a, pl.ds(r, margin), :],
                sem.at[a * 2 + h],
            )
            for a in range(angles)
            for h, r in enumerate(starts)
        ]
        edge_col = pl.multiple_of(jnp.where(col == 0, cols - reach, 0), TILE)
        edge_copy = pltpu.make_async_copy(
            proj_ref.at[:, :, pl.ds(edge_col, reach)], edge_ref, sem.at[2 * angles]
        )
        for copy in copies:
            copy.start()
        edge_copy.start()
        build_band(taps_ref, band_ref)
        for copy in copies:
            copy.wait()
        for h, r in enumerate(starts):
            weigh(raw_ref, weighted_ref, h, r, slab * rows, col * cols, sizes, 0, window)
        for h, out_ref in enumerate(outs):
            filter_columns(
                [(reach, width)],
                (first_half, second_half)[h],
                weighted_ref,
                None,
                None,
                band_ref,
                out_ref,
                2 * STACK,
            )
        edge_copy.wait()

    band, edge, *first_out = kernel_call(
        first_kernel,
        [bf16(length, BLOCK), bf16(angles, rows, reach)] + [bf16(part, width)] * early,
        (projections, filter_taps.reshape(taps // TILE, TILE)),
        2 * early * part * length * width,
        scratch=[
            pltpu.VMEM((angles, rows, window), jnp.bfloat16),
            pltpu.VMEM((early * part, window), jnp.bfloat16),
            pltpu.SemaphoreType.DMA((2 * angles + 1,)),
        ],
        name="first_columns",
        specs=[HELD, VMEM],
        grant=FIRST_VMEM_BYTES,
    )

    up = [(i, (i + 1) % slabs) for i in range(slabs - 1)]
    down = [(j, i) for i, j in up]

    def exchange(sends):
        if both:
            return [lax.ppermute(sends[0], "slab", up + down)]
        return [lax.ppermute(sends[0], "slab", up), lax.ppermute(sends[1], "slab", down)]

    assert sides == 2
    received = lax.ppermute(edge, "col", [(0, 1), (1, 0)])
    halo_rows = [exchange(first_out)]

    def write_weights(first_ref, index_ref, frac_ref, own_ref, halo_ref):
        slab = lax.axis_index("slab")
        angle = lax.axis_index("angle")
        if both:
            bases = [jnp.where(slab == 0, rows, rows - margin)]
        else:
            bases = [slab * rows - margin, (slab + 1) * rows]

        def weights(a, base):
            slot = lax.broadcasted_iota(jnp.int32, (margin, depth), 0) + base
            position = index_ref[a] + first_ref[a]
            frac = frac_ref[a]
            high = frac.astype(jnp.bfloat16).astype(jnp.float32)
            low = (1.0 - frac).astype(jnp.bfloat16).astype(jnp.float32)
            return jnp.where(slot == position, low, 0.0) + jnp.where(slot == position + 1, high, 0.0)

        here = [slab * rows + r for r in half_rows(slab)]
        for starts, ref in ((here, own_ref), (bases, halo_ref)):
            table = jnp.concatenate([weights(a, b) for b in starts for a in range(angles)], axis=0)
            turned = table.T.astype(jnp.bfloat16)
            for s in range(line):
                if quick:
                    places = [o.index(s) for o in order]
                    place = places[line - 1]
                    for i in range(line - 1):
                        place = jnp.where(angle == i, places[i], place)
                    at = pl.multiple_of(place * shard, shard)
                else:
                    at = s * shard
                ref[pl.ds(at, shard), :] = turned[s * shard : (s + 1) * shard, :]

    def second_kernel(proj_ref, received_ref, band_ref, first_ref, index_ref, frac_ref,
                      own_ref, halo_ref, *rest):
        outs, (weighted_ref, halo_cols_ref, left_ref, right_ref) = rest[:-4], rest[-4:]
        slab = lax.axis_index("slab")
        col = lax.axis_index("col")
        lower = col == 0
        for h, r in enumerate(half_rows(slab)):
            r = aligned(r)
            weigh(proj_ref, weighted_ref, h, r, slab * rows, col * cols, sizes, 0, cols)
            from_col = jnp.where(lower, cols, col * cols - reach)
            weigh(received_ref, halo_cols_ref, h, r, slab * rows, from_col, sizes, 0, reach)
        none = jnp.zeros(halo_cols_ref.shape, halo_cols_ref.dtype)
        left_ref[...] = jnp.where(lower, none, halo_cols_ref[...])
        right_ref[...] = jnp.where(lower, halo_cols_ref[...], none)
        work = [(chunks[0], second_half)][: 2 - early]
        work += [(chunk, half) for chunk in chunks[1:] for half in (first_half, second_half)]
        for (columns, half), out_ref in zip(work, outs):
            filter_columns(
                columns, half, weighted_ref, left_ref, right_ref, band_ref, out_ref, 2 * STACK
            )
        write_weights(first_ref, index_ref, frac_ref, own_ref, halo_ref)

    shapes = [bf16(part, widths[0])] * (2 - early)
    shapes += [bf16(part, w) for w in widths[1:] for _ in range(2)]
    own_weight, halo_weight, *second_out = kernel_call(
        second_kernel,
        [bf16(depth, 2 * part), bf16(depth, halos * part)] + shapes,
        (projections, received, band, row_first[:, 0], interp_index, interp_frac),
        4 * part * length * (cols - width // 2),
        scratch=[pltpu.VMEM((2 * part, cols), jnp.bfloat16)]
        + [pltpu.VMEM((2 * part, reach), jnp.bfloat16)] * 3,
        name="other_columns",
        specs=[VMEM, VMEM, VMEM, SMEM, VMEM, VMEM],
    )
    filtered = [(*first_out, *second_out[: 2 - early])]
    for at in range(2 - early, len(second_out), 2):
        filtered.append(second_out[at : at + 2])
        halo_rows.append(exchange(second_out[at : at + halos]))

    def project(index, after=()):
        width = widths[index]

        def body(own_ref, halo_ref, *rest):
            sources, outs = rest[: 2 + halos], rest[2 + halos + len(after) :]
            for c in range(0, width, BLOCK):
                cut = slice(c, c + BLOCK)
                own = jnp.concatenate([ref[:, cut] for ref in sources[:2]], axis=0)
                other = [ref[:, cut] for ref in sources[2:]]
                other = other[0] if len(other) == 1 else jnp.concatenate(other, axis=0)
                total = jnp.dot(own_ref[...], own, preferred_element_type=jnp.float32)
                total += jnp.dot(halo_ref[...], other, preferred_element_type=jnp.float32)
                total = total * scale
                at = 0
                for out in outs:
                    out[:, cut] = total[at : at + out.shape[0], :].astype(out.dtype)
                    at += out.shape[0]

        if quick:
            first = [bf16(shard, width)] * 2 if index == len(chunks) - 1 else [bf16(2 * shard, width)]
            shapes = first + [bf16(shard, width), f32(shard, width)]
        else:
            shapes = [f32(depth, width)]
        return kernel_call(
            body,
            shapes,
            (own_weight, halo_weight, *filtered[index], *halo_rows[index], *after),
            2 * depth * (2 + halos) * part * width,
            name="interpolate",
            specs=[VMEM] * (4 + halos) + [HELD] * len(after),
        )

    parts = project(0)

    ends = (angle_index == 0) | (angle_index == line - 1)

    def widen(x):
        return x.astype(jnp.float32)

    def reduce_relayed(pair, far, kept, after=()):
        one = lax.ppermute(pair, "angle", [(0, 1), (1, 0), (2, 3), (3, 2)])

        def body(one_ref, pair_ref, far_ref, *rest):
            relayed_ref, crossed_ref = rest[-2:]
            angle = lax.axis_index("angle")
            end = (angle == 0) | (angle == line - 1)
            near, middle = one_ref[:shard, :], one_ref[shard:, :]
            relayed = widen(far_ref[...]) + jnp.where(end, 0.0, widen(near))
            relayed_ref[...] = relayed.astype(jnp.bfloat16)
            crossed = widen(pair_ref[shard:, :]) + widen(middle)
            crossed_ref[...] = crossed.astype(jnp.bfloat16)

        relayed, crossed = kernel_call(
            body,
            [bf16(*far.shape)] * 2,
            (one, pair, far, *after),
            far.size * 2,
            name="relay",
            specs=[VMEM] * 3 + [HELD] * len(after),
        )
        two = lax.ppermute(relayed, "angle", [(0, 1), (1, 3), (2, 0), (3, 2)])
        three = lax.ppermute(crossed, "angle", [(1, 2), (2, 1), (0, 0), (3, 3)])
        return one, kept + widen(two) + jnp.where(ends, widen(one[:shard]), widen(three))

    def reduce_direct(near, middle, far, kept):
        one = lax.ppermute(near, "angle", [(0, 1), (1, 0), (2, 3), (3, 2)])
        three = lax.ppermute(middle, "angle", [(1, 2), (2, 1), (0, 0), (3, 3)])
        two = lax.ppermute(middle, "angle", [(0, 2), (3, 1), (1, 0), (2, 3)])

        def body(one_ref, three_ref, far_ref, kept_ref, relayed_ref, partial_ref):
            angle = lax.axis_index("angle")
            end = (angle == 0) | (angle == line - 1)
            arrived = widen(one_ref[...])
            relayed = widen(far_ref[...]) + jnp.where(end, 0.0, arrived)
            relayed_ref[...] = relayed.astype(jnp.bfloat16)
            partial_ref[...] = kept_ref[...] + jnp.where(end, arrived, widen(three_ref[...]))

        relayed, partial = kernel_call(
            body, [bf16(*far.shape), f32(*kept.shape)], (one, three, far, kept), far.size * 2,
            name="relay_last",
        )
        four = lax.ppermute(relayed, "angle", [(0, 1), (1, 3), (2, 0), (3, 2)])
        return partial + widen(four) + jnp.where(ends, 0.0, widen(two))

    if quick:
        second = project(1)
        _, result = reduce_relayed(*parts, after=(second[-1],))
        results = [result]
        arrived, result = reduce_relayed(*second)
        results.append(result)
        results.append(reduce_direct(*project(2, (results[0], arrived))))
    else:
        results = [
            lax.psum_scatter(total, "angle", scatter_dimension=0, tiled=True)
            for total in (parts[0], project(1)[0], project(2)[0])
        ]

    pieces = {}
    for segments, result in zip(chunks, results):
        at = 0
        for start, width in segments:
            pieces[start] = result[:, at : at + width]
            at += width
    return jnp.concatenate([pieces[s] for s in sorted(pieces)], axis=1)


def solution(mesh):
    placed = (
        P(("group", "angle"), "slab", "col"),
        P(),
        P(("group", "angle"), "slab"),
        P(("group", "angle"), "slab", None),
        P(("group", "angle"), "slab", None),
    )
    return jax.shard_map(
        on_device,
        mesh=mesh,
        in_specs=placed,
        out_specs=P(("group", "slab", "angle"), "col"),
        check_vma=False,
    )
```

```python
import math

import jax
import jax.numpy as jnp
from jax import lax
from jax.experimental import pallas as pl
from jax.experimental.pallas import tpu as pltpu
from jax.sharding import PartitionSpec as P

BLOCK = 256
TILE = 128
STACK = 4
VMEM_BYTES = 14 * 1024 * 1024
FIRST_VMEM_BYTES = 103 * 512 * 1024
LINE_ORDER = ((3, 2, 1, 0), (0, 2, 3, 1), (3, 1, 0, 2), (0, 1, 2, 3))

VMEM = pl.BlockSpec(memory_space=pltpu.VMEM)
HELD = pl.BlockSpec(memory_space=pltpu.HBM)
SMEM = pl.BlockSpec(memory_space=pltpu.SMEM)


def kernel_call(
    body, out_shape, args, flops, scratch=(), name=None, specs=None, grant=VMEM_BYTES, carried=()
):
    specs = specs or [VMEM] * len(args)
    moved = sum(a.size * a.dtype.itemsize for a in (*args, *out_shape))
    n_in, n_out, n_through = len(args), len(out_shape), len(carried)

    def kernel(*refs):
        ins, refs = refs[:n_in], refs[n_in + n_through :]
        body(*ins, *refs[:n_out], *refs[n_out + n_through :])

    return pl.pallas_call(
        kernel,
        out_shape=[*out_shape, *(jax.ShapeDtypeStruct(c.shape, c.dtype) for c in carried)],
        in_specs=[*specs, *([HELD] * n_through)],
        out_specs=[VMEM] * n_out + [HELD] * n_through,
        input_output_aliases={n_in + i: n_out + i for i in range(n_through)},
        scratch_shapes=list(scratch),
        compiler_params=pltpu.CompilerParams(vmem_limit_bytes=grant),
        cost_estimate=pl.CostEstimate(flops=flops, bytes_accessed=moved, transcendentals=0),
        name=name,
    )(*args, *carried)


def build_band(taps_ref, band_ref):
    count = taps_ref.shape[0]
    steps, tiles = band_ref.shape[1] // TILE, band_ref.shape[0] // TILE
    zero = jnp.zeros((TILE, TILE), jnp.float32)
    ahead = lax.broadcasted_iota(jnp.int32, (TILE, TILE), 1) >= lax.broadcasted_iota(
        jnp.int32, (TILE, TILE), 0
    )
    taps = taps_ref[...].astype(jnp.float32)

    def shifted(d):
        if not 0 <= d < count:
            return zero
        row = jnp.broadcast_to(taps[d : d + 1, :], (TILE, TILE))
        return pltpu.roll(row, 0, 1, stride=1, stride_axis=0)

    before = zero
    for d in range(-(steps - 1), tiles):
        here = shifted(d)
        block = jnp.where(ahead, here, before).T.astype(jnp.bfloat16)
        before = here
        for c in range(steps):
            if 0 <= d + c < tiles:
                band_ref[(d + c) * TILE : (d + c + 1) * TILE, c * TILE : (c + 1) * TILE] = block


def weigh(proj_ref, weighted_ref, half, row_at, row_start, col_start, sizes, start, stop):
    angles = proj_ref.shape[0]
    total_rows, total_cols, count = sizes
    distance = jnp.float32(total_cols)
    v = lax.broadcasted_iota(jnp.int32, (count, 1), 0) + (row_start + row_at)
    v = v.astype(jnp.float32) - total_rows / 2 + 0.5
    step = BLOCK
    for c in range(start, stop, step):
        u = lax.broadcasted_iota(jnp.int32, (1, step), 1) + (col_start + c)
        u = u.astype(jnp.float32) - total_cols / 2 + 0.5
        factor = distance / jnp.sqrt(distance * distance + u * u + v * v)
        for a in range(angles):
            raw = proj_ref[a, pl.ds(row_at, count), c : c + step].astype(jnp.float32)
            at = (half * angles + a) * count
            weighted_ref[at : at + count, c : c + step] = (raw * factor).astype(jnp.bfloat16)


def filter_columns(columns, rows, weighted_ref, left_ref, right_ref, band_ref, out_ref, stack):
    cols = weighted_ref.shape[1]
    length = band_ref.shape[0]
    reach = (length - BLOCK) // 2
    count = rows.stop - rows.start

    def window(c):
        lo, hi = c - reach, c - reach + length
        pieces = []
        if lo < 0:
            pieces.append(left_ref[rows, reach + lo : reach + min(hi, 0)])
        if max(lo, 0) < min(hi, cols):
            pieces.append(weighted_ref[rows, max(lo, 0) : min(hi, cols)])
        if hi > cols:
            pieces.append(right_ref[rows, max(lo - cols, 0) : hi - cols])
        return pieces[0] if len(pieces) == 1 else jnp.concatenate(pieces, axis=1)

    starts = [c for start, width in columns for c in range(start, start + width, BLOCK)]
    for at in range(0, len(starts), stack):
        group = starts[at : at + stack]
        tall = jnp.concatenate([window(c) for c in group], axis=0)
        result = jnp.dot(tall, band_ref[...], preferred_element_type=jnp.float32)
        result = result.astype(jnp.bfloat16)
        for k in range(len(group)):
            out_ref[:, (at + k) * BLOCK : (at + k + 1) * BLOCK] = result[
                k * count : (k + 1) * count, :
            ]


def bf16(*shape):
    return jax.ShapeDtypeStruct(shape, jnp.bfloat16)


def f32(*shape):
    return jax.ShapeDtypeStruct(shape, jnp.float32)


def chunk_plan(cols, reach):
    assert cols >= 2 * reach + 4 * BLOCK
    cut = reach + (cols - 2 * reach) // 2 // BLOCK * BLOCK
    return [
        [(reach, cut - reach)],
        [(cut, cols - reach - cut)],
        [(0, reach), (cols - reach, reach)],
    ]


def on_device(projections, filter_taps, row_first, interp_index, interp_frac):
    angles, rows, cols = projections.shape
    depth = interp_index.shape[2]
    taps = filter_taps.shape[0]
    reach = taps // 2
    length = taps + BLOCK
    margin = rows // 2
    slabs, line, sides = (lax.axis_size(n) for n in ("slab", "angle", "col"))
    scale = math.pi / (angles * line)
    both = slabs == 2
    halos = 1 if both else 2
    quick = line == 4
    shard = depth // line
    order = LINE_ORDER if quick else (tuple(range(line)),) * line
    total_rows, total_cols = rows * slabs, cols * sides
    chunks = chunk_plan(cols, reach)
    widths = [sum(w for _, w in c) for c in chunks]
    part = angles * margin
    first_half, second_half = slice(0, part), slice(part, 2 * part)
    sizes = (total_rows, total_cols, margin)

    def half_rows(slab):
        if both:
            return jnp.where(slab == 0, margin, 0), jnp.where(slab == 0, 0, margin)
        return margin, 0

    def aligned(row):
        return row if isinstance(row, int) else pl.multiple_of(row, margin)

    ((start, width),) = chunks[0]
    assert start == reach
    window = width + 2 * reach
    early = halos

    def first_kernel(proj_ref, taps_ref, band_ref, edge_ref, *rest):
        outs, (raw_ref, weighted_ref, sem) = rest[:-3], rest[-3:]
        slab = lax.axis_index("slab")
        col = lax.axis_index("col")
        starts = [aligned(r) for r in half_rows(slab)][:early]
        copies = [
            pltpu.make_async_copy(
                proj_ref.at[a, pl.ds(r, margin), pl.ds(0, window)],
                raw_ref.at[a, pl.ds(r, margin), :],
                sem.at[a * 2 + h],
            )
            for a in range(angles)
            for h, r in enumerate(starts)
        ]
        edge_col = pl.multiple_of(jnp.where(col == 0, cols - reach, 0), TILE)
        edge_copy = pltpu.make_async_copy(
            proj_ref.at[:, :, pl.ds(edge_col, reach)], edge_ref, sem.at[2 * angles]
        )
        for copy in copies:
            copy.start()
        edge_copy.start()
        build_band(taps_ref, band_ref)
        for copy in copies:
            copy.wait()
        for h, r in enumerate(starts):
            weigh(raw_ref, weighted_ref, h, r, slab * rows, col * cols, sizes, 0, window)
        for h, out_ref in enumerate(outs):
            filter_columns(
                [(reach, width)],
                (first_half, second_half)[h],
                weighted_ref,
                None,
                None,
                band_ref,
                out_ref,
                2 * STACK,
            )
        edge_copy.wait()

    band, edge, *first_out = kernel_call(
        first_kernel,
        [bf16(length, BLOCK), bf16(angles, rows, reach)] + [bf16(part, width)] * early,
        (projections, filter_taps.reshape(taps // TILE, TILE)),
        2 * early * part * length * width,
        scratch=[
            pltpu.VMEM((angles, rows, window), jnp.bfloat16),
            pltpu.VMEM((early * part, window), jnp.bfloat16),
            pltpu.SemaphoreType.DMA((2 * angles + 1,)),
        ],
        name="first_columns",
        specs=[HELD, VMEM],
        grant=FIRST_VMEM_BYTES,
    )

    up = [(i, (i + 1) % slabs) for i in range(slabs - 1)]
    down = [(j, i) for i, j in up]

    def exchange(sends):
        if both:
            return [lax.ppermute(sends[0], "slab", up + down)]
        return [lax.ppermute(sends[0], "slab", up), lax.ppermute(sends[1], "slab", down)]

    assert sides == 2
    received = lax.ppermute(edge, "col", [(0, 1), (1, 0)])
    halo_rows = [exchange(first_out)]

    def write_weights(first_ref, index_ref, frac_ref, own_ref, halo_ref):
        slab = lax.axis_index("slab")
        angle = lax.axis_index("angle")
        if both:
            bases = [jnp.where(slab == 0, rows, rows - margin)]
        else:
            bases = [slab * rows - margin, (slab + 1) * rows]

        def weights(a, base):
            slot = lax.broadcasted_iota(jnp.int32, (margin, depth), 0) + base
            position = index_ref[a] + first_ref[a]
            frac = frac_ref[a]
            high = frac.astype(jnp.bfloat16).astype(jnp.float32)
            low = (1.0 - frac).astype(jnp.bfloat16).astype(jnp.float32)
            return jnp.where(slot == position, low, 0.0) + jnp.where(slot == position + 1, high, 0.0)

        here = [slab * rows + r for r in half_rows(slab)]
        for starts, ref in ((here, own_ref), (bases, halo_ref)):
            table = jnp.concatenate([weights(a, b) for b in starts for a in range(angles)], axis=0)
            turned = table.T.astype(jnp.bfloat16)
            for s in range(line):
                if quick:
                    places = [o.index(s) for o in order]
                    place = places[line - 1]
                    for i in range(line - 1):
                        place = jnp.where(angle == i, places[i], place)
                    at = pl.multiple_of(place * shard, shard)
                else:
                    at = s * shard
                ref[pl.ds(at, shard), :] = turned[s * shard : (s + 1) * shard, :]

    def second_kernel(proj_ref, received_ref, band_ref, first_ref, index_ref, frac_ref,
                      own_ref, halo_ref, *rest):
        outs, (weighted_ref, halo_cols_ref, left_ref, right_ref) = rest[:-4], rest[-4:]
        slab = lax.axis_index("slab")
        col = lax.axis_index("col")
        lower = col == 0
        for h, r in enumerate(half_rows(slab)):
            r = aligned(r)
            weigh(proj_ref, weighted_ref, h, r, slab * rows, col * cols, sizes, 0, cols)
            from_col = jnp.where(lower, cols, col * cols - reach)
            weigh(received_ref, halo_cols_ref, h, r, slab * rows, from_col, sizes, 0, reach)
        none = jnp.zeros(halo_cols_ref.shape, halo_cols_ref.dtype)
        left_ref[...] = jnp.where(lower, none, halo_cols_ref[...])
        right_ref[...] = jnp.where(lower, halo_cols_ref[...], none)
        work = [(chunks[0], second_half)][: 2 - early]
        work += [(chunk, half) for chunk in chunks[1:] for half in (first_half, second_half)]
        for (columns, half), out_ref in zip(work, outs):
            filter_columns(
                columns, half, weighted_ref, left_ref, right_ref, band_ref, out_ref, 2 * STACK
            )
        write_weights(first_ref, index_ref, frac_ref, own_ref, halo_ref)

    shapes = [bf16(part, widths[0])] * (2 - early)
    shapes += [bf16(part, w) for w in widths[1:] for _ in range(2)]
    own_weight, halo_weight, *second_out = kernel_call(
        second_kernel,
        [bf16(depth, 2 * part), bf16(depth, halos * part)] + shapes,
        (projections, received, band, row_first[:, 0], interp_index, interp_frac),
        4 * part * length * (cols - width // 2),
        scratch=[pltpu.VMEM((2 * part, cols), jnp.bfloat16)]
        + [pltpu.VMEM((2 * part, reach), jnp.bfloat16)] * 3,
        name="other_columns",
        specs=[VMEM, VMEM, VMEM, SMEM, VMEM, VMEM],
    )
    filtered = [(*first_out, *second_out[: 2 - early])]
    for at in range(2 - early, len(second_out), 2):
        filtered.append(second_out[at : at + 2])
    halo_rows.append(exchange(filtered[1][:halos]))

    def project(index, after=(), carried=()):
        width = widths[index]

        def body(own_ref, halo_ref, *rest):
            sources, outs = rest[: 2 + halos], rest[2 + halos + len(after) :]
            for c in range(0, width, BLOCK):
                cut = slice(c, c + BLOCK)
                own = jnp.concatenate([ref[:, cut] for ref in sources[:2]], axis=0)
                other = [ref[:, cut] for ref in sources[2:]]
                other = other[0] if len(other) == 1 else jnp.concatenate(other, axis=0)
                total = jnp.dot(own_ref[...], own, preferred_element_type=jnp.float32)
                total += jnp.dot(halo_ref[...], other, preferred_element_type=jnp.float32)
                total = total * scale
                at = 0
                for out in outs:
                    out[:, cut] = total[at : at + out.shape[0], :].astype(out.dtype)
                    at += out.shape[0]

        if quick:
            first = [bf16(shard, width)] * 2 if index == len(chunks) - 1 else [bf16(2 * shard, width)]
            shapes = first + [bf16(shard, width), f32(shard, width)]
        else:
            shapes = [f32(depth, width)]
        return kernel_call(
            body,
            shapes,
            (own_weight, halo_weight, *filtered[index], *halo_rows[index], *after),
            2 * depth * (2 + halos) * part * width,
            name="interpolate",
            specs=[VMEM] * (4 + halos) + [HELD] * len(after),
            carried=carried,
        )

    def widen(x):
        return x.astype(jnp.float32)

    def at_end():
        angle = lax.axis_index("angle")
        return (angle == 0) | (angle == line - 1)

    def first_hop(pair):
        return lax.ppermute(pair, "angle", [(0, 1), (1, 0), (2, 3), (3, 2)])

    def second_hops(one, pair, far, after=()):
        def body(one_ref, pair_ref, far_ref, *rest):
            relayed_ref, crossed_ref = rest[-2:]
            near, middle = one_ref[:shard, :], one_ref[shard:, :]
            relayed = widen(far_ref[...]) + jnp.where(at_end(), 0.0, widen(near))
            relayed_ref[...] = relayed.astype(jnp.bfloat16)
            crossed = widen(pair_ref[shard:, :]) + widen(middle)
            crossed_ref[...] = crossed.astype(jnp.bfloat16)

        relayed, crossed = kernel_call(
            body,
            [bf16(*far.shape)] * 2,
            (one, pair, far, *after),
            far.size * 2,
            name="relay",
            specs=[VMEM] * 3 + [HELD] * len(after),
        )
        two = lax.ppermute(relayed, "angle", [(0, 1), (1, 3), (2, 0), (3, 2)])
        three = lax.ppermute(crossed, "angle", [(1, 2), (2, 1), (0, 0), (3, 3)])
        return crossed, (two, three)

    def finish(one, two, three, kept, after=()):
        def body(one_ref, two_ref, three_ref, kept_ref, *rest):
            direct = jnp.where(at_end(), widen(one_ref[:shard, :]), widen(three_ref[...]))
            rest[-1][...] = kept_ref[...] + widen(two_ref[...]) + direct

        return kernel_call(
            body,
            [f32(*kept.shape)],
            (one, two, three, kept, *after),
            kept.size * 2,
            name="finish",
            specs=[VMEM] * 4 + [HELD] * len(after),
        )[0]

    def reduce_direct(near, middle, far, kept, after=()):
        one = lax.ppermute(near, "angle", [(0, 1), (1, 0), (2, 3), (3, 2)])
        three = lax.ppermute(middle, "angle", [(1, 2), (2, 1), (0, 0), (3, 3)])
        two = lax.ppermute(middle, "angle", [(0, 2), (3, 1)])

        def body(one_ref, three_ref, far_ref, kept_ref, *rest):
            relayed_ref, partial_ref = rest[-2:]
            end = at_end()
            arrived = widen(one_ref[...])
            relayed = widen(far_ref[...]) + jnp.where(end, 0.0, arrived)
            relayed_ref[...] = relayed.astype(jnp.bfloat16)
            partial_ref[...] = kept_ref[...] + jnp.where(end, arrived, widen(three_ref[...]))

        relayed, partial = kernel_call(
            body, [bf16(*far.shape), f32(*kept.shape)], (one, three, far, kept, *after),
            far.size * 2, name="relay_last", specs=[VMEM] * 4 + [HELD] * len(after),
        )
        four = lax.ppermute(relayed, "angle", [(0, 1), (1, 3), (2, 0), (3, 2)])
        return partial + widen(four) + widen(two)

    if quick:
        pair, far, kept, *sends = project(0, carried=filtered[2][:halos])
        one = first_hop(pair)
        filtered[2][:halos] = sends
        halo_rows.append(exchange(sends))
        next_pair, next_far, next_kept = project(1)
        next_one = first_hop(next_pair)
        _, hops = second_hops(one, pair, far, after=(next_kept,))
        results = [finish(one, *hops, kept, after=(next_one,))]
        crossing, hops = second_hops(next_one, next_pair, next_far)
        last = project(2, after=(results[0], crossing))
        results.append(finish(next_one, *hops, next_kept))
        results.append(reduce_direct(*last, after=(results[1],)))
    else:
        halo_rows.append(exchange(filtered[2][:halos]))
        results = [
            lax.psum_scatter(total, "angle", scatter_dimension=0, tiled=True)
            for total in (project(0)[0], project(1)[0], project(2)[0])
        ]

    pieces = {}
    for segments, result in zip(chunks, results):
        at = 0
        for start, width in segments:
            pieces[start] = result[:, at : at + width]
            at += width
    return jnp.concatenate([pieces[s] for s in sorted(pieces)], axis=1)


def solution(mesh):
    placed = (
        P(("group", "angle"), "slab", "col"),
        P(),
        P(("group", "angle"), "slab"),
        P(("group", "angle"), "slab", None),
        P(("group", "angle"), "slab", None),
    )
    return jax.shard_map(
        on_device,
        mesh=mesh,
        in_specs=placed,
        out_specs=P(("group", "slab", "angle"), "col"),
        check_vma=False,
    )
```

```python
import math

import jax
import jax.numpy as jnp
from jax import lax
from jax.experimental import pallas as pl
from jax.experimental.pallas import tpu as pltpu
from jax.sharding import PartitionSpec as P

BLOCK = 256
TILE = 128
STACK = 4
VMEM_BYTES = 14 * 1024 * 1024
FIRST_VMEM_BYTES = 103 * 512 * 1024
LINE_ORDER = ((3, 2, 1, 0), (0, 2, 3, 1), (3, 1, 0, 2), (0, 1, 2, 3))

VMEM = pl.BlockSpec(memory_space=pltpu.VMEM)
HELD = pl.BlockSpec(memory_space=pltpu.HBM)
SMEM = pl.BlockSpec(memory_space=pltpu.SMEM)


def kernel_call(
    body, out_shape, args, flops, scratch=(), name=None, specs=None, grant=VMEM_BYTES, carried=()
):
    specs = specs or [VMEM] * len(args)
    moved = sum(a.size * a.dtype.itemsize for a in (*args, *out_shape))
    n_in, n_out, n_through = len(args), len(out_shape), len(carried)

    def kernel(*refs):
        ins, refs = refs[:n_in], refs[n_in + n_through :]
        body(*ins, *refs[:n_out], *refs[n_out + n_through :])

    return pl.pallas_call(
        kernel,
        out_shape=[*out_shape, *(jax.ShapeDtypeStruct(c.shape, c.dtype) for c in carried)],
        in_specs=[*specs, *([HELD] * n_through)],
        out_specs=[VMEM] * n_out + [HELD] * n_through,
        input_output_aliases={n_in + i: n_out + i for i in range(n_through)},
        scratch_shapes=list(scratch),
        compiler_params=pltpu.CompilerParams(vmem_limit_bytes=grant),
        cost_estimate=pl.CostEstimate(flops=flops, bytes_accessed=moved, transcendentals=0),
        name=name,
    )(*args, *carried)


def build_band(taps_ref, band_ref):
    count = taps_ref.shape[0]
    steps, tiles = band_ref.shape[1] // TILE, band_ref.shape[0] // TILE
    zero = jnp.zeros((TILE, TILE), jnp.float32)
    ahead = lax.broadcasted_iota(jnp.int32, (TILE, TILE), 1) >= lax.broadcasted_iota(
        jnp.int32, (TILE, TILE), 0
    )
    taps = taps_ref[...].astype(jnp.float32)

    def shifted(d):
        if not 0 <= d < count:
            return zero
        row = jnp.broadcast_to(taps[d : d + 1, :], (TILE, TILE))
        return pltpu.roll(row, 0, 1, stride=1, stride_axis=0)

    before = zero
    for d in range(-(steps - 1), tiles):
        here = shifted(d)
        block = jnp.where(ahead, here, before).T.astype(jnp.bfloat16)
        before = here
        for c in range(steps):
            if 0 <= d + c < tiles:
                band_ref[(d + c) * TILE : (d + c + 1) * TILE, c * TILE : (c + 1) * TILE] = block


def weigh(proj_ref, weighted_ref, half, row_at, row_start, col_start, sizes, start, stop):
    angles = proj_ref.shape[0]
    total_rows, total_cols, count = sizes
    distance = jnp.float32(total_cols)
    v = lax.broadcasted_iota(jnp.int32, (count, 1), 0) + (row_start + row_at)
    v = v.astype(jnp.float32) - total_rows / 2 + 0.5
    step = BLOCK
    for c in range(start, stop, step):
        u = lax.broadcasted_iota(jnp.int32, (1, step), 1) + (col_start + c)
        u = u.astype(jnp.float32) - total_cols / 2 + 0.5
        factor = distance / jnp.sqrt(distance * distance + u * u + v * v)
        for a in range(angles):
            raw = proj_ref[a, pl.ds(row_at, count), c : c + step].astype(jnp.float32)
            at = (half * angles + a) * count
            weighted_ref[at : at + count, c : c + step] = (raw * factor).astype(jnp.bfloat16)


def filter_columns(columns, rows, weighted_ref, left_ref, right_ref, band_ref, out_ref, stack):
    cols = weighted_ref.shape[1]
    length = band_ref.shape[0]
    reach = (length - BLOCK) // 2
    count = rows.stop - rows.start

    def window(c):
        lo, hi = c - reach, c - reach + length
        pieces = []
        if lo < 0:
            pieces.append(left_ref[rows, reach + lo : reach + min(hi, 0)])
        if max(lo, 0) < min(hi, cols):
            pieces.append(weighted_ref[rows, max(lo, 0) : min(hi, cols)])
        if hi > cols:
            pieces.append(right_ref[rows, max(lo - cols, 0) : hi - cols])
        return pieces[0] if len(pieces) == 1 else jnp.concatenate(pieces, axis=1)

    starts = range(columns[0], columns[0] + columns[1], BLOCK)
    for at in range(0, len(starts), stack):
        group = starts[at : at + stack]
        tall = jnp.concatenate([window(c) for c in group], axis=0)
        result = jnp.dot(tall, band_ref[...], preferred_element_type=jnp.float32)
        result = result.astype(jnp.bfloat16)
        for k in range(len(group)):
            out_ref[:, (at + k) * BLOCK : (at + k + 1) * BLOCK] = result[
                k * count : (k + 1) * count, :
            ]


def bf16(*shape):
    return jax.ShapeDtypeStruct(shape, jnp.bfloat16)


def f32(*shape):
    return jax.ShapeDtypeStruct(shape, jnp.float32)


def chunk_plan(cols, reach):
    assert cols >= 2 * reach + 4 * BLOCK
    cut = reach + (cols - 2 * reach) // 2 // BLOCK * BLOCK
    return [(reach, cut - reach), (cut, cols - reach - cut), (0, reach), (cols - reach, reach)]


def on_device(projections, filter_taps, row_first, interp_index, interp_frac):
    angles, rows, cols = projections.shape
    depth = interp_index.shape[2]
    taps = filter_taps.shape[0]
    reach = taps // 2
    length = taps + BLOCK
    margin = rows // 2
    slabs, line, sides = (lax.axis_size(n) for n in ("slab", "angle", "col"))
    scale = math.pi / (angles * line)
    both = slabs == 2
    halos = 1 if both else 2
    quick = line == 4
    shard = depth // line
    order = LINE_ORDER if quick else (tuple(range(line)),) * line
    total_rows, total_cols = rows * slabs, cols * sides
    chunks = chunk_plan(cols, reach)
    widths = [w for _, w in chunks]
    part = angles * margin
    first_half, second_half = slice(0, part), slice(part, 2 * part)
    sizes = (total_rows, total_cols, margin)

    def half_rows(slab):
        if both:
            return jnp.where(slab == 0, margin, 0), jnp.where(slab == 0, 0, margin)
        return margin, 0

    def aligned(row):
        return row if isinstance(row, int) else pl.multiple_of(row, margin)

    start, width = chunks[0]
    assert start == reach
    window = width + 2 * reach
    early = halos

    def first_kernel(proj_ref, taps_ref, band_ref, edge_ref, *rest):
        outs, (raw_ref, weighted_ref, sem) = rest[:-3], rest[-3:]
        slab = lax.axis_index("slab")
        col = lax.axis_index("col")
        starts = [aligned(r) for r in half_rows(slab)][:early]
        copies = [
            pltpu.make_async_copy(
                proj_ref.at[a, pl.ds(r, margin), pl.ds(0, window)],
                raw_ref.at[a, pl.ds(r, margin), :],
                sem.at[a * 2 + h],
            )
            for a in range(angles)
            for h, r in enumerate(starts)
        ]
        edge_col = pl.multiple_of(jnp.where(col == 0, cols - reach, 0), TILE)
        edge_copy = pltpu.make_async_copy(
            proj_ref.at[:, :, pl.ds(edge_col, reach)], edge_ref, sem.at[2 * angles]
        )
        for copy in copies:
            copy.start()
        edge_copy.start()
        build_band(taps_ref, band_ref)
        for copy in copies:
            copy.wait()
        for h, r in enumerate(starts):
            weigh(raw_ref, weighted_ref, h, r, slab * rows, col * cols, sizes, 0, window)
        for h, out_ref in enumerate(outs):
            filter_columns(
                (reach, width),
                (first_half, second_half)[h],
                weighted_ref,
                None,
                None,
                band_ref,
                out_ref,
                2 * STACK,
            )
        edge_copy.wait()

    band, edge, *first_out = kernel_call(
        first_kernel,
        [bf16(length, BLOCK), bf16(angles, rows, reach)] + [bf16(part, width)] * early,
        (projections, filter_taps.reshape(taps // TILE, TILE)),
        2 * early * part * length * width,
        scratch=[
            pltpu.VMEM((angles, rows, window), jnp.bfloat16),
            pltpu.VMEM((early * part, window), jnp.bfloat16),
            pltpu.SemaphoreType.DMA((2 * angles + 1,)),
        ],
        name="first_columns",
        specs=[HELD, VMEM],
        grant=FIRST_VMEM_BYTES,
    )

    up = [(i, (i + 1) % slabs) for i in range(slabs - 1)]
    down = [(j, i) for i, j in up]

    def exchange(sends):
        if both:
            return [lax.ppermute(sends[0], "slab", up + down)]
        return [lax.ppermute(sends[0], "slab", up), lax.ppermute(sends[1], "slab", down)]

    assert sides == 2
    received = lax.ppermute(edge, "col", [(0, 1), (1, 0)])
    halo_rows = [exchange(first_out)]

    def write_weights(first_ref, index_ref, frac_ref, own_ref, halo_ref):
        slab = lax.axis_index("slab")
        angle = lax.axis_index("angle")
        if both:
            bases = [jnp.where(slab == 0, rows, rows - margin)]
        else:
            bases = [slab * rows - margin, (slab + 1) * rows]

        def weights(a, base):
            slot = lax.broadcasted_iota(jnp.int32, (margin, depth), 0) + base
            position = index_ref[a] + first_ref[a]
            frac = frac_ref[a]
            high = frac.astype(jnp.bfloat16).astype(jnp.float32)
            low = (1.0 - frac).astype(jnp.bfloat16).astype(jnp.float32)
            return jnp.where(slot == position, low, 0.0) + jnp.where(slot == position + 1, high, 0.0)

        here = [slab * rows + r for r in half_rows(slab)]
        for starts, ref in ((here, own_ref), (bases, halo_ref)):
            table = jnp.concatenate([weights(a, b) for b in starts for a in range(angles)], axis=0)
            turned = table.T.astype(jnp.bfloat16)
            for s in range(line):
                if quick:
                    places = [o.index(s) for o in order]
                    place = places[line - 1]
                    for i in range(line - 1):
                        place = jnp.where(angle == i, places[i], place)
                    at = pl.multiple_of(place * shard, shard)
                else:
                    at = s * shard
                ref[pl.ds(at, shard), :] = turned[s * shard : (s + 1) * shard, :]

    def second_kernel(proj_ref, received_ref, band_ref, first_ref, index_ref, frac_ref,
                      own_ref, halo_ref, *rest):
        outs, (weighted_ref, halo_cols_ref, left_ref, right_ref) = rest[:-4], rest[-4:]
        slab = lax.axis_index("slab")
        col = lax.axis_index("col")
        lower = col == 0
        for h, r in enumerate(half_rows(slab)):
            r = aligned(r)
            weigh(proj_ref, weighted_ref, h, r, slab * rows, col * cols, sizes, 0, cols)
            from_col = jnp.where(lower, cols, col * cols - reach)
            weigh(received_ref, halo_cols_ref, h, r, slab * rows, from_col, sizes, 0, reach)
        none = jnp.zeros(halo_cols_ref.shape, halo_cols_ref.dtype)
        left_ref[...] = jnp.where(lower, none, halo_cols_ref[...])
        right_ref[...] = jnp.where(lower, halo_cols_ref[...], none)
        work = [(chunks[0], second_half)][: 2 - early]
        work += [(chunk, half) for chunk in chunks[1:] for half in (first_half, second_half)]
        for (columns, half), out_ref in zip(work, outs):
            filter_columns(
                columns, half, weighted_ref, left_ref, right_ref, band_ref, out_ref, 2 * STACK
            )
        write_weights(first_ref, index_ref, frac_ref, own_ref, halo_ref)

    shapes = [bf16(part, widths[0])] * (2 - early)
    shapes += [bf16(part, w) for w in widths[1:] for _ in range(2)]
    own_weight, halo_weight, *second_out = kernel_call(
        second_kernel,
        [bf16(depth, 2 * part), bf16(depth, halos * part)] + shapes,
        (projections, received, band, row_first[:, 0], interp_index, interp_frac),
        4 * part * length * (cols - width // 2),
        scratch=[pltpu.VMEM((2 * part, cols), jnp.bfloat16)]
        + [pltpu.VMEM((2 * part, reach), jnp.bfloat16)] * 3,
        name="other_columns",
        specs=[VMEM, VMEM, VMEM, SMEM, VMEM, VMEM],
    )
    filtered = [(*first_out, *second_out[: 2 - early])]
    for at in range(2 - early, len(second_out), 2):
        filtered.append(second_out[at : at + 2])
        halo_rows.append(exchange(second_out[at : at + halos]))

    def project(index, after=()):
        width = widths[index]

        def body(own_ref, halo_ref, *rest):
            sources, outs = rest[: 2 + halos], rest[2 + halos + len(after) :]
            for c in range(0, width, BLOCK):
                cut = slice(c, c + BLOCK)
                own = jnp.concatenate([ref[:, cut] for ref in sources[:2]], axis=0)
                other = [ref[:, cut] for ref in sources[2:]]
                other = other[0] if len(other) == 1 else jnp.concatenate(other, axis=0)
                total = jnp.dot(own_ref[...], own, preferred_element_type=jnp.float32)
                total += jnp.dot(halo_ref[...], other, preferred_element_type=jnp.float32)
                total = total * scale
                at = 0
                for out in outs:
                    out[:, cut] = total[at : at + out.shape[0], :].astype(out.dtype)
                    at += out.shape[0]

        if quick:
            shapes = [bf16(shard, width)] * 3 + [f32(shard, width)]
        else:
            shapes = [f32(depth, width)]
        return kernel_call(
            body,
            shapes,
            (own_weight, halo_weight, *filtered[index], *halo_rows[index], *after),
            2 * depth * (2 + halos) * part * width,
            name="interpolate",
            specs=[VMEM] * (4 + halos) + [HELD] * len(after),
        )

    def widen(x):
        return x.astype(jnp.float32)

    def at_end():
        angle = lax.axis_index("angle")
        return (angle == 0) | (angle == line - 1)

    def line_sends(near, middle):
        one = lax.ppermute(near, "angle", [(0, 1), (1, 0), (2, 3), (3, 2)])
        three = lax.ppermute(middle, "angle", [(1, 2), (2, 1), (0, 0), (3, 3)])
        two = lax.ppermute(middle, "angle", [(0, 2), (3, 1)])
        return one, three, two

    def relay(one, three, far, kept, after=()):
        def body(one_ref, three_ref, far_ref, kept_ref, *rest):
            relayed_ref, partial_ref = rest[-2:]
            end = at_end()
            arrived = widen(one_ref[...])
            relayed = widen(far_ref[...]) + jnp.where(end, 0.0, arrived)
            relayed_ref[...] = relayed.astype(jnp.bfloat16)
            partial_ref[...] = kept_ref[...] + jnp.where(end, arrived, widen(three_ref[...]))

        relayed, partial = kernel_call(
            body,
            [bf16(*far.shape), f32(*kept.shape)],
            (one, three, far, kept, *after),
            far.size * 2,
            name="relay",
            specs=[VMEM] * 4 + [HELD] * len(after),
        )
        return lax.ppermute(relayed, "angle", [(0, 1), (1, 3), (2, 0), (3, 2)]), partial

    def finish(partial, two, four):
        def body(partial_ref, two_ref, four_ref, out_ref):
            out_ref[...] = partial_ref[...] + widen(two_ref[...]) + widen(four_ref[...])

        return kernel_call(
            body, [f32(*partial.shape)], (partial, two, four), partial.size * 2, name="finish"
        )[0]

    def store(partial, two, four, done, volume):
        def body(partial_ref, two_ref, four_ref, *rest):
            volume_ref, total_ref, sem = rest[-3:]
            total_ref[...] = partial_ref[...] + widen(two_ref[...]) + widen(four_ref[...])
            copies = [
                pltpu.make_async_copy(
                    source, volume_ref.at[:, pl.ds(first, source.shape[1])], sem.at[i]
                )
                for i, (source, (first, _)) in enumerate(
                    [(total_ref, chunks[index]), *zip(rest, (chunks[i] for i, _ in done))]
                )
            ]
            for copy in copies:
                copy.start()
            for copy in copies:
                copy.wait()

        given = [partial, two, four, *(array for _, array in done)]
        index = len(chunks) - 1 if volume is not None else len(chunks) - 2
        shape = f32(shard, cols)
        return pl.pallas_call(
            body,
            out_shape=shape,
            in_specs=[VMEM] * len(given) + [HELD] * (volume is not None),
            out_specs=HELD,
            input_output_aliases={len(given): 0} if volume is not None else {},
            scratch_shapes=[
                pltpu.VMEM(partial.shape, jnp.float32),
                pltpu.SemaphoreType.DMA((1 + len(done),)),
            ],
            compiler_params=pltpu.CompilerParams(vmem_limit_bytes=VMEM_BYTES),
            name="store",
        )(*given, *([] if volume is None else [volume]))

    if not quick:
        sums = [
            lax.psum_scatter(project(i)[0], "angle", scatter_dimension=0, tiled=True)
            for i in range(len(chunks))
        ]
        return jnp.concatenate([sums[i] for i in sorted(range(len(chunks)), key=chunks.__getitem__)], 1)

    last = len(chunks) - 1
    near, middle, far, kept = project(0)
    sent = line_sends(near, middle)
    done, volume = [], None
    for j in range(last + 1):
        one, three, two = sent
        here, after = (far, kept), ()
        if j < last:
            near, middle, far, kept = project(j + 1, after=[array for _, array in done[-1:]])
            sent = line_sends(near, middle)
            after = (kept, two) if j == 0 else (kept,)
        four, partial = relay(one, three, *here, after=after)
        if j < last - 1:
            done.append((j, finish(partial, two, four)))
        else:
            volume = store(partial, two, four, done if j < last else [], volume)
    return volume


def solution(mesh):
    placed = (
        P(("group", "angle"), "slab", "col"),
        P(),
        P(("group", "angle"), "slab"),
        P(("group", "angle"), "slab", None),
        P(("group", "angle"), "slab", None),
    )
    return jax.shard_map(
        on_device,
        mesh=mesh,
        in_specs=placed,
        out_specs=P(("group", "slab", "angle"), "col"),
        check_vma=False,
    )
```

```python
import math

import jax
import jax.numpy as jnp
from jax import lax
from jax.experimental import pallas as pl
from jax.experimental.pallas import tpu as pltpu
from jax.sharding import PartitionSpec as P

BLOCK = 256
TILE = 128
STACK = 4
VMEM_BYTES = 14 * 1024 * 1024
FIRST_VMEM_BYTES = 103 * 512 * 1024
LINE_ORDER = ((3, 2, 1, 0), (0, 2, 3, 1), (3, 1, 0, 2), (0, 1, 2, 3))

VMEM = pl.BlockSpec(memory_space=pltpu.VMEM)
HELD = pl.BlockSpec(memory_space=pltpu.HBM)
SMEM = pl.BlockSpec(memory_space=pltpu.SMEM)


def kernel_call(
    body, out_shape, args, flops, scratch=(), name=None, specs=None, grant=VMEM_BYTES, carried=()
):
    specs = specs or [VMEM] * len(args)
    moved = sum(a.size * a.dtype.itemsize for a in (*args, *out_shape))
    n_in, n_out, n_through = len(args), len(out_shape), len(carried)

    def kernel(*refs):
        ins, refs = refs[:n_in], refs[n_in + n_through :]
        body(*ins, *refs[:n_out], *refs[n_out + n_through :])

    return pl.pallas_call(
        kernel,
        out_shape=[*out_shape, *(jax.ShapeDtypeStruct(c.shape, c.dtype) for c in carried)],
        in_specs=[*specs, *([HELD] * n_through)],
        out_specs=[VMEM] * n_out + [HELD] * n_through,
        input_output_aliases={n_in + i: n_out + i for i in range(n_through)},
        scratch_shapes=list(scratch),
        compiler_params=pltpu.CompilerParams(vmem_limit_bytes=grant),
        cost_estimate=pl.CostEstimate(flops=flops, bytes_accessed=moved, transcendentals=0),
        name=name,
    )(*args, *carried)


def build_band(taps_ref, band_ref):
    count = taps_ref.shape[0]
    steps, tiles = band_ref.shape[1] // TILE, band_ref.shape[0] // TILE
    zero = jnp.zeros((TILE, TILE), jnp.float32)
    ahead = lax.broadcasted_iota(jnp.int32, (TILE, TILE), 1) >= lax.broadcasted_iota(
        jnp.int32, (TILE, TILE), 0
    )
    taps = taps_ref[...].astype(jnp.float32)

    def shifted(d):
        if not 0 <= d < count:
            return zero
        row = jnp.broadcast_to(taps[d : d + 1, :], (TILE, TILE))
        return pltpu.roll(row, 0, 1, stride=1, stride_axis=0)

    before = zero
    for d in range(-(steps - 1), tiles):
        here = shifted(d)
        block = jnp.where(ahead, here, before).T.astype(jnp.bfloat16)
        before = here
        for c in range(steps):
            if 0 <= d + c < tiles:
                band_ref[(d + c) * TILE : (d + c + 1) * TILE, c * TILE : (c + 1) * TILE] = block


def weigh(proj_ref, weighted_ref, half, row_at, row_start, col_start, sizes, start, stop):
    angles = proj_ref.shape[0]
    total_rows, total_cols, count = sizes
    distance = jnp.float32(total_cols)
    v = lax.broadcasted_iota(jnp.int32, (count, 1), 0) + (row_start + row_at)
    v = v.astype(jnp.float32) - total_rows / 2 + 0.5
    step = BLOCK
    for c in range(start, stop, step):
        u = lax.broadcasted_iota(jnp.int32, (1, step), 1) + (col_start + c)
        u = u.astype(jnp.float32) - total_cols / 2 + 0.5
        factor = distance / jnp.sqrt(distance * distance + u * u + v * v)
        for a in range(angles):
            raw = proj_ref[a, pl.ds(row_at, count), c : c + step].astype(jnp.float32)
            at = (half * angles + a) * count
            weighted_ref[at : at + count, c : c + step] = (raw * factor).astype(jnp.bfloat16)


def filter_columns(columns, rows, weighted_ref, left_ref, right_ref, band_ref, out_ref, stack):
    cols = weighted_ref.shape[1]
    length = band_ref.shape[0]
    reach = (length - BLOCK) // 2
    count = rows.stop - rows.start

    def window(c):
        lo, hi = c - reach, c - reach + length
        pieces = []
        if lo < 0:
            pieces.append(left_ref[rows, reach + lo : reach + min(hi, 0)])
        if max(lo, 0) < min(hi, cols):
            pieces.append(weighted_ref[rows, max(lo, 0) : min(hi, cols)])
        if hi > cols:
            pieces.append(right_ref[rows, max(lo - cols, 0) : hi - cols])
        return pieces[0] if len(pieces) == 1 else jnp.concatenate(pieces, axis=1)

    starts = range(columns[0], columns[0] + columns[1], BLOCK)
    for at in range(0, len(starts), stack):
        group = starts[at : at + stack]
        tall = jnp.concatenate([window(c) for c in group], axis=0)
        result = jnp.dot(tall, band_ref[...], preferred_element_type=jnp.float32)
        result = result.astype(jnp.bfloat16)
        for k in range(len(group)):
            out_ref[:, (at + k) * BLOCK : (at + k + 1) * BLOCK] = result[
                k * count : (k + 1) * count, :
            ]


def bf16(*shape):
    return jax.ShapeDtypeStruct(shape, jnp.bfloat16)


def f32(*shape):
    return jax.ShapeDtypeStruct(shape, jnp.float32)


def chunk_plan(cols, reach):
    assert cols >= 2 * reach + 4 * BLOCK
    cut = reach + (cols - 2 * reach) // 2 // BLOCK * BLOCK
    return [(reach, cut - reach), (cut, cols - reach - cut), (0, reach), (cols - reach, reach)]


def on_device(projections, filter_taps, row_first, interp_index, interp_frac):
    angles, rows, cols = projections.shape
    depth = interp_index.shape[2]
    taps = filter_taps.shape[0]
    reach = taps // 2
    length = taps + BLOCK
    margin = rows // 2
    slabs, line, sides = (lax.axis_size(n) for n in ("slab", "angle", "col"))
    scale = math.pi / (angles * line)
    both = slabs == 2
    halos = 1 if both else 2
    quick = line == 4
    shard = depth // line
    order = LINE_ORDER if quick else (tuple(range(line)),) * line
    total_rows, total_cols = rows * slabs, cols * sides
    chunks = chunk_plan(cols, reach)
    widths = [w for _, w in chunks]
    part = angles * margin
    first_half, second_half = slice(0, part), slice(part, 2 * part)
    sizes = (total_rows, total_cols, margin)

    def half_rows(slab):
        if both:
            return jnp.where(slab == 0, margin, 0), jnp.where(slab == 0, 0, margin)
        return margin, 0

    def aligned(row):
        return row if isinstance(row, int) else pl.multiple_of(row, margin)

    start, width = chunks[0]
    assert start == reach
    window = width + 2 * reach
    early = halos

    def first_kernel(proj_ref, taps_ref, band_ref, edge_ref, *rest):
        outs, (raw_ref, weighted_ref, sem) = rest[:-3], rest[-3:]
        slab = lax.axis_index("slab")
        col = lax.axis_index("col")
        starts = [aligned(r) for r in half_rows(slab)][:early]
        copies = [
            pltpu.make_async_copy(
                proj_ref.at[a, pl.ds(r, margin), pl.ds(0, window)],
                raw_ref.at[a, pl.ds(r, margin), :],
                sem.at[a * 2 + h],
            )
            for a in range(angles)
            for h, r in enumerate(starts)
        ]
        edge_col = pl.multiple_of(jnp.where(col == 0, cols - reach, 0), TILE)
        edge_copy = pltpu.make_async_copy(
            proj_ref.at[:, :, pl.ds(edge_col, reach)], edge_ref, sem.at[2 * angles]
        )
        for copy in copies:
            copy.start()
        edge_copy.start()
        build_band(taps_ref, band_ref)
        for copy in copies:
            copy.wait()
        for h, r in enumerate(starts):
            weigh(raw_ref, weighted_ref, h, r, slab * rows, col * cols, sizes, 0, window)
        for h, out_ref in enumerate(outs):
            filter_columns(
                (reach, width),
                (first_half, second_half)[h],
                weighted_ref,
                None,
                None,
                band_ref,
                out_ref,
                2 * STACK,
            )
        edge_copy.wait()

    band, edge, *first_out = kernel_call(
        first_kernel,
        [bf16(length, BLOCK), bf16(angles, rows, reach)] + [bf16(part, width)] * early,
        (projections, filter_taps.reshape(taps // TILE, TILE)),
        2 * early * part * length * width,
        scratch=[
            pltpu.VMEM((angles, rows, window), jnp.bfloat16),
            pltpu.VMEM((early * part, window), jnp.bfloat16),
            pltpu.SemaphoreType.DMA((2 * angles + 1,)),
        ],
        name="first_columns",
        specs=[HELD, VMEM],
        grant=FIRST_VMEM_BYTES,
    )

    up = [(i, (i + 1) % slabs) for i in range(slabs - 1)]
    down = [(j, i) for i, j in up]

    def exchange(sends):
        if both:
            return [lax.ppermute(sends[0], "slab", up + down)]
        return [lax.ppermute(sends[0], "slab", up), lax.ppermute(sends[1], "slab", down)]

    assert sides == 2
    received = lax.ppermute(edge, "col", [(0, 1), (1, 0)])
    halo_rows = [exchange(first_out)]

    def write_weights(first_ref, index_ref, frac_ref, own_ref, halo_ref):
        slab = lax.axis_index("slab")
        angle = lax.axis_index("angle")
        if both:
            bases = [jnp.where(slab == 0, rows, rows - margin)]
        else:
            bases = [slab * rows - margin, (slab + 1) * rows]

        def weights(a, base):
            slot = lax.broadcasted_iota(jnp.int32, (margin, depth), 0) + base
            position = index_ref[a] + first_ref[a]
            frac = frac_ref[a]
            high = frac.astype(jnp.bfloat16).astype(jnp.float32)
            low = (1.0 - frac).astype(jnp.bfloat16).astype(jnp.float32)
            return jnp.where(slot == position, low, 0.0) + jnp.where(slot == position + 1, high, 0.0)

        here = [slab * rows + r for r in half_rows(slab)]
        for starts, ref in ((here, own_ref), (bases, halo_ref)):
            table = jnp.concatenate([weights(a, b) for b in starts for a in range(angles)], axis=0)
            turned = table.T.astype(jnp.bfloat16)
            for s in range(line):
                if quick:
                    places = [o.index(s) for o in order]
                    place = places[line - 1]
                    for i in range(line - 1):
                        place = jnp.where(angle == i, places[i], place)
                    at = pl.multiple_of(place * shard, shard)
                else:
                    at = s * shard
                ref[pl.ds(at, shard), :] = turned[s * shard : (s + 1) * shard, :]

    def second_kernel(proj_ref, received_ref, band_ref, first_ref, index_ref, frac_ref,
                      own_ref, halo_ref, *rest):
        outs, (weighted_ref, halo_cols_ref, left_ref, right_ref) = rest[:-4], rest[-4:]
        slab = lax.axis_index("slab")
        col = lax.axis_index("col")
        lower = col == 0
        for h, r in enumerate(half_rows(slab)):
            r = aligned(r)
            weigh(proj_ref, weighted_ref, h, r, slab * rows, col * cols, sizes, 0, cols)
            from_col = jnp.where(lower, cols, col * cols - reach)
            weigh(received_ref, halo_cols_ref, h, r, slab * rows, from_col, sizes, 0, reach)
        none = jnp.zeros(halo_cols_ref.shape, halo_cols_ref.dtype)
        left_ref[...] = jnp.where(lower, none, halo_cols_ref[...])
        right_ref[...] = jnp.where(lower, halo_cols_ref[...], none)
        work = [(chunks[0], second_half)][: 2 - early]
        work += [(chunk, half) for chunk in chunks[1:] for half in (first_half, second_half)]
        for (columns, half), out_ref in zip(work, outs):
            filter_columns(
                columns, half, weighted_ref, left_ref, right_ref, band_ref, out_ref, 2 * STACK
            )
        write_weights(first_ref, index_ref, frac_ref, own_ref, halo_ref)

    shapes = [bf16(part, widths[0])] * (2 - early)
    shapes += [bf16(part, w) for w in widths[1:] for _ in range(2)]
    own_weight, halo_weight, *second_out = kernel_call(
        second_kernel,
        [bf16(depth, 2 * part), bf16(depth, halos * part)] + shapes,
        (projections, received, band, row_first[:, 0], interp_index, interp_frac),
        4 * part * length * (cols - width // 2),
        scratch=[pltpu.VMEM((2 * part, cols), jnp.bfloat16)]
        + [pltpu.VMEM((2 * part, reach), jnp.bfloat16)] * 3,
        name="other_columns",
        specs=[VMEM, VMEM, VMEM, SMEM, VMEM, VMEM],
    )
    filtered = [(*first_out, *second_out[: 2 - early])]
    for at in range(2 - early, len(second_out), 2):
        filtered.append(second_out[at : at + 2])
        halo_rows.append(exchange(second_out[at : at + halos]))

    def project(index, after=()):
        width = widths[index]

        def body(own_ref, halo_ref, *rest):
            sources, outs = rest[: 2 + halos], rest[2 + halos + len(after) :]
            for c in range(0, width, BLOCK):
                cut = slice(c, c + BLOCK)
                own = jnp.concatenate([ref[:, cut] for ref in sources[:2]], axis=0)
                other = [ref[:, cut] for ref in sources[2:]]
                other = other[0] if len(other) == 1 else jnp.concatenate(other, axis=0)
                total = jnp.dot(own_ref[...], own, preferred_element_type=jnp.float32)
                total += jnp.dot(halo_ref[...], other, preferred_element_type=jnp.float32)
                total = total * scale
                at = 0
                for out in outs:
                    out[:, cut] = total[at : at + out.shape[0], :].astype(out.dtype)
                    at += out.shape[0]

        if quick:
            shapes = [bf16(shard, width)] * 3 + [f32(shard, width)]
        else:
            shapes = [f32(depth, width)]
        return kernel_call(
            body,
            shapes,
            (own_weight, halo_weight, *filtered[index], *halo_rows[index], *after),
            2 * depth * (2 + halos) * part * width,
            name="interpolate",
            specs=[VMEM] * (4 + halos) + [HELD] * len(after),
        )

    def widen(x):
        return x.astype(jnp.float32)

    def at_end():
        angle = lax.axis_index("angle")
        return (angle == 0) | (angle == line - 1)

    def line_sends(near, middle):
        one = lax.ppermute(near, "angle", [(0, 1), (1, 0), (2, 3), (3, 2)])
        three = lax.ppermute(middle, "angle", [(1, 2), (2, 1), (0, 0), (3, 3)])
        two = lax.ppermute(middle, "angle", [(0, 2), (3, 1), (1, 0), (2, 3)])
        return one, three, two

    def relay(one, three, far, kept, after=()):
        def body(one_ref, three_ref, far_ref, kept_ref, *rest):
            relayed_ref, partial_ref = rest[-2:]
            end = at_end()
            arrived = widen(one_ref[...])
            relayed = widen(far_ref[...]) + jnp.where(end, 0.0, arrived)
            relayed_ref[...] = relayed.astype(jnp.bfloat16)
            partial_ref[...] = kept_ref[...] + jnp.where(end, arrived, widen(three_ref[...]))

        relayed, partial = kernel_call(
            body,
            [bf16(*far.shape), f32(*kept.shape)],
            (one, three, far, kept, *after),
            far.size * 2,
            name="relay",
            specs=[VMEM] * 4 + [HELD] * len(after),
        )
        return lax.ppermute(relayed, "angle", [(0, 1), (1, 3), (2, 0), (3, 2)]), partial

    def total(partial_ref, two_ref, four_ref):
        direct = jnp.where(at_end(), 0.0, widen(two_ref[...]))
        return partial_ref[...] + direct + widen(four_ref[...])

    def finish(partial, two, four):
        def body(partial_ref, two_ref, four_ref, out_ref):
            out_ref[...] = total(partial_ref, two_ref, four_ref)

        return kernel_call(
            body, [f32(*partial.shape)], (partial, two, four), partial.size * 2, name="finish"
        )[0]

    def store(partial, two, four, done, volume):
        def body(partial_ref, two_ref, four_ref, *rest):
            volume_ref, total_ref, sem = rest[-3:]
            total_ref[...] = total(partial_ref, two_ref, four_ref)
            copies = [
                pltpu.make_async_copy(
                    source, volume_ref.at[:, pl.ds(first, source.shape[1])], sem.at[i]
                )
                for i, (source, (first, _)) in enumerate(
                    [(total_ref, chunks[index]), *zip(rest, (chunks[i] for i, _ in done))]
                )
            ]
            for copy in copies:
                copy.start()
            for copy in copies:
                copy.wait()

        given = [partial, two, four, *(array for _, array in done)]
        index = len(chunks) - 1 if volume is not None else len(chunks) - 2
        shape = f32(shard, cols)
        return pl.pallas_call(
            body,
            out_shape=shape,
            in_specs=[VMEM] * len(given) + [HELD] * (volume is not None),
            out_specs=HELD,
            input_output_aliases={len(given): 0} if volume is not None else {},
            scratch_shapes=[
                pltpu.VMEM(partial.shape, jnp.float32),
                pltpu.SemaphoreType.DMA((1 + len(done),)),
            ],
            compiler_params=pltpu.CompilerParams(vmem_limit_bytes=VMEM_BYTES),
            name="store",
        )(*given, *([] if volume is None else [volume]))

    if not quick:
        sums = [
            lax.psum_scatter(project(i)[0], "angle", scatter_dimension=0, tiled=True)
            for i in range(len(chunks))
        ]
        return jnp.concatenate([sums[i] for i in sorted(range(len(chunks)), key=chunks.__getitem__)], 1)

    last = len(chunks) - 1
    near, middle, far, kept = project(0)
    sent = line_sends(near, middle)
    done, volume = [], None
    for j in range(last + 1):
        one, three, two = sent
        here, after = (far, kept), ()
        if j < last:
            near, middle, far, kept = project(j + 1, after=[array for _, array in done[-1:]])
            sent = line_sends(near, middle)
            after = (kept, two) if j == 0 else (kept,)
        four, partial = relay(one, three, *here, after=after)
        if j < last - 1:
            done.append((j, finish(partial, two, four)))
        else:
            volume = store(partial, two, four, done if j < last else [], volume)
    return volume


def solution(mesh):
    placed = (
        P(("group", "angle"), "slab", "col"),
        P(),
        P(("group", "angle"), "slab"),
        P(("group", "angle"), "slab", None),
        P(("group", "angle"), "slab", None),
    )
    return jax.shard_map(
        on_device,
        mesh=mesh,
        in_specs=placed,
        out_specs=P(("group", "slab", "angle"), "col"),
        check_vma=False,
    )
```

```python
import math

import jax
import jax.numpy as jnp
from jax import lax
from jax.experimental import pallas as pl
from jax.experimental.pallas import tpu as pltpu
from jax.sharding import PartitionSpec as P

BLOCK = 256
TILE = 128
STACK = 4
WEIGHTS = (40000, 40000, 1, 1)
VMEM_BYTES = 14 * 1024 * 1024
FIRST_VMEM_BYTES = 103 * 512 * 1024
LINE_ORDER = ((3, 2, 1, 0), (0, 2, 3, 1), (3, 1, 0, 2), (0, 1, 2, 3))

VMEM = pl.BlockSpec(memory_space=pltpu.VMEM)
HELD = pl.BlockSpec(memory_space=pltpu.HBM)
SMEM = pl.BlockSpec(memory_space=pltpu.SMEM)


def kernel_call(
    body, out_shape, args, flops, scratch=(), name=None, specs=None, grant=VMEM_BYTES, carried=()
):
    specs = specs or [VMEM] * len(args)
    moved = sum(a.size * a.dtype.itemsize for a in (*args, *out_shape))
    n_in, n_out, n_through = len(args), len(out_shape), len(carried)

    def kernel(*refs):
        ins, refs = refs[:n_in], refs[n_in + n_through :]
        body(*ins, *refs[:n_out], *refs[n_out + n_through :])

    return pl.pallas_call(
        kernel,
        out_shape=[*out_shape, *(jax.ShapeDtypeStruct(c.shape, c.dtype) for c in carried)],
        in_specs=[*specs, *([HELD] * n_through)],
        out_specs=[VMEM] * n_out + [HELD] * n_through,
        input_output_aliases={n_in + i: n_out + i for i in range(n_through)},
        scratch_shapes=list(scratch),
        compiler_params=pltpu.CompilerParams(vmem_limit_bytes=grant),
        cost_estimate=pl.CostEstimate(flops=flops, bytes_accessed=moved, transcendentals=0),
        name=name,
    )(*args, *carried)


def build_band(taps_ref, band_ref):
    count = taps_ref.shape[0]
    steps, tiles = band_ref.shape[1] // TILE, band_ref.shape[0] // TILE
    zero = jnp.zeros((TILE, TILE), jnp.float32)
    ahead = lax.broadcasted_iota(jnp.int32, (TILE, TILE), 1) >= lax.broadcasted_iota(
        jnp.int32, (TILE, TILE), 0
    )
    taps = taps_ref[...].astype(jnp.float32)

    def shifted(d):
        if not 0 <= d < count:
            return zero
        row = jnp.broadcast_to(taps[d : d + 1, :], (TILE, TILE))
        return pltpu.roll(row, 0, 1, stride=1, stride_axis=0)

    before = zero
    for d in range(-(steps - 1), tiles):
        here = shifted(d)
        block = jnp.where(ahead, here, before).T.astype(jnp.bfloat16)
        before = here
        for c in range(steps):
            if 0 <= d + c < tiles:
                band_ref[(d + c) * TILE : (d + c + 1) * TILE, c * TILE : (c + 1) * TILE] = block


def weigh(proj_ref, weighted_ref, half, row_at, row_start, col_start, sizes, start, stop):
    angles = proj_ref.shape[0]
    total_rows, total_cols, count = sizes
    distance = jnp.float32(total_cols)
    v = lax.broadcasted_iota(jnp.int32, (count, 1), 0) + (row_start + row_at)
    v = v.astype(jnp.float32) - total_rows / 2 + 0.5
    step = BLOCK
    for c in range(start, stop, step):
        u = lax.broadcasted_iota(jnp.int32, (1, step), 1) + (col_start + c)
        u = u.astype(jnp.float32) - total_cols / 2 + 0.5
        factor = distance / jnp.sqrt(distance * distance + u * u + v * v)
        for a in range(angles):
            raw = proj_ref[a, pl.ds(row_at, count), c : c + step].astype(jnp.float32)
            at = (half * angles + a) * count
            weighted_ref[at : at + count, c : c + step] = (raw * factor).astype(jnp.bfloat16)


def filter_columns(columns, rows, weighted_ref, left_ref, right_ref, band_ref, out_ref, stack):
    cols = weighted_ref.shape[1]
    length = band_ref.shape[0]
    reach = (length - BLOCK) // 2
    count = rows.stop - rows.start

    def window(c):
        lo, hi = c - reach, c - reach + length
        pieces = []
        if lo < 0:
            pieces.append(left_ref[rows, reach + lo : reach + min(hi, 0)])
        if max(lo, 0) < min(hi, cols):
            pieces.append(weighted_ref[rows, max(lo, 0) : min(hi, cols)])
        if hi > cols:
            pieces.append(right_ref[rows, max(lo - cols, 0) : hi - cols])
        return pieces[0] if len(pieces) == 1 else jnp.concatenate(pieces, axis=1)

    starts = range(columns[0], columns[0] + columns[1], BLOCK)
    for at in range(0, len(starts), stack):
        group = starts[at : at + stack]
        tall = jnp.concatenate([window(c) for c in group], axis=0)
        result = jnp.dot(tall, band_ref[...], preferred_element_type=jnp.float32)
        result = result.astype(jnp.bfloat16)
        for k in range(len(group)):
            out_ref[:, (at + k) * BLOCK : (at + k + 1) * BLOCK] = result[
                k * count : (k + 1) * count, :
            ]


def bf16(*shape):
    return jax.ShapeDtypeStruct(shape, jnp.bfloat16)


def f32(*shape):
    return jax.ShapeDtypeStruct(shape, jnp.float32)


def chunk_plan(cols, reach):
    assert cols >= 2 * reach + 4 * BLOCK
    cut = reach + (cols - 2 * reach) // 2 // BLOCK * BLOCK
    return [(reach, cut - reach), (cut, cols - reach - cut), (0, reach), (cols - reach, reach)]


def on_device(projections, filter_taps, row_first, interp_index, interp_frac):
    angles, rows, cols = projections.shape
    depth = interp_index.shape[2]
    taps = filter_taps.shape[0]
    reach = taps // 2
    length = taps + BLOCK
    margin = rows // 2
    slabs, line, sides = (lax.axis_size(n) for n in ("slab", "angle", "col"))
    scale = math.pi / (angles * line)
    both = slabs == 2
    halos = 1 if both else 2
    quick = line == 4
    shard = depth // line
    order = LINE_ORDER if quick else (tuple(range(line)),) * line
    total_rows, total_cols = rows * slabs, cols * sides
    chunks = chunk_plan(cols, reach)
    widths = [w for _, w in chunks]
    part = angles * margin
    first_half, second_half = slice(0, part), slice(part, 2 * part)
    sizes = (total_rows, total_cols, margin)

    def half_rows(slab):
        if both:
            return jnp.where(slab == 0, margin, 0), jnp.where(slab == 0, 0, margin)
        return margin, 0

    def aligned(row):
        return row if isinstance(row, int) else pl.multiple_of(row, margin)

    start, width = chunks[0]
    assert start == reach
    window = width + 2 * reach
    early = halos

    def first_kernel(proj_ref, taps_ref, band_ref, edge_ref, *rest):
        outs, (raw_ref, weighted_ref, sem) = rest[:-3], rest[-3:]
        slab = lax.axis_index("slab")
        col = lax.axis_index("col")
        starts = [aligned(r) for r in half_rows(slab)][:early]
        copies = [
            pltpu.make_async_copy(
                proj_ref.at[a, pl.ds(r, margin), pl.ds(0, window)],
                raw_ref.at[a, pl.ds(r, margin), :],
                sem.at[a * 2 + h],
            )
            for a in range(angles)
            for h, r in enumerate(starts)
        ]
        edge_col = pl.multiple_of(jnp.where(col == 0, cols - reach, 0), TILE)
        edge_copy = pltpu.make_async_copy(
            proj_ref.at[:, :, pl.ds(edge_col, reach)], edge_ref, sem.at[2 * angles]
        )
        for copy in copies:
            copy.start()
        edge_copy.start()
        build_band(taps_ref, band_ref)
        for copy in copies:
            copy.wait()
        for h, r in enumerate(starts):
            weigh(raw_ref, weighted_ref, h, r, slab * rows, col * cols, sizes, 0, window)
        for h, out_ref in enumerate(outs):
            filter_columns(
                (reach, width),
                (first_half, second_half)[h],
                weighted_ref,
                None,
                None,
                band_ref,
                out_ref,
                2 * STACK,
            )
        edge_copy.wait()

    band, edge, *first_out = kernel_call(
        first_kernel,
        [bf16(length, BLOCK), bf16(angles, rows, reach)] + [bf16(part, width)] * early,
        (projections, filter_taps.reshape(taps // TILE, TILE)),
        2 * early * part * length * width,
        scratch=[
            pltpu.VMEM((angles, rows, window), jnp.bfloat16),
            pltpu.VMEM((early * part, window), jnp.bfloat16),
            pltpu.SemaphoreType.DMA((2 * angles + 1,)),
        ],
        name="first_columns",
        specs=[HELD, VMEM],
        grant=FIRST_VMEM_BYTES,
    )

    up = [(i, (i + 1) % slabs) for i in range(slabs - 1)]
    down = [(j, i) for i, j in up]

    def exchange(sends):
        if both:
            return [lax.ppermute(sends[0], "slab", up + down)]
        return [lax.ppermute(sends[0], "slab", up), lax.ppermute(sends[1], "slab", down)]

    assert sides == 2
    received = lax.ppermute(edge, "col", [(0, 1), (1, 0)])
    halo_rows = [exchange(first_out)]

    def write_weights(first_ref, index_ref, frac_ref, own_ref, halo_ref):
        slab = lax.axis_index("slab")
        angle = lax.axis_index("angle")
        if both:
            bases = [jnp.where(slab == 0, rows, rows - margin)]
        else:
            bases = [slab * rows - margin, (slab + 1) * rows]

        def weights(a, base):
            slot = lax.broadcasted_iota(jnp.int32, (margin, depth), 0) + base
            position = index_ref[a] + first_ref[a]
            frac = frac_ref[a]
            high = frac.astype(jnp.bfloat16).astype(jnp.float32)
            low = (1.0 - frac).astype(jnp.bfloat16).astype(jnp.float32)
            return jnp.where(slot == position, low, 0.0) + jnp.where(slot == position + 1, high, 0.0)

        here = [slab * rows + r for r in half_rows(slab)]
        for starts, ref in ((here, own_ref), (bases, halo_ref)):
            table = jnp.concatenate([weights(a, b) for b in starts for a in range(angles)], axis=0)
            turned = table.T.astype(jnp.bfloat16)
            for s in range(line):
                if quick:
                    places = [o.index(s) for o in order]
                    place = places[line - 1]
                    for i in range(line - 1):
                        place = jnp.where(angle == i, places[i], place)
                    at = pl.multiple_of(place * shard, shard)
                else:
                    at = s * shard
                ref[pl.ds(at, shard), :] = turned[s * shard : (s + 1) * shard, :]

    def second_kernel(proj_ref, received_ref, band_ref, first_ref, index_ref, frac_ref,
                      own_ref, halo_ref, *rest):
        outs, (weighted_ref, halo_cols_ref, left_ref, right_ref) = rest[:-4], rest[-4:]
        slab = lax.axis_index("slab")
        col = lax.axis_index("col")
        lower = col == 0
        for h, r in enumerate(half_rows(slab)):
            r = aligned(r)
            weigh(proj_ref, weighted_ref, h, r, slab * rows, col * cols, sizes, 0, cols)
            from_col = jnp.where(lower, cols, col * cols - reach)
            weigh(received_ref, halo_cols_ref, h, r, slab * rows, from_col, sizes, 0, reach)
        none = jnp.zeros(halo_cols_ref.shape, halo_cols_ref.dtype)
        left_ref[...] = jnp.where(lower, none, halo_cols_ref[...])
        right_ref[...] = jnp.where(lower, halo_cols_ref[...], none)
        work = [(chunks[0], second_half)][: 2 - early]
        work += [(chunk, half) for chunk in chunks[1:] for half in (first_half, second_half)]
        for (columns, half), out_ref in zip(work, outs):
            filter_columns(
                columns, half, weighted_ref, left_ref, right_ref, band_ref, out_ref, 2 * STACK
            )
        write_weights(first_ref, index_ref, frac_ref, own_ref, halo_ref)

    shapes = [bf16(part, widths[0])] * (2 - early)
    shapes += [bf16(part, w) for w in widths[1:] for _ in range(2)]
    own_weight, halo_weight, *second_out = kernel_call(
        second_kernel,
        [bf16(depth, 2 * part), bf16(depth, halos * part)] + shapes,
        (projections, received, band, row_first[:, 0], interp_index, interp_frac),
        4 * part * length * (cols - width // 2),
        scratch=[pltpu.VMEM((2 * part, cols), jnp.bfloat16)]
        + [pltpu.VMEM((2 * part, reach), jnp.bfloat16)] * 3,
        name="other_columns",
        specs=[VMEM, VMEM, VMEM, SMEM, VMEM, VMEM],
    )
    filtered = [(*first_out, *second_out[: 2 - early])]
    for at in range(2 - early, len(second_out), 2):
        filtered.append(second_out[at : at + 2])
        halo_rows.append(exchange(second_out[at : at + halos]))

    def project(index, after=()):
        width = widths[index]

        def body(own_ref, halo_ref, *rest):
            sources, outs = rest[: 2 + halos], rest[2 + halos + len(after) :]
            for c in range(0, width, BLOCK):
                cut = slice(c, c + BLOCK)
                own = jnp.concatenate([ref[:, cut] for ref in sources[:2]], axis=0)
                other = [ref[:, cut] for ref in sources[2:]]
                other = other[0] if len(other) == 1 else jnp.concatenate(other, axis=0)
                total = jnp.dot(own_ref[...], own, preferred_element_type=jnp.float32)
                total += jnp.dot(halo_ref[...], other, preferred_element_type=jnp.float32)
                total = total * scale
                at = 0
                for out in outs:
                    out[:, cut] = total[at : at + out.shape[0], :].astype(out.dtype)
                    at += out.shape[0]

        if quick:
            shapes = [bf16(shard, width)] * 3 + [f32(shard, width)]
        else:
            shapes = [f32(depth, width)]
        return kernel_call(
            body,
            shapes,
            (own_weight, halo_weight, *filtered[index], *halo_rows[index], *after),
            2 * depth * (2 + halos) * part * width,
            name="interpolate",
            specs=[VMEM] * (4 + halos) + [HELD] * len(after),
        )

    def widen(x):
        return x.astype(jnp.float32)

    def at_end():
        angle = lax.axis_index("angle")
        return (angle == 0) | (angle == line - 1)

    def line_sends(near, middle):
        one = lax.ppermute(near, "angle", [(0, 1), (1, 0), (2, 3), (3, 2)])
        three = lax.ppermute(middle, "angle", [(1, 2), (2, 1), (0, 0), (3, 3)])
        two = lax.ppermute(middle, "angle", [(0, 2), (3, 1), (1, 0), (2, 3)])
        return one, three, two

    def relay(one, three, far, kept, after=(), weight=1):
        def body(one_ref, three_ref, far_ref, kept_ref, *rest):
            relayed_ref, partial_ref = rest[-2:]
            end = at_end()
            arrived = widen(one_ref[...])
            relayed = widen(far_ref[...]) + jnp.where(end, 0.0, arrived)
            relayed_ref[...] = relayed.astype(jnp.bfloat16)
            partial_ref[...] = kept_ref[...] + jnp.where(end, arrived, widen(three_ref[...]))

        relayed, partial = kernel_call(
            body,
            [bf16(*far.shape), f32(*kept.shape)],
            (one, three, far, kept, *after),
            far.size * 2 * weight,
            name="relay",
            specs=[VMEM] * 4 + [HELD] * len(after),
        )
        return lax.ppermute(relayed, "angle", [(0, 1), (1, 3), (2, 0), (3, 2)]), partial

    def total(partial_ref, two_ref, four_ref):
        direct = jnp.where(at_end(), 0.0, widen(two_ref[...]))
        return partial_ref[...] + direct + widen(four_ref[...])

    def finish(partial, two, four):
        def body(partial_ref, two_ref, four_ref, out_ref):
            out_ref[...] = total(partial_ref, two_ref, four_ref)

        return kernel_call(
            body, [f32(*partial.shape)], (partial, two, four), partial.size * 2, name="finish"
        )[0]

    def store(partial, two, four, done, volume):
        def body(partial_ref, two_ref, four_ref, *rest):
            volume_ref, total_ref, sem = rest[-3:]
            total_ref[...] = total(partial_ref, two_ref, four_ref)
            copies = [
                pltpu.make_async_copy(
                    source, volume_ref.at[:, pl.ds(first, source.shape[1])], sem.at[i]
                )
                for i, (source, (first, _)) in enumerate(
                    [(total_ref, chunks[index]), *zip(rest, (chunks[i] for i, _ in done))]
                )
            ]
            for copy in copies:
                copy.start()
            for copy in copies:
                copy.wait()

        given = [partial, two, four, *(array for _, array in done)]
        index = len(chunks) - 1 if volume is not None else len(chunks) - 2
        shape = f32(shard, cols)
        return pl.pallas_call(
            body,
            out_shape=shape,
            in_specs=[VMEM] * len(given) + [HELD] * (volume is not None),
            out_specs=HELD,
            input_output_aliases={len(given): 0} if volume is not None else {},
            scratch_shapes=[
                pltpu.VMEM(partial.shape, jnp.float32),
                pltpu.SemaphoreType.DMA((1 + len(done),)),
            ],
            compiler_params=pltpu.CompilerParams(vmem_limit_bytes=VMEM_BYTES),
            name="store",
        )(*given, *([] if volume is None else [volume]))

    if not quick:
        sums = [
            lax.psum_scatter(project(i)[0], "angle", scatter_dimension=0, tiled=True)
            for i in range(len(chunks))
        ]
        return jnp.concatenate([sums[i] for i in sorted(range(len(chunks)), key=chunks.__getitem__)], 1)

    last = len(chunks) - 1
    near, middle, far, kept = project(0)
    sent = line_sends(near, middle)
    done, volume, partial = [], None, None
    for j in range(last + 1):
        one, three, two = sent
        here = (far, kept)
        after = [two] if j == 0 else [array for _, array in done[-1:] if j < last]
        if j < last:
            near, middle, far, kept = project(j + 1, after=[] if partial is None else [partial])
            sent = line_sends(near, middle)
            after.append(kept)
        four, partial = relay(one, three, *here, after=after, weight=WEIGHTS[j])
        if j < last - 1:
            done.append((j, finish(partial, two, four)))
        else:
            volume = store(partial, two, four, done if j < last else [], volume)
    return volume


def solution(mesh):
    placed = (
        P(("group", "angle"), "slab", "col"),
        P(),
        P(("group", "angle"), "slab"),
        P(("group", "angle"), "slab", None),
        P(("group", "angle"), "slab", None),
    )
    return jax.shard_map(
        on_device,
        mesh=mesh,
        in_specs=placed,
        out_specs=P(("group", "slab", "angle"), "col"),
        check_vma=False,
    )
```

```python
import math

import jax
import jax.numpy as jnp
from jax import lax
from jax.experimental import pallas as pl
from jax.experimental.pallas import tpu as pltpu
from jax.sharding import PartitionSpec as P

BLOCK = 256
TILE = 128
STACK = 4
DIRECT = (True, False, False, True)
WEIGHTS = (40000, 40000, 1, 1)
VMEM_BYTES = 14 * 1024 * 1024
FIRST_VMEM_BYTES = 103 * 512 * 1024
LINE_ORDER = ((3, 2, 1, 0), (0, 2, 3, 1), (3, 1, 0, 2), (0, 1, 2, 3))

VMEM = pl.BlockSpec(memory_space=pltpu.VMEM)
HELD = pl.BlockSpec(memory_space=pltpu.HBM)
SMEM = pl.BlockSpec(memory_space=pltpu.SMEM)


def kernel_call(
    body, out_shape, args, flops, scratch=(), name=None, specs=None, grant=VMEM_BYTES, carried=()
):
    specs = specs or [VMEM] * len(args)
    moved = sum(a.size * a.dtype.itemsize for a in (*args, *out_shape))
    n_in, n_out, n_through = len(args), len(out_shape), len(carried)

    def kernel(*refs):
        ins, refs = refs[:n_in], refs[n_in + n_through :]
        body(*ins, *refs[:n_out], *refs[n_out + n_through :])

    return pl.pallas_call(
        kernel,
        out_shape=[*out_shape, *(jax.ShapeDtypeStruct(c.shape, c.dtype) for c in carried)],
        in_specs=[*specs, *([HELD] * n_through)],
        out_specs=[VMEM] * n_out + [HELD] * n_through,
        input_output_aliases={n_in + i: n_out + i for i in range(n_through)},
        scratch_shapes=list(scratch),
        compiler_params=pltpu.CompilerParams(vmem_limit_bytes=grant),
        cost_estimate=pl.CostEstimate(flops=flops, bytes_accessed=moved, transcendentals=0),
        name=name,
    )(*args, *carried)


def build_band(taps_ref, band_ref):
    count = taps_ref.shape[0]
    steps, tiles = band_ref.shape[1] // TILE, band_ref.shape[0] // TILE
    zero = jnp.zeros((TILE, TILE), jnp.float32)
    ahead = lax.broadcasted_iota(jnp.int32, (TILE, TILE), 1) >= lax.broadcasted_iota(
        jnp.int32, (TILE, TILE), 0
    )
    taps = taps_ref[...].astype(jnp.float32)

    def shifted(d):
        if not 0 <= d < count:
            return zero
        row = jnp.broadcast_to(taps[d : d + 1, :], (TILE, TILE))
        return pltpu.roll(row, 0, 1, stride=1, stride_axis=0)

    before = zero
    for d in range(-(steps - 1), tiles):
        here = shifted(d)
        block = jnp.where(ahead, here, before).T.astype(jnp.bfloat16)
        before = here
        for c in range(steps):
            if 0 <= d + c < tiles:
                band_ref[(d + c) * TILE : (d + c + 1) * TILE, c * TILE : (c + 1) * TILE] = block


def weigh(proj_ref, weighted_ref, half, row_at, row_start, col_start, sizes, start, stop):
    angles = proj_ref.shape[0]
    total_rows, total_cols, count = sizes
    distance = jnp.float32(total_cols)
    v = lax.broadcasted_iota(jnp.int32, (count, 1), 0) + (row_start + row_at)
    v = v.astype(jnp.float32) - total_rows / 2 + 0.5
    step = BLOCK
    for c in range(start, stop, step):
        u = lax.broadcasted_iota(jnp.int32, (1, step), 1) + (col_start + c)
        u = u.astype(jnp.float32) - total_cols / 2 + 0.5
        factor = distance / jnp.sqrt(distance * distance + u * u + v * v)
        for a in range(angles):
            raw = proj_ref[a, pl.ds(row_at, count), c : c + step].astype(jnp.float32)
            at = (half * angles + a) * count
            weighted_ref[at : at + count, c : c + step] = (raw * factor).astype(jnp.bfloat16)


def filter_columns(columns, rows, weighted_ref, left_ref, right_ref, band_ref, out_ref, stack):
    cols = weighted_ref.shape[1]
    length = band_ref.shape[0]
    reach = (length - BLOCK) // 2
    count = rows.stop - rows.start

    def window(c):
        lo, hi = c - reach, c - reach + length
        pieces = []
        if lo < 0:
            pieces.append(left_ref[rows, reach + lo : reach + min(hi, 0)])
        if max(lo, 0) < min(hi, cols):
            pieces.append(weighted_ref[rows, max(lo, 0) : min(hi, cols)])
        if hi > cols:
            pieces.append(right_ref[rows, max(lo - cols, 0) : hi - cols])
        return pieces[0] if len(pieces) == 1 else jnp.concatenate(pieces, axis=1)

    starts = range(columns[0], columns[0] + columns[1], BLOCK)
    for at in range(0, len(starts), stack):
        group = starts[at : at + stack]
        tall = jnp.concatenate([window(c) for c in group], axis=0)
        result = jnp.dot(tall, band_ref[...], preferred_element_type=jnp.float32)
        result = result.astype(jnp.bfloat16)
        for k in range(len(group)):
            out_ref[:, (at + k) * BLOCK : (at + k + 1) * BLOCK] = result[
                k * count : (k + 1) * count, :
            ]


def bf16(*shape):
    return jax.ShapeDtypeStruct(shape, jnp.bfloat16)


def f32(*shape):
    return jax.ShapeDtypeStruct(shape, jnp.float32)


def chunk_plan(cols, reach):
    assert cols >= 2 * reach + 4 * BLOCK
    cut = reach + (cols - 2 * reach) // 2 // BLOCK * BLOCK
    return [(reach, cut - reach), (cut, cols - reach - cut), (0, reach), (cols - reach, reach)]


def on_device(projections, filter_taps, row_first, interp_index, interp_frac):
    angles, rows, cols = projections.shape
    depth = interp_index.shape[2]
    taps = filter_taps.shape[0]
    reach = taps // 2
    length = taps + BLOCK
    margin = rows // 2
    slabs, line, sides = (lax.axis_size(n) for n in ("slab", "angle", "col"))
    scale = math.pi / (angles * line)
    both = slabs == 2
    halos = 1 if both else 2
    quick = line == 4
    shard = depth // line
    order = LINE_ORDER if quick else (tuple(range(line)),) * line
    total_rows, total_cols = rows * slabs, cols * sides
    chunks = chunk_plan(cols, reach)
    widths = [w for _, w in chunks]
    part = angles * margin
    first_half, second_half = slice(0, part), slice(part, 2 * part)
    sizes = (total_rows, total_cols, margin)

    def half_rows(slab):
        if both:
            return jnp.where(slab == 0, margin, 0), jnp.where(slab == 0, 0, margin)
        return margin, 0

    def aligned(row):
        return row if isinstance(row, int) else pl.multiple_of(row, margin)

    start, width = chunks[0]
    assert start == reach
    window = width + 2 * reach
    early = halos

    def first_kernel(proj_ref, taps_ref, band_ref, edge_ref, *rest):
        outs, (raw_ref, weighted_ref, sem) = rest[:-3], rest[-3:]
        slab = lax.axis_index("slab")
        col = lax.axis_index("col")
        starts = [aligned(r) for r in half_rows(slab)][:early]
        copies = [
            pltpu.make_async_copy(
                proj_ref.at[a, pl.ds(r, margin), pl.ds(0, window)],
                raw_ref.at[a, pl.ds(r, margin), :],
                sem.at[a * 2 + h],
            )
            for a in range(angles)
            for h, r in enumerate(starts)
        ]
        edge_col = pl.multiple_of(jnp.where(col == 0, cols - reach, 0), TILE)
        edge_copy = pltpu.make_async_copy(
            proj_ref.at[:, :, pl.ds(edge_col, reach)], edge_ref, sem.at[2 * angles]
        )
        for copy in copies:
            copy.start()
        edge_copy.start()
        build_band(taps_ref, band_ref)
        for copy in copies:
            copy.wait()
        for h, r in enumerate(starts):
            weigh(raw_ref, weighted_ref, h, r, slab * rows, col * cols, sizes, 0, window)
        for h, out_ref in enumerate(outs):
            filter_columns(
                (reach, width),
                (first_half, second_half)[h],
                weighted_ref,
                None,
                None,
                band_ref,
                out_ref,
                2 * STACK,
            )
        edge_copy.wait()

    band, edge, *first_out = kernel_call(
        first_kernel,
        [bf16(length, BLOCK), bf16(angles, rows, reach)] + [bf16(part, width)] * early,
        (projections, filter_taps.reshape(taps // TILE, TILE)),
        2 * early * part * length * width,
        scratch=[
            pltpu.VMEM((angles, rows, window), jnp.bfloat16),
            pltpu.VMEM((early * part, window), jnp.bfloat16),
            pltpu.SemaphoreType.DMA((2 * angles + 1,)),
        ],
        name="first_columns",
        specs=[HELD, VMEM],
        grant=FIRST_VMEM_BYTES,
    )

    up = [(i, (i + 1) % slabs) for i in range(slabs - 1)]
    down = [(j, i) for i, j in up]

    def exchange(sends):
        if both:
            return [lax.ppermute(sends[0], "slab", up + down)]
        return [lax.ppermute(sends[0], "slab", up), lax.ppermute(sends[1], "slab", down)]

    assert sides == 2
    received = lax.ppermute(edge, "col", [(0, 1), (1, 0)])
    halo_rows = [exchange(first_out)]

    def write_weights(first_ref, index_ref, frac_ref, own_ref, halo_ref):
        slab = lax.axis_index("slab")
        angle = lax.axis_index("angle")
        if both:
            bases = [jnp.where(slab == 0, rows, rows - margin)]
        else:
            bases = [slab * rows - margin, (slab + 1) * rows]

        def weights(a, base):
            slot = lax.broadcasted_iota(jnp.int32, (margin, depth), 0) + base
            position = index_ref[a] + first_ref[a]
            frac = frac_ref[a]
            high = frac.astype(jnp.bfloat16).astype(jnp.float32)
            low = (1.0 - frac).astype(jnp.bfloat16).astype(jnp.float32)
            return jnp.where(slot == position, low, 0.0) + jnp.where(slot == position + 1, high, 0.0)

        here = [slab * rows + r for r in half_rows(slab)]
        for starts, ref in ((here, own_ref), (bases, halo_ref)):
            table = jnp.concatenate([weights(a, b) for b in starts for a in range(angles)], axis=0)
            turned = table.T.astype(jnp.bfloat16)
            for s in range(line):
                if quick:
                    places = [o.index(s) for o in order]
                    place = places[line - 1]
                    for i in range(line - 1):
                        place = jnp.where(angle == i, places[i], place)
                    at = pl.multiple_of(place * shard, shard)
                else:
                    at = s * shard
                ref[pl.ds(at, shard), :] = turned[s * shard : (s + 1) * shard, :]

    def second_kernel(proj_ref, received_ref, band_ref, first_ref, index_ref, frac_ref,
                      own_ref, halo_ref, *rest):
        outs, (weighted_ref, halo_cols_ref, left_ref, right_ref) = rest[:-4], rest[-4:]
        slab = lax.axis_index("slab")
        col = lax.axis_index("col")
        lower = col == 0
        for h, r in enumerate(half_rows(slab)):
            r = aligned(r)
            weigh(proj_ref, weighted_ref, h, r, slab * rows, col * cols, sizes, 0, cols)
            from_col = jnp.where(lower, cols, col * cols - reach)
            weigh(received_ref, halo_cols_ref, h, r, slab * rows, from_col, sizes, 0, reach)
        none = jnp.zeros(halo_cols_ref.shape, halo_cols_ref.dtype)
        left_ref[...] = jnp.where(lower, none, halo_cols_ref[...])
        right_ref[...] = jnp.where(lower, halo_cols_ref[...], none)
        work = [(chunks[0], second_half)][: 2 - early]
        work += [(chunk, half) for chunk in chunks[1:] for half in (first_half, second_half)]
        for (columns, half), out_ref in zip(work, outs):
            filter_columns(
                columns, half, weighted_ref, left_ref, right_ref, band_ref, out_ref, 2 * STACK
            )
        write_weights(first_ref, index_ref, frac_ref, own_ref, halo_ref)

    shapes = [bf16(part, widths[0])] * (2 - early)
    shapes += [bf16(part, w) for w in widths[1:] for _ in range(2)]
    own_weight, halo_weight, *second_out = kernel_call(
        second_kernel,
        [bf16(depth, 2 * part), bf16(depth, halos * part)] + shapes,
        (projections, received, band, row_first[:, 0], interp_index, interp_frac),
        4 * part * length * (cols - width // 2),
        scratch=[pltpu.VMEM((2 * part, cols), jnp.bfloat16)]
        + [pltpu.VMEM((2 * part, reach), jnp.bfloat16)] * 3,
        name="other_columns",
        specs=[VMEM, VMEM, VMEM, SMEM, VMEM, VMEM],
    )
    filtered = [(*first_out, *second_out[: 2 - early])]
    for at in range(2 - early, len(second_out), 2):
        filtered.append(second_out[at : at + 2])
        halo_rows.append(exchange(second_out[at : at + halos]))

    def project(index, after=()):
        width = widths[index]

        def body(own_ref, halo_ref, *rest):
            sources, outs = rest[: 2 + halos], rest[2 + halos + len(after) :]
            for c in range(0, width, BLOCK):
                cut = slice(c, c + BLOCK)
                own = jnp.concatenate([ref[:, cut] for ref in sources[:2]], axis=0)
                other = [ref[:, cut] for ref in sources[2:]]
                other = other[0] if len(other) == 1 else jnp.concatenate(other, axis=0)
                total = jnp.dot(own_ref[...], own, preferred_element_type=jnp.float32)
                total += jnp.dot(halo_ref[...], other, preferred_element_type=jnp.float32)
                total = total * scale
                at = 0
                for out in outs:
                    out[:, cut] = total[at : at + out.shape[0], :].astype(out.dtype)
                    at += out.shape[0]

        if quick:
            first = [bf16(shard, width)] * 2 if DIRECT[index] else [bf16(2 * shard, width)]
            shapes = [*first, bf16(shard, width), f32(shard, width)]
        else:
            shapes = [f32(depth, width)]
        return kernel_call(
            body,
            shapes,
            (own_weight, halo_weight, *filtered[index], *halo_rows[index], *after),
            2 * depth * (2 + halos) * part * width,
            name="interpolate",
            specs=[VMEM] * (4 + halos) + [HELD] * len(after),
        )

    def widen(x):
        return x.astype(jnp.float32)

    def at_end():
        angle = lax.axis_index("angle")
        return (angle == 0) | (angle == line - 1)

    neighbours = [(0, 1), (1, 0), (2, 3), (3, 2)]
    middles = [(1, 2), (2, 1), (0, 0), (3, 3)]
    second_hop = [(0, 1), (1, 3), (2, 0), (3, 2)]
    straight = [(0, 2), (3, 1), (1, 0), (2, 3)]

    def first_hops(*parts):
        if len(parts) == 1:
            return [lax.ppermute(parts[0], "angle", neighbours)]
        near, middle = parts
        two = lax.ppermute(middle, "angle", straight)
        three = lax.ppermute(middle, "angle", middles)
        one = lax.ppermute(near, "angle", neighbours)
        return [one, three, two]

    def relay(sent, own, far, kept, after=(), weight=1):
        direct = len(sent) == 3
        arrived = sent[:2] if direct else [sent[0], own[0]]

        def body(one_ref, other_ref, far_ref, kept_ref, *rest):
            outs = rest[len(after) :]
            end = at_end()
            near = widen(one_ref[:shard, :])
            relayed = widen(far_ref[...]) + jnp.where(end, 0.0, near)
            outs[0][...] = relayed.astype(jnp.bfloat16)
            if direct:
                outs[1][...] = kept_ref[...] + jnp.where(end, near, widen(other_ref[...]))
            else:
                outs[1][...] = kept_ref[...] + jnp.where(end, near, 0.0)
                crossed = widen(one_ref[shard:, :]) + widen(other_ref[shard:, :])
                outs[2][...] = crossed.astype(jnp.bfloat16)

        relayed, partial, *crossed = kernel_call(
            body,
            [bf16(*far.shape), f32(*kept.shape)] + [bf16(*far.shape)] * (not direct),
            (*arrived, far, kept, *after),
            far.size * 2 * weight,
            name="relay",
            specs=[VMEM] * 4 + [HELD] * len(after),
        )
        four = lax.ppermute(relayed, "angle", second_hop)
        three = sent[2] if direct else lax.ppermute(crossed[0], "angle", middles)
        return partial, three, four

    def total(partial_ref, two_ref, four_ref):
        direct = jnp.where(at_end(), 0.0, widen(two_ref[...]))
        return partial_ref[...] + direct + widen(four_ref[...])

    def finish(partial, two, four):
        def body(partial_ref, two_ref, four_ref, out_ref):
            out_ref[...] = total(partial_ref, two_ref, four_ref)

        return kernel_call(
            body, [f32(*partial.shape)], (partial, two, four), partial.size * 2, name="finish"
        )[0]

    def store(partial, two, four, done, volume):
        def body(partial_ref, two_ref, four_ref, *rest):
            volume_ref, total_ref, sem = rest[-3:]
            total_ref[...] = total(partial_ref, two_ref, four_ref)
            copies = [
                pltpu.make_async_copy(
                    source, volume_ref.at[:, pl.ds(first, source.shape[1])], sem.at[i]
                )
                for i, (source, (first, _)) in enumerate(
                    [(total_ref, chunks[index]), *zip(rest, (chunks[i] for i, _ in done))]
                )
            ]
            for copy in copies:
                copy.start()
            for copy in copies:
                copy.wait()

        given = [partial, two, four, *(array for _, array in done)]
        index = len(chunks) - 1 if volume is not None else len(chunks) - 2
        shape = f32(shard, cols)
        return pl.pallas_call(
            body,
            out_shape=shape,
            in_specs=[VMEM] * len(given) + [HELD] * (volume is not None),
            out_specs=HELD,
            input_output_aliases={len(given): 0} if volume is not None else {},
            scratch_shapes=[
                pltpu.VMEM(partial.shape, jnp.float32),
                pltpu.SemaphoreType.DMA((1 + len(done),)),
            ],
            compiler_params=pltpu.CompilerParams(vmem_limit_bytes=VMEM_BYTES),
            name="store",
        )(*given, *([] if volume is None else [volume]))

    if not quick:
        sums = [
            lax.psum_scatter(project(i)[0], "angle", scatter_dimension=0, tiled=True)
            for i in range(len(chunks))
        ]
        return jnp.concatenate([sums[i] for i in sorted(range(len(chunks)), key=chunks.__getitem__)], 1)

    last = len(chunks) - 1
    *own, far, kept = project(0)
    sent = first_hops(*own)
    done, volume, pieces = [], None, None
    for j in range(last + 1):
        here = (sent, own, far, kept)
        after = sent[2:] if j == 0 else [array for _, array in done[-1:] if j < last]
        if j < last:
            *own, far, kept = project(j + 1, after=[] if pieces is None else pieces[:1])
            sent = first_hops(*own)
            after = [*after, kept]
        pieces = relay(*here, after=after, weight=WEIGHTS[j])
        if j < last - 1:
            done.append((j, finish(*pieces)))
        else:
            volume = store(*pieces, done if j < last else [], volume)
    return volume


def solution(mesh):
    placed = (
        P(("group", "angle"), "slab", "col"),
        P(),
        P(("group", "angle"), "slab"),
        P(("group", "angle"), "slab", None),
        P(("group", "angle"), "slab", None),
    )
    return jax.shard_map(
        on_device,
        mesh=mesh,
        in_specs=placed,
        out_specs=P(("group", "slab", "angle"), "col"),
        check_vma=False,
    )
```

```python
import math

import jax
import jax.numpy as jnp
from jax import lax
from jax.experimental import pallas as pl
from jax.experimental.pallas import tpu as pltpu
from jax.sharding import PartitionSpec as P

BLOCK = 256
TILE = 128
STACK = 4
DIRECT = (False, False, False, True)
WEIGHTS = (40000, 40000, 1, 1)
VMEM_BYTES = 14 * 1024 * 1024
FIRST_VMEM_BYTES = 103 * 512 * 1024
LINE_ORDER = ((3, 2, 1, 0), (0, 2, 3, 1), (3, 1, 0, 2), (0, 1, 2, 3))

VMEM = pl.BlockSpec(memory_space=pltpu.VMEM)
HELD = pl.BlockSpec(memory_space=pltpu.HBM)
SMEM = pl.BlockSpec(memory_space=pltpu.SMEM)


def kernel_call(
    body, out_shape, args, flops, scratch=(), name=None, specs=None, grant=VMEM_BYTES, carried=()
):
    specs = specs or [VMEM] * len(args)
    moved = sum(a.size * a.dtype.itemsize for a in (*args, *out_shape))
    n_in, n_out, n_through = len(args), len(out_shape), len(carried)

    def kernel(*refs):
        ins, refs = refs[:n_in], refs[n_in + n_through :]
        body(*ins, *refs[:n_out], *refs[n_out + n_through :])

    return pl.pallas_call(
        kernel,
        out_shape=[*out_shape, *(jax.ShapeDtypeStruct(c.shape, c.dtype) for c in carried)],
        in_specs=[*specs, *([HELD] * n_through)],
        out_specs=[VMEM] * n_out + [HELD] * n_through,
        input_output_aliases={n_in + i: n_out + i for i in range(n_through)},
        scratch_shapes=list(scratch),
        compiler_params=pltpu.CompilerParams(vmem_limit_bytes=grant),
        cost_estimate=pl.CostEstimate(flops=flops, bytes_accessed=moved, transcendentals=0),
        name=name,
    )(*args, *carried)


def build_band(taps_ref, band_ref):
    count = taps_ref.shape[0]
    steps, tiles = band_ref.shape[1] // TILE, band_ref.shape[0] // TILE
    zero = jnp.zeros((TILE, TILE), jnp.float32)
    ahead = lax.broadcasted_iota(jnp.int32, (TILE, TILE), 1) >= lax.broadcasted_iota(
        jnp.int32, (TILE, TILE), 0
    )
    taps = taps_ref[...].astype(jnp.float32)

    def shifted(d):
        if not 0 <= d < count:
            return zero
        row = jnp.broadcast_to(taps[d : d + 1, :], (TILE, TILE))
        return pltpu.roll(row, 0, 1, stride=1, stride_axis=0)

    before = zero
    for d in range(-(steps - 1), tiles):
        here = shifted(d)
        block = jnp.where(ahead, here, before).T.astype(jnp.bfloat16)
        before = here
        for c in range(steps):
            if 0 <= d + c < tiles:
                band_ref[(d + c) * TILE : (d + c + 1) * TILE, c * TILE : (c + 1) * TILE] = block


def weigh(proj_ref, weighted_ref, half, row_at, row_start, col_start, sizes, start, stop):
    angles = proj_ref.shape[0]
    total_rows, total_cols, count = sizes
    distance = jnp.float32(total_cols)
    v = lax.broadcasted_iota(jnp.int32, (count, 1), 0) + (row_start + row_at)
    v = v.astype(jnp.float32) - total_rows / 2 + 0.5
    step = BLOCK
    for c in range(start, stop, step):
        u = lax.broadcasted_iota(jnp.int32, (1, step), 1) + (col_start + c)
        u = u.astype(jnp.float32) - total_cols / 2 + 0.5
        factor = distance / jnp.sqrt(distance * distance + u * u + v * v)
        for a in range(angles):
            raw = proj_ref[a, pl.ds(row_at, count), c : c + step].astype(jnp.float32)
            at = (half * angles + a) * count
            weighted_ref[at : at + count, c : c + step] = (raw * factor).astype(jnp.bfloat16)


def filter_columns(columns, rows, weighted_ref, left_ref, right_ref, band_ref, out_ref, stack):
    cols = weighted_ref.shape[1]
    length = band_ref.shape[0]
    reach = (length - BLOCK) // 2
    count = rows.stop - rows.start

    def window(c):
        lo, hi = c - reach, c - reach + length
        pieces = []
        if lo < 0:
            pieces.append(left_ref[rows, reach + lo : reach + min(hi, 0)])
        if max(lo, 0) < min(hi, cols):
            pieces.append(weighted_ref[rows, max(lo, 0) : min(hi, cols)])
        if hi > cols:
            pieces.append(right_ref[rows, max(lo - cols, 0) : hi - cols])
        return pieces[0] if len(pieces) == 1 else jnp.concatenate(pieces, axis=1)

    starts = range(columns[0], columns[0] + columns[1], BLOCK)
    for at in range(0, len(starts), stack):
        group = starts[at : at + stack]
        tall = jnp.concatenate([window(c) for c in group], axis=0)
        result = jnp.dot(tall, band_ref[...], preferred_element_type=jnp.float32)
        result = result.astype(jnp.bfloat16)
        for k in range(len(group)):
            out_ref[:, (at + k) * BLOCK : (at + k + 1) * BLOCK] = result[
                k * count : (k + 1) * count, :
            ]


def bf16(*shape):
    return jax.ShapeDtypeStruct(shape, jnp.bfloat16)


def f32(*shape):
    return jax.ShapeDtypeStruct(shape, jnp.float32)


def chunk_plan(cols, reach):
    assert cols >= 2 * reach + 4 * BLOCK
    cut = reach + (cols - 2 * reach) // 2 // BLOCK * BLOCK
    return [(reach, cut - reach), (cut, cols - reach - cut), (0, reach), (cols - reach, reach)]


def on_device(projections, filter_taps, row_first, interp_index, interp_frac):
    angles, rows, cols = projections.shape
    depth = interp_index.shape[2]
    taps = filter_taps.shape[0]
    reach = taps // 2
    length = taps + BLOCK
    margin = rows // 2
    slabs, line, sides = (lax.axis_size(n) for n in ("slab", "angle", "col"))
    scale = math.pi / (angles * line)
    both = slabs == 2
    halos = 1 if both else 2
    quick = line == 4
    shard = depth // line
    order = LINE_ORDER if quick else (tuple(range(line)),) * line
    total_rows, total_cols = rows * slabs, cols * sides
    chunks = chunk_plan(cols, reach)
    widths = [w for _, w in chunks]
    part = angles * margin
    first_half, second_half = slice(0, part), slice(part, 2 * part)
    sizes = (total_rows, total_cols, margin)

    def half_rows(slab):
        if both:
            return jnp.where(slab == 0, margin, 0), jnp.where(slab == 0, 0, margin)
        return margin, 0

    def aligned(row):
        return row if isinstance(row, int) else pl.multiple_of(row, margin)

    start, width = chunks[0]
    assert start == reach
    window = width + 2 * reach
    early = halos

    def first_kernel(proj_ref, taps_ref, band_ref, edge_ref, *rest):
        outs, (raw_ref, weighted_ref, sem) = rest[:-3], rest[-3:]
        slab = lax.axis_index("slab")
        col = lax.axis_index("col")
        starts = [aligned(r) for r in half_rows(slab)][:early]
        copies = [
            pltpu.make_async_copy(
                proj_ref.at[a, pl.ds(r, margin), pl.ds(0, window)],
                raw_ref.at[a, pl.ds(r, margin), :],
                sem.at[a * 2 + h],
            )
            for a in range(angles)
            for h, r in enumerate(starts)
        ]
        edge_col = pl.multiple_of(jnp.where(col == 0, cols - reach, 0), TILE)
        edge_copy = pltpu.make_async_copy(
            proj_ref.at[:, :, pl.ds(edge_col, reach)], edge_ref, sem.at[2 * angles]
        )
        for copy in copies:
            copy.start()
        edge_copy.start()
        build_band(taps_ref, band_ref)
        for copy in copies:
            copy.wait()
        for h, r in enumerate(starts):
            weigh(raw_ref, weighted_ref, h, r, slab * rows, col * cols, sizes, 0, window)
        for h, out_ref in enumerate(outs):
            filter_columns(
                (reach, width),
                (first_half, second_half)[h],
                weighted_ref,
                None,
                None,
                band_ref,
                out_ref,
                2 * STACK,
            )
        edge_copy.wait()

    band, edge, *first_out = kernel_call(
        first_kernel,
        [bf16(length, BLOCK), bf16(angles, rows, reach)] + [bf16(part, width)] * early,
        (projections, filter_taps.reshape(taps // TILE, TILE)),
        2 * early * part * length * width,
        scratch=[
            pltpu.VMEM((angles, rows, window), jnp.bfloat16),
            pltpu.VMEM((early * part, window), jnp.bfloat16),
            pltpu.SemaphoreType.DMA((2 * angles + 1,)),
        ],
        name="first_columns",
        specs=[HELD, VMEM],
        grant=FIRST_VMEM_BYTES,
    )

    up = [(i, (i + 1) % slabs) for i in range(slabs - 1)]
    down = [(j, i) for i, j in up]

    def exchange(sends):
        if both:
            return [lax.ppermute(sends[0], "slab", up + down)]
        return [lax.ppermute(sends[0], "slab", up), lax.ppermute(sends[1], "slab", down)]

    assert sides == 2
    received = lax.ppermute(edge, "col", [(0, 1), (1, 0)])
    halo_rows = [exchange(first_out)]

    def write_weights(first_ref, index_ref, frac_ref, own_ref, halo_ref):
        slab = lax.axis_index("slab")
        angle = lax.axis_index("angle")
        if both:
            bases = [jnp.where(slab == 0, rows, rows - margin)]
        else:
            bases = [slab * rows - margin, (slab + 1) * rows]

        def weights(a, base):
            slot = lax.broadcasted_iota(jnp.int32, (margin, depth), 0) + base
            position = index_ref[a] + first_ref[a]
            frac = frac_ref[a]
            high = frac.astype(jnp.bfloat16).astype(jnp.float32)
            low = (1.0 - frac).astype(jnp.bfloat16).astype(jnp.float32)
            return jnp.where(slot == position, low, 0.0) + jnp.where(slot == position + 1, high, 0.0)

        here = [slab * rows + r for r in half_rows(slab)]
        for starts, ref in ((here, own_ref), (bases, halo_ref)):
            table = jnp.concatenate([weights(a, b) for b in starts for a in range(angles)], axis=0)
            turned = table.T.astype(jnp.bfloat16)
            for s in range(line):
                if quick:
                    places = [o.index(s) for o in order]
                    place = places[line - 1]
                    for i in range(line - 1):
                        place = jnp.where(angle == i, places[i], place)
                    at = pl.multiple_of(place * shard, shard)
                else:
                    at = s * shard
                ref[pl.ds(at, shard), :] = turned[s * shard : (s + 1) * shard, :]

    def second_kernel(proj_ref, received_ref, band_ref, first_ref, index_ref, frac_ref,
                      own_ref, halo_ref, *rest):
        outs, (weighted_ref, halo_cols_ref, left_ref, right_ref) = rest[:-4], rest[-4:]
        slab = lax.axis_index("slab")
        col = lax.axis_index("col")
        lower = col == 0
        for h, r in enumerate(half_rows(slab)):
            r = aligned(r)
            weigh(proj_ref, weighted_ref, h, r, slab * rows, col * cols, sizes, 0, cols)
            from_col = jnp.where(lower, cols, col * cols - reach)
            weigh(received_ref, halo_cols_ref, h, r, slab * rows, from_col, sizes, 0, reach)
        none = jnp.zeros(halo_cols_ref.shape, halo_cols_ref.dtype)
        left_ref[...] = jnp.where(lower, none, halo_cols_ref[...])
        right_ref[...] = jnp.where(lower, halo_cols_ref[...], none)
        work = [(chunks[0], second_half)][: 2 - early]
        work += [(chunk, half) for chunk in chunks[1:] for half in (first_half, second_half)]
        for (columns, half), out_ref in zip(work, outs):
            filter_columns(
                columns, half, weighted_ref, left_ref, right_ref, band_ref, out_ref, 2 * STACK
            )
        write_weights(first_ref, index_ref, frac_ref, own_ref, halo_ref)

    shapes = [bf16(part, widths[0])] * (2 - early)
    shapes += [bf16(part, w) for w in widths[1:] for _ in range(2)]
    own_weight, halo_weight, *second_out = kernel_call(
        second_kernel,
        [bf16(depth, 2 * part), bf16(depth, halos * part)] + shapes,
        (projections, received, band, row_first[:, 0], interp_index, interp_frac),
        4 * part * length * (cols - width // 2),
        scratch=[pltpu.VMEM((2 * part, cols), jnp.bfloat16)]
        + [pltpu.VMEM((2 * part, reach), jnp.bfloat16)] * 3,
        name="other_columns",
        specs=[VMEM, VMEM, VMEM, SMEM, VMEM, VMEM],
    )
    filtered = [(*first_out, *second_out[: 2 - early])]
    for at in range(2 - early, len(second_out), 2):
        filtered.append(second_out[at : at + 2])
        halo_rows.append(exchange(second_out[at : at + halos]))

    def project(index, after=()):
        width = widths[index]

        def body(own_ref, halo_ref, *rest):
            sources, outs = rest[: 2 + halos], rest[2 + halos + len(after) :]
            for c in range(0, width, BLOCK):
                cut = slice(c, c + BLOCK)
                own = jnp.concatenate([ref[:, cut] for ref in sources[:2]], axis=0)
                other = [ref[:, cut] for ref in sources[2:]]
                other = other[0] if len(other) == 1 else jnp.concatenate(other, axis=0)
                total = jnp.dot(own_ref[...], own, preferred_element_type=jnp.float32)
                total += jnp.dot(halo_ref[...], other, preferred_element_type=jnp.float32)
                total = total * scale
                at = 0
                for out in outs:
                    out[:, cut] = total[at : at + out.shape[0], :].astype(out.dtype)
                    at += out.shape[0]

        if quick:
            first = [bf16(shard, width)] * 2 if DIRECT[index] else [bf16(2 * shard, width)]
            shapes = [*first, bf16(shard, width), f32(shard, width)]
        else:
            shapes = [f32(depth, width)]
        return kernel_call(
            body,
            shapes,
            (own_weight, halo_weight, *filtered[index], *halo_rows[index], *after),
            2 * depth * (2 + halos) * part * width,
            name="interpolate",
            specs=[VMEM] * (4 + halos) + [HELD] * len(after),
        )

    def widen(x):
        return x.astype(jnp.float32)

    def at_end():
        angle = lax.axis_index("angle")
        return (angle == 0) | (angle == line - 1)

    neighbours = [(0, 1), (1, 0), (2, 3), (3, 2)]
    middles = [(1, 2), (2, 1), (0, 0), (3, 3)]
    second_hop = [(0, 1), (1, 3), (2, 0), (3, 2)]
    straight = [(0, 2), (3, 1), (1, 0), (2, 3)]

    def first_hops(*parts):
        if len(parts) == 1:
            return [lax.ppermute(parts[0], "angle", neighbours)]
        near, middle = parts
        two = lax.ppermute(middle, "angle", straight)
        three = lax.ppermute(middle, "angle", middles)
        one = lax.ppermute(near, "angle", neighbours)
        return [one, three, two]

    def relay(sent, own, far, kept, after=(), weight=1):
        direct = len(sent) == 3
        arrived = sent[:2] if direct else [sent[0], own[0]]

        def body(one_ref, other_ref, far_ref, kept_ref, *rest):
            outs = rest[len(after) :]
            end = at_end()
            near = widen(one_ref[:shard, :])
            relayed = widen(far_ref[...]) + jnp.where(end, 0.0, near)
            outs[0][...] = relayed.astype(jnp.bfloat16)
            if direct:
                outs[1][...] = kept_ref[...] + jnp.where(end, near, widen(other_ref[...]))
            else:
                outs[1][...] = kept_ref[...] + jnp.where(end, near, 0.0)
                crossed = widen(one_ref[shard:, :]) + widen(other_ref[shard:, :])
                outs[2][...] = crossed.astype(jnp.bfloat16)

        relayed, partial, *crossed = kernel_call(
            body,
            [bf16(*far.shape), f32(*kept.shape)] + [bf16(*far.shape)] * (not direct),
            (*arrived, far, kept, *after),
            far.size * 2 * weight,
            name="relay",
            specs=[VMEM] * 4 + [HELD] * len(after),
        )
        four = lax.ppermute(relayed, "angle", second_hop)
        three = sent[2] if direct else lax.ppermute(crossed[0], "angle", middles)
        return partial, three, four

    def total(partial_ref, two_ref, four_ref):
        direct = jnp.where(at_end(), 0.0, widen(two_ref[...]))
        return partial_ref[...] + direct + widen(four_ref[...])

    def finish(partial, two, four):
        def body(partial_ref, two_ref, four_ref, out_ref):
            out_ref[...] = total(partial_ref, two_ref, four_ref)

        return kernel_call(
            body, [f32(*partial.shape)], (partial, two, four), partial.size * 2, name="finish"
        )[0]

    def store(done, pieces):
        first = len(done)
        given = [*done, *(piece for triple in pieces for piece in triple)]

        def body(*refs):
            ready, refs = refs[:first], refs[first:]
            volume_ref, sem = refs[3 * len(pieces)], refs[-1]
            totals = refs[3 * len(pieces) + 1 : -1]

            def copy(index, source):
                at = pl.ds(chunks[index][0], chunks[index][1])
                return pltpu.make_async_copy(source, volume_ref.at[:, at], sem.at[index])

            copies = [copy(i, ref) for i, ref in enumerate(ready)]
            for c in copies:
                c.start()
            for i, total_ref in enumerate(totals):
                total_ref[...] = total(*refs[3 * i : 3 * i + 3])
                copies.append(copy(first + i, total_ref))
                copies[-1].start()
            for c in copies:
                c.wait()

        return pl.pallas_call(
            body,
            out_shape=f32(shard, cols),
            in_specs=[VMEM] * len(given),
            out_specs=HELD,
            scratch_shapes=[
                *(pltpu.VMEM((shard, w), jnp.float32) for w in widths[first:]),
                pltpu.SemaphoreType.DMA((len(chunks),)),
            ],
            compiler_params=pltpu.CompilerParams(vmem_limit_bytes=VMEM_BYTES),
            name="store",
        )(*given)

    if not quick:
        sums = [
            lax.psum_scatter(project(i)[0], "angle", scatter_dimension=0, tiled=True)
            for i in range(len(chunks))
        ]
        return jnp.concatenate([sums[i] for i in sorted(range(len(chunks)), key=chunks.__getitem__)], 1)

    last = len(chunks) - 1
    *own, far, kept = project(0)
    sent = first_hops(*own)
    done, pieces = [], []
    for j in range(last + 1):
        here = (sent, own, far, kept)
        after = sent[2:] if j == 0 else done[-1:] if j < last else []
        if j < last:
            *own, far, kept = project(j + 1, after=[p[0] for p in pieces[-1:]])
            sent = first_hops(*own)
            after = [*after, kept]
        pieces.append(relay(*here, after=after, weight=WEIGHTS[j]))
        if j < last - 1:
            done.append(finish(*pieces[j]))
    return store(done, pieces[last - 1 :])


def solution(mesh):
    placed = (
        P(("group", "angle"), "slab", "col"),
        P(),
        P(("group", "angle"), "slab"),
        P(("group", "angle"), "slab", None),
        P(("group", "angle"), "slab", None),
    )
    return jax.shard_map(
        on_device,
        mesh=mesh,
        in_specs=placed,
        out_specs=P(("group", "slab", "angle"), "col"),
        check_vma=False,
    )
```

```python
import math

import jax
import jax.numpy as jnp
from jax import lax
from jax.experimental import pallas as pl
from jax.experimental.pallas import tpu as pltpu
from jax.sharding import PartitionSpec as P

BLOCK = 256
TILE = 128
STACK = 4
DIRECT = (False, False, False, True)
WEIGHTS = (40000, 40000, 1, 1)
FINISH_WEIGHTS = (1, 1, 10000)
VMEM_BYTES = 14 * 1024 * 1024
FIRST_VMEM_BYTES = 103 * 512 * 1024
LINE_ORDER = ((3, 2, 1, 0), (0, 2, 3, 1), (3, 1, 0, 2), (0, 1, 2, 3))

VMEM = pl.BlockSpec(memory_space=pltpu.VMEM)
HELD = pl.BlockSpec(memory_space=pltpu.HBM)
SMEM = pl.BlockSpec(memory_space=pltpu.SMEM)


def kernel_call(
    body, out_shape, args, flops, scratch=(), name=None, specs=None, grant=VMEM_BYTES, carried=()
):
    specs = specs or [VMEM] * len(args)
    moved = sum(a.size * a.dtype.itemsize for a in (*args, *out_shape))
    n_in, n_out, n_through = len(args), len(out_shape), len(carried)

    def kernel(*refs):
        ins, refs = refs[:n_in], refs[n_in + n_through :]
        body(*ins, *refs[:n_out], *refs[n_out + n_through :])

    return pl.pallas_call(
        kernel,
        out_shape=[*out_shape, *(jax.ShapeDtypeStruct(c.shape, c.dtype) for c in carried)],
        in_specs=[*specs, *([HELD] * n_through)],
        out_specs=[VMEM] * n_out + [HELD] * n_through,
        input_output_aliases={n_in + i: n_out + i for i in range(n_through)},
        scratch_shapes=list(scratch),
        compiler_params=pltpu.CompilerParams(vmem_limit_bytes=grant),
        cost_estimate=pl.CostEstimate(flops=flops, bytes_accessed=moved, transcendentals=0),
        name=name,
    )(*args, *carried)


def build_band(taps_ref, band_ref):
    count = taps_ref.shape[0]
    steps, tiles = band_ref.shape[1] // TILE, band_ref.shape[0] // TILE
    zero = jnp.zeros((TILE, TILE), jnp.float32)
    ahead = lax.broadcasted_iota(jnp.int32, (TILE, TILE), 1) >= lax.broadcasted_iota(
        jnp.int32, (TILE, TILE), 0
    )
    taps = taps_ref[...].astype(jnp.float32)

    def shifted(d):
        if not 0 <= d < count:
            return zero
        row = jnp.broadcast_to(taps[d : d + 1, :], (TILE, TILE))
        return pltpu.roll(row, 0, 1, stride=1, stride_axis=0)

    before = zero
    for d in range(-(steps - 1), tiles):
        here = shifted(d)
        block = jnp.where(ahead, here, before).T.astype(jnp.bfloat16)
        before = here
        for c in range(steps):
            if 0 <= d + c < tiles:
                band_ref[(d + c) * TILE : (d + c + 1) * TILE, c * TILE : (c + 1) * TILE] = block


def weigh(proj_ref, weighted_ref, half, row_at, row_start, col_start, sizes, start, stop):
    angles = proj_ref.shape[0]
    total_rows, total_cols, count = sizes
    distance = jnp.float32(total_cols)
    v = lax.broadcasted_iota(jnp.int32, (count, 1), 0) + (row_start + row_at)
    v = v.astype(jnp.float32) - total_rows / 2 + 0.5
    step = BLOCK
    for c in range(start, stop, step):
        u = lax.broadcasted_iota(jnp.int32, (1, step), 1) + (col_start + c)
        u = u.astype(jnp.float32) - total_cols / 2 + 0.5
        factor = distance / jnp.sqrt(distance * distance + u * u + v * v)
        for a in range(angles):
            raw = proj_ref[a, pl.ds(row_at, count), c : c + step].astype(jnp.float32)
            at = (half * angles + a) * count
            weighted_ref[at : at + count, c : c + step] = (raw * factor).astype(jnp.bfloat16)


def filter_columns(columns, rows, weighted_ref, left_ref, right_ref, band_ref, out_ref, stack):
    cols = weighted_ref.shape[1]
    length = band_ref.shape[0]
    reach = (length - BLOCK) // 2
    count = rows.stop - rows.start

    def window(c):
        lo, hi = c - reach, c - reach + length
        pieces = []
        if lo < 0:
            pieces.append(left_ref[rows, reach + lo : reach + min(hi, 0)])
        if max(lo, 0) < min(hi, cols):
            pieces.append(weighted_ref[rows, max(lo, 0) : min(hi, cols)])
        if hi > cols:
            pieces.append(right_ref[rows, max(lo - cols, 0) : hi - cols])
        return pieces[0] if len(pieces) == 1 else jnp.concatenate(pieces, axis=1)

    starts = range(columns[0], columns[0] + columns[1], BLOCK)
    for at in range(0, len(starts), stack):
        group = starts[at : at + stack]
        tall = jnp.concatenate([window(c) for c in group], axis=0)
        result = jnp.dot(tall, band_ref[...], preferred_element_type=jnp.float32)
        result = result.astype(jnp.bfloat16)
        for k in range(len(group)):
            out_ref[:, (at + k) * BLOCK : (at + k + 1) * BLOCK] = result[
                k * count : (k + 1) * count, :
            ]


def bf16(*shape):
    return jax.ShapeDtypeStruct(shape, jnp.bfloat16)


def f32(*shape):
    return jax.ShapeDtypeStruct(shape, jnp.float32)


def chunk_plan(cols, reach):
    assert cols >= 2 * reach + 4 * BLOCK
    cut = reach + (cols - 2 * reach) // 2 // BLOCK * BLOCK
    return [(reach, cut - reach), (cut, cols - reach - cut), (0, reach), (cols - reach, reach)]


def on_device(projections, filter_taps, row_first, interp_index, interp_frac):
    angles, rows, cols = projections.shape
    depth = interp_index.shape[2]
    taps = filter_taps.shape[0]
    reach = taps // 2
    length = taps + BLOCK
    margin = rows // 2
    slabs, line, sides = (lax.axis_size(n) for n in ("slab", "angle", "col"))
    scale = math.pi / (angles * line)
    both = slabs == 2
    halos = 1 if both else 2
    quick = line == 4
    shard = depth // line
    order = LINE_ORDER if quick else (tuple(range(line)),) * line
    total_rows, total_cols = rows * slabs, cols * sides
    chunks = chunk_plan(cols, reach)
    widths = [w for _, w in chunks]
    part = angles * margin
    first_half, second_half = slice(0, part), slice(part, 2 * part)
    sizes = (total_rows, total_cols, margin)

    def half_rows(slab):
        if both:
            return jnp.where(slab == 0, margin, 0), jnp.where(slab == 0, 0, margin)
        return margin, 0

    def aligned(row):
        return row if isinstance(row, int) else pl.multiple_of(row, margin)

    start, width = chunks[0]
    assert start == reach
    window = width + 2 * reach
    early = halos

    def first_kernel(proj_ref, taps_ref, band_ref, edge_ref, *rest):
        outs, (raw_ref, weighted_ref, sem) = rest[:-3], rest[-3:]
        slab = lax.axis_index("slab")
        col = lax.axis_index("col")
        starts = [aligned(r) for r in half_rows(slab)][:early]
        copies = [
            pltpu.make_async_copy(
                proj_ref.at[a, pl.ds(r, margin), pl.ds(0, window)],
                raw_ref.at[a, pl.ds(r, margin), :],
                sem.at[a * 2 + h],
            )
            for a in range(angles)
            for h, r in enumerate(starts)
        ]
        edge_col = pl.multiple_of(jnp.where(col == 0, cols - reach, 0), TILE)
        edge_copy = pltpu.make_async_copy(
            proj_ref.at[:, :, pl.ds(edge_col, reach)], edge_ref, sem.at[2 * angles]
        )
        for copy in copies:
            copy.start()
        edge_copy.start()
        build_band(taps_ref, band_ref)
        for copy in copies:
            copy.wait()
        for h, r in enumerate(starts):
            weigh(raw_ref, weighted_ref, h, r, slab * rows, col * cols, sizes, 0, window)
        for h, out_ref in enumerate(outs):
            filter_columns(
                (reach, width),
                (first_half, second_half)[h],
                weighted_ref,
                None,
                None,
                band_ref,
                out_ref,
                2 * STACK,
            )
        edge_copy.wait()

    band, edge, *first_out = kernel_call(
        first_kernel,
        [bf16(length, BLOCK), bf16(angles, rows, reach)] + [bf16(part, width)] * early,
        (projections, filter_taps.reshape(taps // TILE, TILE)),
        2 * early * part * length * width,
        scratch=[
            pltpu.VMEM((angles, rows, window), jnp.bfloat16),
            pltpu.VMEM((early * part, window), jnp.bfloat16),
            pltpu.SemaphoreType.DMA((2 * angles + 1,)),
        ],
        name="first_columns",
        specs=[HELD, VMEM],
        grant=FIRST_VMEM_BYTES,
    )

    up = [(i, (i + 1) % slabs) for i in range(slabs - 1)]
    down = [(j, i) for i, j in up]

    def exchange(sends):
        if both:
            return [lax.ppermute(sends[0], "slab", up + down)]
        return [lax.ppermute(sends[0], "slab", up), lax.ppermute(sends[1], "slab", down)]

    assert sides == 2
    received = lax.ppermute(edge, "col", [(0, 1), (1, 0)])
    halo_rows = [exchange(first_out)]

    def write_weights(first_ref, index_ref, frac_ref, own_ref, halo_ref):
        slab = lax.axis_index("slab")
        angle = lax.axis_index("angle")
        if both:
            bases = [jnp.where(slab == 0, rows, rows - margin)]
        else:
            bases = [slab * rows - margin, (slab + 1) * rows]

        def weights(a, base):
            slot = lax.broadcasted_iota(jnp.int32, (margin, depth), 0) + base
            position = index_ref[a] + first_ref[a]
            frac = frac_ref[a]
            high = frac.astype(jnp.bfloat16).astype(jnp.float32)
            low = (1.0 - frac).astype(jnp.bfloat16).astype(jnp.float32)
            return jnp.where(slot == position, low, 0.0) + jnp.where(slot == position + 1, high, 0.0)

        here = [slab * rows + r for r in half_rows(slab)]
        for starts, ref in ((here, own_ref), (bases, halo_ref)):
            table = jnp.concatenate([weights(a, b) for b in starts for a in range(angles)], axis=0)
            turned = table.T.astype(jnp.bfloat16)
            for s in range(line):
                if quick:
                    places = [o.index(s) for o in order]
                    place = places[line - 1]
                    for i in range(line - 1):
                        place = jnp.where(angle == i, places[i], place)
                    at = pl.multiple_of(place * shard, shard)
                else:
                    at = s * shard
                ref[pl.ds(at, shard), :] = turned[s * shard : (s + 1) * shard, :]

    def second_kernel(proj_ref, received_ref, band_ref, first_ref, index_ref, frac_ref,
                      own_ref, halo_ref, *rest):
        outs, (weighted_ref, halo_cols_ref, left_ref, right_ref) = rest[:-4], rest[-4:]
        slab = lax.axis_index("slab")
        col = lax.axis_index("col")
        lower = col == 0
        for h, r in enumerate(half_rows(slab)):
            r = aligned(r)
            weigh(proj_ref, weighted_ref, h, r, slab * rows, col * cols, sizes, 0, cols)
            from_col = jnp.where(lower, cols, col * cols - reach)
            weigh(received_ref, halo_cols_ref, h, r, slab * rows, from_col, sizes, 0, reach)
        none = jnp.zeros(halo_cols_ref.shape, halo_cols_ref.dtype)
        left_ref[...] = jnp.where(lower, none, halo_cols_ref[...])
        right_ref[...] = jnp.where(lower, halo_cols_ref[...], none)
        work = [(chunks[0], second_half)][: 2 - early]
        work += [(chunk, half) for chunk in chunks[1:] for half in (first_half, second_half)]
        for (columns, half), out_ref in zip(work, outs):
            filter_columns(
                columns, half, weighted_ref, left_ref, right_ref, band_ref, out_ref, 2 * STACK
            )
        write_weights(first_ref, index_ref, frac_ref, own_ref, halo_ref)

    shapes = [bf16(part, widths[0])] * (2 - early)
    shapes += [bf16(part, w) for w in widths[1:] for _ in range(2)]
    own_weight, halo_weight, *second_out = kernel_call(
        second_kernel,
        [bf16(depth, 2 * part), bf16(depth, halos * part)] + shapes,
        (projections, received, band, row_first[:, 0], interp_index, interp_frac),
        4 * part * length * (cols - width // 2),
        scratch=[pltpu.VMEM((2 * part, cols), jnp.bfloat16)]
        + [pltpu.VMEM((2 * part, reach), jnp.bfloat16)] * 3,
        name="other_columns",
        specs=[VMEM, VMEM, VMEM, SMEM, VMEM, VMEM],
    )
    filtered = [(*first_out, *second_out[: 2 - early])]
    for at in range(2 - early, len(second_out), 2):
        filtered.append(second_out[at : at + 2])
        halo_rows.append(exchange(second_out[at : at + halos]))

    def project(index, after=()):
        width = widths[index]

        def body(own_ref, halo_ref, *rest):
            sources, outs = rest[: 2 + halos], rest[2 + halos + len(after) :]
            for c in range(0, width, BLOCK):
                cut = slice(c, c + BLOCK)
                own = jnp.concatenate([ref[:, cut] for ref in sources[:2]], axis=0)
                other = [ref[:, cut] for ref in sources[2:]]
                other = other[0] if len(other) == 1 else jnp.concatenate(other, axis=0)
                total = jnp.dot(own_ref[...], own, preferred_element_type=jnp.float32)
                total += jnp.dot(halo_ref[...], other, preferred_element_type=jnp.float32)
                total = total * scale
                at = 0
                for out in outs:
                    out[:, cut] = total[at : at + out.shape[0], :].astype(out.dtype)
                    at += out.shape[0]

        if quick:
            first = [bf16(shard, width)] * 2 if DIRECT[index] else [bf16(2 * shard, width)]
            shapes = [*first, bf16(shard, width), f32(shard, width)]
        else:
            shapes = [f32(depth, width)]
        return kernel_call(
            body,
            shapes,
            (own_weight, halo_weight, *filtered[index], *halo_rows[index], *after),
            2 * depth * (2 + halos) * part * width,
            name="interpolate",
            specs=[VMEM] * (4 + halos) + [HELD] * len(after),
        )

    def widen(x):
        return x.astype(jnp.float32)

    def at_end():
        angle = lax.axis_index("angle")
        return (angle == 0) | (angle == line - 1)

    neighbours = [(0, 1), (1, 0), (2, 3), (3, 2)]
    middles = [(1, 2), (2, 1), (0, 0), (3, 3)]
    second_hop = [(0, 1), (1, 3), (2, 0), (3, 2)]
    straight = [(0, 2), (3, 1), (1, 0), (2, 3)]

    def first_hops(*parts):
        if len(parts) == 1:
            return [lax.ppermute(parts[0], "angle", neighbours)]
        near, middle = parts
        two = lax.ppermute(middle, "angle", straight)
        three = lax.ppermute(middle, "angle", middles)
        one = lax.ppermute(near, "angle", neighbours)
        return [one, three, two]

    def relay(sent, own, far, kept, after=(), weight=1):
        direct = len(sent) == 3
        arrived = sent[:2] if direct else [sent[0], own[0]]

        def body(one_ref, other_ref, far_ref, kept_ref, *rest):
            outs = rest[len(after) :]
            end = at_end()
            near = widen(one_ref[:shard, :])
            relayed = widen(far_ref[...]) + jnp.where(end, 0.0, near)
            outs[0][...] = relayed.astype(jnp.bfloat16)
            if direct:
                outs[1][...] = kept_ref[...] + jnp.where(end, near, widen(other_ref[...]))
            else:
                outs[1][...] = kept_ref[...] + jnp.where(end, near, 0.0)
                crossed = widen(one_ref[shard:, :]) + widen(other_ref[shard:, :])
                outs[2][...] = crossed.astype(jnp.bfloat16)

        relayed, partial, *crossed = kernel_call(
            body,
            [bf16(*far.shape), f32(*kept.shape)] + [bf16(*far.shape)] * (not direct),
            (*arrived, far, kept, *after),
            far.size * 2 * weight,
            name="relay",
            specs=[VMEM] * 4 + [HELD] * len(after),
        )
        four = lax.ppermute(relayed, "angle", second_hop)
        three = sent[2] if direct else lax.ppermute(crossed[0], "angle", middles)
        return partial, three, four

    def total(partial_ref, two_ref, four_ref):
        direct = jnp.where(at_end(), 0.0, widen(two_ref[...]))
        return partial_ref[...] + direct + widen(four_ref[...])

    def finish(partial, two, four, weight=1):
        def body(partial_ref, two_ref, four_ref, out_ref):
            out_ref[...] = total(partial_ref, two_ref, four_ref)

        return kernel_call(
            body, [f32(*partial.shape)], (partial, two, four), partial.size * 2 * weight, name="finish"
        )[0]

    def store(done, pieces):
        first = len(done)
        given = [*done, *(piece for triple in pieces for piece in triple)]

        def body(*refs):
            ready, refs = refs[:first], refs[first:]
            volume_ref, sem = refs[3 * len(pieces)], refs[-1]
            totals = refs[3 * len(pieces) + 1 : -1]

            def copy(index, source):
                at = pl.ds(chunks[index][0], chunks[index][1])
                return pltpu.make_async_copy(source, volume_ref.at[:, at], sem.at[index])

            copies = [copy(i, ref) for i, ref in enumerate(ready)]
            for c in copies:
                c.start()
            for i, total_ref in enumerate(totals):
                total_ref[...] = total(*refs[3 * i : 3 * i + 3])
                copies.append(copy(first + i, total_ref))
                copies[-1].start()
            for c in copies:
                c.wait()

        return pl.pallas_call(
            body,
            out_shape=f32(shard, cols),
            in_specs=[VMEM] * len(given),
            out_specs=HELD,
            scratch_shapes=[
                *(pltpu.VMEM((shard, w), jnp.float32) for w in widths[first:]),
                pltpu.SemaphoreType.DMA((len(chunks),)),
            ],
            compiler_params=pltpu.CompilerParams(vmem_limit_bytes=VMEM_BYTES),
            name="store",
        )(*given)

    if not quick:
        sums = [
            lax.psum_scatter(project(i)[0], "angle", scatter_dimension=0, tiled=True)
            for i in range(len(chunks))
        ]
        return jnp.concatenate([sums[i] for i in sorted(range(len(chunks)), key=chunks.__getitem__)], 1)

    last = len(chunks) - 1
    *own, far, kept = project(0)
    sent = first_hops(*own)
    done, pieces = [], []
    for j in range(last + 1):
        here = (sent, own, far, kept)
        after = sent[2:] if j == 0 else done[-1:] if j < last else []
        if j < last:
            *own, far, kept = project(j + 1, after=[p[0] for p in pieces[-1:]])
            sent = first_hops(*own)
            after = [*after, kept]
        pieces.append(relay(*here, after=after, weight=WEIGHTS[j]))
        if j < last:
            done.append(finish(*pieces[j], weight=FINISH_WEIGHTS[j]))
    return store(done, pieces[last:])


def solution(mesh):
    placed = (
        P(("group", "angle"), "slab", "col"),
        P(),
        P(("group", "angle"), "slab"),
        P(("group", "angle"), "slab", None),
        P(("group", "angle"), "slab", None),
    )
    return jax.shard_map(
        on_device,
        mesh=mesh,
        in_specs=placed,
        out_specs=P(("group", "slab", "angle"), "col"),
        check_vma=False,
    )
```

```python
import math

import jax
import jax.numpy as jnp
from jax import lax
from jax.experimental import pallas as pl
from jax.experimental.pallas import tpu as pltpu
from jax.sharding import PartitionSpec as P

BLOCK = 256
TILE = 128
STACK = 4
DIRECT = (True, True, True, True)
WEIGHTS = (40000, 40000, 1, 1)
FINISH_WEIGHTS = (1, 1, 10000)
VMEM_BYTES = 14 * 1024 * 1024
FIRST_VMEM_BYTES = 103 * 512 * 1024
LINE_ORDER = ((3, 2, 1, 0), (0, 2, 3, 1), (3, 1, 0, 2), (0, 1, 2, 3))

VMEM = pl.BlockSpec(memory_space=pltpu.VMEM)
HELD = pl.BlockSpec(memory_space=pltpu.HBM)
SMEM = pl.BlockSpec(memory_space=pltpu.SMEM)


def kernel_call(
    body, out_shape, args, flops, scratch=(), name=None, specs=None, grant=VMEM_BYTES, carried=()
):
    specs = specs or [VMEM] * len(args)
    moved = sum(a.size * a.dtype.itemsize for a in (*args, *out_shape))
    n_in, n_out, n_through = len(args), len(out_shape), len(carried)

    def kernel(*refs):
        ins, refs = refs[:n_in], refs[n_in + n_through :]
        body(*ins, *refs[:n_out], *refs[n_out + n_through :])

    return pl.pallas_call(
        kernel,
        out_shape=[*out_shape, *(jax.ShapeDtypeStruct(c.shape, c.dtype) for c in carried)],
        in_specs=[*specs, *([HELD] * n_through)],
        out_specs=[VMEM] * n_out + [HELD] * n_through,
        input_output_aliases={n_in + i: n_out + i for i in range(n_through)},
        scratch_shapes=list(scratch),
        compiler_params=pltpu.CompilerParams(vmem_limit_bytes=grant),
        cost_estimate=pl.CostEstimate(flops=flops, bytes_accessed=moved, transcendentals=0),
        name=name,
    )(*args, *carried)


def build_band(taps_ref, band_ref):
    count = taps_ref.shape[0]
    steps, tiles = band_ref.shape[1] // TILE, band_ref.shape[0] // TILE
    zero = jnp.zeros((TILE, TILE), jnp.float32)
    ahead = lax.broadcasted_iota(jnp.int32, (TILE, TILE), 1) >= lax.broadcasted_iota(
        jnp.int32, (TILE, TILE), 0
    )
    taps = taps_ref[...].astype(jnp.float32)

    def shifted(d):
        if not 0 <= d < count:
            return zero
        row = jnp.broadcast_to(taps[d : d + 1, :], (TILE, TILE))
        return pltpu.roll(row, 0, 1, stride=1, stride_axis=0)

    before = zero
    for d in range(-(steps - 1), tiles):
        here = shifted(d)
        block = jnp.where(ahead, here, before).T.astype(jnp.bfloat16)
        before = here
        for c in range(steps):
            if 0 <= d + c < tiles:
                band_ref[(d + c) * TILE : (d + c + 1) * TILE, c * TILE : (c + 1) * TILE] = block


def weigh(proj_ref, weighted_ref, half, row_at, row_start, col_start, sizes, start, stop):
    angles = proj_ref.shape[0]
    total_rows, total_cols, count = sizes
    distance = jnp.float32(total_cols)
    v = lax.broadcasted_iota(jnp.int32, (count, 1), 0) + (row_start + row_at)
    v = v.astype(jnp.float32) - total_rows / 2 + 0.5
    step = BLOCK
    for c in range(start, stop, step):
        u = lax.broadcasted_iota(jnp.int32, (1, step), 1) + (col_start + c)
        u = u.astype(jnp.float32) - total_cols / 2 + 0.5
        factor = distance / jnp.sqrt(distance * distance + u * u + v * v)
        for a in range(angles):
            raw = proj_ref[a, pl.ds(row_at, count), c : c + step].astype(jnp.float32)
            at = (half * angles + a) * count
            weighted_ref[at : at + count, c : c + step] = (raw * factor).astype(jnp.bfloat16)


def filter_columns(columns, rows, weighted_ref, left_ref, right_ref, band_ref, out_ref, stack):
    cols = weighted_ref.shape[1]
    length = band_ref.shape[0]
    reach = (length - BLOCK) // 2
    count = rows.stop - rows.start

    def window(c):
        lo, hi = c - reach, c - reach + length
        pieces = []
        if lo < 0:
            pieces.append(left_ref[rows, reach + lo : reach + min(hi, 0)])
        if max(lo, 0) < min(hi, cols):
            pieces.append(weighted_ref[rows, max(lo, 0) : min(hi, cols)])
        if hi > cols:
            pieces.append(right_ref[rows, max(lo - cols, 0) : hi - cols])
        return pieces[0] if len(pieces) == 1 else jnp.concatenate(pieces, axis=1)

    starts = range(columns[0], columns[0] + columns[1], BLOCK)
    for at in range(0, len(starts), stack):
        group = starts[at : at + stack]
        tall = jnp.concatenate([window(c) for c in group], axis=0)
        result = jnp.dot(tall, band_ref[...], preferred_element_type=jnp.float32)
        result = result.astype(jnp.bfloat16)
        for k in range(len(group)):
            out_ref[:, (at + k) * BLOCK : (at + k + 1) * BLOCK] = result[
                k * count : (k + 1) * count, :
            ]


def bf16(*shape):
    return jax.ShapeDtypeStruct(shape, jnp.bfloat16)


def f32(*shape):
    return jax.ShapeDtypeStruct(shape, jnp.float32)


def chunk_plan(cols, reach):
    assert cols >= 2 * reach + 4 * BLOCK
    cut = reach + (cols - 2 * reach) // 2 // BLOCK * BLOCK
    return [(reach, cut - reach), (cut, cols - reach - cut), (0, reach), (cols - reach, reach)]


def on_device(projections, filter_taps, row_first, interp_index, interp_frac):
    angles, rows, cols = projections.shape
    depth = interp_index.shape[2]
    taps = filter_taps.shape[0]
    reach = taps // 2
    length = taps + BLOCK
    margin = rows // 2
    slabs, line, sides = (lax.axis_size(n) for n in ("slab", "angle", "col"))
    scale = math.pi / (angles * line)
    both = slabs == 2
    halos = 1 if both else 2
    quick = line == 4
    shard = depth // line
    order = LINE_ORDER if quick else (tuple(range(line)),) * line
    total_rows, total_cols = rows * slabs, cols * sides
    chunks = chunk_plan(cols, reach)
    widths = [w for _, w in chunks]
    part = angles * margin
    first_half, second_half = slice(0, part), slice(part, 2 * part)
    sizes = (total_rows, total_cols, margin)

    def half_rows(slab):
        if both:
            return jnp.where(slab == 0, margin, 0), jnp.where(slab == 0, 0, margin)
        return margin, 0

    def aligned(row):
        return row if isinstance(row, int) else pl.multiple_of(row, margin)

    start, width = chunks[0]
    assert start == reach
    window = width + 2 * reach
    early = halos

    def first_kernel(proj_ref, taps_ref, band_ref, edge_ref, *rest):
        outs, (raw_ref, weighted_ref, sem) = rest[:-3], rest[-3:]
        slab = lax.axis_index("slab")
        col = lax.axis_index("col")
        starts = [aligned(r) for r in half_rows(slab)][:early]
        copies = [
            pltpu.make_async_copy(
                proj_ref.at[a, pl.ds(r, margin), pl.ds(0, window)],
                raw_ref.at[a, pl.ds(r, margin), :],
                sem.at[a * 2 + h],
            )
            for a in range(angles)
            for h, r in enumerate(starts)
        ]
        edge_col = pl.multiple_of(jnp.where(col == 0, cols - reach, 0), TILE)
        edge_copy = pltpu.make_async_copy(
            proj_ref.at[:, :, pl.ds(edge_col, reach)], edge_ref, sem.at[2 * angles]
        )
        for copy in copies:
            copy.start()
        edge_copy.start()
        build_band(taps_ref, band_ref)
        for copy in copies:
            copy.wait()
        for h, r in enumerate(starts):
            weigh(raw_ref, weighted_ref, h, r, slab * rows, col * cols, sizes, 0, window)
        for h, out_ref in enumerate(outs):
            filter_columns(
                (reach, width),
                (first_half, second_half)[h],
                weighted_ref,
                None,
                None,
                band_ref,
                out_ref,
                2 * STACK,
            )
        edge_copy.wait()

    band, edge, *first_out = kernel_call(
        first_kernel,
        [bf16(length, BLOCK), bf16(angles, rows, reach)] + [bf16(part, width)] * early,
        (projections, filter_taps.reshape(taps // TILE, TILE)),
        2 * early * part * length * width,
        scratch=[
            pltpu.VMEM((angles, rows, window), jnp.bfloat16),
            pltpu.VMEM((early * part, window), jnp.bfloat16),
            pltpu.SemaphoreType.DMA((2 * angles + 1,)),
        ],
        name="first_columns",
        specs=[HELD, VMEM],
        grant=FIRST_VMEM_BYTES,
    )

    up = [(i, (i + 1) % slabs) for i in range(slabs - 1)]
    down = [(j, i) for i, j in up]

    def exchange(sends):
        if both:
            return [lax.ppermute(sends[0], "slab", up + down)]
        return [lax.ppermute(sends[0], "slab", up), lax.ppermute(sends[1], "slab", down)]

    assert sides == 2
    received = lax.ppermute(edge, "col", [(0, 1), (1, 0)])
    halo_rows = [exchange(first_out)]

    def write_weights(first_ref, index_ref, frac_ref, own_ref, halo_ref):
        slab = lax.axis_index("slab")
        angle = lax.axis_index("angle")
        if both:
            bases = [jnp.where(slab == 0, rows, rows - margin)]
        else:
            bases = [slab * rows - margin, (slab + 1) * rows]

        def weights(a, base):
            slot = lax.broadcasted_iota(jnp.int32, (margin, depth), 0) + base
            position = index_ref[a] + first_ref[a]
            frac = frac_ref[a]
            high = frac.astype(jnp.bfloat16).astype(jnp.float32)
            low = (1.0 - frac).astype(jnp.bfloat16).astype(jnp.float32)
            return jnp.where(slot == position, low, 0.0) + jnp.where(slot == position + 1, high, 0.0)

        here = [slab * rows + r for r in half_rows(slab)]
        for starts, ref in ((here, own_ref), (bases, halo_ref)):
            table = jnp.concatenate([weights(a, b) for b in starts for a in range(angles)], axis=0)
            turned = table.T.astype(jnp.bfloat16)
            for s in range(line):
                if quick:
                    places = [o.index(s) for o in order]
                    place = places[line - 1]
                    for i in range(line - 1):
                        place = jnp.where(angle == i, places[i], place)
                    at = pl.multiple_of(place * shard, shard)
                else:
                    at = s * shard
                ref[pl.ds(at, shard), :] = turned[s * shard : (s + 1) * shard, :]

    def second_kernel(proj_ref, received_ref, band_ref, first_ref, index_ref, frac_ref,
                      own_ref, halo_ref, *rest):
        outs, (weighted_ref, halo_cols_ref, left_ref, right_ref) = rest[:-4], rest[-4:]
        slab = lax.axis_index("slab")
        col = lax.axis_index("col")
        lower = col == 0
        for h, r in enumerate(half_rows(slab)):
            r = aligned(r)
            weigh(proj_ref, weighted_ref, h, r, slab * rows, col * cols, sizes, 0, cols)
            from_col = jnp.where(lower, cols, col * cols - reach)
            weigh(received_ref, halo_cols_ref, h, r, slab * rows, from_col, sizes, 0, reach)
        none = jnp.zeros(halo_cols_ref.shape, halo_cols_ref.dtype)
        left_ref[...] = jnp.where(lower, none, halo_cols_ref[...])
        right_ref[...] = jnp.where(lower, halo_cols_ref[...], none)
        work = [(chunks[0], second_half)][: 2 - early]
        work += [(chunk, half) for chunk in chunks[1:] for half in (first_half, second_half)]
        for (columns, half), out_ref in zip(work, outs):
            filter_columns(
                columns, half, weighted_ref, left_ref, right_ref, band_ref, out_ref, 2 * STACK
            )
        write_weights(first_ref, index_ref, frac_ref, own_ref, halo_ref)

    shapes = [bf16(part, widths[0])] * (2 - early)
    shapes += [bf16(part, w) for w in widths[1:] for _ in range(2)]
    own_weight, halo_weight, *second_out = kernel_call(
        second_kernel,
        [bf16(depth, 2 * part), bf16(depth, halos * part)] + shapes,
        (projections, received, band, row_first[:, 0], interp_index, interp_frac),
        4 * part * length * (cols - width // 2),
        scratch=[pltpu.VMEM((2 * part, cols), jnp.bfloat16)]
        + [pltpu.VMEM((2 * part, reach), jnp.bfloat16)] * 3,
        name="other_columns",
        specs=[VMEM, VMEM, VMEM, SMEM, VMEM, VMEM],
    )
    filtered = [(*first_out, *second_out[: 2 - early])]
    for at in range(2 - early, len(second_out), 2):
        filtered.append(second_out[at : at + 2])
        halo_rows.append(exchange(second_out[at : at + halos]))

    def project(index, after=()):
        width = widths[index]

        def body(own_ref, halo_ref, *rest):
            sources, outs = rest[: 2 + halos], rest[2 + halos + len(after) :]
            for c in range(0, width, BLOCK):
                cut = slice(c, c + BLOCK)
                own = jnp.concatenate([ref[:, cut] for ref in sources[:2]], axis=0)
                other = [ref[:, cut] for ref in sources[2:]]
                other = other[0] if len(other) == 1 else jnp.concatenate(other, axis=0)
                total = jnp.dot(own_ref[...], own, preferred_element_type=jnp.float32)
                total += jnp.dot(halo_ref[...], other, preferred_element_type=jnp.float32)
                total = total * scale
                at = 0
                for out in outs:
                    out[:, cut] = total[at : at + out.shape[0], :].astype(out.dtype)
                    at += out.shape[0]

        if quick:
            first = [bf16(shard, width)] * 2 if DIRECT[index] else [bf16(2 * shard, width)]
            shapes = [*first, bf16(shard, width), f32(shard, width)]
        else:
            shapes = [f32(depth, width)]
        return kernel_call(
            body,
            shapes,
            (own_weight, halo_weight, *filtered[index], *halo_rows[index], *after),
            2 * depth * (2 + halos) * part * width,
            name="interpolate",
            specs=[VMEM] * (4 + halos) + [HELD] * len(after),
        )

    def widen(x):
        return x.astype(jnp.float32)

    def at_end():
        angle = lax.axis_index("angle")
        return (angle == 0) | (angle == line - 1)

    neighbours = [(0, 1), (1, 0), (2, 3), (3, 2)]
    middles = [(1, 2), (2, 1), (0, 0), (3, 3)]
    second_hop = [(0, 1), (1, 3), (2, 0), (3, 2)]
    straight = [(0, 2), (3, 1), (1, 0), (2, 3)]

    def first_hops(*parts):
        if len(parts) == 1:
            return [lax.ppermute(parts[0], "angle", neighbours)]
        near, middle = parts
        two = lax.ppermute(middle, "angle", straight)
        three = lax.ppermute(middle, "angle", middles)
        one = lax.ppermute(near, "angle", neighbours)
        return [one, three, two]

    def relay(sent, own, far, kept, after=(), weight=1):
        direct = len(sent) == 3
        arrived = sent[:2] if direct else [sent[0], own[0]]

        def body(one_ref, other_ref, far_ref, kept_ref, *rest):
            outs = rest[len(after) :]
            end = at_end()
            near = widen(one_ref[:shard, :])
            relayed = widen(far_ref[...]) + jnp.where(end, 0.0, near)
            outs[0][...] = relayed.astype(jnp.bfloat16)
            if direct:
                outs[1][...] = kept_ref[...] + jnp.where(end, near, widen(other_ref[...]))
            else:
                outs[1][...] = kept_ref[...] + jnp.where(end, near, 0.0)
                crossed = widen(one_ref[shard:, :]) + widen(other_ref[shard:, :])
                outs[2][...] = crossed.astype(jnp.bfloat16)

        relayed, partial, *crossed = kernel_call(
            body,
            [bf16(*far.shape), f32(*kept.shape)] + [bf16(*far.shape)] * (not direct),
            (*arrived, far, kept, *after),
            far.size * 2 * weight,
            name="relay",
            specs=[VMEM] * 4 + [HELD] * len(after),
        )
        four = lax.ppermute(relayed, "angle", second_hop)
        three = sent[2] if direct else lax.ppermute(crossed[0], "angle", middles)
        return partial, three, four

    def total(partial_ref, two_ref, four_ref):
        direct = jnp.where(at_end(), 0.0, widen(two_ref[...]))
        return partial_ref[...] + direct + widen(four_ref[...])

    def finish(partial, two, four, weight=1):
        def body(partial_ref, two_ref, four_ref, out_ref):
            out_ref[...] = total(partial_ref, two_ref, four_ref)

        return kernel_call(
            body, [f32(*partial.shape)], (partial, two, four), partial.size * 2 * weight, name="finish"
        )[0]

    def store(done, pieces):
        first = len(done)
        given = [*done, *(piece for triple in pieces for piece in triple)]

        def body(*refs):
            ready, refs = refs[:first], refs[first:]
            volume_ref, sem = refs[3 * len(pieces)], refs[-1]
            totals = refs[3 * len(pieces) + 1 : -1]

            def copy(index, source):
                at = pl.ds(chunks[index][0], chunks[index][1])
                return pltpu.make_async_copy(source, volume_ref.at[:, at], sem.at[index])

            copies = [copy(i, ref) for i, ref in enumerate(ready)]
            for c in copies:
                c.start()
            for i, total_ref in enumerate(totals):
                total_ref[...] = total(*refs[3 * i : 3 * i + 3])
                copies.append(copy(first + i, total_ref))
                copies[-1].start()
            for c in copies:
                c.wait()

        return pl.pallas_call(
            body,
            out_shape=f32(shard, cols),
            in_specs=[VMEM] * len(given),
            out_specs=HELD,
            scratch_shapes=[
                *(pltpu.VMEM((shard, w), jnp.float32) for w in widths[first:]),
                pltpu.SemaphoreType.DMA((len(chunks),)),
            ],
            compiler_params=pltpu.CompilerParams(vmem_limit_bytes=VMEM_BYTES),
            name="store",
        )(*given)

    if not quick:
        sums = [
            lax.psum_scatter(project(i)[0], "angle", scatter_dimension=0, tiled=True)
            for i in range(len(chunks))
        ]
        return jnp.concatenate([sums[i] for i in sorted(range(len(chunks)), key=chunks.__getitem__)], 1)

    last = len(chunks) - 1
    *own, far, kept = project(0)
    sent = first_hops(*own)
    done, pieces = [], []
    for j in range(last + 1):
        here = (sent, own, far, kept)
        after = sent[2:] if j == 0 else done[-1:] if j < last else []
        if j < last:
            *own, far, kept = project(j + 1, after=[p[0] for p in pieces[-1:]])
            sent = first_hops(*own)
            after = [*after, kept]
        pieces.append(relay(*here, after=after, weight=WEIGHTS[j]))
        if j < last:
            done.append(finish(*pieces[j], weight=FINISH_WEIGHTS[j]))
    return store(done, pieces[last:])


def solution(mesh):
    placed = (
        P(("group", "angle"), "slab", "col"),
        P(),
        P(("group", "angle"), "slab"),
        P(("group", "angle"), "slab", None),
        P(("group", "angle"), "slab", None),
    )
    return jax.shard_map(
        on_device,
        mesh=mesh,
        in_specs=placed,
        out_specs=P(("group", "slab", "angle"), "col"),
        check_vma=False,
    )
```

```python
import math

import jax
import jax.numpy as jnp
from jax import lax
from jax.experimental import pallas as pl
from jax.experimental.pallas import tpu as pltpu
from jax.sharding import PartitionSpec as P

BLOCK = 256
TILE = 128
STACK = 8
DIRECT = (True, True, True, True)
WEIGHTS = (40000, 40000, 1, 1)
FINISH_WEIGHTS = (1, 1, 10000)
VMEM_BYTES = 14 * 1024 * 1024
FIRST_VMEM_BYTES = 103 * 512 * 1024
LINE_ORDER = ((3, 2, 1, 0), (0, 2, 3, 1), (3, 1, 0, 2), (0, 1, 2, 3))

VMEM = pl.BlockSpec(memory_space=pltpu.VMEM)
HELD = pl.BlockSpec(memory_space=pltpu.HBM)
SMEM = pl.BlockSpec(memory_space=pltpu.SMEM)


def kernel_call(
    body, out_shape, args, flops, scratch=(), name=None, specs=None, grant=VMEM_BYTES, carried=()
):
    specs = specs or [VMEM] * len(args)
    moved = sum(a.size * a.dtype.itemsize for a in (*args, *out_shape))
    n_in, n_out, n_through = len(args), len(out_shape), len(carried)

    def kernel(*refs):
        ins, refs = refs[:n_in], refs[n_in + n_through :]
        body(*ins, *refs[:n_out], *refs[n_out + n_through :])

    return pl.pallas_call(
        kernel,
        out_shape=[*out_shape, *(jax.ShapeDtypeStruct(c.shape, c.dtype) for c in carried)],
        in_specs=[*specs, *([HELD] * n_through)],
        out_specs=[VMEM] * n_out + [HELD] * n_through,
        input_output_aliases={n_in + i: n_out + i for i in range(n_through)},
        scratch_shapes=list(scratch),
        compiler_params=pltpu.CompilerParams(vmem_limit_bytes=grant),
        cost_estimate=pl.CostEstimate(flops=flops, bytes_accessed=moved, transcendentals=0),
        name=name,
    )(*args, *carried)


def build_band(taps_ref, band_ref):
    count = taps_ref.shape[0]
    steps, tiles = band_ref.shape[1] // TILE, band_ref.shape[0] // TILE
    zero = jnp.zeros((TILE, TILE), jnp.float32)
    ahead = lax.broadcasted_iota(jnp.int32, (TILE, TILE), 1) >= lax.broadcasted_iota(
        jnp.int32, (TILE, TILE), 0
    )
    taps = taps_ref[...].astype(jnp.float32)

    def shifted(d):
        if not 0 <= d < count:
            return zero
        row = jnp.broadcast_to(taps[d : d + 1, :], (TILE, TILE))
        return pltpu.roll(row, 0, 1, stride=1, stride_axis=0)

    before = zero
    for d in range(-(steps - 1), tiles):
        here = shifted(d)
        block = jnp.where(ahead, here, before).T.astype(jnp.bfloat16)
        before = here
        for c in range(steps):
            if 0 <= d + c < tiles:
                band_ref[(d + c) * TILE : (d + c + 1) * TILE, c * TILE : (c + 1) * TILE] = block


def weigh(proj_ref, weighted_ref, half, row_at, row_start, col_start, sizes, c):
    angles = proj_ref.shape[0]
    total_rows, total_cols, count = sizes
    distance = jnp.float32(total_cols)
    v = lax.broadcasted_iota(jnp.int32, (count, 1), 0) + (row_start + row_at)
    v = v.astype(jnp.float32) - total_rows / 2 + 0.5
    u = lax.broadcasted_iota(jnp.int32, (1, BLOCK), 1) + (col_start + c)
    u = u.astype(jnp.float32) - total_cols / 2 + 0.5
    factor = distance / jnp.sqrt(distance * distance + u * u + v * v)
    for a in range(angles):
        raw = proj_ref[a, pl.ds(row_at, count), c : c + BLOCK].astype(jnp.float32)
        at = (half * angles + a) * count
        weighted_ref[at : at + count, c : c + BLOCK] = (raw * factor).astype(jnp.bfloat16)


def filter_columns(work, count, band_ref, weighted_at):
    length = band_ref.shape[0]
    reach = (length - BLOCK) // 2
    groups = []
    for half, first, width, out_ref in work:
        starts = range(first, first + width, BLOCK)
        for at in range(0, len(starts), STACK):
            groups.append((half, starts[at : at + STACK], out_ref, at))

    def touch(index):
        if index < len(groups):
            half, starts, _, _ = groups[index]
            for c in range(starts[0] - reach, starts[-1] + BLOCK + reach, BLOCK):
                weighted_at(half, c)

    touch(0)
    for index, (half, starts, out_ref, at) in enumerate(groups):
        touch(index + 1)
        tall = jnp.concatenate(
            [
                jnp.concatenate(
                    [weighted_at(half, c)() for c in range(s - reach, s + BLOCK + reach, BLOCK)],
                    axis=1,
                )
                for s in starts
            ],
            axis=0,
        )
        result = jnp.dot(tall, band_ref[...], preferred_element_type=jnp.float32)
        result = result.astype(jnp.bfloat16)
        for k in range(len(starts)):
            out_ref[:, (at + k) * BLOCK : (at + k + 1) * BLOCK] = result[
                k * count : (k + 1) * count, :
            ]


def bf16(*shape):
    return jax.ShapeDtypeStruct(shape, jnp.bfloat16)


def f32(*shape):
    return jax.ShapeDtypeStruct(shape, jnp.float32)


def chunk_plan(cols, reach):
    assert cols >= 4 * reach and reach % (4 * BLOCK) == 0
    return [
        (reach + BLOCK, reach - BLOCK),
        (2 * reach, cols - 3 * reach),
        (cols - reach, reach),
        (0, reach + BLOCK),
    ]


def on_device(projections, filter_taps, row_first, interp_index, interp_frac):
    angles, rows, cols = projections.shape
    depth = interp_index.shape[2]
    taps = filter_taps.shape[0]
    reach = taps // 2
    length = taps + BLOCK
    margin = rows // 2
    slabs, line, sides = (lax.axis_size(n) for n in ("slab", "angle", "col"))
    scale = math.pi / (angles * line)
    both = slabs == 2
    halos = 1 if both else 2
    quick = line == 4
    shard = depth // line
    order = LINE_ORDER if quick else (tuple(range(line)),) * line
    total_rows, total_cols = rows * slabs, cols * sides
    chunks = chunk_plan(cols, reach)
    widths = [w for _, w in chunks]
    part = angles * margin
    sizes = (total_rows, total_cols, margin)

    def half_rows(slab):
        if both:
            return jnp.where(slab == 0, margin, 0), jnp.where(slab == 0, 0, margin)
        return margin, 0

    def aligned(row):
        return row if isinstance(row, int) else pl.multiple_of(row, margin)

    start, width = chunks[0]
    window_at, window = start - reach, width + 2 * reach
    early = halos

    def first_kernel(proj_ref, taps_ref, band_ref, edge_ref, *rest):
        outs, (raw_ref, weighted_ref, sem) = rest[:-3], rest[-3:]
        slab = lax.axis_index("slab")
        col = lax.axis_index("col")
        starts = [aligned(r) for r in half_rows(slab)][:early]
        copies = [
            pltpu.make_async_copy(
                proj_ref.at[a, pl.ds(r, margin), pl.ds(window_at, window)],
                raw_ref.at[a, pl.ds(r, margin), :],
                sem.at[a * 2 + h],
            )
            for a in range(angles)
            for h, r in enumerate(starts)
        ]
        edge_col = pl.multiple_of(jnp.where(col == 0, cols - reach, 0), TILE)
        edge_copy = pltpu.make_async_copy(
            proj_ref.at[:, :, pl.ds(edge_col, reach)], edge_ref, sem.at[2 * angles]
        )
        for copy in copies:
            copy.start()
        edge_copy.start()
        build_band(taps_ref, band_ref)
        for copy in copies:
            copy.wait()
        known = set()

        def weighted_at(half, c):
            c -= window_at
            if (half, c) not in known:
                known.add((half, c))
                weigh(
                    raw_ref, weighted_ref, half, starts[half], slab * rows,
                    col * cols + window_at, sizes, c,
                )
            return lambda: weighted_ref[half * part : (half + 1) * part, c : c + BLOCK]

        work = [(h, start, width, out_ref) for h, out_ref in enumerate(outs)]
        filter_columns(work, part, band_ref, weighted_at)
        edge_copy.wait()

    band, edge, *first_out = kernel_call(
        first_kernel,
        [bf16(length, BLOCK), bf16(angles, rows, reach)] + [bf16(part, width)] * early,
        (projections, filter_taps.reshape(taps // TILE, TILE)),
        2 * early * part * length * width,
        scratch=[
            pltpu.VMEM((angles, rows, window), jnp.bfloat16),
            pltpu.VMEM((early * part, window), jnp.bfloat16),
            pltpu.SemaphoreType.DMA((2 * angles + 1,)),
        ],
        name="first_columns",
        specs=[HELD, VMEM],
        grant=FIRST_VMEM_BYTES,
    )

    up = [(i, (i + 1) % slabs) for i in range(slabs - 1)]
    down = [(j, i) for i, j in up]

    def exchange(sends):
        if both:
            return [lax.ppermute(sends[0], "slab", up + down)]
        return [lax.ppermute(sends[0], "slab", up), lax.ppermute(sends[1], "slab", down)]

    assert sides == 2
    received = lax.ppermute(edge, "col", [(0, 1), (1, 0)])
    halo_rows = [exchange(first_out)]

    def write_weights(first_ref, index_ref, frac_ref, own_ref, halo_ref):
        slab = lax.axis_index("slab")
        angle = lax.axis_index("angle")
        if both:
            bases = [jnp.where(slab == 0, rows, rows - margin)]
        else:
            bases = [slab * rows - margin, (slab + 1) * rows]

        def weights(a, base):
            slot = lax.broadcasted_iota(jnp.int32, (margin, depth), 0) + base
            position = index_ref[a] + first_ref[a]
            frac = frac_ref[a]
            high = frac.astype(jnp.bfloat16).astype(jnp.float32)
            low = (1.0 - frac).astype(jnp.bfloat16).astype(jnp.float32)
            return jnp.where(slot == position, low, 0.0) + jnp.where(slot == position + 1, high, 0.0)

        here = [slab * rows + r for r in half_rows(slab)]
        for starts, ref in ((here, own_ref), (bases, halo_ref)):
            table = jnp.concatenate([weights(a, b) for b in starts for a in range(angles)], axis=0)
            turned = table.T.astype(jnp.bfloat16)
            for s in range(line):
                if quick:
                    places = [o.index(s) for o in order]
                    place = places[line - 1]
                    for i in range(line - 1):
                        place = jnp.where(angle == i, places[i], place)
                    at = pl.multiple_of(place * shard, shard)
                else:
                    at = s * shard
                ref[pl.ds(at, shard), :] = turned[s * shard : (s + 1) * shard, :]

    def second_kernel(proj_ref, received_ref, band_ref, first_ref, index_ref, frac_ref,
                      own_ref, halo_ref, *rest):
        outs, (weighted_ref, halo_cols_ref) = rest[:-2], rest[-2:]
        slab = lax.axis_index("slab")
        col = lax.axis_index("col")
        starts = [aligned(r) for r in half_rows(slab)]
        lower = col == 0
        from_col = jnp.where(lower, cols, col * cols - reach)
        none = jnp.zeros((part, BLOCK), jnp.bfloat16)
        known = set()

        def weighted_at(half, c):
            inside = 0 <= c < cols
            source, into = (proj_ref, weighted_ref) if inside else (received_ref, halo_cols_ref)
            first_col = col * cols if inside else from_col
            at = c if inside else c % reach
            if (half, at, inside) not in known:
                known.add((half, at, inside))
                weigh(
                    source, into, half, starts[half], slab * rows, first_col, sizes, at
                )

            def load():
                block = into[half * part : (half + 1) * part, at : at + BLOCK]
                if c < 0:
                    block = jnp.where(lower, none, block)
                elif c >= cols:
                    block = jnp.where(lower, block, none)
                return block

            return load

        work = [(1, *chunks[0])][: 2 - early]
        work += [(half, *chunk) for chunk in chunks[1:] for half in (0, 1)]
        filter_columns(
            [(*w, out_ref) for w, out_ref in zip(work, outs)], part, band_ref, weighted_at
        )
        write_weights(first_ref, index_ref, frac_ref, own_ref, halo_ref)

    shapes = [bf16(part, widths[0])] * (2 - early)
    shapes += [bf16(part, w) for w in widths[1:] for _ in range(2)]
    own_weight, halo_weight, *second_out = kernel_call(
        second_kernel,
        [bf16(depth, 2 * part), bf16(depth, halos * part)] + shapes,
        (projections, received, band, row_first[:, 0], interp_index, interp_frac),
        4 * part * length * (cols - width // 2),
        scratch=[pltpu.VMEM((2 * part, cols), jnp.bfloat16)]
        + [pltpu.VMEM((2 * part, reach), jnp.bfloat16)],
        name="other_columns",
        specs=[VMEM, VMEM, VMEM, SMEM, VMEM, VMEM],
    )
    filtered = [(*first_out, *second_out[: 2 - early])]
    for at in range(2 - early, len(second_out), 2):
        filtered.append(second_out[at : at + 2])
        halo_rows.append(exchange(second_out[at : at + halos]))

    def project(index, after=()):
        width = widths[index]

        def body(own_ref, halo_ref, *rest):
            sources, outs = rest[: 2 + halos], rest[2 + halos + len(after) :]
            for c in range(0, width, BLOCK):
                cut = slice(c, c + BLOCK)
                own = jnp.concatenate([ref[:, cut] for ref in sources[:2]], axis=0)
                other = [ref[:, cut] for ref in sources[2:]]
                other = other[0] if len(other) == 1 else jnp.concatenate(other, axis=0)
                total = jnp.dot(own_ref[...], own, preferred_element_type=jnp.float32)
                total += jnp.dot(halo_ref[...], other, preferred_element_type=jnp.float32)
                total = total * scale
                at = 0
                for out in outs:
                    out[:, cut] = total[at : at + out.shape[0], :].astype(out.dtype)
                    at += out.shape[0]

        if quick:
            first = [bf16(shard, width)] * 2 if DIRECT[index] else [bf16(2 * shard, width)]
            shapes = [*first, bf16(shard, width), f32(shard, width)]
        else:
            shapes = [f32(depth, width)]
        return kernel_call(
            body,
            shapes,
            (own_weight, halo_weight, *filtered[index], *halo_rows[index], *after),
            2 * depth * (2 + halos) * part * width,
            name="interpolate",
            specs=[VMEM] * (4 + halos) + [HELD] * len(after),
        )

    def widen(x):
        return x.astype(jnp.float32)

    def at_end():
        angle = lax.axis_index("angle")
        return (angle == 0) | (angle == line - 1)

    neighbours = [(0, 1), (1, 0), (2, 3), (3, 2)]
    middles = [(1, 2), (2, 1), (0, 0), (3, 3)]
    second_hop = [(0, 1), (1, 3), (2, 0), (3, 2)]
    straight = [(0, 2), (3, 1), (1, 0), (2, 3)]

    def first_hops(*parts):
        if len(parts) == 1:
            return [lax.ppermute(parts[0], "angle", neighbours)]
        near, middle = parts
        two = lax.ppermute(middle, "angle", straight)
        three = lax.ppermute(middle, "angle", middles)
        one = lax.ppermute(near, "angle", neighbours)
        return [one, three, two]

    def relay(sent, own, far, kept, after=(), weight=1):
        direct = len(sent) == 3
        arrived = sent[:2] if direct else [sent[0], own[0]]

        def body(one_ref, other_ref, far_ref, kept_ref, *rest):
            outs = rest[len(after) :]
            end = at_end()
            near = widen(one_ref[:shard, :])
            relayed = widen(far_ref[...]) + jnp.where(end, 0.0, near)
            outs[0][...] = relayed.astype(jnp.bfloat16)
            if direct:
                outs[1][...] = kept_ref[...] + jnp.where(end, near, widen(other_ref[...]))
            else:
                outs[1][...] = kept_ref[...] + jnp.where(end, near, 0.0)
                crossed = widen(one_ref[shard:, :]) + widen(other_ref[shard:, :])
                outs[2][...] = crossed.astype(jnp.bfloat16)

        relayed, partial, *crossed = kernel_call(
            body,
            [bf16(*far.shape), f32(*kept.shape)] + [bf16(*far.shape)] * (not direct),
            (*arrived, far, kept, *after),
            far.size * 2 * weight,
            name="relay",
            specs=[VMEM] * 4 + [HELD] * len(after),
        )
        four = lax.ppermute(relayed, "angle", second_hop)
        three = sent[2] if direct else lax.ppermute(crossed[0], "angle", middles)
        return partial, three, four

    def total(partial_ref, two_ref, four_ref):
        direct = jnp.where(at_end(), 0.0, widen(two_ref[...]))
        return partial_ref[...] + direct + widen(four_ref[...])

    def finish(partial, two, four, weight=1):
        def body(partial_ref, two_ref, four_ref, out_ref):
            out_ref[...] = total(partial_ref, two_ref, four_ref)

        return kernel_call(
            body, [f32(*partial.shape)], (partial, two, four), partial.size * 2 * weight, name="finish"
        )[0]

    def store(done, pieces):
        first = len(done)
        given = [*done, *(piece for triple in pieces for piece in triple)]

        def body(*refs):
            ready, refs = refs[:first], refs[first:]
            volume_ref, sem = refs[3 * len(pieces)], refs[-1]
            totals = refs[3 * len(pieces) + 1 : -1]

            def copy(index, source):
                at = pl.ds(chunks[index][0], chunks[index][1])
                return pltpu.make_async_copy(source, volume_ref.at[:, at], sem.at[index])

            copies = [copy(i, ref) for i, ref in enumerate(ready)]
            for c in copies:
                c.start()
            for i, total_ref in enumerate(totals):
                total_ref[...] = total(*refs[3 * i : 3 * i + 3])
                copies.append(copy(first + i, total_ref))
                copies[-1].start()
            for c in copies:
                c.wait()

        return pl.pallas_call(
            body,
            out_shape=f32(shard, cols),
            in_specs=[VMEM] * len(given),
            out_specs=HELD,
            scratch_shapes=[
                *(pltpu.VMEM((shard, w), jnp.float32) for w in widths[first:]),
                pltpu.SemaphoreType.DMA((len(chunks),)),
            ],
            compiler_params=pltpu.CompilerParams(vmem_limit_bytes=VMEM_BYTES),
            name="store",
        )(*given)

    if not quick:
        sums = [
            lax.psum_scatter(project(i)[0], "angle", scatter_dimension=0, tiled=True)
            for i in range(len(chunks))
        ]
        return jnp.concatenate([sums[i] for i in sorted(range(len(chunks)), key=chunks.__getitem__)], 1)

    last = len(chunks) - 1
    *own, far, kept = project(0)
    sent = first_hops(*own)
    done, pieces = [], []
    for j in range(last + 1):
        here = (sent, own, far, kept)
        after = sent[2:] if j == 0 else done[-1:] if j < last else []
        if j < last:
            *own, far, kept = project(j + 1, after=[p[0] for p in pieces[-1:]])
            sent = first_hops(*own)
            after = [*after, kept]
        pieces.append(relay(*here, after=after, weight=WEIGHTS[j]))
        if j < last:
            done.append(finish(*pieces[j], weight=FINISH_WEIGHTS[j]))
    return store(done, pieces[last:])


def solution(mesh):
    placed = (
        P(("group", "angle"), "slab", "col"),
        P(),
        P(("group", "angle"), "slab"),
        P(("group", "angle"), "slab", None),
        P(("group", "angle"), "slab", None),
    )
    return jax.shard_map(
        on_device,
        mesh=mesh,
        in_specs=placed,
        out_specs=P(("group", "slab", "angle"), "col"),
        check_vma=False,
    )
```

```python
import math

import jax
import jax.numpy as jnp
from jax import lax
from jax.experimental import pallas as pl
from jax.experimental.pallas import tpu as pltpu
from jax.sharding import PartitionSpec as P

BLOCK = 256
TILE = 128
STACK = 8
DIRECT = (True, True, True, True)
WEIGHTS = (40000, 40000, 1, 1)
FINISH_WEIGHTS = (1, 1, 10000)
VMEM_BYTES = 14 * 1024 * 1024
FIRST_VMEM_BYTES = 103 * 512 * 1024
LINE_ORDER = ((3, 2, 1, 0), (0, 2, 3, 1), (3, 1, 0, 2), (0, 1, 2, 3))

VMEM = pl.BlockSpec(memory_space=pltpu.VMEM)
HELD = pl.BlockSpec(memory_space=pltpu.HBM)
SMEM = pl.BlockSpec(memory_space=pltpu.SMEM)


def kernel_call(
    body, out_shape, args, flops, scratch=(), name=None, specs=None, grant=VMEM_BYTES, carried=()
):
    specs = specs or [VMEM] * len(args)
    moved = sum(a.size * a.dtype.itemsize for a in (*args, *out_shape))
    n_in, n_out, n_through = len(args), len(out_shape), len(carried)

    def kernel(*refs):
        ins, refs = refs[:n_in], refs[n_in + n_through :]
        body(*ins, *refs[:n_out], *refs[n_out + n_through :])

    return pl.pallas_call(
        kernel,
        out_shape=[*out_shape, *(jax.ShapeDtypeStruct(c.shape, c.dtype) for c in carried)],
        in_specs=[*specs, *([HELD] * n_through)],
        out_specs=[VMEM] * n_out + [HELD] * n_through,
        input_output_aliases={n_in + i: n_out + i for i in range(n_through)},
        scratch_shapes=list(scratch),
        compiler_params=pltpu.CompilerParams(vmem_limit_bytes=grant),
        cost_estimate=pl.CostEstimate(flops=flops, bytes_accessed=moved, transcendentals=0),
        name=name,
    )(*args, *carried)


def build_band(taps_ref, band_ref):
    count = taps_ref.shape[0]
    steps, tiles = band_ref.shape[1] // TILE, band_ref.shape[0] // TILE
    zero = jnp.zeros((TILE, TILE), jnp.float32)
    ahead = lax.broadcasted_iota(jnp.int32, (TILE, TILE), 1) >= lax.broadcasted_iota(
        jnp.int32, (TILE, TILE), 0
    )
    taps = taps_ref[...].astype(jnp.float32)

    def shifted(d):
        if not 0 <= d < count:
            return zero
        row = jnp.broadcast_to(taps[d : d + 1, :], (TILE, TILE))
        return pltpu.roll(row, 0, 1, stride=1, stride_axis=0)

    before = zero
    for d in range(-(steps - 1), tiles):
        here = shifted(d)
        block = jnp.where(ahead, here, before).T.astype(jnp.bfloat16)
        before = here
        for c in range(steps):
            if 0 <= d + c < tiles:
                band_ref[(d + c) * TILE : (d + c + 1) * TILE, c * TILE : (c + 1) * TILE] = block


def weigh(proj_ref, weighted_ref, half, row_at, row_start, col_start, sizes, c):
    angles = proj_ref.shape[0]
    total_rows, total_cols, count = sizes
    distance = jnp.float32(total_cols)
    v = lax.broadcasted_iota(jnp.int32, (count, 1), 0) + (row_start + row_at)
    v = v.astype(jnp.float32) - total_rows / 2 + 0.5
    u = lax.broadcasted_iota(jnp.int32, (1, BLOCK), 1) + (col_start + c)
    u = u.astype(jnp.float32) - total_cols / 2 + 0.5
    factor = distance / jnp.sqrt(distance * distance + u * u + v * v)
    for a in range(angles):
        raw = proj_ref[a, pl.ds(row_at, count), c : c + BLOCK].astype(jnp.float32)
        at = (half * angles + a) * count
        weighted_ref[at : at + count, c : c + BLOCK] = (raw * factor).astype(jnp.bfloat16)


def filter_columns(work, count, band_ref, weighted_at):
    length = band_ref.shape[0]
    reach = (length - BLOCK) // 2
    groups = []
    for half, first, width, out_ref in work:
        starts = range(first, first + width, BLOCK)
        for at in range(0, len(starts), STACK):
            groups.append((half, starts[at : at + STACK], out_ref, at))

    def touch(index):
        if index < len(groups):
            half, starts, _, _ = groups[index]
            for c in range(starts[0] - reach, starts[-1] + BLOCK + reach, BLOCK):
                weighted_at(half, c)

    touch(0)
    for index, (half, starts, out_ref, at) in enumerate(groups):
        touch(index + 1)
        tall = jnp.concatenate(
            [
                jnp.concatenate(
                    [weighted_at(half, c)() for c in range(s - reach, s + BLOCK + reach, BLOCK)],
                    axis=1,
                )
                for s in starts
            ],
            axis=0,
        )
        result = jnp.dot(tall, band_ref[...], preferred_element_type=jnp.float32)
        result = result.astype(jnp.bfloat16)
        for k in range(len(starts)):
            out_ref[:, (at + k) * BLOCK : (at + k + 1) * BLOCK] = result[
                k * count : (k + 1) * count, :
            ]


def bf16(*shape):
    return jax.ShapeDtypeStruct(shape, jnp.bfloat16)


def f32(*shape):
    return jax.ShapeDtypeStruct(shape, jnp.float32)


def chunk_plan(cols, reach):
    assert cols >= 4 * reach and reach % (4 * BLOCK) == 0
    return [
        (reach + BLOCK, reach - BLOCK),
        (2 * reach, cols - 3 * reach),
        (cols - reach, reach),
        (0, reach + BLOCK),
    ]


def on_device(projections, filter_taps, row_first, interp_index, interp_frac):
    angles, rows, cols = projections.shape
    depth = interp_index.shape[2]
    taps = filter_taps.shape[0]
    reach = taps // 2
    length = taps + BLOCK
    margin = rows // 2
    slabs, line, sides = (lax.axis_size(n) for n in ("slab", "angle", "col"))
    scale = math.pi / (angles * line)
    both = slabs == 2
    halos = 1 if both else 2
    quick = line == 4
    shard = depth // line
    order = LINE_ORDER if quick else (tuple(range(line)),) * line
    total_rows, total_cols = rows * slabs, cols * sides
    chunks = chunk_plan(cols, reach)
    widths = [w for _, w in chunks]
    part = angles * margin
    sizes = (total_rows, total_cols, margin)

    def half_rows(slab):
        if both:
            return jnp.where(slab == 0, margin, 0), jnp.where(slab == 0, 0, margin)
        return margin, 0

    def aligned(row):
        return row if isinstance(row, int) else pl.multiple_of(row, margin)

    start, width = chunks[0]
    window_at, window = start - reach, width + 2 * reach
    early = halos

    def first_kernel(proj_ref, taps_ref, band_ref, edge_ref, *rest):
        outs, (raw_ref, weighted_ref, sem) = rest[:-3], rest[-3:]
        slab = lax.axis_index("slab")
        col = lax.axis_index("col")
        starts = [aligned(r) for r in half_rows(slab)][:early]
        copies = [
            pltpu.make_async_copy(
                proj_ref.at[a, pl.ds(r, margin), pl.ds(window_at, window)],
                raw_ref.at[a, pl.ds(r, margin), :],
                sem.at[a * 2 + h],
            )
            for a in range(angles)
            for h, r in enumerate(starts)
        ]
        edge_col = pl.multiple_of(jnp.where(col == 0, cols - reach, 0), TILE)
        edge_copy = pltpu.make_async_copy(
            proj_ref.at[:, :, pl.ds(edge_col, reach)], edge_ref, sem.at[2 * angles]
        )
        for copy in copies:
            copy.start()
        edge_copy.start()
        build_band(taps_ref, band_ref)
        for copy in copies:
            copy.wait()
        known = set()

        def weighted_at(half, c):
            c -= window_at
            if (half, c) not in known:
                known.add((half, c))
                weigh(
                    raw_ref, weighted_ref, half, starts[half], slab * rows,
                    col * cols + window_at, sizes, c,
                )
            return lambda: weighted_ref[half * part : (half + 1) * part, c : c + BLOCK]

        work = [(h, start, width, out_ref) for h, out_ref in enumerate(outs)]
        filter_columns(work, part, band_ref, weighted_at)
        edge_copy.wait()

    band, edge, *first_out = kernel_call(
        first_kernel,
        [bf16(length, BLOCK), bf16(angles, rows, reach)] + [bf16(part, width)] * early,
        (projections, filter_taps.reshape(taps // TILE, TILE)),
        2 * early * part * length * width,
        scratch=[
            pltpu.VMEM((angles, rows, window), jnp.bfloat16),
            pltpu.VMEM((early * part, window), jnp.bfloat16),
            pltpu.SemaphoreType.DMA((2 * angles + 1,)),
        ],
        name="first_columns",
        specs=[HELD, VMEM],
        grant=FIRST_VMEM_BYTES,
    )

    up = [(i, (i + 1) % slabs) for i in range(slabs - 1)]
    down = [(j, i) for i, j in up]

    def exchange(sends):
        if both:
            return [lax.ppermute(sends[0], "slab", up + down)]
        return [lax.ppermute(sends[0], "slab", up), lax.ppermute(sends[1], "slab", down)]

    assert sides == 2
    received = lax.ppermute(edge, "col", [(0, 1), (1, 0)])
    halo_rows = [exchange(first_out)]

    def write_weights(first_ref, index_ref, frac_ref, own_ref, halo_ref):
        slab = lax.axis_index("slab")
        angle = lax.axis_index("angle")
        if both:
            bases = [jnp.where(slab == 0, rows, rows - margin)]
        else:
            bases = [slab * rows - margin, (slab + 1) * rows]

        def weights(a, base):
            slot = lax.broadcasted_iota(jnp.int32, (margin, depth), 0) + base
            position = index_ref[a] + first_ref[a]
            frac = frac_ref[a]
            high = frac.astype(jnp.bfloat16).astype(jnp.float32)
            low = (1.0 - frac).astype(jnp.bfloat16).astype(jnp.float32)
            return jnp.where(slot == position, low, 0.0) + jnp.where(slot == position + 1, high, 0.0)

        here = [slab * rows + r for r in half_rows(slab)]
        for starts, ref in ((here, own_ref), (bases, halo_ref)):
            table = jnp.concatenate([weights(a, b) for b in starts for a in range(angles)], axis=0)
            turned = table.T.astype(jnp.bfloat16)
            for s in range(line):
                if quick:
                    places = [o.index(s) for o in order]
                    place = places[line - 1]
                    for i in range(line - 1):
                        place = jnp.where(angle == i, places[i], place)
                    at = pl.multiple_of(place * shard, shard)
                else:
                    at = s * shard
                ref[pl.ds(at, shard), :] = turned[s * shard : (s + 1) * shard, :]

    def filter_here(refs, work, band_ref):
        proj_ref, received_ref, weighted_ref, halo_cols_ref = refs
        slab = lax.axis_index("slab")
        col = lax.axis_index("col")
        starts = [aligned(r) for r in half_rows(slab)]
        lower = col == 0
        from_col = jnp.where(lower, cols, col * cols - reach)
        none = jnp.zeros((part, BLOCK), jnp.bfloat16)
        known = set()

        def weighted_at(half, c):
            inside = 0 <= c < cols
            source, into = (proj_ref, weighted_ref) if inside else (received_ref, halo_cols_ref)
            first_col = col * cols if inside else from_col
            at = c if inside else c % reach
            if (half, at, inside) not in known:
                known.add((half, at, inside))
                weigh(source, into, half, starts[half], slab * rows, first_col, sizes, at)

            def load():
                block = into[half * part : (half + 1) * part, at : at + BLOCK]
                if c < 0:
                    block = jnp.where(lower, none, block)
                elif c >= cols:
                    block = jnp.where(lower, block, none)
                return block

            return load

        filter_columns(work, part, band_ref, weighted_at)

    scratch = [pltpu.VMEM((2 * part, n), jnp.bfloat16) for n in (cols, reach)]

    work = [(1, *chunks[0])][: 2 - early]
    work += [(half, *chunk) for chunk in chunks[1:-1] for half in (0, 1)]

    def second_kernel(proj_ref, received_ref, band_ref, first_ref, index_ref, frac_ref,
                      own_ref, halo_ref, *rest):
        outs = [(*w, ref) for w, ref in zip(work, rest)]
        filter_here((proj_ref, received_ref, *rest[-2:]), outs, band_ref)
        write_weights(first_ref, index_ref, frac_ref, own_ref, halo_ref)

    own_weight, halo_weight, *second_out = kernel_call(
        second_kernel,
        [bf16(depth, 2 * part), bf16(depth, halos * part)] + [bf16(part, w[2]) for w in work],
        (projections, received, band, row_first[:, 0], interp_index, interp_frac),
        2 * part * length * sum(w[2] for w in work),
        scratch=scratch,
        name="other_columns",
        specs=[VMEM, VMEM, VMEM, SMEM, VMEM, VMEM],
    )

    def last_kernel(proj_ref, received_ref, taps_ref, *rest):
        *outs, band_ref, weighted_ref, halo_cols_ref = rest
        build_band(taps_ref, band_ref)
        filter_here(
            (proj_ref, received_ref, weighted_ref, halo_cols_ref),
            [(half, *chunks[-1], ref) for half, ref in enumerate(outs)],
            band_ref,
        )

    last_out = kernel_call(
        last_kernel,
        [bf16(part, widths[-1])] * 2,
        (projections, received, filter_taps.reshape(taps // TILE, TILE)),
        4 * part * length * widths[-1],
        scratch=[pltpu.VMEM((length, BLOCK), jnp.bfloat16)] + scratch,
        name="last_columns",
    )
    second_out += last_out
    filtered = [(*first_out, *second_out[: 2 - early])]
    for at in range(2 - early, len(second_out), 2):
        filtered.append(second_out[at : at + 2])
        halo_rows.append(exchange(second_out[at : at + halos]))

    def project(index, after=()):
        width = widths[index]

        def body(own_ref, halo_ref, *rest):
            sources, outs = rest[: 2 + halos], rest[2 + halos + len(after) :]
            for c in range(0, width, BLOCK):
                cut = slice(c, c + BLOCK)
                own = jnp.concatenate([ref[:, cut] for ref in sources[:2]], axis=0)
                other = [ref[:, cut] for ref in sources[2:]]
                other = other[0] if len(other) == 1 else jnp.concatenate(other, axis=0)
                total = jnp.dot(own_ref[...], own, preferred_element_type=jnp.float32)
                total += jnp.dot(halo_ref[...], other, preferred_element_type=jnp.float32)
                total = total * scale
                at = 0
                for out in outs:
                    out[:, cut] = total[at : at + out.shape[0], :].astype(out.dtype)
                    at += out.shape[0]

        if quick:
            first = [bf16(shard, width)] * 2 if DIRECT[index] else [bf16(2 * shard, width)]
            shapes = [*first, bf16(shard, width), f32(shard, width)]
        else:
            shapes = [f32(depth, width)]
        return kernel_call(
            body,
            shapes,
            (own_weight, halo_weight, *filtered[index], *halo_rows[index], *after),
            2 * depth * (2 + halos) * part * width,
            name="interpolate",
            specs=[VMEM] * (4 + halos) + [HELD] * len(after),
        )

    def widen(x):
        return x.astype(jnp.float32)

    def at_end():
        angle = lax.axis_index("angle")
        return (angle == 0) | (angle == line - 1)

    neighbours = [(0, 1), (1, 0), (2, 3), (3, 2)]
    middles = [(1, 2), (2, 1), (0, 0), (3, 3)]
    second_hop = [(0, 1), (1, 3), (2, 0), (3, 2)]
    straight = [(0, 2), (3, 1), (1, 0), (2, 3)]

    def first_hops(*parts):
        if len(parts) == 1:
            return [lax.ppermute(parts[0], "angle", neighbours)]
        near, middle = parts
        two = lax.ppermute(middle, "angle", straight)
        three = lax.ppermute(middle, "angle", middles)
        one = lax.ppermute(near, "angle", neighbours)
        return [one, three, two]

    def relay(sent, own, far, kept, after=(), weight=1):
        direct = len(sent) == 3
        arrived = sent[:2] if direct else [sent[0], own[0]]

        def body(one_ref, other_ref, far_ref, kept_ref, *rest):
            outs = rest[len(after) :]
            end = at_end()
            near = widen(one_ref[:shard, :])
            relayed = widen(far_ref[...]) + jnp.where(end, 0.0, near)
            outs[0][...] = relayed.astype(jnp.bfloat16)
            if direct:
                outs[1][...] = kept_ref[...] + jnp.where(end, near, widen(other_ref[...]))
            else:
                outs[1][...] = kept_ref[...] + jnp.where(end, near, 0.0)
                crossed = widen(one_ref[shard:, :]) + widen(other_ref[shard:, :])
                outs[2][...] = crossed.astype(jnp.bfloat16)

        relayed, partial, *crossed = kernel_call(
            body,
            [bf16(*far.shape), f32(*kept.shape)] + [bf16(*far.shape)] * (not direct),
            (*arrived, far, kept, *after),
            far.size * 2 * weight,
            name="relay",
            specs=[VMEM] * 4 + [HELD] * len(after),
        )
        four = lax.ppermute(relayed, "angle", second_hop)
        three = sent[2] if direct else lax.ppermute(crossed[0], "angle", middles)
        return partial, three, four

    def total(partial_ref, two_ref, four_ref):
        direct = jnp.where(at_end(), 0.0, widen(two_ref[...]))
        return partial_ref[...] + direct + widen(four_ref[...])

    def finish(partial, two, four, weight=1):
        def body(partial_ref, two_ref, four_ref, out_ref):
            out_ref[...] = total(partial_ref, two_ref, four_ref)

        return kernel_call(
            body, [f32(*partial.shape)], (partial, two, four), partial.size * 2 * weight, name="finish"
        )[0]

    def store(done, pieces):
        first = len(done)
        given = [*done, *(piece for triple in pieces for piece in triple)]

        def body(*refs):
            ready, refs = refs[:first], refs[first:]
            volume_ref, sem = refs[3 * len(pieces)], refs[-1]
            totals = refs[3 * len(pieces) + 1 : -1]

            def copy(index, source):
                at = pl.ds(chunks[index][0], chunks[index][1])
                return pltpu.make_async_copy(source, volume_ref.at[:, at], sem.at[index])

            copies = [copy(i, ref) for i, ref in enumerate(ready)]
            for c in copies:
                c.start()
            for i, total_ref in enumerate(totals):
                total_ref[...] = total(*refs[3 * i : 3 * i + 3])
                copies.append(copy(first + i, total_ref))
                copies[-1].start()
            for c in copies:
                c.wait()

        return pl.pallas_call(
            body,
            out_shape=f32(shard, cols),
            in_specs=[VMEM] * len(given),
            out_specs=HELD,
            scratch_shapes=[
                *(pltpu.VMEM((shard, w), jnp.float32) for w in widths[first:]),
                pltpu.SemaphoreType.DMA((len(chunks),)),
            ],
            compiler_params=pltpu.CompilerParams(vmem_limit_bytes=VMEM_BYTES),
            name="store",
        )(*given)

    if not quick:
        sums = [
            lax.psum_scatter(project(i)[0], "angle", scatter_dimension=0, tiled=True)
            for i in range(len(chunks))
        ]
        return jnp.concatenate([sums[i] for i in sorted(range(len(chunks)), key=chunks.__getitem__)], 1)

    last = len(chunks) - 1
    *own, far, kept = project(0)
    sent = first_hops(*own)
    done, pieces = [], []
    for j in range(last + 1):
        here = (sent, own, far, kept)
        after = sent[2:] if j == 0 else done[-1:] if j < last else []
        if j < last:
            *own, far, kept = project(j + 1, after=[p[0] for p in pieces[-1:]])
            sent = first_hops(*own)
            after = [*after, kept]
        pieces.append(relay(*here, after=after, weight=WEIGHTS[j]))
        if j < last:
            done.append(finish(*pieces[j], weight=FINISH_WEIGHTS[j]))
    return store(done, pieces[last:])


def solution(mesh):
    placed = (
        P(("group", "angle"), "slab", "col"),
        P(),
        P(("group", "angle"), "slab"),
        P(("group", "angle"), "slab", None),
        P(("group", "angle"), "slab", None),
    )
    return jax.shard_map(
        on_device,
        mesh=mesh,
        in_specs=placed,
        out_specs=P(("group", "slab", "angle"), "col"),
        check_vma=False,
    )
```

```python
import math

import jax
import jax.numpy as jnp
from jax import lax
from jax.experimental import pallas as pl
from jax.experimental.pallas import tpu as pltpu
from jax.sharding import PartitionSpec as P

BLOCK = 256
TILE = 128
STACK = 8
DIRECT = (True, True, True, True)
SOON = (True, False, False, False)
WEIGHTS = (40000, 40000, 1, 1)
FINISH_WEIGHTS = (1, 1, 10000)
MARKS = (1000000000,)
VMEM_BYTES = 14 * 1024 * 1024
FIRST_VMEM_BYTES = 103 * 512 * 1024
LINE_ORDER = ((3, 2, 1, 0), (0, 2, 3, 1), (3, 1, 0, 2), (0, 1, 2, 3))

VMEM = pl.BlockSpec(memory_space=pltpu.VMEM)
HELD = pl.BlockSpec(memory_space=pltpu.HBM)
SMEM = pl.BlockSpec(memory_space=pltpu.SMEM)


def kernel_call(
    body, out_shape, args, flops, scratch=(), name=None, specs=None, grant=VMEM_BYTES, carried=()
):
    specs = specs or [VMEM] * len(args)
    moved = sum(a.size * a.dtype.itemsize for a in (*args, *out_shape))
    n_in, n_out, n_through = len(args), len(out_shape), len(carried)

    def kernel(*refs):
        ins, refs = refs[:n_in], refs[n_in + n_through :]
        body(*ins, *refs[:n_out], *refs[n_out + n_through :])

    return pl.pallas_call(
        kernel,
        out_shape=[*out_shape, *(jax.ShapeDtypeStruct(c.shape, c.dtype) for c in carried)],
        in_specs=[*specs, *([HELD] * n_through)],
        out_specs=[VMEM] * n_out + [HELD] * n_through,
        input_output_aliases={n_in + i: n_out + i for i in range(n_through)},
        scratch_shapes=list(scratch),
        compiler_params=pltpu.CompilerParams(vmem_limit_bytes=grant),
        cost_estimate=pl.CostEstimate(flops=flops, bytes_accessed=moved, transcendentals=0),
        name=name,
    )(*args, *carried)


def build_band(taps_ref, band_ref):
    count = taps_ref.shape[0]
    steps, tiles = band_ref.shape[1] // TILE, band_ref.shape[0] // TILE
    zero = jnp.zeros((TILE, TILE), jnp.float32)
    ahead = lax.broadcasted_iota(jnp.int32, (TILE, TILE), 1) >= lax.broadcasted_iota(
        jnp.int32, (TILE, TILE), 0
    )
    taps = taps_ref[...].astype(jnp.float32)

    def shifted(d):
        if not 0 <= d < count:
            return zero
        row = jnp.broadcast_to(taps[d : d + 1, :], (TILE, TILE))
        return pltpu.roll(row, 0, 1, stride=1, stride_axis=0)

    before = zero
    for d in range(-(steps - 1), tiles):
        here = shifted(d)
        block = jnp.where(ahead, here, before).T.astype(jnp.bfloat16)
        before = here
        for c in range(steps):
            if 0 <= d + c < tiles:
                band_ref[(d + c) * TILE : (d + c + 1) * TILE, c * TILE : (c + 1) * TILE] = block


def weigh(proj_ref, weighted_ref, half, row_at, row_start, col_start, sizes, c):
    angles = proj_ref.shape[0]
    total_rows, total_cols, count = sizes
    distance = jnp.float32(total_cols)
    v = lax.broadcasted_iota(jnp.int32, (count, 1), 0) + (row_start + row_at)
    v = v.astype(jnp.float32) - total_rows / 2 + 0.5
    u = lax.broadcasted_iota(jnp.int32, (1, BLOCK), 1) + (col_start + c)
    u = u.astype(jnp.float32) - total_cols / 2 + 0.5
    factor = distance / jnp.sqrt(distance * distance + u * u + v * v)
    for a in range(angles):
        raw = proj_ref[a, pl.ds(row_at, count), c : c + BLOCK].astype(jnp.float32)
        at = (half * angles + a) * count
        weighted_ref[at : at + count, c : c + BLOCK] = (raw * factor).astype(jnp.bfloat16)


def filter_columns(work, count, band_ref, weighted_at):
    length = band_ref.shape[0]
    reach = (length - BLOCK) // 2
    groups = []
    for half, first, width, out_ref in work:
        starts = range(first, first + width, BLOCK)
        for at in range(0, len(starts), STACK):
            groups.append((half, starts[at : at + STACK], out_ref, at))

    def touch(index):
        if index < len(groups):
            half, starts, _, _ = groups[index]
            for c in range(starts[0] - reach, starts[-1] + BLOCK + reach, BLOCK):
                weighted_at(half, c)

    touch(0)
    for index, (half, starts, out_ref, at) in enumerate(groups):
        touch(index + 1)
        tall = jnp.concatenate(
            [
                jnp.concatenate(
                    [weighted_at(half, c)() for c in range(s - reach, s + BLOCK + reach, BLOCK)],
                    axis=1,
                )
                for s in starts
            ],
            axis=0,
        )
        result = jnp.dot(tall, band_ref[...], preferred_element_type=jnp.float32)
        result = result.astype(jnp.bfloat16)
        for k in range(len(starts)):
            out_ref[:, (at + k) * BLOCK : (at + k + 1) * BLOCK] = result[
                k * count : (k + 1) * count, :
            ]


def bf16(*shape):
    return jax.ShapeDtypeStruct(shape, jnp.bfloat16)


def f32(*shape):
    return jax.ShapeDtypeStruct(shape, jnp.float32)


def chunk_plan(cols, reach):
    assert cols >= 4 * reach and reach % (4 * BLOCK) == 0
    first, second = reach + BLOCK, 2 * reach
    third = second + (cols - 2 * reach) * 3 // 8
    return [(first, second - first), (second, third - second), (third, cols - third), (0, first)]


def on_device(projections, filter_taps, row_first, interp_index, interp_frac):
    angles, rows, cols = projections.shape
    depth = interp_index.shape[2]
    taps = filter_taps.shape[0]
    reach = taps // 2
    length = taps + BLOCK
    margin = rows // 2
    slabs, line, sides = (lax.axis_size(n) for n in ("slab", "angle", "col"))
    scale = math.pi / (angles * line)
    both = slabs == 2
    halos = 1 if both else 2
    quick = line == 4
    shard = depth // line
    order = LINE_ORDER if quick else (tuple(range(line)),) * line
    total_rows, total_cols = rows * slabs, cols * sides
    chunks = chunk_plan(cols, reach)
    widths = [w for _, w in chunks]
    part = angles * margin
    sizes = (total_rows, total_cols, margin)

    def half_rows(slab):
        if both:
            return jnp.where(slab == 0, margin, 0), jnp.where(slab == 0, 0, margin)
        return margin, 0

    def aligned(row):
        return row if isinstance(row, int) else pl.multiple_of(row, margin)

    start, width = chunks[0]
    window_at, window = start - reach, width + 2 * reach
    early = halos

    def first_kernel(proj_ref, taps_ref, band_ref, edge_ref, *rest):
        outs, (raw_ref, weighted_ref, sem) = rest[:-3], rest[-3:]
        slab = lax.axis_index("slab")
        col = lax.axis_index("col")
        starts = [aligned(r) for r in half_rows(slab)][:early]
        copies = [
            pltpu.make_async_copy(
                proj_ref.at[a, pl.ds(r, margin), pl.ds(window_at, window)],
                raw_ref.at[a, pl.ds(r, margin), :],
                sem.at[a * 2 + h],
            )
            for a in range(angles)
            for h, r in enumerate(starts)
        ]
        edge_col = pl.multiple_of(jnp.where(col == 0, cols - reach, 0), TILE)
        edge_copy = pltpu.make_async_copy(
            proj_ref.at[:, :, pl.ds(edge_col, reach)], edge_ref, sem.at[2 * angles]
        )
        for copy in copies:
            copy.start()
        edge_copy.start()
        build_band(taps_ref, band_ref)
        for copy in copies:
            copy.wait()
        known = set()

        def weighted_at(half, c):
            c -= window_at
            if (half, c) not in known:
                known.add((half, c))
                weigh(
                    raw_ref, weighted_ref, half, starts[half], slab * rows,
                    col * cols + window_at, sizes, c,
                )
            return lambda: weighted_ref[half * part : (half + 1) * part, c : c + BLOCK]

        work = [(h, start, width, out_ref) for h, out_ref in enumerate(outs)]
        filter_columns(work, part, band_ref, weighted_at)
        edge_copy.wait()

    band, edge, *first_out = kernel_call(
        first_kernel,
        [bf16(length, BLOCK), bf16(angles, rows, reach)] + [bf16(part, width)] * early,
        (projections, filter_taps.reshape(taps // TILE, TILE)),
        2 * early * part * length * width,
        scratch=[
            pltpu.VMEM((angles, rows, window), jnp.bfloat16),
            pltpu.VMEM((early * part, window), jnp.bfloat16),
            pltpu.SemaphoreType.DMA((2 * angles + 1,)),
        ],
        name="first_columns",
        specs=[HELD, VMEM],
        grant=FIRST_VMEM_BYTES,
    )

    up = [(i, (i + 1) % slabs) for i in range(slabs - 1)]
    down = [(j, i) for i, j in up]

    def exchange(sends):
        if both:
            return [lax.ppermute(sends[0], "slab", up + down)]
        return [lax.ppermute(sends[0], "slab", up), lax.ppermute(sends[1], "slab", down)]

    assert sides == 2
    received = lax.ppermute(edge, "col", [(0, 1), (1, 0)])
    halo_rows = [exchange(first_out)]

    def write_weights(first_ref, index_ref, frac_ref, own_ref, halo_ref):
        slab = lax.axis_index("slab")
        angle = lax.axis_index("angle")
        if both:
            bases = [jnp.where(slab == 0, rows, rows - margin)]
        else:
            bases = [slab * rows - margin, (slab + 1) * rows]

        def weights(a, base):
            slot = lax.broadcasted_iota(jnp.int32, (margin, depth), 0) + base
            position = index_ref[a] + first_ref[a]
            frac = frac_ref[a]
            high = frac.astype(jnp.bfloat16).astype(jnp.float32)
            low = (1.0 - frac).astype(jnp.bfloat16).astype(jnp.float32)
            return jnp.where(slot == position, low, 0.0) + jnp.where(slot == position + 1, high, 0.0)

        here = [slab * rows + r for r in half_rows(slab)]
        for starts, ref in ((here, own_ref), (bases, halo_ref)):
            table = jnp.concatenate([weights(a, b) for b in starts for a in range(angles)], axis=0)
            turned = table.T.astype(jnp.bfloat16)
            for s in range(line):
                if quick:
                    places = [o.index(s) for o in order]
                    place = places[line - 1]
                    for i in range(line - 1):
                        place = jnp.where(angle == i, places[i], place)
                    at = pl.multiple_of(place * shard, shard)
                else:
                    at = s * shard
                ref[pl.ds(at, shard), :] = turned[s * shard : (s + 1) * shard, :]

    def filter_here(refs, work, band_ref):
        proj_ref, received_ref, weighted_ref, halo_cols_ref = refs
        slab = lax.axis_index("slab")
        col = lax.axis_index("col")
        starts = [aligned(r) for r in half_rows(slab)]
        lower = col == 0
        from_col = jnp.where(lower, cols, col * cols - reach)
        none = jnp.zeros((part, BLOCK), jnp.bfloat16)
        known = set()

        def weighted_at(half, c):
            inside = 0 <= c < cols
            source, into = (proj_ref, weighted_ref) if inside else (received_ref, halo_cols_ref)
            first_col = col * cols if inside else from_col
            at = c if inside else c % reach
            if (half, at, inside) not in known:
                known.add((half, at, inside))
                weigh(source, into, half, starts[half], slab * rows, first_col, sizes, at)

            def load():
                block = into[half * part : (half + 1) * part, at : at + BLOCK]
                if c < 0:
                    block = jnp.where(lower, none, block)
                elif c >= cols:
                    block = jnp.where(lower, block, none)
                return block

            return load

        filter_columns(work, part, band_ref, weighted_at)

    scratch = [pltpu.VMEM((2 * part, n), jnp.bfloat16) for n in (cols, reach)]

    work = [(1, *chunks[0])][: 2 - early]
    work += [(half, *chunk) for chunk in chunks[1:-1] for half in (0, 1)]

    def second_kernel(proj_ref, received_ref, band_ref, first_ref, index_ref, frac_ref,
                      own_ref, halo_ref, *rest):
        outs = [(*w, ref) for w, ref in zip(work, rest)]
        filter_here((proj_ref, received_ref, *rest[-2:]), outs, band_ref)
        write_weights(first_ref, index_ref, frac_ref, own_ref, halo_ref)

    own_weight, halo_weight, *second_out = kernel_call(
        second_kernel,
        [bf16(depth, 2 * part), bf16(depth, halos * part)] + [bf16(part, w[2]) for w in work],
        (projections, received, band, row_first[:, 0], interp_index, interp_frac),
        2 * part * length * sum(w[2] for w in work),
        scratch=scratch,
        name="other_columns",
        specs=[VMEM, VMEM, VMEM, SMEM, VMEM, VMEM],
    )

    def last_kernel(proj_ref, received_ref, taps_ref, *rest):
        *outs, band_ref, weighted_ref, halo_cols_ref = rest
        build_band(taps_ref, band_ref)
        filter_here(
            (proj_ref, received_ref, weighted_ref, halo_cols_ref),
            [(half, *chunks[-1], ref) for half, ref in enumerate(outs)],
            band_ref,
        )

    last_out = kernel_call(
        last_kernel,
        [bf16(part, widths[-1])] * 2,
        (projections, received, filter_taps.reshape(taps // TILE, TILE)),
        4 * part * length * widths[-1],
        scratch=[pltpu.VMEM((length, BLOCK), jnp.bfloat16)] + scratch,
        name="last_columns",
    )
    second_out += last_out
    filtered = [(*first_out, *second_out[: 2 - early])]
    for at in range(2 - early, len(second_out), 2):
        filtered.append(second_out[at : at + 2])
        halo_rows.append(exchange(second_out[at : at + halos]))

    def project(index, after=()):
        width = widths[index]

        def body(own_ref, halo_ref, *rest):
            sources, outs = rest[: 2 + halos], rest[2 + halos + len(after) :]
            for c in range(0, width, BLOCK):
                cut = slice(c, c + BLOCK)
                own = jnp.concatenate([ref[:, cut] for ref in sources[:2]], axis=0)
                other = [ref[:, cut] for ref in sources[2:]]
                other = other[0] if len(other) == 1 else jnp.concatenate(other, axis=0)
                total = jnp.dot(own_ref[...], own, preferred_element_type=jnp.float32)
                total += jnp.dot(halo_ref[...], other, preferred_element_type=jnp.float32)
                total = total * scale
                at = 0
                for out in outs:
                    out[:, cut] = total[at : at + out.shape[0], :].astype(out.dtype)
                    at += out.shape[0]

        if quick:
            first = [bf16(shard, width)] * 2 if DIRECT[index] else [bf16(2 * shard, width)]
            shapes = [*first, bf16(shard, width), f32(shard, width)]
        else:
            shapes = [f32(depth, width)]
        return kernel_call(
            body,
            shapes,
            (own_weight, halo_weight, *filtered[index], *halo_rows[index], *after),
            2 * depth * (2 + halos) * part * width,
            name="interpolate",
            specs=[VMEM] * (4 + halos) + [HELD] * len(after),
        )

    def widen(x):
        return x.astype(jnp.float32)

    def at_end():
        angle = lax.axis_index("angle")
        return (angle == 0) | (angle == line - 1)

    neighbours = [(0, 1), (1, 0), (2, 3), (3, 2)]
    middles = [(1, 2), (2, 1), (0, 0), (3, 3)]
    second_hop = [(0, 1), (1, 3), (2, 0), (3, 2)]
    straight = [(0, 2), (3, 1), (1, 0), (2, 3)]

    def first_hops(*parts):
        if len(parts) == 1:
            return [lax.ppermute(parts[0], "angle", neighbours)]
        near, middle = parts
        two = lax.ppermute(middle, "angle", straight)
        three = lax.ppermute(middle, "angle", middles)
        one = lax.ppermute(near, "angle", neighbours)
        return [one, three, two]

    def relay(sent, own, far, kept, after=(), weight=1, soon=False):
        direct = len(sent) == 3
        arrived = sent[: 1 if soon else 2] if direct else [sent[0], own[0]]
        extra = len(arrived) - 1

        def body(one_ref, *rest):
            other_ref = rest[0]
            far_ref, kept_ref = rest[extra : extra + 2]
            outs = rest[extra + 2 + len(after) :]
            end = at_end()
            near = widen(one_ref[:shard, :])
            relayed = widen(far_ref[...]) + jnp.where(end, 0.0, near)
            outs[0][...] = relayed.astype(jnp.bfloat16)
            if soon:
                outs[1][...] = kept_ref[...] + jnp.where(end, near, 0.0)
            elif direct:
                outs[1][...] = kept_ref[...] + jnp.where(end, near, widen(other_ref[...]))
            else:
                outs[1][...] = kept_ref[...] + jnp.where(end, near, 0.0)
                crossed = widen(one_ref[shard:, :]) + widen(other_ref[shard:, :])
                outs[2][...] = crossed.astype(jnp.bfloat16)

        relayed, partial, *crossed = kernel_call(
            body,
            [bf16(*far.shape), f32(*kept.shape)] + [bf16(*far.shape)] * (not direct),
            (*arrived, far, kept, *after),
            far.size * 2 * weight,
            name="relay",
            specs=[VMEM] * (3 + extra) + [HELD] * len(after),
        )
        four = lax.ppermute(relayed, "angle", second_hop)
        three = sent[2] if direct else lax.ppermute(crossed[0], "angle", middles)
        return (partial, four, three, *([sent[1]] if soon else []))

    def total(partial_ref, four_ref, *fillers):
        direct = sum(widen(ref[...]) for ref in fillers)
        return partial_ref[...] + widen(four_ref[...]) + jnp.where(at_end(), 0.0, direct)

    def mark(array, weight):
        def body(array_ref, out_ref):
            out_ref[...] = jnp.zeros_like(out_ref)

        return kernel_call(body, [f32(8, TILE)], (array,), weight, name="mark", specs=[HELD])[0]

    def finish(pieces, weight=1, after=()):
        def body(*refs):
            refs[-1][...] = total(*refs[: len(pieces)])

        return kernel_call(
            body,
            [f32(*pieces[0].shape)],
            (*pieces, *after),
            pieces[0].size * 2 * weight,
            name="finish",
            specs=[VMEM] * len(pieces) + [HELD] * len(after),
        )[0]

    def store(done, pieces):
        first = len(done)
        given = [*done, *(piece for triple in pieces for piece in triple)]

        def body(*refs):
            ready, refs = refs[:first], refs[first:]
            volume_ref, sem = refs[3 * len(pieces)], refs[-1]
            totals = refs[3 * len(pieces) + 1 : -1]

            def copy(index, source):
                at = pl.ds(chunks[index][0], chunks[index][1])
                return pltpu.make_async_copy(source, volume_ref.at[:, at], sem.at[index])

            copies = [copy(i, ref) for i, ref in enumerate(ready)]
            for c in copies:
                c.start()
            for i, total_ref in enumerate(totals):
                total_ref[...] = total(*refs[3 * i : 3 * i + 3])
                copies.append(copy(first + i, total_ref))
                copies[-1].start()
            for c in copies:
                c.wait()

        return pl.pallas_call(
            body,
            out_shape=f32(shard, cols),
            in_specs=[VMEM] * len(given),
            out_specs=HELD,
            scratch_shapes=[
                *(pltpu.VMEM((shard, w), jnp.float32) for w in widths[first:]),
                pltpu.SemaphoreType.DMA((len(chunks),)),
            ],
            compiler_params=pltpu.CompilerParams(vmem_limit_bytes=VMEM_BYTES),
            name="store",
        )(*given)

    if not quick:
        sums = [
            lax.psum_scatter(project(i)[0], "angle", scatter_dimension=0, tiled=True)
            for i in range(len(chunks))
        ]
        return jnp.concatenate([sums[i] for i in sorted(range(len(chunks)), key=chunks.__getitem__)], 1)

    last = len(chunks) - 1
    *own, far, kept = project(0)
    sent = first_hops(*own)
    done, pieces = [], []
    for j in range(last + 1):
        here = (sent, own, far, kept)
        after = sent[2:] if j == 0 else done[-1:] if j < last else []
        if j < last:
            *own, far, kept = project(j + 1, after=[p[0] for p in pieces[-1:]])
            sent = first_hops(*own)
            after = [*after, kept]
        if j == 0:
            after.append(mark(here[0][0], MARKS[0]))
        pieces.append(relay(*here, after=after, weight=WEIGHTS[j], soon=SOON[j]))
        if j < last:
            early_hop = [mark(sent[0], MARKS[j + 1])] if j + 1 < len(MARKS) else []
            done.append(finish(pieces[j], weight=FINISH_WEIGHTS[j], after=early_hop))
    return store(done, pieces[last:])


def solution(mesh):
    placed = (
        P(("group", "angle"), "slab", "col"),
        P(),
        P(("group", "angle"), "slab"),
        P(("group", "angle"), "slab", None),
        P(("group", "angle"), "slab", None),
    )
    return jax.shard_map(
        on_device,
        mesh=mesh,
        in_specs=placed,
        out_specs=P(("group", "slab", "angle"), "col"),
        check_vma=False,
    )
```

```python
import math

import jax
import jax.numpy as jnp
from jax import lax
from jax.experimental import pallas as pl
from jax.experimental.pallas import tpu as pltpu
from jax.sharding import PartitionSpec as P

BLOCK = 256
TILE = 128
STACK = 8
DIRECT = (False, False, False, True)
SOON = (False,) * 4
WEIGHTS = (40000, 40000, 1, 1)
FINISH_WEIGHTS = (1, 1, 10000)
MARKS = ()
VMEM_BYTES = 14 * 1024 * 1024
FIRST_VMEM_BYTES = 103 * 512 * 1024
LINE_ORDER = ((3, 2, 1, 0), (0, 2, 3, 1), (3, 1, 0, 2), (0, 1, 2, 3))

VMEM = pl.BlockSpec(memory_space=pltpu.VMEM)
HELD = pl.BlockSpec(memory_space=pltpu.HBM)
SMEM = pl.BlockSpec(memory_space=pltpu.SMEM)


def kernel_call(
    body, out_shape, args, flops, scratch=(), name=None, specs=None, grant=VMEM_BYTES, carried=()
):
    specs = specs or [VMEM] * len(args)
    moved = sum(a.size * a.dtype.itemsize for a in (*args, *out_shape))
    n_in, n_out, n_through = len(args), len(out_shape), len(carried)

    def kernel(*refs):
        ins, refs = refs[:n_in], refs[n_in + n_through :]
        body(*ins, *refs[:n_out], *refs[n_out + n_through :])

    return pl.pallas_call(
        kernel,
        out_shape=[*out_shape, *(jax.ShapeDtypeStruct(c.shape, c.dtype) for c in carried)],
        in_specs=[*specs, *([HELD] * n_through)],
        out_specs=[VMEM] * n_out + [HELD] * n_through,
        input_output_aliases={n_in + i: n_out + i for i in range(n_through)},
        scratch_shapes=list(scratch),
        compiler_params=pltpu.CompilerParams(vmem_limit_bytes=grant),
        cost_estimate=pl.CostEstimate(flops=flops, bytes_accessed=moved, transcendentals=0),
        name=name,
    )(*args, *carried)


def build_band(taps_ref, band_ref):
    count = taps_ref.shape[0]
    steps, tiles = band_ref.shape[1] // TILE, band_ref.shape[0] // TILE
    zero = jnp.zeros((TILE, TILE), jnp.float32)
    ahead = lax.broadcasted_iota(jnp.int32, (TILE, TILE), 1) >= lax.broadcasted_iota(
        jnp.int32, (TILE, TILE), 0
    )
    taps = taps_ref[...].astype(jnp.float32)

    def shifted(d):
        if not 0 <= d < count:
            return zero
        row = jnp.broadcast_to(taps[d : d + 1, :], (TILE, TILE))
        return pltpu.roll(row, 0, 1, stride=1, stride_axis=0)

    before = zero
    for d in range(-(steps - 1), tiles):
        here = shifted(d)
        block = jnp.where(ahead, here, before).T.astype(jnp.bfloat16)
        before = here
        for c in range(steps):
            if 0 <= d + c < tiles:
                band_ref[(d + c) * TILE : (d + c + 1) * TILE, c * TILE : (c + 1) * TILE] = block


def weigh(proj_ref, weighted_ref, half, row_at, row_start, col_start, sizes, c):
    angles = proj_ref.shape[0]
    total_rows, total_cols, count = sizes
    distance = jnp.float32(total_cols)
    v = lax.broadcasted_iota(jnp.int32, (count, 1), 0) + (row_start + row_at)
    v = v.astype(jnp.float32) - total_rows / 2 + 0.5
    u = lax.broadcasted_iota(jnp.int32, (1, BLOCK), 1) + (col_start + c)
    u = u.astype(jnp.float32) - total_cols / 2 + 0.5
    factor = distance / jnp.sqrt(distance * distance + u * u + v * v)
    for a in range(angles):
        raw = proj_ref[a, pl.ds(row_at, count), c : c + BLOCK].astype(jnp.float32)
        at = (half * angles + a) * count
        weighted_ref[at : at + count, c : c + BLOCK] = (raw * factor).astype(jnp.bfloat16)


def filter_columns(work, count, band_ref, weighted_at):
    length = band_ref.shape[0]
    reach = (length - BLOCK) // 2
    groups = []
    for half, first, width, out_ref in work:
        starts = range(first, first + width, BLOCK)
        for at in range(0, len(starts), STACK):
            groups.append((half, starts[at : at + STACK], out_ref, at))

    def touch(index):
        if index < len(groups):
            half, starts, _, _ = groups[index]
            for c in range(starts[0] - reach, starts[-1] + BLOCK + reach, BLOCK):
                weighted_at(half, c)

    touch(0)
    for index, (half, starts, out_ref, at) in enumerate(groups):
        touch(index + 1)
        tall = jnp.concatenate(
            [
                jnp.concatenate(
                    [weighted_at(half, c)() for c in range(s - reach, s + BLOCK + reach, BLOCK)],
                    axis=1,
                )
                for s in starts
            ],
            axis=0,
        )
        result = jnp.dot(tall, band_ref[...], preferred_element_type=jnp.float32)
        result = result.astype(jnp.bfloat16)
        for k in range(len(starts)):
            out_ref[:, (at + k) * BLOCK : (at + k + 1) * BLOCK] = result[
                k * count : (k + 1) * count, :
            ]


def bf16(*shape):
    return jax.ShapeDtypeStruct(shape, jnp.bfloat16)


def f32(*shape):
    return jax.ShapeDtypeStruct(shape, jnp.float32)


def chunk_plan(cols, reach):
    assert cols >= 4 * reach and reach % (4 * BLOCK) == 0
    first, second = reach + BLOCK, 2 * reach
    third = second + (cols - 2 * reach) * 3 // 8
    return [(first, second - first), (second, third - second), (third, cols - third), (0, first)]


def on_device(projections, filter_taps, row_first, interp_index, interp_frac):
    angles, rows, cols = projections.shape
    depth = interp_index.shape[2]
    taps = filter_taps.shape[0]
    reach = taps // 2
    length = taps + BLOCK
    margin = rows // 2
    slabs, line, sides = (lax.axis_size(n) for n in ("slab", "angle", "col"))
    scale = math.pi / (angles * line)
    both = slabs == 2
    halos = 1 if both else 2
    quick = line == 4
    shard = depth // line
    order = LINE_ORDER if quick else (tuple(range(line)),) * line
    total_rows, total_cols = rows * slabs, cols * sides
    chunks = chunk_plan(cols, reach)
    widths = [w for _, w in chunks]
    part = angles * margin
    sizes = (total_rows, total_cols, margin)

    def half_rows(slab):
        if both:
            return jnp.where(slab == 0, margin, 0), jnp.where(slab == 0, 0, margin)
        return margin, 0

    def aligned(row):
        return row if isinstance(row, int) else pl.multiple_of(row, margin)

    start, width = chunks[0]
    window_at, window = start - reach, width + 2 * reach
    early = halos

    def first_kernel(proj_ref, taps_ref, band_ref, edge_ref, *rest):
        outs, (raw_ref, weighted_ref, sem) = rest[:-3], rest[-3:]
        slab = lax.axis_index("slab")
        col = lax.axis_index("col")
        starts = [aligned(r) for r in half_rows(slab)][:early]
        copies = [
            pltpu.make_async_copy(
                proj_ref.at[a, pl.ds(r, margin), pl.ds(window_at, window)],
                raw_ref.at[a, pl.ds(r, margin), :],
                sem.at[a * 2 + h],
            )
            for a in range(angles)
            for h, r in enumerate(starts)
        ]
        edge_col = pl.multiple_of(jnp.where(col == 0, cols - reach, 0), TILE)
        edge_copy = pltpu.make_async_copy(
            proj_ref.at[:, :, pl.ds(edge_col, reach)], edge_ref, sem.at[2 * angles]
        )
        for copy in copies:
            copy.start()
        edge_copy.start()
        build_band(taps_ref, band_ref)
        for copy in copies:
            copy.wait()
        known = set()

        def weighted_at(half, c):
            c -= window_at
            if (half, c) not in known:
                known.add((half, c))
                weigh(
                    raw_ref, weighted_ref, half, starts[half], slab * rows,
                    col * cols + window_at, sizes, c,
                )
            return lambda: weighted_ref[half * part : (half + 1) * part, c : c + BLOCK]

        work = [(h, start, width, out_ref) for h, out_ref in enumerate(outs)]
        filter_columns(work, part, band_ref, weighted_at)
        edge_copy.wait()

    band, edge, *first_out = kernel_call(
        first_kernel,
        [bf16(length, BLOCK), bf16(angles, rows, reach)] + [bf16(part, width)] * early,
        (projections, filter_taps.reshape(taps // TILE, TILE)),
        2 * early * part * length * width,
        scratch=[
            pltpu.VMEM((angles, rows, window), jnp.bfloat16),
            pltpu.VMEM((early * part, window), jnp.bfloat16),
            pltpu.SemaphoreType.DMA((2 * angles + 1,)),
        ],
        name="first_columns",
        specs=[HELD, VMEM],
        grant=FIRST_VMEM_BYTES,
    )

    up = [(i, (i + 1) % slabs) for i in range(slabs - 1)]
    down = [(j, i) for i, j in up]

    def exchange(sends):
        if both:
            return [lax.ppermute(sends[0], "slab", up + down)]
        return [lax.ppermute(sends[0], "slab", up), lax.ppermute(sends[1], "slab", down)]

    assert sides == 2
    received = lax.ppermute(edge, "col", [(0, 1), (1, 0)])
    halo_rows = [exchange(first_out)]

    def write_weights(first_ref, index_ref, frac_ref, own_ref, halo_ref):
        slab = lax.axis_index("slab")
        angle = lax.axis_index("angle")
        if both:
            bases = [jnp.where(slab == 0, rows, rows - margin)]
        else:
            bases = [slab * rows - margin, (slab + 1) * rows]

        def weights(a, base):
            slot = lax.broadcasted_iota(jnp.int32, (margin, depth), 0) + base
            position = index_ref[a] + first_ref[a]
            frac = frac_ref[a]
            high = frac.astype(jnp.bfloat16).astype(jnp.float32)
            low = (1.0 - frac).astype(jnp.bfloat16).astype(jnp.float32)
            return jnp.where(slot == position, low, 0.0) + jnp.where(slot == position + 1, high, 0.0)

        here = [slab * rows + r for r in half_rows(slab)]
        for starts, ref in ((here, own_ref), (bases, halo_ref)):
            table = jnp.concatenate([weights(a, b) for b in starts for a in range(angles)], axis=0)
            turned = table.T.astype(jnp.bfloat16)
            for s in range(line):
                if quick:
                    places = [o.index(s) for o in order]
                    place = places[line - 1]
                    for i in range(line - 1):
                        place = jnp.where(angle == i, places[i], place)
                    at = pl.multiple_of(place * shard, shard)
                else:
                    at = s * shard
                ref[pl.ds(at, shard), :] = turned[s * shard : (s + 1) * shard, :]

    def filter_here(refs, work, band_ref):
        proj_ref, received_ref, weighted_ref, halo_cols_ref = refs
        slab = lax.axis_index("slab")
        col = lax.axis_index("col")
        starts = [aligned(r) for r in half_rows(slab)]
        lower = col == 0
        from_col = jnp.where(lower, cols, col * cols - reach)
        none = jnp.zeros((part, BLOCK), jnp.bfloat16)
        known = set()

        def weighted_at(half, c):
            inside = 0 <= c < cols
            source, into = (proj_ref, weighted_ref) if inside else (received_ref, halo_cols_ref)
            first_col = col * cols if inside else from_col
            at = c if inside else c % reach
            if (half, at, inside) not in known:
                known.add((half, at, inside))
                weigh(source, into, half, starts[half], slab * rows, first_col, sizes, at)

            def load():
                block = into[half * part : (half + 1) * part, at : at + BLOCK]
                if c < 0:
                    block = jnp.where(lower, none, block)
                elif c >= cols:
                    block = jnp.where(lower, block, none)
                return block

            return load

        filter_columns(work, part, band_ref, weighted_at)

    scratch = [pltpu.VMEM((2 * part, n), jnp.bfloat16) for n in (cols, reach)]

    work = [(1, *chunks[0])][: 2 - early]
    work += [(half, *chunk) for chunk in chunks[1:-1] for half in (0, 1)]

    def second_kernel(proj_ref, received_ref, band_ref, first_ref, index_ref, frac_ref,
                      own_ref, halo_ref, *rest):
        outs = [(*w, ref) for w, ref in zip(work, rest)]
        filter_here((proj_ref, received_ref, *rest[-2:]), outs, band_ref)
        write_weights(first_ref, index_ref, frac_ref, own_ref, halo_ref)

    own_weight, halo_weight, *second_out = kernel_call(
        second_kernel,
        [bf16(depth, 2 * part), bf16(depth, halos * part)] + [bf16(part, w[2]) for w in work],
        (projections, received, band, row_first[:, 0], interp_index, interp_frac),
        2 * part * length * sum(w[2] for w in work),
        scratch=scratch,
        name="other_columns",
        specs=[VMEM, VMEM, VMEM, SMEM, VMEM, VMEM],
    )

    def last_kernel(proj_ref, received_ref, taps_ref, *rest):
        *outs, band_ref, weighted_ref, halo_cols_ref = rest
        build_band(taps_ref, band_ref)
        filter_here(
            (proj_ref, received_ref, weighted_ref, halo_cols_ref),
            [(half, *chunks[-1], ref) for half, ref in enumerate(outs)],
            band_ref,
        )

    last_out = kernel_call(
        last_kernel,
        [bf16(part, widths[-1])] * 2,
        (projections, received, filter_taps.reshape(taps // TILE, TILE)),
        4 * part * length * widths[-1],
        scratch=[pltpu.VMEM((length, BLOCK), jnp.bfloat16)] + scratch,
        name="last_columns",
    )
    second_out += last_out
    filtered = [(*first_out, *second_out[: 2 - early])]
    for at in range(2 - early, len(second_out), 2):
        filtered.append(second_out[at : at + 2])
        halo_rows.append(exchange(second_out[at : at + halos]))

    def project(index, after=()):
        width = widths[index]

        def body(own_ref, halo_ref, *rest):
            sources, outs = rest[: 2 + halos], rest[2 + halos + len(after) :]
            for c in range(0, width, BLOCK):
                cut = slice(c, c + BLOCK)
                own = jnp.concatenate([ref[:, cut] for ref in sources[:2]], axis=0)
                other = [ref[:, cut] for ref in sources[2:]]
                other = other[0] if len(other) == 1 else jnp.concatenate(other, axis=0)
                total = jnp.dot(own_ref[...], own, preferred_element_type=jnp.float32)
                total += jnp.dot(halo_ref[...], other, preferred_element_type=jnp.float32)
                total = total * scale
                at = 0
                for out in outs:
                    out[:, cut] = total[at : at + out.shape[0], :].astype(out.dtype)
                    at += out.shape[0]

        if quick:
            first = [bf16(shard, width)] * 2 if DIRECT[index] else [bf16(2 * shard, width)]
            shapes = [*first, bf16(shard, width), f32(shard, width)]
        else:
            shapes = [f32(depth, width)]
        return kernel_call(
            body,
            shapes,
            (own_weight, halo_weight, *filtered[index], *halo_rows[index], *after),
            2 * depth * (2 + halos) * part * width,
            name="interpolate",
            specs=[VMEM] * (4 + halos) + [HELD] * len(after),
        )

    def widen(x):
        return x.astype(jnp.float32)

    def at_end():
        angle = lax.axis_index("angle")
        return (angle == 0) | (angle == line - 1)

    neighbours = [(0, 1), (1, 0), (2, 3), (3, 2)]
    middles = [(1, 2), (2, 1), (0, 0), (3, 3)]
    second_hop = [(0, 1), (1, 3), (2, 0), (3, 2)]
    straight = [(0, 2), (3, 1), (1, 0), (2, 3)]

    def first_hops(*parts):
        if len(parts) == 1:
            return [lax.ppermute(parts[0], "angle", neighbours)]
        near, middle = parts
        two = lax.ppermute(middle, "angle", straight)
        three = lax.ppermute(middle, "angle", middles)
        one = lax.ppermute(near, "angle", neighbours)
        return [one, three, two]

    def relay(sent, own, far, kept, after=(), weight=1, soon=False):
        direct = len(sent) == 3
        arrived = sent[: 1 if soon else 2] if direct else [sent[0], own[0]]
        extra = len(arrived) - 1

        def body(one_ref, *rest):
            other_ref = rest[0]
            far_ref, kept_ref = rest[extra : extra + 2]
            outs = rest[extra + 2 + len(after) :]
            end = at_end()
            near = widen(one_ref[:shard, :])
            relayed = widen(far_ref[...]) + jnp.where(end, 0.0, near)
            outs[0][...] = relayed.astype(jnp.bfloat16)
            if soon:
                outs[1][...] = kept_ref[...] + jnp.where(end, near, 0.0)
            elif direct:
                outs[1][...] = kept_ref[...] + jnp.where(end, near, widen(other_ref[...]))
            else:
                outs[1][...] = kept_ref[...] + jnp.where(end, near, 0.0)
                crossed = widen(one_ref[shard:, :]) + widen(other_ref[shard:, :])
                outs[2][...] = crossed.astype(jnp.bfloat16)

        relayed, partial, *crossed = kernel_call(
            body,
            [bf16(*far.shape), f32(*kept.shape)] + [bf16(*far.shape)] * (not direct),
            (*arrived, far, kept, *after),
            far.size * 2 * weight,
            name="relay",
            specs=[VMEM] * (3 + extra) + [HELD] * len(after),
        )
        four = lax.ppermute(relayed, "angle", second_hop)
        three = sent[2] if direct else lax.ppermute(crossed[0], "angle", middles)
        return (partial, four, three, *([sent[1]] if soon else []))

    def total(partial_ref, four_ref, *fillers):
        direct = sum(widen(ref[...]) for ref in fillers)
        return partial_ref[...] + widen(four_ref[...]) + jnp.where(at_end(), 0.0, direct)

    def mark(array, weight):
        def body(array_ref, out_ref):
            out_ref[...] = jnp.zeros_like(out_ref)

        return kernel_call(body, [f32(8, TILE)], (array,), weight, name="mark", specs=[HELD])[0]

    def finish(pieces, weight=1, after=()):
        def body(*refs):
            refs[-1][...] = total(*refs[: len(pieces)])

        return kernel_call(
            body,
            [f32(*pieces[0].shape)],
            (*pieces, *after),
            pieces[0].size * 2 * weight,
            name="finish",
            specs=[VMEM] * len(pieces) + [HELD] * len(after),
        )[0]

    def store(done, pieces):
        first = len(done)
        given = [*done, *(piece for triple in pieces for piece in triple)]

        def body(*refs):
            ready, refs = refs[:first], refs[first:]
            volume_ref, sem = refs[3 * len(pieces)], refs[-1]
            totals = refs[3 * len(pieces) + 1 : -1]

            def copy(index, source):
                at = pl.ds(chunks[index][0], chunks[index][1])
                return pltpu.make_async_copy(source, volume_ref.at[:, at], sem.at[index])

            copies = [copy(i, ref) for i, ref in enumerate(ready)]
            for c in copies:
                c.start()
            for i, total_ref in enumerate(totals):
                total_ref[...] = total(*refs[3 * i : 3 * i + 3])
                copies.append(copy(first + i, total_ref))
                copies[-1].start()
            for c in copies:
                c.wait()

        return pl.pallas_call(
            body,
            out_shape=f32(shard, cols),
            in_specs=[VMEM] * len(given),
            out_specs=HELD,
            scratch_shapes=[
                *(pltpu.VMEM((shard, w), jnp.float32) for w in widths[first:]),
                pltpu.SemaphoreType.DMA((len(chunks),)),
            ],
            compiler_params=pltpu.CompilerParams(vmem_limit_bytes=VMEM_BYTES),
            name="store",
        )(*given)

    if not quick:
        sums = [
            lax.psum_scatter(project(i)[0], "angle", scatter_dimension=0, tiled=True)
            for i in range(len(chunks))
        ]
        return jnp.concatenate([sums[i] for i in sorted(range(len(chunks)), key=chunks.__getitem__)], 1)

    last = len(chunks) - 1
    *own, far, kept = project(0)
    sent = first_hops(*own)
    done, pieces = [], []
    for j in range(last + 1):
        here = (sent, own, far, kept)
        after = sent[2:] if j == 0 else done[-1:] if j < last else []
        if j < last:
            *own, far, kept = project(j + 1, after=[p[0] for p in pieces[-1:]])
            sent = first_hops(*own)
            after = [*after, kept]
        if j == 0 and MARKS:
            after.append(mark(here[0][0], MARKS[0]))
        pieces.append(relay(*here, after=after, weight=WEIGHTS[j], soon=SOON[j]))
        if j < last:
            early_hop = [mark(sent[0], MARKS[j + 1])] if j + 1 < len(MARKS) else []
            done.append(finish(pieces[j], weight=FINISH_WEIGHTS[j], after=early_hop))
    return store(done, pieces[last:])


def solution(mesh):
    placed = (
        P(("group", "angle"), "slab", "col"),
        P(),
        P(("group", "angle"), "slab"),
        P(("group", "angle"), "slab", None),
        P(("group", "angle"), "slab", None),
    )
    return jax.shard_map(
        on_device,
        mesh=mesh,
        in_specs=placed,
        out_specs=P(("group", "slab", "angle"), "col"),
        check_vma=False,
    )
```

```python
import math

import jax
import jax.numpy as jnp
from jax import lax
from jax.experimental import pallas as pl
from jax.experimental.pallas import tpu as pltpu
from jax.sharding import PartitionSpec as P

BLOCK = 256
TILE = 128
STACK = 8
DIRECT = (False, False, False, True)
SOON = (False,) * 4
WEIGHTS = (40000, 20000, 1, 1)
FINISH_WEIGHTS = (1, 1, 10000)
MARKS = ()
VMEM_BYTES = 14 * 1024 * 1024
FIRST_VMEM_BYTES = 103 * 512 * 1024
LINE_ORDER = ((3, 2, 1, 0), (0, 2, 3, 1), (3, 1, 0, 2), (0, 1, 2, 3))

VMEM = pl.BlockSpec(memory_space=pltpu.VMEM)
HELD = pl.BlockSpec(memory_space=pltpu.HBM)
SMEM = pl.BlockSpec(memory_space=pltpu.SMEM)


def kernel_call(
    body, out_shape, args, flops, scratch=(), name=None, specs=None, grant=VMEM_BYTES, carried=()
):
    specs = specs or [VMEM] * len(args)
    moved = sum(a.size * a.dtype.itemsize for a in (*args, *out_shape))
    n_in, n_out, n_through = len(args), len(out_shape), len(carried)

    def kernel(*refs):
        ins, refs = refs[:n_in], refs[n_in + n_through :]
        body(*ins, *refs[:n_out], *refs[n_out + n_through :])

    return pl.pallas_call(
        kernel,
        out_shape=[*out_shape, *(jax.ShapeDtypeStruct(c.shape, c.dtype) for c in carried)],
        in_specs=[*specs, *([HELD] * n_through)],
        out_specs=[VMEM] * n_out + [HELD] * n_through,
        input_output_aliases={n_in + i: n_out + i for i in range(n_through)},
        scratch_shapes=list(scratch),
        compiler_params=pltpu.CompilerParams(vmem_limit_bytes=grant),
        cost_estimate=pl.CostEstimate(flops=flops, bytes_accessed=moved, transcendentals=0),
        name=name,
    )(*args, *carried)


def build_band(taps_ref, band_ref):
    count = taps_ref.shape[0]
    steps, tiles = band_ref.shape[1] // TILE, band_ref.shape[0] // TILE
    zero = jnp.zeros((TILE, TILE), jnp.float32)
    ahead = lax.broadcasted_iota(jnp.int32, (TILE, TILE), 1) >= lax.broadcasted_iota(
        jnp.int32, (TILE, TILE), 0
    )
    taps = taps_ref[...].astype(jnp.float32)

    def shifted(d):
        if not 0 <= d < count:
            return zero
        row = jnp.broadcast_to(taps[d : d + 1, :], (TILE, TILE))
        return pltpu.roll(row, 0, 1, stride=1, stride_axis=0)

    before = zero
    for d in range(-(steps - 1), tiles):
        here = shifted(d)
        block = jnp.where(ahead, here, before).T.astype(jnp.bfloat16)
        before = here
        for c in range(steps):
            if 0 <= d + c < tiles:
                band_ref[(d + c) * TILE : (d + c + 1) * TILE, c * TILE : (c + 1) * TILE] = block


def weigh(proj_ref, weighted_ref, half, row_at, row_start, col_start, sizes, c):
    angles = proj_ref.shape[0]
    total_rows, total_cols, count = sizes
    distance = jnp.float32(total_cols)
    v = lax.broadcasted_iota(jnp.int32, (count, 1), 0) + (row_start + row_at)
    v = v.astype(jnp.float32) - total_rows / 2 + 0.5
    u = lax.broadcasted_iota(jnp.int32, (1, BLOCK), 1) + (col_start + c)
    u = u.astype(jnp.float32) - total_cols / 2 + 0.5
    factor = distance / jnp.sqrt(distance * distance + u * u + v * v)
    for a in range(angles):
        raw = proj_ref[a, pl.ds(row_at, count), c : c + BLOCK].astype(jnp.float32)
        at = (half * angles + a) * count
        weighted_ref[at : at + count, c : c + BLOCK] = (raw * factor).astype(jnp.bfloat16)


def filter_columns(work, count, band_ref, weighted_at):
    length = band_ref.shape[0]
    reach = (length - BLOCK) // 2
    groups = []
    for half, first, width, out_ref in work:
        starts = range(first, first + width, BLOCK)
        for at in range(0, len(starts), STACK):
            groups.append((half, starts[at : at + STACK], out_ref, at))

    def touch(index):
        if index < len(groups):
            half, starts, _, _ = groups[index]
            for c in range(starts[0] - reach, starts[-1] + BLOCK + reach, BLOCK):
                weighted_at(half, c)

    touch(0)
    for index, (half, starts, out_ref, at) in enumerate(groups):
        touch(index + 1)
        tall = jnp.concatenate(
            [
                jnp.concatenate(
                    [weighted_at(half, c)() for c in range(s - reach, s + BLOCK + reach, BLOCK)],
                    axis=1,
                )
                for s in starts
            ],
            axis=0,
        )
        result = jnp.dot(tall, band_ref[...], preferred_element_type=jnp.float32)
        result = result.astype(jnp.bfloat16)
        for k in range(len(starts)):
            out_ref[:, (at + k) * BLOCK : (at + k + 1) * BLOCK] = result[
                k * count : (k + 1) * count, :
            ]


def bf16(*shape):
    return jax.ShapeDtypeStruct(shape, jnp.bfloat16)


def f32(*shape):
    return jax.ShapeDtypeStruct(shape, jnp.float32)


def chunk_plan(cols, reach):
    assert cols >= 4 * reach and reach % (4 * BLOCK) == 0
    first, second = reach + BLOCK, 2 * reach
    third = second + (cols - 2 * reach) * 3 // 8
    return [(first, second - first), (second, third - second), (third, cols - third), (0, first)]


def on_device(projections, filter_taps, row_first, interp_index, interp_frac):
    angles, rows, cols = projections.shape
    depth = interp_index.shape[2]
    taps = filter_taps.shape[0]
    reach = taps // 2
    length = taps + BLOCK
    margin = rows // 2
    slabs, line, sides = (lax.axis_size(n) for n in ("slab", "angle", "col"))
    scale = math.pi / (angles * line)
    both = slabs == 2
    halos = 1 if both else 2
    quick = line == 4
    shard = depth // line
    order = LINE_ORDER if quick else (tuple(range(line)),) * line
    total_rows, total_cols = rows * slabs, cols * sides
    chunks = chunk_plan(cols, reach)
    widths = [w for _, w in chunks]
    part = angles * margin
    sizes = (total_rows, total_cols, margin)

    def half_rows(slab):
        if both:
            return jnp.where(slab == 0, margin, 0), jnp.where(slab == 0, 0, margin)
        return margin, 0

    def aligned(row):
        return row if isinstance(row, int) else pl.multiple_of(row, margin)

    start, width = chunks[0]
    window_at, window = start - reach, width + 2 * reach
    early = halos

    def first_kernel(proj_ref, taps_ref, band_ref, edge_ref, *rest):
        outs, (raw_ref, weighted_ref, sem) = rest[:-3], rest[-3:]
        slab = lax.axis_index("slab")
        col = lax.axis_index("col")
        starts = [aligned(r) for r in half_rows(slab)][:early]
        copies = [
            pltpu.make_async_copy(
                proj_ref.at[a, pl.ds(r, margin), pl.ds(window_at, window)],
                raw_ref.at[a, pl.ds(r, margin), :],
                sem.at[a * 2 + h],
            )
            for a in range(angles)
            for h, r in enumerate(starts)
        ]
        edge_col = pl.multiple_of(jnp.where(col == 0, cols - reach, 0), TILE)
        edge_copy = pltpu.make_async_copy(
            proj_ref.at[:, :, pl.ds(edge_col, reach)], edge_ref, sem.at[2 * angles]
        )
        for copy in copies:
            copy.start()
        edge_copy.start()
        build_band(taps_ref, band_ref)
        for copy in copies:
            copy.wait()
        known = set()

        def weighted_at(half, c):
            c -= window_at
            if (half, c) not in known:
                known.add((half, c))
                weigh(
                    raw_ref, weighted_ref, half, starts[half], slab * rows,
                    col * cols + window_at, sizes, c,
                )
            return lambda: weighted_ref[half * part : (half + 1) * part, c : c + BLOCK]

        work = [(h, start, width, out_ref) for h, out_ref in enumerate(outs)]
        filter_columns(work, part, band_ref, weighted_at)
        edge_copy.wait()

    band, edge, *first_out = kernel_call(
        first_kernel,
        [bf16(length, BLOCK), bf16(angles, rows, reach)] + [bf16(part, width)] * early,
        (projections, filter_taps.reshape(taps // TILE, TILE)),
        2 * early * part * length * width,
        scratch=[
            pltpu.VMEM((angles, rows, window), jnp.bfloat16),
            pltpu.VMEM((early * part, window), jnp.bfloat16),
            pltpu.SemaphoreType.DMA((2 * angles + 1,)),
        ],
        name="first_columns",
        specs=[HELD, VMEM],
        grant=FIRST_VMEM_BYTES,
    )

    up = [(i, (i + 1) % slabs) for i in range(slabs - 1)]
    down = [(j, i) for i, j in up]

    def exchange(sends):
        if both:
            return [lax.ppermute(sends[0], "slab", up + down)]
        return [lax.ppermute(sends[0], "slab", up), lax.ppermute(sends[1], "slab", down)]

    assert sides == 2
    received = lax.ppermute(edge, "col", [(0, 1), (1, 0)])
    halo_rows = [exchange(first_out)]

    def write_weights(first_ref, index_ref, frac_ref, own_ref, halo_ref):
        slab = lax.axis_index("slab")
        angle = lax.axis_index("angle")
        if both:
            bases = [jnp.where(slab == 0, rows, rows - margin)]
        else:
            bases = [slab * rows - margin, (slab + 1) * rows]

        def weights(a, base):
            slot = lax.broadcasted_iota(jnp.int32, (margin, depth), 0) + base
            position = index_ref[a] + first_ref[a]
            frac = frac_ref[a]
            high = frac.astype(jnp.bfloat16).astype(jnp.float32)
            low = (1.0 - frac).astype(jnp.bfloat16).astype(jnp.float32)
            return jnp.where(slot == position, low, 0.0) + jnp.where(slot == position + 1, high, 0.0)

        here = [slab * rows + r for r in half_rows(slab)]
        for starts, ref in ((here, own_ref), (bases, halo_ref)):
            table = jnp.concatenate([weights(a, b) for b in starts for a in range(angles)], axis=0)
            turned = table.T.astype(jnp.bfloat16)
            for s in range(line):
                if quick:
                    places = [o.index(s) for o in order]
                    place = places[line - 1]
                    for i in range(line - 1):
                        place = jnp.where(angle == i, places[i], place)
                    at = pl.multiple_of(place * shard, shard)
                else:
                    at = s * shard
                ref[pl.ds(at, shard), :] = turned[s * shard : (s + 1) * shard, :]

    def filter_here(refs, work, band_ref):
        proj_ref, received_ref, weighted_ref, halo_cols_ref = refs
        slab = lax.axis_index("slab")
        col = lax.axis_index("col")
        starts = [aligned(r) for r in half_rows(slab)]
        lower = col == 0
        from_col = jnp.where(lower, cols, col * cols - reach)
        none = jnp.zeros((part, BLOCK), jnp.bfloat16)
        known = set()

        def weighted_at(half, c):
            inside = 0 <= c < cols
            source, into = (proj_ref, weighted_ref) if inside else (received_ref, halo_cols_ref)
            first_col = col * cols if inside else from_col
            at = c if inside else c % reach
            if (half, at, inside) not in known:
                known.add((half, at, inside))
                weigh(source, into, half, starts[half], slab * rows, first_col, sizes, at)

            def load():
                block = into[half * part : (half + 1) * part, at : at + BLOCK]
                if c < 0:
                    block = jnp.where(lower, none, block)
                elif c >= cols:
                    block = jnp.where(lower, block, none)
                return block

            return load

        filter_columns(work, part, band_ref, weighted_at)

    scratch = [pltpu.VMEM((2 * part, n), jnp.bfloat16) for n in (cols, reach)]

    work = [(1, *chunks[0])][: 2 - early]
    work += [(half, *chunk) for chunk in chunks[1:-1] for half in (0, 1)]

    def second_kernel(proj_ref, received_ref, band_ref, first_ref, index_ref, frac_ref,
                      own_ref, halo_ref, *rest):
        outs = [(*w, ref) for w, ref in zip(work, rest)]
        filter_here((proj_ref, received_ref, *rest[-2:]), outs, band_ref)
        write_weights(first_ref, index_ref, frac_ref, own_ref, halo_ref)

    own_weight, halo_weight, *second_out = kernel_call(
        second_kernel,
        [bf16(depth, 2 * part), bf16(depth, halos * part)] + [bf16(part, w[2]) for w in work],
        (projections, received, band, row_first[:, 0], interp_index, interp_frac),
        2 * part * length * sum(w[2] for w in work),
        scratch=scratch,
        name="other_columns",
        specs=[VMEM, VMEM, VMEM, SMEM, VMEM, VMEM],
    )

    def last_kernel(proj_ref, received_ref, taps_ref, *rest):
        *outs, band_ref, weighted_ref, halo_cols_ref = rest
        build_band(taps_ref, band_ref)
        filter_here(
            (proj_ref, received_ref, weighted_ref, halo_cols_ref),
            [(half, *chunks[-1], ref) for half, ref in enumerate(outs)],
            band_ref,
        )

    before = second_out[-2:]
    *last_out, before[0] = kernel_call(
        last_kernel,
        [bf16(part, widths[-1])] * 2,
        (projections, received, filter_taps.reshape(taps // TILE, TILE)),
        4 * part * length * widths[-1],
        scratch=[pltpu.VMEM((length, BLOCK), jnp.bfloat16)] + scratch,
        name="last_columns",
        carried=before[:1],
    )
    second_out = [*second_out[:-2], *before, *last_out]
    filtered = [(*first_out, *second_out[: 2 - early])]
    for at in range(2 - early, len(second_out), 2):
        filtered.append(second_out[at : at + 2])
        halo_rows.append(exchange(second_out[at : at + halos]))

    def project(index, after=()):
        width = widths[index]

        def body(own_ref, halo_ref, *rest):
            sources, outs = rest[: 2 + halos], rest[2 + halos + len(after) :]
            for c in range(0, width, BLOCK):
                cut = slice(c, c + BLOCK)
                own = jnp.concatenate([ref[:, cut] for ref in sources[:2]], axis=0)
                other = [ref[:, cut] for ref in sources[2:]]
                other = other[0] if len(other) == 1 else jnp.concatenate(other, axis=0)
                total = jnp.dot(own_ref[...], own, preferred_element_type=jnp.float32)
                total += jnp.dot(halo_ref[...], other, preferred_element_type=jnp.float32)
                total = total * scale
                at = 0
                for out in outs:
                    out[:, cut] = total[at : at + out.shape[0], :].astype(out.dtype)
                    at += out.shape[0]

        if quick:
            first = [bf16(shard, width)] * 2 if DIRECT[index] else [bf16(2 * shard, width)]
            shapes = [*first, bf16(shard, width), f32(shard, width)]
        else:
            shapes = [f32(depth, width)]
        return kernel_call(
            body,
            shapes,
            (own_weight, halo_weight, *filtered[index], *halo_rows[index], *after),
            2 * depth * (2 + halos) * part * width,
            name="interpolate",
            specs=[VMEM] * (4 + halos) + [HELD] * len(after),
        )

    def widen(x):
        return x.astype(jnp.float32)

    def at_end():
        angle = lax.axis_index("angle")
        return (angle == 0) | (angle == line - 1)

    neighbours = [(0, 1), (1, 0), (2, 3), (3, 2)]
    middles = [(1, 2), (2, 1), (0, 0), (3, 3)]
    second_hop = [(0, 1), (1, 3), (2, 0), (3, 2)]
    straight = [(0, 2), (3, 1), (1, 0), (2, 3)]

    def first_hops(*parts):
        if len(parts) == 1:
            return [lax.ppermute(parts[0], "angle", neighbours)]
        near, middle = parts
        two = lax.ppermute(middle, "angle", straight)
        three = lax.ppermute(middle, "angle", middles)
        one = lax.ppermute(near, "angle", neighbours)
        return [one, three, two]

    def relay(sent, own, far, kept, after=(), weight=1, soon=False):
        direct = len(sent) == 3
        arrived = sent[: 1 if soon else 2] if direct else [sent[0], own[0]]
        extra = len(arrived) - 1

        def body(one_ref, *rest):
            other_ref = rest[0]
            far_ref, kept_ref = rest[extra : extra + 2]
            outs = rest[extra + 2 + len(after) :]
            end = at_end()
            near = widen(one_ref[:shard, :])
            relayed = widen(far_ref[...]) + jnp.where(end, 0.0, near)
            outs[0][...] = relayed.astype(jnp.bfloat16)
            if soon:
                outs[1][...] = kept_ref[...] + jnp.where(end, near, 0.0)
            elif direct:
                outs[1][...] = kept_ref[...] + jnp.where(end, near, widen(other_ref[...]))
            else:
                outs[1][...] = kept_ref[...] + jnp.where(end, near, 0.0)
                crossed = widen(one_ref[shard:, :]) + widen(other_ref[shard:, :])
                outs[2][...] = crossed.astype(jnp.bfloat16)

        relayed, partial, *crossed = kernel_call(
            body,
            [bf16(*far.shape), f32(*kept.shape)] + [bf16(*far.shape)] * (not direct),
            (*arrived, far, kept, *after),
            far.size * 2 * weight,
            name="relay",
            specs=[VMEM] * (3 + extra) + [HELD] * len(after),
        )
        four = lax.ppermute(relayed, "angle", second_hop)
        three = sent[2] if direct else lax.ppermute(crossed[0], "angle", middles)
        return (partial, four, three, *([sent[1]] if soon else []))

    def total(partial_ref, four_ref, *fillers):
        direct = sum(widen(ref[...]) for ref in fillers)
        return partial_ref[...] + widen(four_ref[...]) + jnp.where(at_end(), 0.0, direct)

    def mark(array, weight):
        def body(array_ref, out_ref):
            out_ref[...] = jnp.zeros_like(out_ref)

        return kernel_call(body, [f32(8, TILE)], (array,), weight, name="mark", specs=[HELD])[0]

    def finish(pieces, weight=1, after=()):
        def body(*refs):
            refs[-1][...] = total(*refs[: len(pieces)])

        return kernel_call(
            body,
            [f32(*pieces[0].shape)],
            (*pieces, *after),
            pieces[0].size * 2 * weight,
            name="finish",
            specs=[VMEM] * len(pieces) + [HELD] * len(after),
        )[0]

    def store(done, pieces):
        first = len(done)
        given = [*done, *(piece for triple in pieces for piece in triple)]

        def body(*refs):
            ready, refs = refs[:first], refs[first:]
            volume_ref, sem = refs[3 * len(pieces)], refs[-1]
            totals = refs[3 * len(pieces) + 1 : -1]

            def copy(index, source):
                at = pl.ds(chunks[index][0], chunks[index][1])
                return pltpu.make_async_copy(source, volume_ref.at[:, at], sem.at[index])

            copies = [copy(i, ref) for i, ref in enumerate(ready)]
            for c in copies:
                c.start()
            for i, total_ref in enumerate(totals):
                total_ref[...] = total(*refs[3 * i : 3 * i + 3])
                copies.append(copy(first + i, total_ref))
                copies[-1].start()
            for c in copies:
                c.wait()

        return pl.pallas_call(
            body,
            out_shape=f32(shard, cols),
            in_specs=[VMEM] * len(given),
            out_specs=HELD,
            scratch_shapes=[
                *(pltpu.VMEM((shard, w), jnp.float32) for w in widths[first:]),
                pltpu.SemaphoreType.DMA((len(chunks),)),
            ],
            compiler_params=pltpu.CompilerParams(vmem_limit_bytes=VMEM_BYTES),
            name="store",
        )(*given)

    if not quick:
        sums = [
            lax.psum_scatter(project(i)[0], "angle", scatter_dimension=0, tiled=True)
            for i in range(len(chunks))
        ]
        return jnp.concatenate([sums[i] for i in sorted(range(len(chunks)), key=chunks.__getitem__)], 1)

    last = len(chunks) - 1
    *own, far, kept = project(0)
    sent = first_hops(*own)
    done, pieces = [], []
    for j in range(last + 1):
        here = (sent, own, far, kept)
        after = sent[2:] if j == 0 else done[-1:] if j < last else []
        if j < last:
            earlier = [p[0] for p in pieces[-1:]] if j else [last_out[-1]]
            *own, far, kept = project(j + 1, after=earlier)
            sent = first_hops(*own)
            after = [*after, kept]
        if j == 0 and MARKS:
            after.append(mark(here[0][0], MARKS[0]))
        pieces.append(relay(*here, after=after, weight=WEIGHTS[j], soon=SOON[j]))
        if j < last:
            early_hop = [mark(sent[0], MARKS[j + 1])] if j + 1 < len(MARKS) else []
            done.append(finish(pieces[j], weight=FINISH_WEIGHTS[j], after=early_hop))
    return store(done, pieces[last:])


def solution(mesh):
    placed = (
        P(("group", "angle"), "slab", "col"),
        P(),
        P(("group", "angle"), "slab"),
        P(("group", "angle"), "slab", None),
        P(("group", "angle"), "slab", None),
    )
    return jax.shard_map(
        on_device,
        mesh=mesh,
        in_specs=placed,
        out_specs=P(("group", "slab", "angle"), "col"),
        check_vma=False,
    )
```

```python
import math

import jax
import jax.numpy as jnp
from jax import lax
from jax.experimental import pallas as pl
from jax.experimental.pallas import tpu as pltpu
from jax.sharding import PartitionSpec as P

BLOCK = 256
TILE = 128
STACK = 8
DIRECT = (False, False, False, True)
SOON = (False,) * 4
WEIGHTS = (40000, 20000, 1, 1)
FINISH_WEIGHTS = (1, 1, 4000)
MARKS = ()
VMEM_BYTES = 14 * 1024 * 1024
FIRST_VMEM_BYTES = 103 * 512 * 1024
LINE_ORDER = ((3, 2, 1, 0), (0, 2, 3, 1), (3, 1, 0, 2), (0, 1, 2, 3))

VMEM = pl.BlockSpec(memory_space=pltpu.VMEM)
HELD = pl.BlockSpec(memory_space=pltpu.HBM)
SMEM = pl.BlockSpec(memory_space=pltpu.SMEM)


def kernel_call(
    body, out_shape, args, flops, scratch=(), name=None, specs=None, grant=VMEM_BYTES, carried=()
):
    specs = specs or [VMEM] * len(args)
    moved = sum(a.size * a.dtype.itemsize for a in (*args, *out_shape))
    n_in, n_out, n_through = len(args), len(out_shape), len(carried)

    def kernel(*refs):
        ins, refs = refs[:n_in], refs[n_in + n_through :]
        body(*ins, *refs[:n_out], *refs[n_out + n_through :])

    return pl.pallas_call(
        kernel,
        out_shape=[*out_shape, *(jax.ShapeDtypeStruct(c.shape, c.dtype) for c in carried)],
        in_specs=[*specs, *([HELD] * n_through)],
        out_specs=[VMEM] * n_out + [HELD] * n_through,
        input_output_aliases={n_in + i: n_out + i for i in range(n_through)},
        scratch_shapes=list(scratch),
        compiler_params=pltpu.CompilerParams(vmem_limit_bytes=grant),
        cost_estimate=pl.CostEstimate(flops=flops, bytes_accessed=moved, transcendentals=0),
        name=name,
    )(*args, *carried)


def build_band(taps_ref, band_ref):
    count = taps_ref.shape[0]
    steps, tiles = band_ref.shape[1] // TILE, band_ref.shape[0] // TILE
    zero = jnp.zeros((TILE, TILE), jnp.float32)
    ahead = lax.broadcasted_iota(jnp.int32, (TILE, TILE), 1) >= lax.broadcasted_iota(
        jnp.int32, (TILE, TILE), 0
    )
    taps = taps_ref[...].astype(jnp.float32)

    def shifted(d):
        if not 0 <= d < count:
            return zero
        row = jnp.broadcast_to(taps[d : d + 1, :], (TILE, TILE))
        return pltpu.roll(row, 0, 1, stride=1, stride_axis=0)

    before = zero
    for d in range(-(steps - 1), tiles):
        here = shifted(d)
        block = jnp.where(ahead, here, before).T.astype(jnp.bfloat16)
        before = here
        for c in range(steps):
            if 0 <= d + c < tiles:
                band_ref[(d + c) * TILE : (d + c + 1) * TILE, c * TILE : (c + 1) * TILE] = block


def weigh(proj_ref, weighted_ref, half, row_at, row_start, col_start, sizes, c):
    angles = proj_ref.shape[0]
    total_rows, total_cols, count = sizes
    distance = jnp.float32(total_cols)
    v = lax.broadcasted_iota(jnp.int32, (count, 1), 0) + (row_start + row_at)
    v = v.astype(jnp.float32) - total_rows / 2 + 0.5
    u = lax.broadcasted_iota(jnp.int32, (1, BLOCK), 1) + (col_start + c)
    u = u.astype(jnp.float32) - total_cols / 2 + 0.5
    factor = distance / jnp.sqrt(distance * distance + u * u + v * v)
    for a in range(angles):
        raw = proj_ref[a, pl.ds(row_at, count), c : c + BLOCK].astype(jnp.float32)
        at = (half * angles + a) * count
        weighted_ref[at : at + count, c : c + BLOCK] = (raw * factor).astype(jnp.bfloat16)


def filter_columns(work, count, band_ref, weighted_at):
    length = band_ref.shape[0]
    reach = (length - BLOCK) // 2
    groups = []
    for half, first, width, out_ref in work:
        starts = range(first, first + width, BLOCK)
        for at in range(0, len(starts), STACK):
            groups.append((half, starts[at : at + STACK], out_ref, at))

    def touch(index):
        if index < len(groups):
            half, starts, _, _ = groups[index]
            for c in range(starts[0] - reach, starts[-1] + BLOCK + reach, BLOCK):
                weighted_at(half, c)

    touch(0)
    for index, (half, starts, out_ref, at) in enumerate(groups):
        touch(index + 1)
        tall = jnp.concatenate(
            [
                jnp.concatenate(
                    [weighted_at(half, c)() for c in range(s - reach, s + BLOCK + reach, BLOCK)],
                    axis=1,
                )
                for s in starts
            ],
            axis=0,
        )
        result = jnp.dot(tall, band_ref[...], preferred_element_type=jnp.float32)
        result = result.astype(jnp.bfloat16)
        for k in range(len(starts)):
            out_ref[:, (at + k) * BLOCK : (at + k + 1) * BLOCK] = result[
                k * count : (k + 1) * count, :
            ]


def bf16(*shape):
    return jax.ShapeDtypeStruct(shape, jnp.bfloat16)


def f32(*shape):
    return jax.ShapeDtypeStruct(shape, jnp.float32)


def chunk_plan(cols, reach):
    assert cols >= 4 * reach and reach % (4 * BLOCK) == 0
    first, third = reach + BLOCK, cols - reach
    return [
        (first, reach - BLOCK),
        (2 * reach, third - 2 * reach),
        (0, first),
        (third, cols - third),
    ]


def on_device(projections, filter_taps, row_first, interp_index, interp_frac):
    angles, rows, cols = projections.shape
    depth = interp_index.shape[2]
    taps = filter_taps.shape[0]
    reach = taps // 2
    length = taps + BLOCK
    margin = rows // 2
    slabs, line, sides = (lax.axis_size(n) for n in ("slab", "angle", "col"))
    scale = math.pi / (angles * line)
    both = slabs == 2
    halos = 1 if both else 2
    quick = line == 4
    shard = depth // line
    order = LINE_ORDER if quick else (tuple(range(line)),) * line
    total_rows, total_cols = rows * slabs, cols * sides
    chunks = chunk_plan(cols, reach)
    widths = [w for _, w in chunks]
    part = angles * margin
    sizes = (total_rows, total_cols, margin)

    def half_rows(slab):
        if both:
            return jnp.where(slab == 0, margin, 0), jnp.where(slab == 0, 0, margin)
        return margin, 0

    def aligned(row):
        return row if isinstance(row, int) else pl.multiple_of(row, margin)

    start, width = chunks[0]
    window_at, window = start - reach, width + 2 * reach
    early = halos

    def first_kernel(proj_ref, taps_ref, band_ref, edge_ref, *rest):
        outs, (raw_ref, weighted_ref, sem) = rest[:-3], rest[-3:]
        slab = lax.axis_index("slab")
        col = lax.axis_index("col")
        starts = [aligned(r) for r in half_rows(slab)][:early]
        copies = [
            pltpu.make_async_copy(
                proj_ref.at[a, pl.ds(r, margin), pl.ds(window_at, window)],
                raw_ref.at[a, pl.ds(r, margin), :],
                sem.at[a * 2 + h],
            )
            for a in range(angles)
            for h, r in enumerate(starts)
        ]
        edge_col = pl.multiple_of(jnp.where(col == 0, cols - reach, 0), TILE)
        edge_copy = pltpu.make_async_copy(
            proj_ref.at[:, :, pl.ds(edge_col, reach)], edge_ref, sem.at[2 * angles]
        )
        for copy in copies:
            copy.start()
        edge_copy.start()
        build_band(taps_ref, band_ref)
        for copy in copies:
            copy.wait()
        known = set()

        def weighted_at(half, c):
            c -= window_at
            if (half, c) not in known:
                known.add((half, c))
                weigh(
                    raw_ref, weighted_ref, half, starts[half], slab * rows,
                    col * cols + window_at, sizes, c,
                )
            return lambda: weighted_ref[half * part : (half + 1) * part, c : c + BLOCK]

        work = [(h, start, width, out_ref) for h, out_ref in enumerate(outs)]
        filter_columns(work, part, band_ref, weighted_at)
        edge_copy.wait()

    band, edge, *first_out = kernel_call(
        first_kernel,
        [bf16(length, BLOCK), bf16(angles, rows, reach)] + [bf16(part, width)] * early,
        (projections, filter_taps.reshape(taps // TILE, TILE)),
        2 * early * part * length * width,
        scratch=[
            pltpu.VMEM((angles, rows, window), jnp.bfloat16),
            pltpu.VMEM((early * part, window), jnp.bfloat16),
            pltpu.SemaphoreType.DMA((2 * angles + 1,)),
        ],
        name="first_columns",
        specs=[HELD, VMEM],
        grant=FIRST_VMEM_BYTES,
    )

    up = [(i, (i + 1) % slabs) for i in range(slabs - 1)]
    down = [(j, i) for i, j in up]

    def exchange(sends):
        if both:
            return [lax.ppermute(sends[0], "slab", up + down)]
        return [lax.ppermute(sends[0], "slab", up), lax.ppermute(sends[1], "slab", down)]

    assert sides == 2
    received = lax.ppermute(edge, "col", [(0, 1), (1, 0)])
    halo_rows = [exchange(first_out)]

    def write_weights(first_ref, index_ref, frac_ref, own_ref, halo_ref):
        slab = lax.axis_index("slab")
        angle = lax.axis_index("angle")
        if both:
            bases = [jnp.where(slab == 0, rows, rows - margin)]
        else:
            bases = [slab * rows - margin, (slab + 1) * rows]

        def weights(a, base):
            slot = lax.broadcasted_iota(jnp.int32, (margin, depth), 0) + base
            position = index_ref[a] + first_ref[a]
            frac = frac_ref[a]
            high = frac.astype(jnp.bfloat16).astype(jnp.float32)
            low = (1.0 - frac).astype(jnp.bfloat16).astype(jnp.float32)
            return jnp.where(slot == position, low, 0.0) + jnp.where(slot == position + 1, high, 0.0)

        here = [slab * rows + r for r in half_rows(slab)]
        for starts, ref in ((here, own_ref), (bases, halo_ref)):
            table = jnp.concatenate([weights(a, b) for b in starts for a in range(angles)], axis=0)
            turned = table.T.astype(jnp.bfloat16)
            for s in range(line):
                if quick:
                    places = [o.index(s) for o in order]
                    place = places[line - 1]
                    for i in range(line - 1):
                        place = jnp.where(angle == i, places[i], place)
                    at = pl.multiple_of(place * shard, shard)
                else:
                    at = s * shard
                ref[pl.ds(at, shard), :] = turned[s * shard : (s + 1) * shard, :]

    def filter_here(refs, work, band_ref):
        proj_ref, received_ref, weighted_ref, halo_cols_ref = refs
        slab = lax.axis_index("slab")
        col = lax.axis_index("col")
        starts = [aligned(r) for r in half_rows(slab)]
        lower = col == 0
        from_col = jnp.where(lower, cols, col * cols - reach)
        none = jnp.zeros((part, BLOCK), jnp.bfloat16)
        known = set()

        def weighted_at(half, c):
            inside = 0 <= c < cols
            source, into = (proj_ref, weighted_ref) if inside else (received_ref, halo_cols_ref)
            first_col = col * cols if inside else from_col
            at = c if inside else c % reach
            if (half, at, inside) not in known:
                known.add((half, at, inside))
                weigh(source, into, half, starts[half], slab * rows, first_col, sizes, at)

            def load():
                block = into[half * part : (half + 1) * part, at : at + BLOCK]
                if c < 0:
                    block = jnp.where(lower, none, block)
                elif c >= cols:
                    block = jnp.where(lower, block, none)
                return block

            return load

        filter_columns(work, part, band_ref, weighted_at)

    scratch = [pltpu.VMEM((2 * part, n), jnp.bfloat16) for n in (cols, reach)]

    work = [(1, *chunks[0])][: 2 - early]
    work += [(half, *chunk) for chunk in chunks[1:-1] for half in (0, 1)]

    def second_kernel(proj_ref, received_ref, band_ref, first_ref, index_ref, frac_ref,
                      own_ref, halo_ref, *rest):
        outs = [(*w, ref) for w, ref in zip(work, rest)]
        filter_here((proj_ref, received_ref, *rest[-2:]), outs, band_ref)
        write_weights(first_ref, index_ref, frac_ref, own_ref, halo_ref)

    own_weight, halo_weight, *second_out = kernel_call(
        second_kernel,
        [bf16(depth, 2 * part), bf16(depth, halos * part)] + [bf16(part, w[2]) for w in work],
        (projections, received, band, row_first[:, 0], interp_index, interp_frac),
        2 * part * length * sum(w[2] for w in work),
        scratch=scratch,
        name="other_columns",
        specs=[VMEM, VMEM, VMEM, SMEM, VMEM, VMEM],
    )

    def last_kernel(proj_ref, received_ref, taps_ref, *rest):
        *outs, band_ref, weighted_ref, halo_cols_ref = rest
        build_band(taps_ref, band_ref)
        filter_here(
            (proj_ref, received_ref, weighted_ref, halo_cols_ref),
            [(half, *chunks[-1], ref) for half, ref in enumerate(outs)],
            band_ref,
        )

    before = second_out[-2:]
    *last_out, before[0] = kernel_call(
        last_kernel,
        [bf16(part, widths[-1])] * 2,
        (projections, received, filter_taps.reshape(taps // TILE, TILE)),
        4 * part * length * widths[-1],
        scratch=[pltpu.VMEM((length, BLOCK), jnp.bfloat16)] + scratch,
        name="last_columns",
        carried=before[:1],
    )
    second_out = [*second_out[:-2], *before, *last_out]
    filtered = [(*first_out, *second_out[: 2 - early])]
    for at in range(2 - early, len(second_out), 2):
        filtered.append(second_out[at : at + 2])
        halo_rows.append(exchange(second_out[at : at + halos]))

    def project(index, after=()):
        width = widths[index]

        def body(own_ref, halo_ref, *rest):
            sources, outs = rest[: 2 + halos], rest[2 + halos + len(after) :]
            for c in range(0, width, BLOCK):
                cut = slice(c, c + BLOCK)
                own = jnp.concatenate([ref[:, cut] for ref in sources[:2]], axis=0)
                other = [ref[:, cut] for ref in sources[2:]]
                other = other[0] if len(other) == 1 else jnp.concatenate(other, axis=0)
                total = jnp.dot(own_ref[...], own, preferred_element_type=jnp.float32)
                total += jnp.dot(halo_ref[...], other, preferred_element_type=jnp.float32)
                total = total * scale
                at = 0
                for out in outs:
                    out[:, cut] = total[at : at + out.shape[0], :].astype(out.dtype)
                    at += out.shape[0]

        if quick:
            first = [bf16(shard, width)] * 2 if DIRECT[index] else [bf16(2 * shard, width)]
            shapes = [*first, bf16(shard, width), f32(shard, width)]
        else:
            shapes = [f32(depth, width)]
        return kernel_call(
            body,
            shapes,
            (own_weight, halo_weight, *filtered[index], *halo_rows[index], *after),
            2 * depth * (2 + halos) * part * width,
            name="interpolate",
            specs=[VMEM] * (4 + halos) + [HELD] * len(after),
        )

    def widen(x):
        return x.astype(jnp.float32)

    def at_end():
        angle = lax.axis_index("angle")
        return (angle == 0) | (angle == line - 1)

    neighbours = [(0, 1), (1, 0), (2, 3), (3, 2)]
    middles = [(1, 2), (2, 1), (0, 0), (3, 3)]
    second_hop = [(0, 1), (1, 3), (2, 0), (3, 2)]
    straight = [(0, 2), (3, 1), (1, 0), (2, 3)]

    def first_hops(*parts):
        if len(parts) == 1:
            return [lax.ppermute(parts[0], "angle", neighbours)]
        near, middle = parts
        two = lax.ppermute(middle, "angle", straight)
        three = lax.ppermute(middle, "angle", middles)
        one = lax.ppermute(near, "angle", neighbours)
        return [one, three, two]

    def relay(sent, own, far, kept, after=(), weight=1, soon=False):
        direct = len(sent) == 3
        arrived = sent[: 1 if soon else 2] if direct else [sent[0], own[0]]
        extra = len(arrived) - 1

        def body(one_ref, *rest):
            other_ref = rest[0]
            far_ref, kept_ref = rest[extra : extra + 2]
            outs = rest[extra + 2 + len(after) :]
            end = at_end()
            near = widen(one_ref[:shard, :])
            relayed = widen(far_ref[...]) + jnp.where(end, 0.0, near)
            outs[0][...] = relayed.astype(jnp.bfloat16)
            if soon:
                outs[1][...] = kept_ref[...] + jnp.where(end, near, 0.0)
            elif direct:
                outs[1][...] = kept_ref[...] + jnp.where(end, near, widen(other_ref[...]))
            else:
                outs[1][...] = kept_ref[...] + jnp.where(end, near, 0.0)
                crossed = widen(one_ref[shard:, :]) + widen(other_ref[shard:, :])
                outs[2][...] = crossed.astype(jnp.bfloat16)

        relayed, partial, *crossed = kernel_call(
            body,
            [bf16(*far.shape), f32(*kept.shape)] + [bf16(*far.shape)] * (not direct),
            (*arrived, far, kept, *after),
            far.size * 2 * weight,
            name="relay",
            specs=[VMEM] * (3 + extra) + [HELD] * len(after),
        )
        four = lax.ppermute(relayed, "angle", second_hop)
        three = sent[2] if direct else lax.ppermute(crossed[0], "angle", middles)
        return (partial, four, three, *([sent[1]] if soon else []))

    def total(partial_ref, four_ref, *fillers):
        direct = sum(widen(ref[...]) for ref in fillers)
        return partial_ref[...] + widen(four_ref[...]) + jnp.where(at_end(), 0.0, direct)

    def mark(array, weight):
        def body(array_ref, out_ref):
            out_ref[...] = jnp.zeros_like(out_ref)

        return kernel_call(body, [f32(8, TILE)], (array,), weight, name="mark", specs=[HELD])[0]

    def finish(pieces, weight=1, after=()):
        def body(*refs):
            refs[-1][...] = total(*refs[: len(pieces)])

        return kernel_call(
            body,
            [f32(*pieces[0].shape)],
            (*pieces, *after),
            pieces[0].size * 2 * weight,
            name="finish",
            specs=[VMEM] * len(pieces) + [HELD] * len(after),
        )[0]

    def store(done, pieces):
        first = len(done)
        given = [*done, *(piece for triple in pieces for piece in triple)]

        def body(*refs):
            ready, refs = refs[:first], refs[first:]
            volume_ref, sem = refs[3 * len(pieces)], refs[-1]
            totals = refs[3 * len(pieces) + 1 : -1]

            def copy(index, source):
                at = pl.ds(chunks[index][0], chunks[index][1])
                return pltpu.make_async_copy(source, volume_ref.at[:, at], sem.at[index])

            copies = [copy(i, ref) for i, ref in enumerate(ready)]
            for c in copies:
                c.start()
            for i, total_ref in enumerate(totals):
                total_ref[...] = total(*refs[3 * i : 3 * i + 3])
                copies.append(copy(first + i, total_ref))
                copies[-1].start()
            for c in copies:
                c.wait()

        return pl.pallas_call(
            body,
            out_shape=f32(shard, cols),
            in_specs=[VMEM] * len(given),
            out_specs=HELD,
            scratch_shapes=[
                *(pltpu.VMEM((shard, w), jnp.float32) for w in widths[first:]),
                pltpu.SemaphoreType.DMA((len(chunks),)),
            ],
            compiler_params=pltpu.CompilerParams(vmem_limit_bytes=VMEM_BYTES),
            name="store",
        )(*given)

    if not quick:
        sums = [
            lax.psum_scatter(project(i)[0], "angle", scatter_dimension=0, tiled=True)
            for i in range(len(chunks))
        ]
        return jnp.concatenate([sums[i] for i in sorted(range(len(chunks)), key=chunks.__getitem__)], 1)

    last = len(chunks) - 1
    *own, far, kept = project(0)
    sent = first_hops(*own)
    done, pieces = [], []
    for j in range(last + 1):
        here = (sent, own, far, kept)
        after = sent[2:] if j == 0 else done[-1:] if j < last else []
        if j < last:
            earlier = [p[0] for p in pieces[-1:]] if j else [last_out[-1]]
            *own, far, kept = project(j + 1, after=earlier)
            sent = first_hops(*own)
            after = [*after, kept]
        if j == 0 and MARKS:
            after.append(mark(here[0][0], MARKS[0]))
        pieces.append(relay(*here, after=after, weight=WEIGHTS[j], soon=SOON[j]))
        if j < last:
            early_hop = [mark(sent[0], MARKS[j + 1])] if j + 1 < len(MARKS) else []
            done.append(finish(pieces[j], weight=FINISH_WEIGHTS[j], after=early_hop))
    return store(done, pieces[last:])


def solution(mesh):
    placed = (
        P(("group", "angle"), "slab", "col"),
        P(),
        P(("group", "angle"), "slab"),
        P(("group", "angle"), "slab", None),
        P(("group", "angle"), "slab", None),
    )
    return jax.shard_map(
        on_device,
        mesh=mesh,
        in_specs=placed,
        out_specs=P(("group", "slab", "angle"), "col"),
        check_vma=False,
    )
```

```python
import math

import jax
import jax.numpy as jnp
from jax import lax
from jax.experimental import pallas as pl
from jax.experimental.pallas import tpu as pltpu
from jax.sharding import PartitionSpec as P

BLOCK = 256
TILE = 128
STACK = 8
DIRECT = (False, False, False, False)
SOON = (False,) * 4
WEIGHTS = (40000, 20000, 1, 1)
FINISH_WEIGHTS = (1, 1, 4000)
MARKS = ()
VMEM_BYTES = 14 * 1024 * 1024
FIRST_VMEM_BYTES = 103 * 512 * 1024
LINE_ORDER = ((3, 2, 1, 0), (0, 2, 3, 1), (3, 1, 0, 2), (0, 1, 2, 3))

VMEM = pl.BlockSpec(memory_space=pltpu.VMEM)
HELD = pl.BlockSpec(memory_space=pltpu.HBM)
SMEM = pl.BlockSpec(memory_space=pltpu.SMEM)


def kernel_call(
    body, out_shape, args, flops, scratch=(), name=None, specs=None, grant=VMEM_BYTES, carried=()
):
    specs = specs or [VMEM] * len(args)
    moved = sum(a.size * a.dtype.itemsize for a in (*args, *out_shape))
    n_in, n_out, n_through = len(args), len(out_shape), len(carried)

    def kernel(*refs):
        ins, refs = refs[:n_in], refs[n_in + n_through :]
        body(*ins, *refs[:n_out], *refs[n_out + n_through :])

    return pl.pallas_call(
        kernel,
        out_shape=[*out_shape, *(jax.ShapeDtypeStruct(c.shape, c.dtype) for c in carried)],
        in_specs=[*specs, *([HELD] * n_through)],
        out_specs=[VMEM] * n_out + [HELD] * n_through,
        input_output_aliases={n_in + i: n_out + i for i in range(n_through)},
        scratch_shapes=list(scratch),
        compiler_params=pltpu.CompilerParams(vmem_limit_bytes=grant),
        cost_estimate=pl.CostEstimate(flops=flops, bytes_accessed=moved, transcendentals=0),
        name=name,
    )(*args, *carried)


def build_band(taps_ref, band_ref):
    count = taps_ref.shape[0]
    steps, tiles = band_ref.shape[1] // TILE, band_ref.shape[0] // TILE
    zero = jnp.zeros((TILE, TILE), jnp.float32)
    ahead = lax.broadcasted_iota(jnp.int32, (TILE, TILE), 1) >= lax.broadcasted_iota(
        jnp.int32, (TILE, TILE), 0
    )
    taps = taps_ref[...].astype(jnp.float32)

    def shifted(d):
        if not 0 <= d < count:
            return zero
        row = jnp.broadcast_to(taps[d : d + 1, :], (TILE, TILE))
        return pltpu.roll(row, 0, 1, stride=1, stride_axis=0)

    before = zero
    for d in range(-(steps - 1), tiles):
        here = shifted(d)
        block = jnp.where(ahead, here, before).T.astype(jnp.bfloat16)
        before = here
        for c in range(steps):
            if 0 <= d + c < tiles:
                band_ref[(d + c) * TILE : (d + c + 1) * TILE, c * TILE : (c + 1) * TILE] = block


def weigh(proj_ref, weighted_ref, half, row_at, row_start, col_start, sizes, c):
    angles = proj_ref.shape[0]
    total_rows, total_cols, count = sizes
    distance = jnp.float32(total_cols)
    v = lax.broadcasted_iota(jnp.int32, (count, 1), 0) + (row_start + row_at)
    v = v.astype(jnp.float32) - total_rows / 2 + 0.5
    u = lax.broadcasted_iota(jnp.int32, (1, BLOCK), 1) + (col_start + c)
    u = u.astype(jnp.float32) - total_cols / 2 + 0.5
    factor = distance / jnp.sqrt(distance * distance + u * u + v * v)
    for a in range(angles):
        raw = proj_ref[a, pl.ds(row_at, count), c : c + BLOCK].astype(jnp.float32)
        at = (half * angles + a) * count
        weighted_ref[at : at + count, c : c + BLOCK] = (raw * factor).astype(jnp.bfloat16)


def filter_columns(work, count, band_ref, weighted_at):
    length = band_ref.shape[0]
    reach = (length - BLOCK) // 2
    groups = []
    for half, first, width, out_ref in work:
        starts = range(first, first + width, BLOCK)
        for at in range(0, len(starts), STACK):
            groups.append((half, starts[at : at + STACK], out_ref, at))

    def touch(index):
        if index < len(groups):
            half, starts, _, _ = groups[index]
            for c in range(starts[0] - reach, starts[-1] + BLOCK + reach, BLOCK):
                weighted_at(half, c)

    touch(0)
    for index, (half, starts, out_ref, at) in enumerate(groups):
        touch(index + 1)
        tall = jnp.concatenate(
            [
                jnp.concatenate(
                    [weighted_at(half, c)() for c in range(s - reach, s + BLOCK + reach, BLOCK)],
                    axis=1,
                )
                for s in starts
            ],
            axis=0,
        )
        result = jnp.dot(tall, band_ref[...], preferred_element_type=jnp.float32)
        result = result.astype(jnp.bfloat16)
        for k in range(len(starts)):
            out_ref[:, (at + k) * BLOCK : (at + k + 1) * BLOCK] = result[
                k * count : (k + 1) * count, :
            ]


def bf16(*shape):
    return jax.ShapeDtypeStruct(shape, jnp.bfloat16)


def f32(*shape):
    return jax.ShapeDtypeStruct(shape, jnp.float32)


def chunk_plan(cols, reach):
    assert cols >= 4 * reach and reach % (4 * BLOCK) == 0
    first, third = reach + BLOCK, cols - reach
    return [
        (first, reach - BLOCK),
        (2 * reach, third - 2 * reach),
        (0, first),
        (third, cols - third),
    ]


def on_device(projections, filter_taps, row_first, interp_index, interp_frac):
    angles, rows, cols = projections.shape
    depth = interp_index.shape[2]
    taps = filter_taps.shape[0]
    reach = taps // 2
    length = taps + BLOCK
    margin = rows // 2
    slabs, line, sides = (lax.axis_size(n) for n in ("slab", "angle", "col"))
    scale = math.pi / (angles * line)
    both = slabs == 2
    halos = 1 if both else 2
    quick = line == 4
    shard = depth // line
    order = LINE_ORDER if quick else (tuple(range(line)),) * line
    total_rows, total_cols = rows * slabs, cols * sides
    chunks = chunk_plan(cols, reach)
    widths = [w for _, w in chunks]
    part = angles * margin
    sizes = (total_rows, total_cols, margin)

    def half_rows(slab):
        if both:
            return jnp.where(slab == 0, margin, 0), jnp.where(slab == 0, 0, margin)
        return margin, 0

    def aligned(row):
        return row if isinstance(row, int) else pl.multiple_of(row, margin)

    start, width = chunks[0]
    window_at, window = start - reach, width + 2 * reach
    early = halos

    def first_kernel(proj_ref, taps_ref, band_ref, edge_ref, *rest):
        outs, (raw_ref, weighted_ref, sem) = rest[:-3], rest[-3:]
        slab = lax.axis_index("slab")
        col = lax.axis_index("col")
        starts = [aligned(r) for r in half_rows(slab)][:early]
        copies = [
            pltpu.make_async_copy(
                proj_ref.at[a, pl.ds(r, margin), pl.ds(window_at, window)],
                raw_ref.at[a, pl.ds(r, margin), :],
                sem.at[a * 2 + h],
            )
            for a in range(angles)
            for h, r in enumerate(starts)
        ]
        edge_col = pl.multiple_of(jnp.where(col == 0, cols - reach, 0), TILE)
        edge_copy = pltpu.make_async_copy(
            proj_ref.at[:, :, pl.ds(edge_col, reach)], edge_ref, sem.at[2 * angles]
        )
        for copy in copies:
            copy.start()
        edge_copy.start()
        build_band(taps_ref, band_ref)
        for copy in copies:
            copy.wait()
        known = set()

        def weighted_at(half, c):
            c -= window_at
            if (half, c) not in known:
                known.add((half, c))
                weigh(
                    raw_ref, weighted_ref, half, starts[half], slab * rows,
                    col * cols + window_at, sizes, c,
                )
            return lambda: weighted_ref[half * part : (half + 1) * part, c : c + BLOCK]

        work = [(h, start, width, out_ref) for h, out_ref in enumerate(outs)]
        filter_columns(work, part, band_ref, weighted_at)
        edge_copy.wait()

    band, edge, *first_out = kernel_call(
        first_kernel,
        [bf16(length, BLOCK), bf16(angles, rows, reach)] + [bf16(part, width)] * early,
        (projections, filter_taps.reshape(taps // TILE, TILE)),
        2 * early * part * length * width,
        scratch=[
            pltpu.VMEM((angles, rows, window), jnp.bfloat16),
            pltpu.VMEM((early * part, window), jnp.bfloat16),
            pltpu.SemaphoreType.DMA((2 * angles + 1,)),
        ],
        name="first_columns",
        specs=[HELD, VMEM],
        grant=FIRST_VMEM_BYTES,
    )

    up = [(i, (i + 1) % slabs) for i in range(slabs - 1)]
    down = [(j, i) for i, j in up]

    def exchange(sends):
        if both:
            return [lax.ppermute(sends[0], "slab", up + down)]
        return [lax.ppermute(sends[0], "slab", up), lax.ppermute(sends[1], "slab", down)]

    assert sides == 2
    received = lax.ppermute(edge, "col", [(0, 1), (1, 0)])
    halo_rows = [exchange(first_out)]

    def write_weights(first_ref, index_ref, frac_ref, own_ref, halo_ref):
        slab = lax.axis_index("slab")
        angle = lax.axis_index("angle")
        if both:
            bases = [jnp.where(slab == 0, rows, rows - margin)]
        else:
            bases = [slab * rows - margin, (slab + 1) * rows]

        def weights(a, base):
            slot = lax.broadcasted_iota(jnp.int32, (margin, depth), 0) + base
            position = index_ref[a] + first_ref[a]
            frac = frac_ref[a]
            high = frac.astype(jnp.bfloat16).astype(jnp.float32)
            low = (1.0 - frac).astype(jnp.bfloat16).astype(jnp.float32)
            return jnp.where(slot == position, low, 0.0) + jnp.where(slot == position + 1, high, 0.0)

        here = [slab * rows + r for r in half_rows(slab)]
        for starts, ref in ((here, own_ref), (bases, halo_ref)):
            table = jnp.concatenate([weights(a, b) for b in starts for a in range(angles)], axis=0)
            turned = table.T.astype(jnp.bfloat16)
            for s in range(line):
                if quick:
                    places = [o.index(s) for o in order]
                    place = places[line - 1]
                    for i in range(line - 1):
                        place = jnp.where(angle == i, places[i], place)
                    at = pl.multiple_of(place * shard, shard)
                else:
                    at = s * shard
                ref[pl.ds(at, shard), :] = turned[s * shard : (s + 1) * shard, :]

    def filter_here(refs, work, band_ref):
        proj_ref, received_ref, weighted_ref, halo_cols_ref = refs
        slab = lax.axis_index("slab")
        col = lax.axis_index("col")
        starts = [aligned(r) for r in half_rows(slab)]
        lower = col == 0
        from_col = jnp.where(lower, cols, col * cols - reach)
        none = jnp.zeros((part, BLOCK), jnp.bfloat16)
        known = set()

        def weighted_at(half, c):
            inside = 0 <= c < cols
            source, into = (proj_ref, weighted_ref) if inside else (received_ref, halo_cols_ref)
            first_col = col * cols if inside else from_col
            at = c if inside else c % reach
            if (half, at, inside) not in known:
                known.add((half, at, inside))
                weigh(source, into, half, starts[half], slab * rows, first_col, sizes, at)

            def load():
                block = into[half * part : (half + 1) * part, at : at + BLOCK]
                if c < 0:
                    block = jnp.where(lower, none, block)
                elif c >= cols:
                    block = jnp.where(lower, block, none)
                return block

            return load

        filter_columns(work, part, band_ref, weighted_at)

    scratch = [pltpu.VMEM((2 * part, n), jnp.bfloat16) for n in (cols, reach)]

    work = [(1, *chunks[0])][: 2 - early]
    work += [(half, *chunk) for chunk in chunks[1:-1] for half in (0, 1)]

    def second_kernel(proj_ref, received_ref, band_ref, first_ref, index_ref, frac_ref,
                      own_ref, halo_ref, *rest):
        outs = [(*w, ref) for w, ref in zip(work, rest)]
        filter_here((proj_ref, received_ref, *rest[-2:]), outs, band_ref)
        write_weights(first_ref, index_ref, frac_ref, own_ref, halo_ref)

    own_weight, halo_weight, *second_out = kernel_call(
        second_kernel,
        [bf16(depth, 2 * part), bf16(depth, halos * part)] + [bf16(part, w[2]) for w in work],
        (projections, received, band, row_first[:, 0], interp_index, interp_frac),
        2 * part * length * sum(w[2] for w in work),
        scratch=scratch,
        name="other_columns",
        specs=[VMEM, VMEM, VMEM, SMEM, VMEM, VMEM],
    )

    def last_kernel(proj_ref, received_ref, taps_ref, *rest):
        *outs, band_ref, weighted_ref, halo_cols_ref = rest
        build_band(taps_ref, band_ref)
        filter_here(
            (proj_ref, received_ref, weighted_ref, halo_cols_ref),
            [(half, *chunks[-1], ref) for half, ref in enumerate(outs)],
            band_ref,
        )

    before = second_out[-2:]
    *last_out, before[0] = kernel_call(
        last_kernel,
        [bf16(part, widths[-1])] * 2,
        (projections, received, filter_taps.reshape(taps // TILE, TILE)),
        4 * part * length * widths[-1],
        scratch=[pltpu.VMEM((length, BLOCK), jnp.bfloat16)] + scratch,
        name="last_columns",
        carried=before[:1],
    )
    second_out = [*second_out[:-2], *before, *last_out]
    filtered = [(*first_out, *second_out[: 2 - early])]
    for at in range(2 - early, len(second_out), 2):
        filtered.append(second_out[at : at + 2])
        halo_rows.append(exchange(second_out[at : at + halos]))

    def project(index, after=()):
        width = widths[index]

        def body(own_ref, halo_ref, *rest):
            sources, outs = rest[: 2 + halos], rest[2 + halos + len(after) :]
            for c in range(0, width, BLOCK):
                cut = slice(c, c + BLOCK)
                own = jnp.concatenate([ref[:, cut] for ref in sources[:2]], axis=0)
                other = [ref[:, cut] for ref in sources[2:]]
                other = other[0] if len(other) == 1 else jnp.concatenate(other, axis=0)
                total = jnp.dot(own_ref[...], own, preferred_element_type=jnp.float32)
                total += jnp.dot(halo_ref[...], other, preferred_element_type=jnp.float32)
                total = total * scale
                at = 0
                for out in outs:
                    out[:, cut] = total[at : at + out.shape[0], :].astype(out.dtype)
                    at += out.shape[0]

        if quick:
            first = [bf16(shard, width)] * 2 if DIRECT[index] else [bf16(2 * shard, width)]
            shapes = [*first, bf16(shard, width), f32(shard, width)]
        else:
            shapes = [f32(depth, width)]
        return kernel_call(
            body,
            shapes,
            (own_weight, halo_weight, *filtered[index], *halo_rows[index], *after),
            2 * depth * (2 + halos) * part * width,
            name="interpolate",
            specs=[VMEM] * (4 + halos) + [HELD] * len(after),
        )

    def widen(x):
        return x.astype(jnp.float32)

    def at_end():
        angle = lax.axis_index("angle")
        return (angle == 0) | (angle == line - 1)

    neighbours = [(0, 1), (1, 0), (2, 3), (3, 2)]
    middles = [(1, 2), (2, 1), (0, 0), (3, 3)]
    second_hop = [(0, 1), (1, 3), (2, 0), (3, 2)]
    straight = [(0, 2), (3, 1), (1, 0), (2, 3)]

    def first_hops(*parts):
        if len(parts) == 1:
            return [lax.ppermute(parts[0], "angle", neighbours)]
        near, middle = parts
        two = lax.ppermute(middle, "angle", straight)
        three = lax.ppermute(middle, "angle", middles)
        one = lax.ppermute(near, "angle", neighbours)
        return [one, three, two]

    def relay(sent, own, far, kept, after=(), weight=1, soon=False):
        direct = len(sent) == 3
        arrived = sent[: 1 if soon else 2] if direct else [sent[0], own[0]]
        extra = len(arrived) - 1

        def body(one_ref, *rest):
            other_ref = rest[0]
            far_ref, kept_ref = rest[extra : extra + 2]
            outs = rest[extra + 2 + len(after) :]
            end = at_end()
            near = widen(one_ref[:shard, :])
            relayed = widen(far_ref[...]) + jnp.where(end, 0.0, near)
            outs[0][...] = relayed.astype(jnp.bfloat16)
            if soon:
                outs[1][...] = kept_ref[...] + jnp.where(end, near, 0.0)
            elif direct:
                outs[1][...] = kept_ref[...] + jnp.where(end, near, widen(other_ref[...]))
            else:
                outs[1][...] = kept_ref[...] + jnp.where(end, near, 0.0)
                crossed = widen(one_ref[shard:, :]) + widen(other_ref[shard:, :])
                outs[2][...] = crossed.astype(jnp.bfloat16)

        relayed, partial, *crossed = kernel_call(
            body,
            [bf16(*far.shape), f32(*kept.shape)] + [bf16(*far.shape)] * (not direct),
            (*arrived, far, kept, *after),
            far.size * 2 * weight,
            name="relay",
            specs=[VMEM] * (3 + extra) + [HELD] * len(after),
        )
        four = lax.ppermute(relayed, "angle", second_hop)
        three = sent[2] if direct else lax.ppermute(crossed[0], "angle", middles)
        return (partial, four, three, *([sent[1]] if soon else []))

    def total(partial_ref, four_ref, *fillers):
        direct = sum(widen(ref[...]) for ref in fillers)
        return partial_ref[...] + widen(four_ref[...]) + jnp.where(at_end(), 0.0, direct)

    def mark(array, weight):
        def body(array_ref, out_ref):
            out_ref[...] = jnp.zeros_like(out_ref)

        return kernel_call(body, [f32(8, TILE)], (array,), weight, name="mark", specs=[HELD])[0]

    def finish(pieces, weight=1, after=()):
        def body(*refs):
            refs[-1][...] = total(*refs[: len(pieces)])

        return kernel_call(
            body,
            [f32(*pieces[0].shape)],
            (*pieces, *after),
            pieces[0].size * 2 * weight,
            name="finish",
            specs=[VMEM] * len(pieces) + [HELD] * len(after),
        )[0]

    def store(done, pieces):
        first = len(done)
        given = [*done, *(piece for triple in pieces for piece in triple)]

        def body(*refs):
            ready, refs = refs[:first], refs[first:]
            volume_ref, sem = refs[3 * len(pieces)], refs[-1]
            totals = refs[3 * len(pieces) + 1 : -1]

            def copy(index, source):
                at = pl.ds(chunks[index][0], chunks[index][1])
                return pltpu.make_async_copy(source, volume_ref.at[:, at], sem.at[index])

            copies = [copy(i, ref) for i, ref in enumerate(ready)]
            for c in copies:
                c.start()
            for i, total_ref in enumerate(totals):
                total_ref[...] = total(*refs[3 * i : 3 * i + 3])
                copies.append(copy(first + i, total_ref))
                copies[-1].start()
            for c in copies:
                c.wait()

        return pl.pallas_call(
            body,
            out_shape=f32(shard, cols),
            in_specs=[VMEM] * len(given),
            out_specs=HELD,
            scratch_shapes=[
                *(pltpu.VMEM((shard, w), jnp.float32) for w in widths[first:]),
                pltpu.SemaphoreType.DMA((len(chunks),)),
            ],
            compiler_params=pltpu.CompilerParams(vmem_limit_bytes=VMEM_BYTES),
            name="store",
        )(*given)

    if not quick:
        sums = [
            lax.psum_scatter(project(i)[0], "angle", scatter_dimension=0, tiled=True)
            for i in range(len(chunks))
        ]
        return jnp.concatenate([sums[i] for i in sorted(range(len(chunks)), key=chunks.__getitem__)], 1)

    last = len(chunks) - 1
    *own, far, kept = project(0)
    sent = first_hops(*own)
    done, pieces = [], []
    for j in range(last + 1):
        here = (sent, own, far, kept)
        after = sent[2:] if j == 0 else done[-1:] if j < last else []
        if j < last:
            earlier = [p[0] for p in pieces[-1:]] if j else [last_out[-1]]
            *own, far, kept = project(j + 1, after=earlier)
            sent = first_hops(*own)
            after = [*after, kept]
        if j == 0 and MARKS:
            after.append(mark(here[0][0], MARKS[0]))
        pieces.append(relay(*here, after=after, weight=WEIGHTS[j], soon=SOON[j]))
        if j < last:
            early_hop = [mark(sent[0], MARKS[j + 1])] if j + 1 < len(MARKS) else []
            done.append(finish(pieces[j], weight=FINISH_WEIGHTS[j], after=early_hop))
    return store(done, pieces[last:])


def solution(mesh):
    placed = (
        P(("group", "angle"), "slab", "col"),
        P(),
        P(("group", "angle"), "slab"),
        P(("group", "angle"), "slab", None),
        P(("group", "angle"), "slab", None),
    )
    return jax.shard_map(
        on_device,
        mesh=mesh,
        in_specs=placed,
        out_specs=P(("group", "slab", "angle"), "col"),
        check_vma=False,
    )
```

```python
import math

import jax
import jax.numpy as jnp
from jax import lax
from jax.experimental import pallas as pl
from jax.experimental.pallas import tpu as pltpu
from jax.sharding import PartitionSpec as P

BLOCK = 256
TILE = 128
STACK = 8
DIRECT = (False, False, False, True)
SOON = (False, False, False, True)
WEIGHTS = (40000, 28000, 1, 1)
FINISH_WEIGHTS = (1, 1, 10000)
MARK = 1000000000
VMEM_BYTES = 14 * 1024 * 1024
FIRST_VMEM_BYTES = 103 * 512 * 1024
LINE_ORDER = ((3, 2, 1, 0), (0, 2, 3, 1), (3, 1, 0, 2), (0, 1, 2, 3))

VMEM = pl.BlockSpec(memory_space=pltpu.VMEM)
HELD = pl.BlockSpec(memory_space=pltpu.HBM)
SMEM = pl.BlockSpec(memory_space=pltpu.SMEM)


def kernel_call(
    body, out_shape, args, flops, scratch=(), name=None, specs=None, grant=VMEM_BYTES, carried=()
):
    specs = specs or [VMEM] * len(args)
    moved = sum(a.size * a.dtype.itemsize for a in (*args, *out_shape))
    n_in, n_out, n_through = len(args), len(out_shape), len(carried)

    def kernel(*refs):
        ins, refs = refs[:n_in], refs[n_in + n_through :]
        body(*ins, *refs[:n_out], *refs[n_out + n_through :])

    return pl.pallas_call(
        kernel,
        out_shape=[*out_shape, *(jax.ShapeDtypeStruct(c.shape, c.dtype) for c in carried)],
        in_specs=[*specs, *([HELD] * n_through)],
        out_specs=[VMEM] * n_out + [HELD] * n_through,
        input_output_aliases={n_in + i: n_out + i for i in range(n_through)},
        scratch_shapes=list(scratch),
        compiler_params=pltpu.CompilerParams(vmem_limit_bytes=grant),
        cost_estimate=pl.CostEstimate(flops=flops, bytes_accessed=moved, transcendentals=0),
        name=name,
    )(*args, *carried)


def build_band(taps_ref, band_ref):
    count = taps_ref.shape[0]
    steps, tiles = band_ref.shape[1] // TILE, band_ref.shape[0] // TILE
    zero = jnp.zeros((TILE, TILE), jnp.float32)
    ahead = lax.broadcasted_iota(jnp.int32, (TILE, TILE), 1) >= lax.broadcasted_iota(
        jnp.int32, (TILE, TILE), 0
    )
    taps = taps_ref[...].astype(jnp.float32)

    def shifted(d):
        if not 0 <= d < count:
            return zero
        row = jnp.broadcast_to(taps[d : d + 1, :], (TILE, TILE))
        return pltpu.roll(row, 0, 1, stride=1, stride_axis=0)

    before = zero
    for d in range(-(steps - 1), tiles):
        here = shifted(d)
        block = jnp.where(ahead, here, before).T.astype(jnp.bfloat16)
        before = here
        for c in range(steps):
            if 0 <= d + c < tiles:
                band_ref[(d + c) * TILE : (d + c + 1) * TILE, c * TILE : (c + 1) * TILE] = block


def weigh(proj_ref, weighted_ref, half, row_at, row_start, col_start, sizes, c):
    angles = proj_ref.shape[0]
    total_rows, total_cols, count = sizes
    distance = jnp.float32(total_cols)
    v = lax.broadcasted_iota(jnp.int32, (count, 1), 0) + (row_start + row_at)
    v = v.astype(jnp.float32) - total_rows / 2 + 0.5
    u = lax.broadcasted_iota(jnp.int32, (1, BLOCK), 1) + (col_start + c)
    u = u.astype(jnp.float32) - total_cols / 2 + 0.5
    factor = distance / jnp.sqrt(distance * distance + u * u + v * v)
    for a in range(angles):
        raw = proj_ref[a, pl.ds(row_at, count), c : c + BLOCK].astype(jnp.float32)
        at = (half * angles + a) * count
        weighted_ref[at : at + count, c : c + BLOCK] = (raw * factor).astype(jnp.bfloat16)


def filter_columns(work, count, band_ref, weighted_at):
    length = band_ref.shape[0]
    reach = (length - BLOCK) // 2
    groups = []
    for half, first, width, out_ref in work:
        starts = range(first, first + width, BLOCK)
        for at in range(0, len(starts), STACK):
            groups.append((half, starts[at : at + STACK], out_ref, at))

    def touch(index):
        if index < len(groups):
            half, starts, _, _ = groups[index]
            for c in range(starts[0] - reach, starts[-1] + BLOCK + reach, BLOCK):
                weighted_at(half, c)

    touch(0)
    for index, (half, starts, out_ref, at) in enumerate(groups):
        touch(index + 1)
        tall = jnp.concatenate(
            [
                jnp.concatenate(
                    [weighted_at(half, c)() for c in range(s - reach, s + BLOCK + reach, BLOCK)],
                    axis=1,
                )
                for s in starts
            ],
            axis=0,
        )
        result = jnp.dot(tall, band_ref[...], preferred_element_type=jnp.float32)
        result = result.astype(jnp.bfloat16)
        for k in range(len(starts)):
            out_ref[:, (at + k) * BLOCK : (at + k + 1) * BLOCK] = result[
                k * count : (k + 1) * count, :
            ]


def bf16(*shape):
    return jax.ShapeDtypeStruct(shape, jnp.bfloat16)


def f32(*shape):
    return jax.ShapeDtypeStruct(shape, jnp.float32)


def chunk_plan(cols, reach):
    assert cols >= 4 * reach and reach % (4 * BLOCK) == 0
    first, second = reach + BLOCK, 2 * reach
    third = second + (cols - 2 * reach) * 3 // 8
    return [(first, second - first), (second, third - second), (third, cols - third), (0, first)]


def on_device(projections, filter_taps, row_first, interp_index, interp_frac):
    angles, rows, cols = projections.shape
    depth = interp_index.shape[2]
    taps = filter_taps.shape[0]
    reach = taps // 2
    length = taps + BLOCK
    margin = rows // 2
    slabs, line, sides = (lax.axis_size(n) for n in ("slab", "angle", "col"))
    scale = math.pi / (angles * line)
    both = slabs == 2
    halos = 1 if both else 2
    quick = line == 4
    shard = depth // line
    order = LINE_ORDER if quick else (tuple(range(line)),) * line
    total_rows, total_cols = rows * slabs, cols * sides
    chunks = chunk_plan(cols, reach)
    widths = [w for _, w in chunks]
    part = angles * margin
    sizes = (total_rows, total_cols, margin)

    def half_rows(slab):
        if both:
            return jnp.where(slab == 0, margin, 0), jnp.where(slab == 0, 0, margin)
        return margin, 0

    def aligned(row):
        return row if isinstance(row, int) else pl.multiple_of(row, margin)

    start, width = chunks[0]
    window_at, window = start - reach, width + 2 * reach
    early = halos

    def first_kernel(proj_ref, taps_ref, band_ref, edge_ref, *rest):
        outs, (raw_ref, weighted_ref, sem) = rest[:-3], rest[-3:]
        slab = lax.axis_index("slab")
        col = lax.axis_index("col")
        starts = [aligned(r) for r in half_rows(slab)][:early]
        copies = [
            pltpu.make_async_copy(
                proj_ref.at[a, pl.ds(r, margin), pl.ds(window_at, window)],
                raw_ref.at[a, pl.ds(r, margin), :],
                sem.at[a * 2 + h],
            )
            for a in range(angles)
            for h, r in enumerate(starts)
        ]
        edge_col = pl.multiple_of(jnp.where(col == 0, cols - reach, 0), TILE)
        edge_copy = pltpu.make_async_copy(
            proj_ref.at[:, :, pl.ds(edge_col, reach)], edge_ref, sem.at[2 * angles]
        )
        for copy in copies:
            copy.start()
        edge_copy.start()
        build_band(taps_ref, band_ref)
        for copy in copies:
            copy.wait()
        known = set()

        def weighted_at(half, c):
            c -= window_at
            if (half, c) not in known:
                known.add((half, c))
                weigh(
                    raw_ref, weighted_ref, half, starts[half], slab * rows,
                    col * cols + window_at, sizes, c,
                )
            return lambda: weighted_ref[half * part : (half + 1) * part, c : c + BLOCK]

        work = [(h, start, width, out_ref) for h, out_ref in enumerate(outs)]
        filter_columns(work, part, band_ref, weighted_at)
        edge_copy.wait()

    band, edge, *first_out = kernel_call(
        first_kernel,
        [bf16(length, BLOCK), bf16(angles, rows, reach)] + [bf16(part, width)] * early,
        (projections, filter_taps.reshape(taps // TILE, TILE)),
        2 * early * part * length * width,
        scratch=[
            pltpu.VMEM((angles, rows, window), jnp.bfloat16),
            pltpu.VMEM((early * part, window), jnp.bfloat16),
            pltpu.SemaphoreType.DMA((2 * angles + 1,)),
        ],
        name="first_columns",
        specs=[HELD, VMEM],
        grant=FIRST_VMEM_BYTES,
    )

    up = [(i, (i + 1) % slabs) for i in range(slabs - 1)]
    down = [(j, i) for i, j in up]

    def exchange(sends):
        if both:
            return [lax.ppermute(sends[0], "slab", up + down)]
        return [lax.ppermute(sends[0], "slab", up), lax.ppermute(sends[1], "slab", down)]

    assert sides == 2
    received = lax.ppermute(edge, "col", [(0, 1), (1, 0)])
    halo_rows = [exchange(first_out)]

    def write_weights(first_ref, index_ref, frac_ref, own_ref, halo_ref):
        slab = lax.axis_index("slab")
        angle = lax.axis_index("angle")
        if both:
            bases = [jnp.where(slab == 0, rows, rows - margin)]
        else:
            bases = [slab * rows - margin, (slab + 1) * rows]

        def weights(a, base):
            slot = lax.broadcasted_iota(jnp.int32, (margin, depth), 0) + base
            position = index_ref[a] + first_ref[a]
            frac = frac_ref[a]
            high = frac.astype(jnp.bfloat16).astype(jnp.float32)
            low = (1.0 - frac).astype(jnp.bfloat16).astype(jnp.float32)
            return jnp.where(slot == position, low, 0.0) + jnp.where(slot == position + 1, high, 0.0)

        here = [slab * rows + r for r in half_rows(slab)]
        for starts, ref in ((here, own_ref), (bases, halo_ref)):
            table = jnp.concatenate([weights(a, b) for b in starts for a in range(angles)], axis=0)
            turned = table.T.astype(jnp.bfloat16)
            for s in range(line):
                if quick:
                    places = [o.index(s) for o in order]
                    place = places[line - 1]
                    for i in range(line - 1):
                        place = jnp.where(angle == i, places[i], place)
                    at = pl.multiple_of(place * shard, shard)
                else:
                    at = s * shard
                ref[pl.ds(at, shard), :] = turned[s * shard : (s + 1) * shard, :]

    def filter_here(refs, work, band_ref):
        proj_ref, received_ref, weighted_ref, halo_cols_ref = refs
        slab = lax.axis_index("slab")
        col = lax.axis_index("col")
        starts = [aligned(r) for r in half_rows(slab)]
        lower = col == 0
        from_col = jnp.where(lower, cols, col * cols - reach)
        none = jnp.zeros((part, BLOCK), jnp.bfloat16)
        known = set()

        def weighted_at(half, c):
            inside = 0 <= c < cols
            source, into = (proj_ref, weighted_ref) if inside else (received_ref, halo_cols_ref)
            first_col = col * cols if inside else from_col
            at = c if inside else c % reach
            if (half, at, inside) not in known:
                known.add((half, at, inside))
                weigh(source, into, half, starts[half], slab * rows, first_col, sizes, at)

            def load():
                block = into[half * part : (half + 1) * part, at : at + BLOCK]
                if c < 0:
                    block = jnp.where(lower, none, block)
                elif c >= cols:
                    block = jnp.where(lower, block, none)
                return block

            return load

        filter_columns(work, part, band_ref, weighted_at)

    scratch = [pltpu.VMEM((2 * part, n), jnp.bfloat16) for n in (cols, reach)]

    work = [(1, *chunks[0])][: 2 - early]
    work += [(half, *chunk) for chunk in chunks[1:-1] for half in (0, 1)]

    def second_kernel(proj_ref, received_ref, band_ref, first_ref, index_ref, frac_ref,
                      own_ref, halo_ref, *rest):
        outs = [(*w, ref) for w, ref in zip(work, rest)]
        filter_here((proj_ref, received_ref, *rest[-2:]), outs, band_ref)
        write_weights(first_ref, index_ref, frac_ref, own_ref, halo_ref)

    own_weight, halo_weight, *second_out = kernel_call(
        second_kernel,
        [bf16(depth, 2 * part), bf16(depth, halos * part)] + [bf16(part, w[2]) for w in work],
        (projections, received, band, row_first[:, 0], interp_index, interp_frac),
        2 * part * length * sum(w[2] for w in work),
        scratch=scratch,
        name="other_columns",
        specs=[VMEM, VMEM, VMEM, SMEM, VMEM, VMEM],
    )

    def last_kernel(proj_ref, received_ref, taps_ref, *rest):
        *outs, band_ref, weighted_ref, halo_cols_ref = rest
        build_band(taps_ref, band_ref)
        filter_here(
            (proj_ref, received_ref, weighted_ref, halo_cols_ref),
            [(half, *chunks[-1], ref) for half, ref in enumerate(outs)],
            band_ref,
        )

    before = second_out[-2:]
    *last_out, before[0] = kernel_call(
        last_kernel,
        [bf16(part, widths[-1])] * 2,
        (projections, received, filter_taps.reshape(taps // TILE, TILE)),
        4 * part * length * widths[-1],
        scratch=[pltpu.VMEM((length, BLOCK), jnp.bfloat16)] + scratch,
        name="last_columns",
        carried=before[:1],
    )
    second_out = [*second_out[:-2], *before, *last_out]
    filtered = [(*first_out, *second_out[: 2 - early])]
    for at in range(2 - early, len(second_out), 2):
        filtered.append(second_out[at : at + 2])
        halo_rows.append(exchange(second_out[at : at + halos]))

    def project(index, after=()):
        width = widths[index]

        def body(own_ref, halo_ref, *rest):
            sources, outs = rest[: 2 + halos], rest[2 + halos + len(after) :]
            for c in range(0, width, BLOCK):
                cut = slice(c, c + BLOCK)
                own = jnp.concatenate([ref[:, cut] for ref in sources[:2]], axis=0)
                other = [ref[:, cut] for ref in sources[2:]]
                other = other[0] if len(other) == 1 else jnp.concatenate(other, axis=0)
                total = jnp.dot(own_ref[...], own, preferred_element_type=jnp.float32)
                total += jnp.dot(halo_ref[...], other, preferred_element_type=jnp.float32)
                total = total * scale
                at = 0
                for out in outs:
                    out[:, cut] = total[at : at + out.shape[0], :].astype(out.dtype)
                    at += out.shape[0]

        if quick:
            first = [bf16(shard, width)] * 2 if DIRECT[index] else [bf16(2 * shard, width)]
            shapes = [*first, bf16(shard, width), f32(shard, width)]
        else:
            shapes = [f32(depth, width)]
        return kernel_call(
            body,
            shapes,
            (own_weight, halo_weight, *filtered[index], *halo_rows[index], *after),
            2 * depth * (2 + halos) * part * width,
            name="interpolate",
            specs=[VMEM] * (4 + halos) + [HELD] * len(after),
        )

    def widen(x):
        return x.astype(jnp.float32)

    def at_end():
        angle = lax.axis_index("angle")
        return (angle == 0) | (angle == line - 1)

    neighbours = [(0, 1), (1, 0), (2, 3), (3, 2)]
    middles = [(1, 2), (2, 1), (0, 0), (3, 3)]
    second_hop = [(0, 1), (1, 3), (2, 0), (3, 2)]
    straight = [(0, 2), (3, 1), (1, 0), (2, 3)]

    def first_hops(*parts):
        if len(parts) == 1:
            return [lax.ppermute(parts[0], "angle", neighbours)]
        near, middle = parts
        two = lax.ppermute(middle, "angle", straight)
        three = lax.ppermute(middle, "angle", middles)
        one = lax.ppermute(near, "angle", neighbours)
        return [one, three, two]

    def relay(sent, own, far, kept, after=(), weight=1, soon=False):
        direct = len(sent) == 3
        arrived = sent[: 1 if soon else 2] if direct else [sent[0], own[0]]
        extra = len(arrived) - 1

        def body(one_ref, *rest):
            other_ref = rest[0]
            far_ref, kept_ref = rest[extra : extra + 2]
            outs = rest[extra + 2 + len(after) :]
            end = at_end()
            near = widen(one_ref[:shard, :])
            relayed = widen(far_ref[...]) + jnp.where(end, 0.0, near)
            outs[0][...] = relayed.astype(jnp.bfloat16)
            if soon:
                outs[1][...] = kept_ref[...] + jnp.where(end, near, 0.0)
            elif direct:
                outs[1][...] = kept_ref[...] + jnp.where(end, near, widen(other_ref[...]))
            else:
                outs[1][...] = kept_ref[...] + jnp.where(end, near, 0.0)
                crossed = widen(one_ref[shard:, :]) + widen(other_ref[shard:, :])
                outs[2][...] = crossed.astype(jnp.bfloat16)

        relayed, partial, *crossed = kernel_call(
            body,
            [bf16(*far.shape), f32(*kept.shape)] + [bf16(*far.shape)] * (not direct),
            (*arrived, far, kept, *after),
            far.size * 2 * weight,
            name="relay",
            specs=[VMEM] * (3 + extra) + [HELD] * len(after),
        )
        four = lax.ppermute(relayed, "angle", second_hop)
        three = sent[2] if direct else lax.ppermute(crossed[0], "angle", middles)
        return (partial, four, three, *([sent[1]] if soon else []))

    def total(partial_ref, four_ref, *fillers):
        direct = sum(widen(ref[...]) for ref in fillers)
        return partial_ref[...] + widen(four_ref[...]) + jnp.where(at_end(), 0.0, direct)

    def mark(array, weight):
        def body(array_ref, out_ref):
            out_ref[...] = jnp.zeros_like(out_ref)

        return kernel_call(body, [f32(8, TILE)], (array,), weight, name="mark", specs=[HELD])[0]

    def finish(pieces, weight=1, after=()):
        def body(*refs):
            refs[-1][...] = total(*refs[: len(pieces)])

        return kernel_call(
            body,
            [f32(*pieces[0].shape)],
            (*pieces, *after),
            pieces[0].size * 2 * weight,
            name="finish",
            specs=[VMEM] * len(pieces) + [HELD] * len(after),
        )[0]

    def store(done, pieces, index, volume=None, weight=1, after=()):
        given = [*done, *pieces]
        held = [*after, *([] if volume is None else [volume])]

        def body(*refs):
            ready, refs = refs[: len(done)], refs[len(done) :]
            volume_ref, total_ref, sem = refs[-3:]

            def copy(i, source):
                at = pl.ds(chunks[i][0], chunks[i][1])
                return pltpu.make_async_copy(source, volume_ref.at[:, at], sem.at[i])

            copies = [copy(i, ref) for i, ref in enumerate(ready)]
            for c in copies:
                c.start()
            total_ref[...] = total(*refs[: len(pieces)])
            copies.append(copy(index, total_ref))
            copies[-1].start()
            for c in copies:
                c.wait()

        size = shard * widths[index]
        return pl.pallas_call(
            body,
            out_shape=f32(shard, cols),
            in_specs=[VMEM] * len(given) + [HELD] * len(held),
            out_specs=HELD,
            input_output_aliases={} if volume is None else {len(given) + len(after): 0},
            scratch_shapes=[
                pltpu.VMEM((shard, widths[index]), jnp.float32),
                pltpu.SemaphoreType.DMA((len(chunks),)),
            ],
            compiler_params=pltpu.CompilerParams(vmem_limit_bytes=VMEM_BYTES),
            cost_estimate=pl.CostEstimate(
                flops=size * 2 * weight, bytes_accessed=size * 4, transcendentals=0
            ),
            name="store",
        )(*given, *held)

    if not quick:
        sums = [
            lax.psum_scatter(project(i)[0], "angle", scatter_dimension=0, tiled=True)
            for i in range(len(chunks))
        ]
        return jnp.concatenate([sums[i] for i in sorted(range(len(chunks)), key=chunks.__getitem__)], 1)

    last = len(chunks) - 1
    *own, far, kept = project(0)
    sent = first_hops(*own)
    done, pieces = [], []
    for j in range(last + 1):
        here = (sent, own, far, kept)
        after = sent[2:] if j == 0 else []
        if j < last:
            earlier = [p[0] for p in pieces[-1:]] if j else [last_out[-1]]
            *own, far, kept = project(j + 1, after=earlier)
            sent = first_hops(*own)
            after = [*after, kept]
            if j:
                done.append(finish(pieces[-1], weight=FINISH_WEIGHTS[j - 1], after=[kept]))
                after.append(done[-1])
        pieces.append(relay(*here, after=after, weight=WEIGHTS[j], soon=SOON[j]))
    swap = [mark(sent[1], MARK)] if SOON[last] else []
    volume = store(done, pieces[last - 1], last - 1, weight=FINISH_WEIGHTS[last - 1], after=swap)
    return store([], pieces[last], last, volume)


def solution(mesh):
    placed = (
        P(("group", "angle"), "slab", "col"),
        P(),
        P(("group", "angle"), "slab"),
        P(("group", "angle"), "slab", None),
        P(("group", "angle"), "slab", None),
    )
    return jax.shard_map(
        on_device,
        mesh=mesh,
        in_specs=placed,
        out_specs=P(("group", "slab", "angle"), "col"),
        check_vma=False,
    )
```

```python
import math

import jax
import jax.numpy as jnp
from jax import lax
from jax.experimental import pallas as pl
from jax.experimental.pallas import tpu as pltpu
from jax.sharding import PartitionSpec as P

BLOCK = 256
TILE = 128
STACK = 8
DIRECT = (False, False, False, True)
SOON = (False, False, False, True)
WEIGHTS = (40000, 28000, 1, 1)
FINISH_WEIGHTS = (1, 1, 10000)
MARK = 1000000000
VMEM_BYTES = 14 * 1024 * 1024
FIRST_VMEM_BYTES = 103 * 512 * 1024
LINE_ORDER = ((3, 2, 1, 0), (0, 2, 3, 1), (3, 1, 0, 2), (0, 1, 2, 3))

VMEM = pl.BlockSpec(memory_space=pltpu.VMEM)
HELD = pl.BlockSpec(memory_space=pltpu.HBM)
SMEM = pl.BlockSpec(memory_space=pltpu.SMEM)


def kernel_call(
    body, out_shape, args, flops, scratch=(), name=None, specs=None, grant=VMEM_BYTES, carried=()
):
    specs = specs or [VMEM] * len(args)
    moved = sum(a.size * a.dtype.itemsize for a in (*args, *out_shape))
    n_in, n_out, n_through = len(args), len(out_shape), len(carried)

    def kernel(*refs):
        ins, refs = refs[:n_in], refs[n_in + n_through :]
        body(*ins, *refs[:n_out], *refs[n_out + n_through :])

    return pl.pallas_call(
        kernel,
        out_shape=[*out_shape, *(jax.ShapeDtypeStruct(c.shape, c.dtype) for c in carried)],
        in_specs=[*specs, *([HELD] * n_through)],
        out_specs=[VMEM] * n_out + [HELD] * n_through,
        input_output_aliases={n_in + i: n_out + i for i in range(n_through)},
        scratch_shapes=list(scratch),
        compiler_params=pltpu.CompilerParams(vmem_limit_bytes=grant),
        cost_estimate=pl.CostEstimate(flops=flops, bytes_accessed=moved, transcendentals=0),
        name=name,
    )(*args, *carried)


def build_band(taps_ref, band_ref):
    count = taps_ref.shape[0]
    steps, tiles = band_ref.shape[1] // TILE, band_ref.shape[0] // TILE
    zero = jnp.zeros((TILE, TILE), jnp.float32)
    ahead = lax.broadcasted_iota(jnp.int32, (TILE, TILE), 1) >= lax.broadcasted_iota(
        jnp.int32, (TILE, TILE), 0
    )
    taps = taps_ref[...].astype(jnp.float32)

    def shifted(d):
        if not 0 <= d < count:
            return zero
        row = jnp.broadcast_to(taps[d : d + 1, :], (TILE, TILE))
        return pltpu.roll(row, 0, 1, stride=1, stride_axis=0)

    before = zero
    for d in range(-(steps - 1), tiles):
        here = shifted(d)
        block = jnp.where(ahead, here, before).T.astype(jnp.bfloat16)
        before = here
        for c in range(steps):
            if 0 <= d + c < tiles:
                band_ref[(d + c) * TILE : (d + c + 1) * TILE, c * TILE : (c + 1) * TILE] = block


def weigh(proj_ref, weighted_ref, half, row_at, row_start, col_start, sizes, c):
    angles = proj_ref.shape[0]
    total_rows, total_cols, count = sizes
    distance = jnp.float32(total_cols)
    v = lax.broadcasted_iota(jnp.int32, (count, 1), 0) + (row_start + row_at)
    v = v.astype(jnp.float32) - total_rows / 2 + 0.5
    u = lax.broadcasted_iota(jnp.int32, (1, BLOCK), 1) + (col_start + c)
    u = u.astype(jnp.float32) - total_cols / 2 + 0.5
    factor = distance / jnp.sqrt(distance * distance + u * u + v * v)
    for a in range(angles):
        raw = proj_ref[a, pl.ds(row_at, count), c : c + BLOCK].astype(jnp.float32)
        at = (half * angles + a) * count
        weighted_ref[at : at + count, c : c + BLOCK] = (raw * factor).astype(jnp.bfloat16)


def filter_columns(work, count, band_ref, weighted_at):
    length = band_ref.shape[0]
    reach = (length - BLOCK) // 2
    groups = []
    for half, first, width, out_ref in work:
        starts = range(first, first + width, BLOCK)
        for at in range(0, len(starts), STACK):
            groups.append((half, starts[at : at + STACK], out_ref, at))

    def touch(index):
        if index < len(groups):
            half, starts, _, _ = groups[index]
            for c in range(starts[0] - reach, starts[-1] + BLOCK + reach, BLOCK):
                weighted_at(half, c)

    touch(0)
    for index, (half, starts, out_ref, at) in enumerate(groups):
        touch(index + 1)
        tall = jnp.concatenate(
            [
                jnp.concatenate(
                    [weighted_at(half, c)() for c in range(s - reach, s + BLOCK + reach, BLOCK)],
                    axis=1,
                )
                for s in starts
            ],
            axis=0,
        )
        result = jnp.dot(tall, band_ref[...], preferred_element_type=jnp.float32)
        result = result.astype(jnp.bfloat16)
        for k in range(len(starts)):
            out_ref[:, (at + k) * BLOCK : (at + k + 1) * BLOCK] = result[
                k * count : (k + 1) * count, :
            ]


def bf16(*shape):
    return jax.ShapeDtypeStruct(shape, jnp.bfloat16)


def f32(*shape):
    return jax.ShapeDtypeStruct(shape, jnp.float32)


def chunk_plan(cols, reach):
    assert cols >= 4 * reach and reach % (4 * BLOCK) == 0
    first, second = reach + BLOCK, 2 * reach
    third = second + (cols - 2 * reach) * 3 // 8
    return [(first, second - first), (second, third - second), (third, cols - third), (0, first)]


def on_device(projections, filter_taps, row_first, interp_index, interp_frac):
    angles, rows, cols = projections.shape
    depth = interp_index.shape[2]
    taps = filter_taps.shape[0]
    reach = taps // 2
    length = taps + BLOCK
    margin = rows // 2
    slabs, line, sides = (lax.axis_size(n) for n in ("slab", "angle", "col"))
    scale = math.pi / (angles * line)
    both = slabs == 2
    halos = 1 if both else 2
    quick = line == 4
    shard = depth // line
    order = LINE_ORDER if quick else (tuple(range(line)),) * line
    total_rows, total_cols = rows * slabs, cols * sides
    chunks = chunk_plan(cols, reach)
    widths = [w for _, w in chunks]
    part = angles * margin
    sizes = (total_rows, total_cols, margin)

    def half_rows(slab):
        if both:
            return jnp.where(slab == 0, margin, 0), jnp.where(slab == 0, 0, margin)
        return margin, 0

    def aligned(row):
        return row if isinstance(row, int) else pl.multiple_of(row, margin)

    start, width = chunks[0]
    window_at, window = start - reach, width + 2 * reach
    early = halos

    def first_kernel(proj_ref, taps_ref, band_ref, edge_ref, *rest):
        outs, (raw_ref, weighted_ref, sem) = rest[:-3], rest[-3:]
        slab = lax.axis_index("slab")
        col = lax.axis_index("col")
        starts = [aligned(r) for r in half_rows(slab)][:early]
        copies = [
            pltpu.make_async_copy(
                proj_ref.at[a, pl.ds(r, margin), pl.ds(window_at, window)],
                raw_ref.at[a, pl.ds(r, margin), :],
                sem.at[a * 2 + h],
            )
            for a in range(angles)
            for h, r in enumerate(starts)
        ]
        edge_col = pl.multiple_of(jnp.where(col == 0, cols - reach, 0), TILE)
        edge_copy = pltpu.make_async_copy(
            proj_ref.at[:, :, pl.ds(edge_col, reach)], edge_ref, sem.at[2 * angles]
        )
        for copy in copies:
            copy.start()
        edge_copy.start()
        build_band(taps_ref, band_ref)
        for copy in copies:
            copy.wait()
        known = set()

        def weighted_at(half, c):
            c -= window_at
            if (half, c) not in known:
                known.add((half, c))
                weigh(
                    raw_ref, weighted_ref, half, starts[half], slab * rows,
                    col * cols + window_at, sizes, c,
                )
            return lambda: weighted_ref[half * part : (half + 1) * part, c : c + BLOCK]

        work = [(h, start, width, out_ref) for h, out_ref in enumerate(outs)]
        filter_columns(work, part, band_ref, weighted_at)
        edge_copy.wait()

    band, edge, *first_out = kernel_call(
        first_kernel,
        [bf16(length, BLOCK), bf16(angles, rows, reach)] + [bf16(part, width)] * early,
        (projections, filter_taps.reshape(taps // TILE, TILE)),
        2 * early * part * length * width,
        scratch=[
            pltpu.VMEM((angles, rows, window), jnp.bfloat16),
            pltpu.VMEM((early * part, window), jnp.bfloat16),
            pltpu.SemaphoreType.DMA((2 * angles + 1,)),
        ],
        name="first_columns",
        specs=[HELD, VMEM],
        grant=FIRST_VMEM_BYTES,
    )

    up = [(i, (i + 1) % slabs) for i in range(slabs - 1)]
    down = [(j, i) for i, j in up]

    def exchange(sends):
        if both:
            return [lax.ppermute(sends[0], "slab", up + down)]
        return [lax.ppermute(sends[0], "slab", up), lax.ppermute(sends[1], "slab", down)]

    assert sides == 2
    received = lax.ppermute(edge, "col", [(0, 1), (1, 0)])
    halo_rows = [exchange(first_out)]

    def write_weights(first_ref, index_ref, frac_ref, own_ref, halo_ref):
        slab = lax.axis_index("slab")
        angle = lax.axis_index("angle")
        if both:
            bases = [jnp.where(slab == 0, rows, rows - margin)]
        else:
            bases = [slab * rows - margin, (slab + 1) * rows]

        def weights(a, base):
            slot = lax.broadcasted_iota(jnp.int32, (margin, depth), 0) + base
            position = index_ref[a] + first_ref[a]
            frac = frac_ref[a]
            high = frac.astype(jnp.bfloat16).astype(jnp.float32)
            low = (1.0 - frac).astype(jnp.bfloat16).astype(jnp.float32)
            return jnp.where(slot == position, low, 0.0) + jnp.where(slot == position + 1, high, 0.0)

        here = [slab * rows + r for r in half_rows(slab)]
        for starts, ref in ((here, own_ref), (bases, halo_ref)):
            table = jnp.concatenate([weights(a, b) for b in starts for a in range(angles)], axis=0)
            turned = table.T.astype(jnp.bfloat16)
            for s in range(line):
                if quick:
                    places = [o.index(s) for o in order]
                    place = places[line - 1]
                    for i in range(line - 1):
                        place = jnp.where(angle == i, places[i], place)
                    at = pl.multiple_of(place * shard, shard)
                else:
                    at = s * shard
                ref[pl.ds(at, shard), :] = turned[s * shard : (s + 1) * shard, :]

    def filter_here(refs, work, band_ref):
        proj_ref, received_ref, weighted_ref, halo_cols_ref = refs
        slab = lax.axis_index("slab")
        col = lax.axis_index("col")
        starts = [aligned(r) for r in half_rows(slab)]
        lower = col == 0
        from_col = jnp.where(lower, cols, col * cols - reach)
        none = jnp.zeros((part, BLOCK), jnp.bfloat16)
        known = set()

        def weighted_at(half, c):
            inside = 0 <= c < cols
            source, into = (proj_ref, weighted_ref) if inside else (received_ref, halo_cols_ref)
            first_col = col * cols if inside else from_col
            at = c if inside else c % reach
            if (half, at, inside) not in known:
                known.add((half, at, inside))
                weigh(source, into, half, starts[half], slab * rows, first_col, sizes, at)

            def load():
                block = into[half * part : (half + 1) * part, at : at + BLOCK]
                if c < 0:
                    block = jnp.where(lower, none, block)
                elif c >= cols:
                    block = jnp.where(lower, block, none)
                return block

            return load

        filter_columns(work, part, band_ref, weighted_at)

    scratch = [pltpu.VMEM((2 * part, n), jnp.bfloat16) for n in (cols, reach)]

    work = [(1, *chunks[0])][: 2 - early]
    work += [(half, *chunk) for chunk in chunks[1:-1] for half in (0, 1)]

    def second_kernel(proj_ref, received_ref, band_ref, first_ref, index_ref, frac_ref,
                      own_ref, halo_ref, *rest):
        outs = [(*w, ref) for w, ref in zip(work, rest)]
        filter_here((proj_ref, received_ref, *rest[-2:]), outs, band_ref)
        write_weights(first_ref, index_ref, frac_ref, own_ref, halo_ref)

    own_weight, halo_weight, *second_out = kernel_call(
        second_kernel,
        [bf16(depth, 2 * part), bf16(depth, halos * part)] + [bf16(part, w[2]) for w in work],
        (projections, received, band, row_first[:, 0], interp_index, interp_frac),
        2 * part * length * sum(w[2] for w in work),
        scratch=scratch,
        name="other_columns",
        specs=[VMEM, VMEM, VMEM, SMEM, VMEM, VMEM],
    )

    def last_kernel(proj_ref, received_ref, taps_ref, *rest):
        *outs, band_ref, weighted_ref, halo_cols_ref = rest
        build_band(taps_ref, band_ref)
        filter_here(
            (proj_ref, received_ref, weighted_ref, halo_cols_ref),
            [(half, *chunks[-1], ref) for half, ref in enumerate(outs)],
            band_ref,
        )

    before = second_out[-2:]
    *last_out, before[0] = kernel_call(
        last_kernel,
        [bf16(part, widths[-1])] * 2,
        (projections, received, filter_taps.reshape(taps // TILE, TILE)),
        4 * part * length * widths[-1],
        scratch=[pltpu.VMEM((length, BLOCK), jnp.bfloat16)] + scratch,
        name="last_columns",
        carried=before[:1],
    )
    second_out = [*second_out[:-2], *before, *last_out]
    filtered = [(*first_out, *second_out[: 2 - early])]
    for at in range(2 - early, len(second_out), 2):
        filtered.append(second_out[at : at + 2])
        halo_rows.append(exchange(second_out[at : at + halos]))

    def project(index, after=()):
        width = widths[index]

        def body(own_ref, halo_ref, *rest):
            sources, outs = rest[: 2 + halos], rest[2 + halos + len(after) :]
            for c in range(0, width, BLOCK):
                cut = slice(c, c + BLOCK)
                own = jnp.concatenate([ref[:, cut] for ref in sources[:2]], axis=0)
                other = [ref[:, cut] for ref in sources[2:]]
                other = other[0] if len(other) == 1 else jnp.concatenate(other, axis=0)
                total = jnp.dot(own_ref[...], own, preferred_element_type=jnp.float32)
                total += jnp.dot(halo_ref[...], other, preferred_element_type=jnp.float32)
                total = total * scale
                at = 0
                for i, out in enumerate(outs):
                    if len(outs) == 5 and i == 2:
                        at -= out.shape[0]
                    out[:, cut] = total[at : at + out.shape[0], :].astype(out.dtype)
                    at += out.shape[0]

        if quick:
            first = [bf16(shard, width)] * 2 if DIRECT[index] else [bf16(2 * shard, width)]
            again = [bf16(shard, width)] * SOON[index]
            shapes = [*first, *again, bf16(shard, width), f32(shard, width)]
        else:
            shapes = [f32(depth, width)]
        return kernel_call(
            body,
            shapes,
            (own_weight, halo_weight, *filtered[index], *halo_rows[index], *after),
            2 * depth * (2 + halos) * part * width,
            name="interpolate",
            specs=[VMEM] * (4 + halos) + [HELD] * len(after),
        )

    def widen(x):
        return x.astype(jnp.float32)

    def at_end():
        angle = lax.axis_index("angle")
        return (angle == 0) | (angle == line - 1)

    neighbours = [(0, 1), (1, 0), (2, 3), (3, 2)]
    middles = [(1, 2), (2, 1), (0, 0), (3, 3)]
    second_hop = [(0, 1), (1, 3), (2, 0), (3, 2)]
    straight = [(0, 2), (3, 1), (1, 0), (2, 3)]

    def first_hops(*parts):
        if len(parts) == 1:
            return [lax.ppermute(parts[0], "angle", neighbours)]
        near, middle, *later = parts
        two = [] if later else [lax.ppermute(middle, "angle", straight)]
        three = lax.ppermute(middle, "angle", middles)
        one = lax.ppermute(near, "angle", neighbours)
        return [one, three, *two]

    def relay(sent, own, far, kept, after=(), weight=1, soon=False):
        direct = len(sent) > 1
        arrived = sent[: 1 if soon else 2] if direct else [sent[0], own[0]]
        later = own[2:]
        extra = len(arrived) - 1

        def body(one_ref, *rest):
            other_ref = rest[0]
            far_ref, kept_ref = rest[extra : extra + 2]
            outs = rest[extra + 2 + len(after) :]
            end = at_end()
            near = widen(one_ref[:shard, :])
            relayed = widen(far_ref[...]) + jnp.where(end, 0.0, near)
            outs[0][...] = relayed.astype(jnp.bfloat16)
            if soon:
                outs[1][...] = kept_ref[...] + jnp.where(end, near, 0.0)
            elif direct:
                outs[1][...] = kept_ref[...] + jnp.where(end, near, widen(other_ref[...]))
            else:
                outs[1][...] = kept_ref[...] + jnp.where(end, near, 0.0)
                crossed = widen(one_ref[shard:, :]) + widen(other_ref[shard:, :])
                outs[2][...] = crossed.astype(jnp.bfloat16)

        relayed, partial, *others = kernel_call(
            body,
            [bf16(*far.shape), f32(*kept.shape)] + [bf16(*far.shape)] * (not direct),
            (*arrived, far, kept, *after),
            far.size * 2 * weight,
            name="relay",
            specs=[VMEM] * (3 + extra) + [HELD] * len(after),
            carried=later,
        )
        four = lax.ppermute(relayed, "angle", second_hop)
        if not direct:
            return partial, four, lax.ppermute(others[0], "angle", middles)
        two = lax.ppermute(others[0], "angle", straight) if later else sent[2]
        return (partial, four, two, *([sent[1]] if soon else []))

    def total(partial_ref, four_ref, *fillers):
        direct = sum(widen(ref[...]) for ref in fillers)
        return partial_ref[...] + widen(four_ref[...]) + jnp.where(at_end(), 0.0, direct)

    def mark(array, weight):
        def body(array_ref, out_ref):
            out_ref[...] = jnp.zeros_like(out_ref)

        return kernel_call(body, [f32(8, TILE)], (array,), weight, name="mark", specs=[HELD])[0]

    def finish(pieces, weight=1, after=()):
        def body(*refs):
            refs[-1][...] = total(*refs[: len(pieces)])

        return kernel_call(
            body,
            [f32(*pieces[0].shape)],
            (*pieces, *after),
            pieces[0].size * 2 * weight,
            name="finish",
            specs=[VMEM] * len(pieces) + [HELD] * len(after),
        )[0]

    def store(done, pieces, index, volume=None, weight=1, after=()):
        given = [*done, *pieces]
        held = [*after, *([] if volume is None else [volume])]

        def body(*refs):
            ready, refs = refs[: len(done)], refs[len(done) :]
            volume_ref, total_ref, sem = refs[-3:]

            def copy(i, source):
                at = pl.ds(chunks[i][0], chunks[i][1])
                return pltpu.make_async_copy(source, volume_ref.at[:, at], sem.at[i])

            copies = [copy(i, ref) for i, ref in enumerate(ready)]
            for c in copies:
                c.start()
            total_ref[...] = total(*refs[: len(pieces)])
            copies.append(copy(index, total_ref))
            copies[-1].start()
            for c in copies:
                c.wait()

        size = shard * widths[index]
        return pl.pallas_call(
            body,
            out_shape=f32(shard, cols),
            in_specs=[VMEM] * len(given) + [HELD] * len(held),
            out_specs=HELD,
            input_output_aliases={} if volume is None else {len(given) + len(after): 0},
            scratch_shapes=[
                pltpu.VMEM((shard, widths[index]), jnp.float32),
                pltpu.SemaphoreType.DMA((len(chunks),)),
            ],
            compiler_params=pltpu.CompilerParams(vmem_limit_bytes=VMEM_BYTES),
            cost_estimate=pl.CostEstimate(
                flops=size * 2 * weight, bytes_accessed=size * 4, transcendentals=0
            ),
            name="store",
        )(*given, *held)

    if not quick:
        sums = [
            lax.psum_scatter(project(i)[0], "angle", scatter_dimension=0, tiled=True)
            for i in range(len(chunks))
        ]
        return jnp.concatenate([sums[i] for i in sorted(range(len(chunks)), key=chunks.__getitem__)], 1)

    last = len(chunks) - 1
    *own, far, kept = project(0)
    sent = first_hops(*own)
    done, pieces = [], []
    for j in range(last + 1):
        here = (sent, own, far, kept)
        after = sent[2:] if j == 0 else []
        if j < last:
            earlier = [p[0] for p in pieces[-1:]] if j else [last_out[-1]]
            *own, far, kept = project(j + 1, after=earlier)
            sent = first_hops(*own)
            after = [*after, kept]
            if j:
                done.append(finish(pieces[-1], weight=FINISH_WEIGHTS[j - 1], after=[kept]))
                after.append(done[-1])
        pieces.append(relay(*here, after=after, weight=WEIGHTS[j], soon=SOON[j]))
    swap = [mark(sent[1], MARK)] if SOON[last] else []
    volume = store(done, pieces[last - 1], last - 1, weight=FINISH_WEIGHTS[last - 1], after=swap)
    return store([], pieces[last], last, volume)


def solution(mesh):
    placed = (
        P(("group", "angle"), "slab", "col"),
        P(),
        P(("group", "angle"), "slab"),
        P(("group", "angle"), "slab", None),
        P(("group", "angle"), "slab", None),
    )
    return jax.shard_map(
        on_device,
        mesh=mesh,
        in_specs=placed,
        out_specs=P(("group", "slab", "angle"), "col"),
        check_vma=False,
    )
```

```python
import math

import jax
import jax.numpy as jnp
from jax import lax
from jax.experimental import pallas as pl
from jax.experimental.pallas import tpu as pltpu
from jax.sharding import PartitionSpec as P

BLOCK = 256
TILE = 128
STACK = 8
DIRECT = (False, False, False, True)
SOON = (False, False, False, True)
WEIGHTS = (40000, 28000, 1, 1)
FINISH_WEIGHTS = (1, 1, 10000)
MARK = 1000000000
VMEM_BYTES = 14 * 1024 * 1024
FIRST_VMEM_BYTES = 104 * 512 * 1024
LINE_ORDER = ((3, 2, 1, 0), (0, 2, 3, 1), (3, 1, 0, 2), (0, 1, 2, 3))

VMEM = pl.BlockSpec(memory_space=pltpu.VMEM)
HELD = pl.BlockSpec(memory_space=pltpu.HBM)
SMEM = pl.BlockSpec(memory_space=pltpu.SMEM)


def kernel_call(
    body, out_shape, args, flops, scratch=(), name=None, specs=None, grant=VMEM_BYTES, carried=()
):
    specs = specs or [VMEM] * len(args)
    moved = sum(a.size * a.dtype.itemsize for a in (*args, *out_shape))
    n_in, n_out, n_through = len(args), len(out_shape), len(carried)

    def kernel(*refs):
        ins, refs = refs[:n_in], refs[n_in + n_through :]
        body(*ins, *refs[:n_out], *refs[n_out + n_through :])

    return pl.pallas_call(
        kernel,
        out_shape=[*out_shape, *(jax.ShapeDtypeStruct(c.shape, c.dtype) for c in carried)],
        in_specs=[*specs, *([HELD] * n_through)],
        out_specs=[VMEM] * n_out + [HELD] * n_through,
        input_output_aliases={n_in + i: n_out + i for i in range(n_through)},
        scratch_shapes=list(scratch),
        compiler_params=pltpu.CompilerParams(vmem_limit_bytes=grant),
        cost_estimate=pl.CostEstimate(flops=flops, bytes_accessed=moved, transcendentals=0),
        name=name,
    )(*args, *carried)


def build_band(taps_ref, band_ref):
    count = taps_ref.shape[0]
    steps, tiles = band_ref.shape[1] // TILE, band_ref.shape[0] // TILE
    zero = jnp.zeros((TILE, TILE), jnp.float32)
    ahead = lax.broadcasted_iota(jnp.int32, (TILE, TILE), 1) >= lax.broadcasted_iota(
        jnp.int32, (TILE, TILE), 0
    )
    taps = taps_ref[...].astype(jnp.float32)

    def shifted(d):
        if not 0 <= d < count:
            return zero
        row = jnp.broadcast_to(taps[d : d + 1, :], (TILE, TILE))
        return pltpu.roll(row, 0, 1, stride=1, stride_axis=0)

    before = zero
    for d in range(-(steps - 1), tiles):
        here = shifted(d)
        block = jnp.where(ahead, here, before).T.astype(jnp.bfloat16)
        before = here
        for c in range(steps):
            if 0 <= d + c < tiles:
                band_ref[(d + c) * TILE : (d + c + 1) * TILE, c * TILE : (c + 1) * TILE] = block


def weigh(proj_ref, weighted_ref, half, row_at, row_start, col_start, sizes, c):
    angles = proj_ref.shape[0]
    total_rows, total_cols, count = sizes
    distance = jnp.float32(total_cols)
    v = lax.broadcasted_iota(jnp.int32, (count, 1), 0) + (row_start + row_at)
    v = v.astype(jnp.float32) - total_rows / 2 + 0.5
    u = lax.broadcasted_iota(jnp.int32, (1, BLOCK), 1) + (col_start + c)
    u = u.astype(jnp.float32) - total_cols / 2 + 0.5
    factor = distance / jnp.sqrt(distance * distance + u * u + v * v)
    for a in range(angles):
        raw = proj_ref[a, pl.ds(row_at, count), c : c + BLOCK].astype(jnp.float32)
        at = (half * angles + a) * count
        weighted_ref[at : at + count, c : c + BLOCK] = (raw * factor).astype(jnp.bfloat16)


def filter_columns(work, count, band_ref, weighted_at):
    length = band_ref.shape[0]
    reach = (length - BLOCK) // 2
    groups = []
    for half, first, width, out_ref in work:
        starts = range(first, first + width, BLOCK)
        for at in range(0, len(starts), STACK):
            groups.append((half, starts[at : at + STACK], out_ref, at))

    def touch(index):
        if index < len(groups):
            half, starts, _, _ = groups[index]
            for c in range(starts[0] - reach, starts[-1] + BLOCK + reach, BLOCK):
                weighted_at(half, c)

    touch(0)
    for index, (half, starts, out_ref, at) in enumerate(groups):
        touch(index + 1)
        tall = jnp.concatenate(
            [
                jnp.concatenate(
                    [weighted_at(half, c)() for c in range(s - reach, s + BLOCK + reach, BLOCK)],
                    axis=1,
                )
                for s in starts
            ],
            axis=0,
        )
        result = jnp.dot(tall, band_ref[...], preferred_element_type=jnp.float32)
        result = result.astype(jnp.bfloat16)
        for k in range(len(starts)):
            out_ref[:, (at + k) * BLOCK : (at + k + 1) * BLOCK] = result[
                k * count : (k + 1) * count, :
            ]


def bf16(*shape):
    return jax.ShapeDtypeStruct(shape, jnp.bfloat16)


def f32(*shape):
    return jax.ShapeDtypeStruct(shape, jnp.float32)


def chunk_plan(cols, reach):
    assert cols >= 4 * reach and reach % (4 * BLOCK) == 0
    first, second = reach + BLOCK, 2 * reach
    third = second + (cols - 2 * reach) * 3 // 8
    return [(first, second - first), (second, third - second), (third, cols - third), (0, first)]


def on_device(projections, filter_taps, row_first, interp_index, interp_frac):
    angles, rows, cols = projections.shape
    depth = interp_index.shape[2]
    taps = filter_taps.shape[0]
    reach = taps // 2
    length = taps + BLOCK
    margin = rows // 2
    slabs, line, sides = (lax.axis_size(n) for n in ("slab", "angle", "col"))
    scale = math.pi / (angles * line)
    both = slabs == 2
    halos = 1 if both else 2
    quick = line == 4
    shard = depth // line
    order = LINE_ORDER if quick else (tuple(range(line)),) * line
    total_rows, total_cols = rows * slabs, cols * sides
    chunks = chunk_plan(cols, reach)
    widths = [w for _, w in chunks]
    part = angles * margin
    sizes = (total_rows, total_cols, margin)

    def half_rows(slab):
        if both:
            return jnp.where(slab == 0, margin, 0), jnp.where(slab == 0, 0, margin)
        return margin, 0

    def aligned(row):
        return row if isinstance(row, int) else pl.multiple_of(row, margin)

    start, width = chunks[0]
    window_at, window = start - reach, width + 2 * reach
    early = halos

    def window_kernel(proj_ref, weighted_ref, edge_ref, raw_ref, sem):
        slab = lax.axis_index("slab")
        col = lax.axis_index("col")
        starts = [aligned(r) for r in half_rows(slab)][:early]
        copies = [
            pltpu.make_async_copy(
                proj_ref.at[a, pl.ds(r, margin), pl.ds(window_at, window)],
                raw_ref.at[a, pl.ds(r, margin), :],
                sem.at[a * 2 + h],
            )
            for a in range(angles)
            for h, r in enumerate(starts)
        ]
        edge_col = pl.multiple_of(jnp.where(col == 0, cols - reach, 0), TILE)
        edge_copy = pltpu.make_async_copy(
            proj_ref.at[:, :, pl.ds(edge_col, reach)], edge_ref, sem.at[2 * angles]
        )
        for copy in copies:
            copy.start()
        edge_copy.start()
        for copy in copies:
            copy.wait()
        for half, r in enumerate(starts):
            for c in range(0, window, BLOCK):
                weigh(
                    raw_ref, weighted_ref, half, r, slab * rows, col * cols + window_at, sizes, c
                )
        edge_copy.wait()

    ahead, edge = kernel_call(
        window_kernel,
        [bf16(early * part, window), bf16(angles, rows, reach)],
        (projections,),
        early * part * window * 4,
        scratch=[
            pltpu.VMEM((angles, rows, window), jnp.bfloat16),
            pltpu.SemaphoreType.DMA((2 * angles + 1,)),
        ],
        name="first_window",
        specs=[HELD],
        grant=FIRST_VMEM_BYTES,
    )

    def first_kernel(weighted_ref, taps_ref, band_ref, *outs):
        build_band(taps_ref, band_ref)

        def weighted_at(half, c):
            at = c - window_at
            return lambda: weighted_ref[half * part : (half + 1) * part, at : at + BLOCK]

        work = [(h, start, width, out_ref) for h, out_ref in enumerate(outs)]
        filter_columns(work, part, band_ref, weighted_at)

    band, *first_out = kernel_call(
        first_kernel,
        [bf16(length, BLOCK)] + [bf16(part, width)] * early,
        (ahead, filter_taps.reshape(taps // TILE, TILE)),
        2 * early * part * length * width,
        name="first_columns",
    )

    up = [(i, (i + 1) % slabs) for i in range(slabs - 1)]
    down = [(j, i) for i, j in up]

    def exchange(sends):
        if both:
            return [lax.ppermute(sends[0], "slab", up + down)]
        return [lax.ppermute(sends[0], "slab", up), lax.ppermute(sends[1], "slab", down)]

    assert sides == 2
    received = lax.ppermute(edge, "col", [(0, 1), (1, 0)])
    halo_rows = [exchange(first_out)]

    def write_weights(first_ref, index_ref, frac_ref, own_ref, halo_ref):
        slab = lax.axis_index("slab")
        angle = lax.axis_index("angle")
        if both:
            bases = [jnp.where(slab == 0, rows, rows - margin)]
        else:
            bases = [slab * rows - margin, (slab + 1) * rows]

        def weights(a, base):
            slot = lax.broadcasted_iota(jnp.int32, (margin, depth), 0) + base
            position = index_ref[a] + first_ref[a]
            frac = frac_ref[a]
            high = frac.astype(jnp.bfloat16).astype(jnp.float32)
            low = (1.0 - frac).astype(jnp.bfloat16).astype(jnp.float32)
            return jnp.where(slot == position, low, 0.0) + jnp.where(slot == position + 1, high, 0.0)

        here = [slab * rows + r for r in half_rows(slab)]
        for starts, ref in ((here, own_ref), (bases, halo_ref)):
            table = jnp.concatenate([weights(a, b) for b in starts for a in range(angles)], axis=0)
            turned = table.T.astype(jnp.bfloat16)
            for s in range(line):
                if quick:
                    places = [o.index(s) for o in order]
                    place = places[line - 1]
                    for i in range(line - 1):
                        place = jnp.where(angle == i, places[i], place)
                    at = pl.multiple_of(place * shard, shard)
                else:
                    at = s * shard
                ref[pl.ds(at, shard), :] = turned[s * shard : (s + 1) * shard, :]

    def filter_here(refs, work, band_ref):
        proj_ref, received_ref, weighted_ref, halo_cols_ref = refs
        slab = lax.axis_index("slab")
        col = lax.axis_index("col")
        starts = [aligned(r) for r in half_rows(slab)]
        lower = col == 0
        from_col = jnp.where(lower, cols, col * cols - reach)
        none = jnp.zeros((part, BLOCK), jnp.bfloat16)
        known = set()

        def weighted_at(half, c):
            inside = 0 <= c < cols
            source, into = (proj_ref, weighted_ref) if inside else (received_ref, halo_cols_ref)
            first_col = col * cols if inside else from_col
            at = c if inside else c % reach
            if (half, at, inside) not in known:
                known.add((half, at, inside))
                weigh(source, into, half, starts[half], slab * rows, first_col, sizes, at)

            def load():
                block = into[half * part : (half + 1) * part, at : at + BLOCK]
                if c < 0:
                    block = jnp.where(lower, none, block)
                elif c >= cols:
                    block = jnp.where(lower, block, none)
                return block

            return load

        filter_columns(work, part, band_ref, weighted_at)

    scratch = [pltpu.VMEM((2 * part, n), jnp.bfloat16) for n in (cols, reach)]

    work = [(1, *chunks[0])][: 2 - early]
    work += [(half, *chunk) for chunk in chunks[1:-1] for half in (0, 1)]

    def second_kernel(proj_ref, received_ref, band_ref, first_ref, index_ref, frac_ref,
                      own_ref, halo_ref, *rest):
        outs = [(*w, ref) for w, ref in zip(work, rest)]
        filter_here((proj_ref, received_ref, *rest[-2:]), outs, band_ref)
        write_weights(first_ref, index_ref, frac_ref, own_ref, halo_ref)

    own_weight, halo_weight, *second_out = kernel_call(
        second_kernel,
        [bf16(depth, 2 * part), bf16(depth, halos * part)] + [bf16(part, w[2]) for w in work],
        (projections, received, band, row_first[:, 0], interp_index, interp_frac),
        2 * part * length * sum(w[2] for w in work),
        scratch=scratch,
        name="other_columns",
        specs=[VMEM, VMEM, VMEM, SMEM, VMEM, VMEM],
    )

    def last_kernel(proj_ref, received_ref, taps_ref, *rest):
        *outs, band_ref, weighted_ref, halo_cols_ref = rest
        build_band(taps_ref, band_ref)
        filter_here(
            (proj_ref, received_ref, weighted_ref, halo_cols_ref),
            [(half, *chunks[-1], ref) for half, ref in enumerate(outs)],
            band_ref,
        )

    before = second_out[-2:]
    *last_out, before[0] = kernel_call(
        last_kernel,
        [bf16(part, widths[-1])] * 2,
        (projections, received, filter_taps.reshape(taps // TILE, TILE)),
        4 * part * length * widths[-1],
        scratch=[pltpu.VMEM((length, BLOCK), jnp.bfloat16)] + scratch,
        name="last_columns",
        carried=before[:1],
    )
    second_out = [*second_out[:-2], *before, *last_out]
    filtered = [(*first_out, *second_out[: 2 - early])]
    for at in range(2 - early, len(second_out), 2):
        filtered.append(second_out[at : at + 2])
        halo_rows.append(exchange(second_out[at : at + halos]))

    def project(index, after=()):
        width = widths[index]

        def body(own_ref, halo_ref, *rest):
            sources, outs = rest[: 2 + halos], rest[2 + halos + len(after) :]
            for c in range(0, width, BLOCK):
                cut = slice(c, c + BLOCK)
                own = jnp.concatenate([ref[:, cut] for ref in sources[:2]], axis=0)
                other = [ref[:, cut] for ref in sources[2:]]
                other = other[0] if len(other) == 1 else jnp.concatenate(other, axis=0)
                total = jnp.dot(own_ref[...], own, preferred_element_type=jnp.float32)
                total += jnp.dot(halo_ref[...], other, preferred_element_type=jnp.float32)
                total = total * scale
                at = 0
                for out in outs:
                    out[:, cut] = total[at : at + out.shape[0], :].astype(out.dtype)
                    at += out.shape[0]

        if quick:
            first = [bf16(shard, width)] * 2 if DIRECT[index] else [bf16(2 * shard, width)]
            shapes = [*first, bf16(shard, width), f32(shard, width)]
        else:
            shapes = [f32(depth, width)]
        return kernel_call(
            body,
            shapes,
            (own_weight, halo_weight, *filtered[index], *halo_rows[index], *after),
            2 * depth * (2 + halos) * part * width,
            name="interpolate",
            specs=[VMEM] * (4 + halos) + [HELD] * len(after),
        )

    def widen(x):
        return x.astype(jnp.float32)

    def at_end():
        angle = lax.axis_index("angle")
        return (angle == 0) | (angle == line - 1)

    neighbours = [(0, 1), (1, 0), (2, 3), (3, 2)]
    middles = [(1, 2), (2, 1), (0, 0), (3, 3)]
    second_hop = [(0, 1), (1, 3), (2, 0), (3, 2)]
    straight = [(0, 2), (3, 1), (1, 0), (2, 3)]

    def first_hops(*parts):
        if len(parts) == 1:
            return [lax.ppermute(parts[0], "angle", neighbours)]
        near, middle = parts
        two = lax.ppermute(middle, "angle", straight)
        three = lax.ppermute(middle, "angle", middles)
        one = lax.ppermute(near, "angle", neighbours)
        return [one, three, two]

    def relay(sent, own, far, kept, after=(), weight=1, soon=False):
        direct = len(sent) == 3
        arrived = sent[: 1 if soon else 2] if direct else [sent[0], own[0]]
        extra = len(arrived) - 1

        def body(one_ref, *rest):
            other_ref = rest[0]
            far_ref, kept_ref = rest[extra : extra + 2]
            outs = rest[extra + 2 + len(after) :]
            end = at_end()
            near = widen(one_ref[:shard, :])
            relayed = widen(far_ref[...]) + jnp.where(end, 0.0, near)
            outs[0][...] = relayed.astype(jnp.bfloat16)
            if soon:
                outs[1][...] = kept_ref[...] + jnp.where(end, near, 0.0)
            elif direct:
                outs[1][...] = kept_ref[...] + jnp.where(end, near, widen(other_ref[...]))
            else:
                outs[1][...] = kept_ref[...] + jnp.where(end, near, 0.0)
                crossed = widen(one_ref[shard:, :]) + widen(other_ref[shard:, :])
                outs[2][...] = crossed.astype(jnp.bfloat16)

        relayed, partial, *crossed = kernel_call(
            body,
            [bf16(*far.shape), f32(*kept.shape)] + [bf16(*far.shape)] * (not direct),
            (*arrived, far, kept, *after),
            far.size * 2 * weight,
            name="relay",
            specs=[VMEM] * (3 + extra) + [HELD] * len(after),
        )
        four = lax.ppermute(relayed, "angle", second_hop)
        three = sent[2] if direct else lax.ppermute(crossed[0], "angle", middles)
        return (partial, four, three, *([sent[1]] if soon else []))

    def total(partial_ref, four_ref, *fillers):
        direct = sum(widen(ref[...]) for ref in fillers)
        return partial_ref[...] + widen(four_ref[...]) + jnp.where(at_end(), 0.0, direct)

    def mark(array, weight):
        def body(array_ref, out_ref):
            out_ref[...] = jnp.zeros_like(out_ref)

        return kernel_call(body, [f32(8, TILE)], (array,), weight, name="mark", specs=[HELD])[0]

    def finish(pieces, weight=1, after=()):
        def body(*refs):
            refs[-1][...] = total(*refs[: len(pieces)])

        return kernel_call(
            body,
            [f32(*pieces[0].shape)],
            (*pieces, *after),
            pieces[0].size * 2 * weight,
            name="finish",
            specs=[VMEM] * len(pieces) + [HELD] * len(after),
        )[0]

    def store(done, pieces, index, volume=None, weight=1, after=()):
        given = [*done, *pieces]
        held = [*after, *([] if volume is None else [volume])]

        def body(*refs):
            ready, refs = refs[: len(done)], refs[len(done) :]
            volume_ref, total_ref, sem = refs[-3:]

            def copy(i, source):
                at = pl.ds(chunks[i][0], chunks[i][1])
                return pltpu.make_async_copy(source, volume_ref.at[:, at], sem.at[i])

            copies = [copy(i, ref) for i, ref in enumerate(ready)]
            for c in copies:
                c.start()
            total_ref[...] = total(*refs[: len(pieces)])
            copies.append(copy(index, total_ref))
            copies[-1].start()
            for c in copies:
                c.wait()

        size = shard * widths[index]
        return pl.pallas_call(
            body,
            out_shape=f32(shard, cols),
            in_specs=[VMEM] * len(given) + [HELD] * len(held),
            out_specs=HELD,
            input_output_aliases={} if volume is None else {len(given) + len(after): 0},
            scratch_shapes=[
                pltpu.VMEM((shard, widths[index]), jnp.float32),
                pltpu.SemaphoreType.DMA((len(chunks),)),
            ],
            compiler_params=pltpu.CompilerParams(vmem_limit_bytes=VMEM_BYTES),
            cost_estimate=pl.CostEstimate(
                flops=size * 2 * weight, bytes_accessed=size * 4, transcendentals=0
            ),
            name="store",
        )(*given, *held)

    if not quick:
        sums = [
            lax.psum_scatter(project(i)[0], "angle", scatter_dimension=0, tiled=True)
            for i in range(len(chunks))
        ]
        return jnp.concatenate([sums[i] for i in sorted(range(len(chunks)), key=chunks.__getitem__)], 1)

    last = len(chunks) - 1
    *own, far, kept = project(0)
    sent = first_hops(*own)
    done, pieces = [], []
    for j in range(last + 1):
        here = (sent, own, far, kept)
        after = sent[2:] if j == 0 else []
        if j < last:
            earlier = [p[0] for p in pieces[-1:]] if j else [last_out[-1]]
            *own, far, kept = project(j + 1, after=earlier)
            sent = first_hops(*own)
            after = [*after, kept]
            if j:
                done.append(finish(pieces[-1], weight=FINISH_WEIGHTS[j - 1], after=[kept]))
                after.append(done[-1])
        pieces.append(relay(*here, after=after, weight=WEIGHTS[j], soon=SOON[j]))
    swap = [mark(sent[1], MARK)] if SOON[last] else []
    volume = store(done, pieces[last - 1], last - 1, weight=FINISH_WEIGHTS[last - 1], after=swap)
    return store([], pieces[last], last, volume)


def solution(mesh):
    placed = (
        P(("group", "angle"), "slab", "col"),
        P(),
        P(("group", "angle"), "slab"),
        P(("group", "angle"), "slab", None),
        P(("group", "angle"), "slab", None),
    )
    return jax.shard_map(
        on_device,
        mesh=mesh,
        in_specs=placed,
        out_specs=P(("group", "slab", "angle"), "col"),
        check_vma=False,
    )
```

```python
import math

import jax
import jax.numpy as jnp
from jax import lax
from jax.experimental import pallas as pl
from jax.experimental.pallas import tpu as pltpu
from jax.sharding import PartitionSpec as P

BLOCK = 256
TILE = 128
STACK = 8
DIRECT = (False, False, False, True)
SOON = (False, False, False, True)
WEIGHTS = (40000, 35000, 1, 1)
FINISH_WEIGHTS = (1, 15000, 10000)
MARK = 1000000000
VMEM_BYTES = 14 * 1024 * 1024
FIRST_VMEM_BYTES = 104 * 512 * 1024
LINE_ORDER = ((3, 2, 1, 0), (0, 2, 3, 1), (3, 1, 0, 2), (0, 1, 2, 3))

VMEM = pl.BlockSpec(memory_space=pltpu.VMEM)
HELD = pl.BlockSpec(memory_space=pltpu.HBM)
SMEM = pl.BlockSpec(memory_space=pltpu.SMEM)


def kernel_call(
    body, out_shape, args, flops, scratch=(), name=None, specs=None, grant=VMEM_BYTES, carried=()
):
    specs = specs or [VMEM] * len(args)
    moved = sum(a.size * a.dtype.itemsize for a in (*args, *out_shape))
    n_in, n_out, n_through = len(args), len(out_shape), len(carried)

    def kernel(*refs):
        ins, refs = refs[:n_in], refs[n_in + n_through :]
        body(*ins, *refs[:n_out], *refs[n_out + n_through :])

    return pl.pallas_call(
        kernel,
        out_shape=[*out_shape, *(jax.ShapeDtypeStruct(c.shape, c.dtype) for c in carried)],
        in_specs=[*specs, *([HELD] * n_through)],
        out_specs=[VMEM] * n_out + [HELD] * n_through,
        input_output_aliases={n_in + i: n_out + i for i in range(n_through)},
        scratch_shapes=list(scratch),
        compiler_params=pltpu.CompilerParams(vmem_limit_bytes=grant),
        cost_estimate=pl.CostEstimate(flops=flops, bytes_accessed=moved, transcendentals=0),
        name=name,
    )(*args, *carried)


def build_band(taps_ref, band_ref):
    count = taps_ref.shape[0]
    steps, tiles = band_ref.shape[1] // TILE, band_ref.shape[0] // TILE
    zero = jnp.zeros((TILE, TILE), jnp.float32)
    ahead = lax.broadcasted_iota(jnp.int32, (TILE, TILE), 1) >= lax.broadcasted_iota(
        jnp.int32, (TILE, TILE), 0
    )
    taps = taps_ref[...].astype(jnp.float32)

    def shifted(d):
        if not 0 <= d < count:
            return zero
        row = jnp.broadcast_to(taps[d : d + 1, :], (TILE, TILE))
        return pltpu.roll(row, 0, 1, stride=1, stride_axis=0)

    before = zero
    for d in range(-(steps - 1), tiles):
        here = shifted(d)
        block = jnp.where(ahead, here, before).T.astype(jnp.bfloat16)
        before = here
        for c in range(steps):
            if 0 <= d + c < tiles:
                band_ref[(d + c) * TILE : (d + c + 1) * TILE, c * TILE : (c + 1) * TILE] = block


def weigh(proj_ref, weighted_ref, half, row_at, row_start, col_start, sizes, c):
    angles = proj_ref.shape[0]
    total_rows, total_cols, count = sizes
    distance = jnp.float32(total_cols)
    v = lax.broadcasted_iota(jnp.int32, (count, 1), 0) + (row_start + row_at)
    v = v.astype(jnp.float32) - total_rows / 2 + 0.5
    u = lax.broadcasted_iota(jnp.int32, (1, BLOCK), 1) + (col_start + c)
    u = u.astype(jnp.float32) - total_cols / 2 + 0.5
    factor = distance / jnp.sqrt(distance * distance + u * u + v * v)
    for a in range(angles):
        raw = proj_ref[a, pl.ds(row_at, count), c : c + BLOCK].astype(jnp.float32)
        at = (half * angles + a) * count
        weighted_ref[at : at + count, c : c + BLOCK] = (raw * factor).astype(jnp.bfloat16)


def filter_columns(work, count, band_ref, weighted_at):
    length = band_ref.shape[0]
    reach = (length - BLOCK) // 2
    groups = []
    for half, first, width, out_ref in work:
        starts = range(first, first + width, BLOCK)
        for at in range(0, len(starts), STACK):
            groups.append((half, starts[at : at + STACK], out_ref, at))

    def touch(index):
        if index < len(groups):
            half, starts, _, _ = groups[index]
            for c in range(starts[0] - reach, starts[-1] + BLOCK + reach, BLOCK):
                weighted_at(half, c)

    touch(0)
    for index, (half, starts, out_ref, at) in enumerate(groups):
        touch(index + 1)
        tall = jnp.concatenate(
            [
                jnp.concatenate(
                    [weighted_at(half, c)() for c in range(s - reach, s + BLOCK + reach, BLOCK)],
                    axis=1,
                )
                for s in starts
            ],
            axis=0,
        )
        result = jnp.dot(tall, band_ref[...], preferred_element_type=jnp.float32)
        result = result.astype(jnp.bfloat16)
        for k in range(len(starts)):
            out_ref[:, (at + k) * BLOCK : (at + k + 1) * BLOCK] = result[
                k * count : (k + 1) * count, :
            ]


def bf16(*shape):
    return jax.ShapeDtypeStruct(shape, jnp.bfloat16)


def f32(*shape):
    return jax.ShapeDtypeStruct(shape, jnp.float32)


def chunk_plan(cols, reach):
    assert cols >= 4 * reach and reach % (4 * BLOCK) == 0
    first = reach * 3 // 2
    second = first + reach * 3 // 4
    third = cols - reach
    return [(first, second - first), (second, third - second), (third, reach), (0, first)]


def on_device(projections, filter_taps, row_first, interp_index, interp_frac):
    angles, rows, cols = projections.shape
    depth = interp_index.shape[2]
    taps = filter_taps.shape[0]
    reach = taps // 2
    length = taps + BLOCK
    margin = rows // 2
    slabs, line, sides = (lax.axis_size(n) for n in ("slab", "angle", "col"))
    scale = math.pi / (angles * line)
    both = slabs == 2
    halos = 1 if both else 2
    quick = line == 4
    shard = depth // line
    order = LINE_ORDER if quick else (tuple(range(line)),) * line
    total_rows, total_cols = rows * slabs, cols * sides
    chunks = chunk_plan(cols, reach)
    widths = [w for _, w in chunks]
    part = angles * margin
    sizes = (total_rows, total_cols, margin)

    def half_rows(slab):
        if both:
            return jnp.where(slab == 0, margin, 0), jnp.where(slab == 0, 0, margin)
        return margin, 0

    def aligned(row):
        return row if isinstance(row, int) else pl.multiple_of(row, margin)

    start, width = chunks[0]
    window_at, window = start - reach, width + 2 * reach
    early = halos

    def window_kernel(proj_ref, weighted_ref, edge_ref, raw_ref, sem):
        slab = lax.axis_index("slab")
        col = lax.axis_index("col")
        starts = [aligned(r) for r in half_rows(slab)][:early]
        copies = [
            pltpu.make_async_copy(
                proj_ref.at[a, pl.ds(r, margin), pl.ds(window_at, window)],
                raw_ref.at[a, pl.ds(r, margin), :],
                sem.at[a * 2 + h],
            )
            for a in range(angles)
            for h, r in enumerate(starts)
        ]
        edge_col = pl.multiple_of(jnp.where(col == 0, cols - reach, 0), TILE)
        edge_copy = pltpu.make_async_copy(
            proj_ref.at[:, :, pl.ds(edge_col, reach)], edge_ref, sem.at[2 * angles]
        )
        for copy in copies:
            copy.start()
        edge_copy.start()
        for copy in copies:
            copy.wait()
        for half, r in enumerate(starts):
            for c in range(0, window, BLOCK):
                weigh(
                    raw_ref, weighted_ref, half, r, slab * rows, col * cols + window_at, sizes, c
                )
        edge_copy.wait()

    ahead, edge = kernel_call(
        window_kernel,
        [bf16(early * part, window), bf16(angles, rows, reach)],
        (projections,),
        early * part * window * 4,
        scratch=[
            pltpu.VMEM((angles, rows, window), jnp.bfloat16),
            pltpu.SemaphoreType.DMA((2 * angles + 1,)),
        ],
        name="first_window",
        specs=[HELD],
        grant=FIRST_VMEM_BYTES,
    )

    def first_kernel(weighted_ref, taps_ref, band_ref, *outs):
        build_band(taps_ref, band_ref)

        def weighted_at(half, c):
            at = c - window_at
            return lambda: weighted_ref[half * part : (half + 1) * part, at : at + BLOCK]

        work = [(h, start, width, out_ref) for h, out_ref in enumerate(outs)]
        filter_columns(work, part, band_ref, weighted_at)

    band, *first_out = kernel_call(
        first_kernel,
        [bf16(length, BLOCK)] + [bf16(part, width)] * early,
        (ahead, filter_taps.reshape(taps // TILE, TILE)),
        2 * early * part * length * width,
        name="first_columns",
    )

    up = [(i, (i + 1) % slabs) for i in range(slabs - 1)]
    down = [(j, i) for i, j in up]

    def exchange(sends):
        if both:
            return [lax.ppermute(sends[0], "slab", up + down)]
        return [lax.ppermute(sends[0], "slab", up), lax.ppermute(sends[1], "slab", down)]

    assert sides == 2
    received = lax.ppermute(edge, "col", [(0, 1), (1, 0)])
    halo_rows = [exchange(first_out)]

    def write_weights(first_ref, index_ref, frac_ref, own_ref, halo_ref):
        slab = lax.axis_index("slab")
        angle = lax.axis_index("angle")
        if both:
            bases = [jnp.where(slab == 0, rows, rows - margin)]
        else:
            bases = [slab * rows - margin, (slab + 1) * rows]

        def weights(a, base):
            slot = lax.broadcasted_iota(jnp.int32, (margin, depth), 0) + base
            position = index_ref[a] + first_ref[a]
            frac = frac_ref[a]
            high = frac.astype(jnp.bfloat16).astype(jnp.float32)
            low = (1.0 - frac).astype(jnp.bfloat16).astype(jnp.float32)
            return jnp.where(slot == position, low, 0.0) + jnp.where(slot == position + 1, high, 0.0)

        here = [slab * rows + r for r in half_rows(slab)]
        for starts, ref in ((here, own_ref), (bases, halo_ref)):
            table = jnp.concatenate([weights(a, b) for b in starts for a in range(angles)], axis=0)
            turned = table.T.astype(jnp.bfloat16)
            for s in range(line):
                if quick:
                    places = [o.index(s) for o in order]
                    place = places[line - 1]
                    for i in range(line - 1):
                        place = jnp.where(angle == i, places[i], place)
                    at = pl.multiple_of(place * shard, shard)
                else:
                    at = s * shard
                ref[pl.ds(at, shard), :] = turned[s * shard : (s + 1) * shard, :]

    def filter_here(refs, work, band_ref):
        proj_ref, received_ref, weighted_ref, halo_cols_ref = refs
        slab = lax.axis_index("slab")
        col = lax.axis_index("col")
        starts = [aligned(r) for r in half_rows(slab)]
        lower = col == 0
        from_col = jnp.where(lower, cols, col * cols - reach)
        none = jnp.zeros((part, BLOCK), jnp.bfloat16)
        known = set()

        def weighted_at(half, c):
            inside = 0 <= c < cols
            source, into = (proj_ref, weighted_ref) if inside else (received_ref, halo_cols_ref)
            first_col = col * cols if inside else from_col
            at = c if inside else c % reach
            if (half, at, inside) not in known:
                known.add((half, at, inside))
                weigh(source, into, half, starts[half], slab * rows, first_col, sizes, at)

            def load():
                block = into[half * part : (half + 1) * part, at : at + BLOCK]
                if c < 0:
                    block = jnp.where(lower, none, block)
                elif c >= cols:
                    block = jnp.where(lower, block, none)
                return block

            return load

        filter_columns(work, part, band_ref, weighted_at)

    scratch = [pltpu.VMEM((2 * part, n), jnp.bfloat16) for n in (cols, reach)]

    work = [(1, *chunks[0])][: 2 - early]
    work += [(half, *chunk) for chunk in chunks[1:-1] for half in (0, 1)]

    def second_kernel(proj_ref, received_ref, band_ref, first_ref, index_ref, frac_ref,
                      own_ref, halo_ref, *rest):
        outs = [(*w, ref) for w, ref in zip(work, rest)]
        filter_here((proj_ref, received_ref, *rest[-2:]), outs, band_ref)
        write_weights(first_ref, index_ref, frac_ref, own_ref, halo_ref)

    own_weight, halo_weight, *second_out = kernel_call(
        second_kernel,
        [bf16(depth, 2 * part), bf16(depth, halos * part)] + [bf16(part, w[2]) for w in work],
        (projections, received, band, row_first[:, 0], interp_index, interp_frac),
        2 * part * length * sum(w[2] for w in work),
        scratch=scratch,
        name="other_columns",
        specs=[VMEM, VMEM, VMEM, SMEM, VMEM, VMEM],
    )

    def last_kernel(proj_ref, received_ref, taps_ref, *rest):
        *outs, band_ref, weighted_ref, halo_cols_ref = rest
        build_band(taps_ref, band_ref)
        filter_here(
            (proj_ref, received_ref, weighted_ref, halo_cols_ref),
            [(half, *chunks[-1], ref) for half, ref in enumerate(outs)],
            band_ref,
        )

    before = second_out[-2:]
    *last_out, before[0] = kernel_call(
        last_kernel,
        [bf16(part, widths[-1])] * 2,
        (projections, received, filter_taps.reshape(taps // TILE, TILE)),
        4 * part * length * widths[-1],
        scratch=[pltpu.VMEM((length, BLOCK), jnp.bfloat16)] + scratch,
        name="last_columns",
        carried=before[:1],
    )
    second_out = [*second_out[:-2], *before, *last_out]
    filtered = [(*first_out, *second_out[: 2 - early])]
    for at in range(2 - early, len(second_out), 2):
        filtered.append(second_out[at : at + 2])
        halo_rows.append(exchange(second_out[at : at + halos]))

    def project(index, after=()):
        width = widths[index]

        def body(own_ref, halo_ref, *rest):
            sources, outs = rest[: 2 + halos], rest[2 + halos + len(after) :]
            for c in range(0, width, BLOCK):
                cut = slice(c, c + BLOCK)
                own = jnp.concatenate([ref[:, cut] for ref in sources[:2]], axis=0)
                other = [ref[:, cut] for ref in sources[2:]]
                other = other[0] if len(other) == 1 else jnp.concatenate(other, axis=0)
                total = jnp.dot(own_ref[...], own, preferred_element_type=jnp.float32)
                total += jnp.dot(halo_ref[...], other, preferred_element_type=jnp.float32)
                total = total * scale
                at = 0
                for out in outs:
                    out[:, cut] = total[at : at + out.shape[0], :].astype(out.dtype)
                    at += out.shape[0]

        if quick:
            first = [bf16(shard, width)] * 2 if DIRECT[index] else [bf16(2 * shard, width)]
            shapes = [*first, bf16(shard, width), f32(shard, width)]
        else:
            shapes = [f32(depth, width)]
        return kernel_call(
            body,
            shapes,
            (own_weight, halo_weight, *filtered[index], *halo_rows[index], *after),
            2 * depth * (2 + halos) * part * width,
            name="interpolate",
            specs=[VMEM] * (4 + halos) + [HELD] * len(after),
        )

    def widen(x):
        return x.astype(jnp.float32)

    def at_end():
        angle = lax.axis_index("angle")
        return (angle == 0) | (angle == line - 1)

    neighbours = [(0, 1), (1, 0), (2, 3), (3, 2)]
    middles = [(1, 2), (2, 1), (0, 0), (3, 3)]
    second_hop = [(0, 1), (1, 3), (2, 0), (3, 2)]
    straight = [(0, 2), (3, 1), (1, 0), (2, 3)]

    def first_hops(*parts):
        if len(parts) == 1:
            return [lax.ppermute(parts[0], "angle", neighbours)]
        near, middle = parts
        two = lax.ppermute(middle, "angle", straight)
        three = lax.ppermute(middle, "angle", middles)
        one = lax.ppermute(near, "angle", neighbours)
        return [one, three, two]

    def relay(sent, own, far, kept, after=(), weight=1, soon=False):
        direct = len(sent) == 3
        arrived = sent[: 1 if soon else 2] if direct else [sent[0], own[0]]
        extra = len(arrived) - 1

        def body(one_ref, *rest):
            other_ref = rest[0]
            far_ref, kept_ref = rest[extra : extra + 2]
            outs = rest[extra + 2 + len(after) :]
            end = at_end()
            near = widen(one_ref[:shard, :])
            relayed = widen(far_ref[...]) + jnp.where(end, 0.0, near)
            outs[0][...] = relayed.astype(jnp.bfloat16)
            if soon:
                outs[1][...] = kept_ref[...] + jnp.where(end, near, 0.0)
            elif direct:
                outs[1][...] = kept_ref[...] + jnp.where(end, near, widen(other_ref[...]))
            else:
                outs[1][...] = kept_ref[...] + jnp.where(end, near, 0.0)
                crossed = widen(one_ref[shard:, :]) + widen(other_ref[shard:, :])
                outs[2][...] = crossed.astype(jnp.bfloat16)

        relayed, partial, *crossed = kernel_call(
            body,
            [bf16(*far.shape), f32(*kept.shape)] + [bf16(*far.shape)] * (not direct),
            (*arrived, far, kept, *after),
            far.size * 2 * weight,
            name="relay",
            specs=[VMEM] * (3 + extra) + [HELD] * len(after),
        )
        four = lax.ppermute(relayed, "angle", second_hop)
        three = sent[2] if direct else lax.ppermute(crossed[0], "angle", middles)
        return (partial, four, three, *([sent[1]] if soon else []))

    def total(partial_ref, four_ref, *fillers):
        direct = sum(widen(ref[...]) for ref in fillers)
        return partial_ref[...] + widen(four_ref[...]) + jnp.where(at_end(), 0.0, direct)

    def mark(array, weight):
        def body(array_ref, out_ref):
            out_ref[...] = jnp.zeros_like(out_ref)

        return kernel_call(body, [f32(8, TILE)], (array,), weight, name="mark", specs=[HELD])[0]

    def finish(pieces, weight=1, after=()):
        def body(*refs):
            refs[-1][...] = total(*refs[: len(pieces)])

        return kernel_call(
            body,
            [f32(*pieces[0].shape)],
            (*pieces, *after),
            pieces[0].size * 2 * weight,
            name="finish",
            specs=[VMEM] * len(pieces) + [HELD] * len(after),
        )[0]

    def store(done, pieces, index, volume=None, weight=1, after=()):
        given = [*done, *pieces]
        held = [*after, *([] if volume is None else [volume])]

        def body(*refs):
            ready, refs = refs[: len(done)], refs[len(done) :]
            volume_ref, total_ref, sem = refs[-3:]

            def copy(i, source):
                at = pl.ds(chunks[i][0], chunks[i][1])
                return pltpu.make_async_copy(source, volume_ref.at[:, at], sem.at[i])

            copies = [copy(i, ref) for i, ref in enumerate(ready)]
            for c in copies:
                c.start()
            total_ref[...] = total(*refs[: len(pieces)])
            copies.append(copy(index, total_ref))
            copies[-1].start()
            for c in copies:
                c.wait()

        size = shard * widths[index]
        return pl.pallas_call(
            body,
            out_shape=f32(shard, cols),
            in_specs=[VMEM] * len(given) + [HELD] * len(held),
            out_specs=HELD,
            input_output_aliases={} if volume is None else {len(given) + len(after): 0},
            scratch_shapes=[
                pltpu.VMEM((shard, widths[index]), jnp.float32),
                pltpu.SemaphoreType.DMA((len(chunks),)),
            ],
            compiler_params=pltpu.CompilerParams(vmem_limit_bytes=VMEM_BYTES),
            cost_estimate=pl.CostEstimate(
                flops=size * 2 * weight, bytes_accessed=size * 4, transcendentals=0
            ),
            name="store",
        )(*given, *held)

    if not quick:
        sums = [
            lax.psum_scatter(project(i)[0], "angle", scatter_dimension=0, tiled=True)
            for i in range(len(chunks))
        ]
        return jnp.concatenate([sums[i] for i in sorted(range(len(chunks)), key=chunks.__getitem__)], 1)

    last = len(chunks) - 1
    *own, far, kept = project(0)
    sent = first_hops(*own)
    done, pieces = [], []
    for j in range(last + 1):
        here = (sent, own, far, kept)
        after = sent[2:] if j == 0 else []
        if j < last:
            earlier = [p[0] for p in pieces[-1:]] if j else [last_out[-1]]
            *own, far, kept = project(j + 1, after=earlier)
            sent = first_hops(*own)
            after = [*after, kept]
            if j:
                done.append(finish(pieces[-1], weight=FINISH_WEIGHTS[j - 1], after=[kept]))
                after.append(done[-1])
        pieces.append(relay(*here, after=after, weight=WEIGHTS[j], soon=SOON[j]))
    swap = [mark(sent[1], MARK)] if SOON[last] else []
    volume = store(done, pieces[last - 1], last - 1, weight=FINISH_WEIGHTS[last - 1], after=swap)
    return store([], pieces[last], last, volume)


def solution(mesh):
    placed = (
        P(("group", "angle"), "slab", "col"),
        P(),
        P(("group", "angle"), "slab"),
        P(("group", "angle"), "slab", None),
        P(("group", "angle"), "slab", None),
    )
    return jax.shard_map(
        on_device,
        mesh=mesh,
        in_specs=placed,
        out_specs=P(("group", "slab", "angle"), "col"),
        check_vma=False,
    )
```

```python
import math

import jax
import jax.numpy as jnp
from jax import lax
from jax.experimental import pallas as pl
from jax.experimental.pallas import tpu as pltpu
from jax.sharding import PartitionSpec as P

BLOCK = 256
TILE = 128
STACK = 8
DIRECT = (False, False, False, True)
SOON = (False, False, False, True)
WEIGHTS = (40000, 28000, 1, 1)
FINISH_WEIGHTS = (1, 1, 10000)
MARK = 1000000000
VMEM_BYTES = 14 * 1024 * 1024
FIRST_VMEM_BYTES = 104 * 512 * 1024
LINE_ORDER = ((3, 2, 1, 0), (0, 2, 3, 1), (3, 1, 0, 2), (0, 1, 2, 3))

VMEM = pl.BlockSpec(memory_space=pltpu.VMEM)
HELD = pl.BlockSpec(memory_space=pltpu.HBM)
SMEM = pl.BlockSpec(memory_space=pltpu.SMEM)


def kernel_call(
    body, out_shape, args, flops, scratch=(), name=None, specs=None, grant=VMEM_BYTES, carried=()
):
    specs = specs or [VMEM] * len(args)
    moved = sum(a.size * a.dtype.itemsize for a in (*args, *out_shape))
    n_in, n_out, n_through = len(args), len(out_shape), len(carried)

    def kernel(*refs):
        ins, refs = refs[:n_in], refs[n_in + n_through :]
        body(*ins, *refs[:n_out], *refs[n_out + n_through :])

    return pl.pallas_call(
        kernel,
        out_shape=[*out_shape, *(jax.ShapeDtypeStruct(c.shape, c.dtype) for c in carried)],
        in_specs=[*specs, *([HELD] * n_through)],
        out_specs=[VMEM] * n_out + [HELD] * n_through,
        input_output_aliases={n_in + i: n_out + i for i in range(n_through)},
        scratch_shapes=list(scratch),
        compiler_params=pltpu.CompilerParams(vmem_limit_bytes=grant),
        cost_estimate=pl.CostEstimate(flops=flops, bytes_accessed=moved, transcendentals=0),
        name=name,
    )(*args, *carried)


def build_band(taps_ref, band_ref):
    count = taps_ref.shape[0]
    steps, tiles = band_ref.shape[1] // TILE, band_ref.shape[0] // TILE
    zero = jnp.zeros((TILE, TILE), jnp.float32)
    ahead = lax.broadcasted_iota(jnp.int32, (TILE, TILE), 1) >= lax.broadcasted_iota(
        jnp.int32, (TILE, TILE), 0
    )
    taps = taps_ref[...].astype(jnp.float32)

    def shifted(d):
        if not 0 <= d < count:
            return zero
        row = jnp.broadcast_to(taps[d : d + 1, :], (TILE, TILE))
        return pltpu.roll(row, 0, 1, stride=1, stride_axis=0)

    before = zero
    for d in range(-(steps - 1), tiles):
        here = shifted(d)
        block = jnp.where(ahead, here, before).T.astype(jnp.bfloat16)
        before = here
        for c in range(steps):
            if 0 <= d + c < tiles:
                band_ref[(d + c) * TILE : (d + c + 1) * TILE, c * TILE : (c + 1) * TILE] = block


def weigh(proj_ref, weighted_ref, half, row_at, row_start, col_start, sizes, c):
    angles = proj_ref.shape[0]
    total_rows, total_cols, count = sizes
    distance = jnp.float32(total_cols)
    v = lax.broadcasted_iota(jnp.int32, (count, 1), 0) + (row_start + row_at)
    v = v.astype(jnp.float32) - total_rows / 2 + 0.5
    u = lax.broadcasted_iota(jnp.int32, (1, BLOCK), 1) + (col_start + c)
    u = u.astype(jnp.float32) - total_cols / 2 + 0.5
    factor = distance / jnp.sqrt(distance * distance + u * u + v * v)
    for a in range(angles):
        raw = proj_ref[a, pl.ds(row_at, count), c : c + BLOCK].astype(jnp.float32)
        at = (half * angles + a) * count
        weighted_ref[at : at + count, c : c + BLOCK] = (raw * factor).astype(jnp.bfloat16)


def filter_columns(work, count, band_ref, weighted_at):
    length = band_ref.shape[0]
    reach = (length - BLOCK) // 2
    groups = []
    for half, first, width, out_ref in work:
        starts = range(first, first + width, BLOCK)
        for at in range(0, len(starts), STACK):
            groups.append((half, starts[at : at + STACK], out_ref, at))

    def touch(index):
        if index < len(groups):
            half, starts, _, _ = groups[index]
            for c in range(starts[0] - reach, starts[-1] + BLOCK + reach, BLOCK):
                weighted_at(half, c)

    touch(0)
    for index, (half, starts, out_ref, at) in enumerate(groups):
        touch(index + 1)
        tall = jnp.concatenate(
            [
                jnp.concatenate(
                    [weighted_at(half, c)() for c in range(s - reach, s + BLOCK + reach, BLOCK)],
                    axis=1,
                )
                for s in starts
            ],
            axis=0,
        )
        result = jnp.dot(tall, band_ref[...], preferred_element_type=jnp.float32)
        result = result.astype(jnp.bfloat16)
        for k in range(len(starts)):
            out_ref[:, (at + k) * BLOCK : (at + k + 1) * BLOCK] = result[
                k * count : (k + 1) * count, :
            ]


def bf16(*shape):
    return jax.ShapeDtypeStruct(shape, jnp.bfloat16)


def f32(*shape):
    return jax.ShapeDtypeStruct(shape, jnp.float32)


def chunk_plan(cols, reach):
    assert cols >= 4 * reach and reach % (4 * BLOCK) == 0
    first, second = reach + BLOCK, 2 * reach
    third = second + (cols - 2 * reach) * 3 // 8
    return [(first, second - first), (second, third - second), (third, cols - third), (0, first)]


def on_device(projections, filter_taps, row_first, interp_index, interp_frac):
    angles, rows, cols = projections.shape
    depth = interp_index.shape[2]
    taps = filter_taps.shape[0]
    reach = taps // 2
    length = taps + BLOCK
    margin = rows // 2
    slabs, line, sides = (lax.axis_size(n) for n in ("slab", "angle", "col"))
    scale = math.pi / (angles * line)
    both = slabs == 2
    halos = 1 if both else 2
    quick = line == 4
    shard = depth // line
    order = LINE_ORDER if quick else (tuple(range(line)),) * line
    total_rows, total_cols = rows * slabs, cols * sides
    chunks = chunk_plan(cols, reach)
    widths = [w for _, w in chunks]
    part = angles * margin
    sizes = (total_rows, total_cols, margin)

    def half_rows(slab):
        if both:
            return jnp.where(slab == 0, margin, 0), jnp.where(slab == 0, 0, margin)
        return margin, 0

    def aligned(row):
        return row if isinstance(row, int) else pl.multiple_of(row, margin)

    start, width = chunks[0]
    window_at, window = start - reach, width + 2 * reach
    early = halos

    def window_kernel(proj_ref, weighted_ref, edge_ref, raw_ref, sem):
        slab = lax.axis_index("slab")
        col = lax.axis_index("col")
        starts = [aligned(r) for r in half_rows(slab)][:early]
        copies = [
            pltpu.make_async_copy(
                proj_ref.at[a, pl.ds(r, margin), pl.ds(window_at, window)],
                raw_ref.at[a, pl.ds(r, margin), :],
                sem.at[a * 2 + h],
            )
            for a in range(angles)
            for h, r in enumerate(starts)
        ]
        edge_col = pl.multiple_of(jnp.where(col == 0, cols - reach, 0), TILE)
        edge_copy = pltpu.make_async_copy(
            proj_ref.at[:, :, pl.ds(edge_col, reach)], edge_ref, sem.at[2 * angles]
        )
        for copy in copies:
            copy.start()
        edge_copy.start()
        for copy in copies:
            copy.wait()
        for half, r in enumerate(starts):
            for c in range(0, window, BLOCK):
                weigh(
                    raw_ref, weighted_ref, half, r, slab * rows, col * cols + window_at, sizes, c
                )
        edge_copy.wait()

    ahead, edge = kernel_call(
        window_kernel,
        [bf16(early * part, window), bf16(angles, rows, reach)],
        (projections,),
        early * part * window * 4,
        scratch=[
            pltpu.VMEM((angles, rows, window), jnp.bfloat16),
            pltpu.SemaphoreType.DMA((2 * angles + 1,)),
        ],
        name="first_window",
        specs=[HELD],
        grant=FIRST_VMEM_BYTES,
    )

    def first_kernel(weighted_ref, taps_ref, band_ref, *outs):
        build_band(taps_ref, band_ref)

        def weighted_at(half, c):
            at = c - window_at
            return lambda: weighted_ref[half * part : (half + 1) * part, at : at + BLOCK]

        work = [(h, start, width, out_ref) for h, out_ref in enumerate(outs)]
        filter_columns(work, part, band_ref, weighted_at)

    band, *first_out = kernel_call(
        first_kernel,
        [bf16(length, BLOCK)] + [bf16(part, width)] * early,
        (ahead, filter_taps.reshape(taps // TILE, TILE)),
        2 * early * part * length * width,
        name="first_columns",
    )

    up = [(i, (i + 1) % slabs) for i in range(slabs - 1)]
    down = [(j, i) for i, j in up]

    def exchange(sends):
        if both:
            return [lax.ppermute(sends[0], "slab", up + down)]
        return [lax.ppermute(sends[0], "slab", up), lax.ppermute(sends[1], "slab", down)]

    assert sides == 2
    received = lax.ppermute(edge, "col", [(0, 1), (1, 0)])
    halo_rows = [exchange(first_out)]

    def write_weights(first_ref, index_ref, frac_ref, own_ref, halo_ref):
        slab = lax.axis_index("slab")
        angle = lax.axis_index("angle")
        if both:
            bases = [jnp.where(slab == 0, rows, rows - margin)]
        else:
            bases = [slab * rows - margin, (slab + 1) * rows]

        def weights(a, base):
            slot = lax.broadcasted_iota(jnp.int32, (margin, depth), 0) + base
            position = index_ref[a] + first_ref[a]
            frac = frac_ref[a]
            high = frac.astype(jnp.bfloat16).astype(jnp.float32)
            low = (1.0 - frac).astype(jnp.bfloat16).astype(jnp.float32)
            return jnp.where(slot == position, low, 0.0) + jnp.where(slot == position + 1, high, 0.0)

        here = [slab * rows + r for r in half_rows(slab)]
        for starts, ref in ((here, own_ref), (bases, halo_ref)):
            table = jnp.concatenate([weights(a, b) for b in starts for a in range(angles)], axis=0)
            turned = table.T.astype(jnp.bfloat16)
            for s in range(line):
                if quick:
                    places = [o.index(s) for o in order]
                    place = places[line - 1]
                    for i in range(line - 1):
                        place = jnp.where(angle == i, places[i], place)
                    at = pl.multiple_of(place * shard, shard)
                else:
                    at = s * shard
                ref[pl.ds(at, shard), :] = turned[s * shard : (s + 1) * shard, :]

    def filter_here(refs, work, band_ref):
        proj_ref, received_ref, weighted_ref, halo_cols_ref = refs
        slab = lax.axis_index("slab")
        col = lax.axis_index("col")
        starts = [aligned(r) for r in half_rows(slab)]
        lower = col == 0
        from_col = jnp.where(lower, cols, col * cols - reach)
        none = jnp.zeros((part, BLOCK), jnp.bfloat16)
        known = set()

        def weighted_at(half, c):
            inside = 0 <= c < cols
            source, into = (proj_ref, weighted_ref) if inside else (received_ref, halo_cols_ref)
            first_col = col * cols if inside else from_col
            at = c if inside else c % reach
            if (half, at, inside) not in known:
                known.add((half, at, inside))
                weigh(source, into, half, starts[half], slab * rows, first_col, sizes, at)

            def load():
                block = into[half * part : (half + 1) * part, at : at + BLOCK]
                if c < 0:
                    block = jnp.where(lower, none, block)
                elif c >= cols:
                    block = jnp.where(lower, block, none)
                return block

            return load

        filter_columns(work, part, band_ref, weighted_at)

    scratch = [pltpu.VMEM((2 * part, n), jnp.bfloat16) for n in (cols, reach)]

    work = [(1, *chunks[0])][: 2 - early]
    work += [(1, *chunks[-1])]
    work += [(half, *chunk) for chunk in chunks[1:-1] for half in (0, 1)]

    def second_kernel(proj_ref, received_ref, band_ref, first_ref, index_ref, frac_ref,
                      own_ref, halo_ref, *rest):
        outs = [(*w, ref) for w, ref in zip(work, rest)]
        filter_here((proj_ref, received_ref, *rest[-2:]), outs, band_ref)
        write_weights(first_ref, index_ref, frac_ref, own_ref, halo_ref)

    own_weight, halo_weight, *second_out = kernel_call(
        second_kernel,
        [bf16(depth, 2 * part), bf16(depth, halos * part)] + [bf16(part, w[2]) for w in work],
        (projections, received, band, row_first[:, 0], interp_index, interp_frac),
        2 * part * length * sum(w[2] for w in work),
        scratch=scratch,
        name="other_columns",
        specs=[VMEM, VMEM, VMEM, SMEM, VMEM, VMEM],
    )

    def last_kernel(proj_ref, received_ref, taps_ref, *rest):
        *outs, band_ref, weighted_ref, halo_cols_ref = rest
        build_band(taps_ref, band_ref)
        filter_here(
            (proj_ref, received_ref, weighted_ref, halo_cols_ref),
            [(0, *chunks[-1], ref) for ref in outs],
            band_ref,
        )

    first_rest, last_rest, *second_out = (
        second_out if early == 1 else [None, *second_out]
    )
    before = second_out[-2:]
    *last_out, before[0] = kernel_call(
        last_kernel,
        [bf16(part, widths[-1])],
        (projections, received, filter_taps.reshape(taps // TILE, TILE)),
        2 * part * length * widths[-1],
        scratch=[pltpu.VMEM((length, BLOCK), jnp.bfloat16)] + scratch,
        name="last_columns",
        carried=before[:1],
    )
    filtered = [[*first_out, first_rest][:2], second_out[:2], before, [last_out[0], last_rest]]
    halo_rows += [exchange(rows_out[:halos]) for rows_out in filtered[1:]]

    def project(index, after=()):
        width = widths[index]

        def body(own_ref, halo_ref, *rest):
            sources, outs = rest[: 2 + halos], rest[2 + halos + len(after) :]
            for c in range(0, width, BLOCK):
                cut = slice(c, c + BLOCK)
                own = jnp.concatenate([ref[:, cut] for ref in sources[:2]], axis=0)
                other = [ref[:, cut] for ref in sources[2:]]
                other = other[0] if len(other) == 1 else jnp.concatenate(other, axis=0)
                total = jnp.dot(own_ref[...], own, preferred_element_type=jnp.float32)
                total += jnp.dot(halo_ref[...], other, preferred_element_type=jnp.float32)
                total = total * scale
                at = 0
                for out in outs:
                    out[:, cut] = total[at : at + out.shape[0], :].astype(out.dtype)
                    at += out.shape[0]

        if quick:
            first = [bf16(shard, width)] * 2 if DIRECT[index] else [bf16(2 * shard, width)]
            shapes = [*first, bf16(shard, width), f32(shard, width)]
        else:
            shapes = [f32(depth, width)]
        return kernel_call(
            body,
            shapes,
            (own_weight, halo_weight, *filtered[index], *halo_rows[index], *after),
            2 * depth * (2 + halos) * part * width,
            name="interpolate",
            specs=[VMEM] * (4 + halos) + [HELD] * len(after),
        )

    def widen(x):
        return x.astype(jnp.float32)

    def at_end():
        angle = lax.axis_index("angle")
        return (angle == 0) | (angle == line - 1)

    neighbours = [(0, 1), (1, 0), (2, 3), (3, 2)]
    middles = [(1, 2), (2, 1), (0, 0), (3, 3)]
    second_hop = [(0, 1), (1, 3), (2, 0), (3, 2)]
    straight = [(0, 2), (3, 1), (1, 0), (2, 3)]

    def first_hops(*parts):
        if len(parts) == 1:
            return [lax.ppermute(parts[0], "angle", neighbours)]
        near, middle = parts
        two = lax.ppermute(middle, "angle", straight)
        three = lax.ppermute(middle, "angle", middles)
        one = lax.ppermute(near, "angle", neighbours)
        return [one, three, two]

    def relay(sent, own, far, kept, after=(), weight=1, soon=False):
        direct = len(sent) == 3
        arrived = sent[: 1 if soon else 2] if direct else [sent[0], own[0]]
        extra = len(arrived) - 1

        def body(one_ref, *rest):
            other_ref = rest[0]
            far_ref, kept_ref = rest[extra : extra + 2]
            outs = rest[extra + 2 + len(after) :]
            end = at_end()
            near = widen(one_ref[:shard, :])
            relayed = widen(far_ref[...]) + jnp.where(end, 0.0, near)
            outs[0][...] = relayed.astype(jnp.bfloat16)
            if soon:
                outs[1][...] = kept_ref[...] + jnp.where(end, near, 0.0)
            elif direct:
                outs[1][...] = kept_ref[...] + jnp.where(end, near, widen(other_ref[...]))
            else:
                outs[1][...] = kept_ref[...] + jnp.where(end, near, 0.0)
                crossed = widen(one_ref[shard:, :]) + widen(other_ref[shard:, :])
                outs[2][...] = crossed.astype(jnp.bfloat16)

        relayed, partial, *crossed = kernel_call(
            body,
            [bf16(*far.shape), f32(*kept.shape)] + [bf16(*far.shape)] * (not direct),
            (*arrived, far, kept, *after),
            far.size * 2 * weight,
            name="relay",
            specs=[VMEM] * (3 + extra) + [HELD] * len(after),
        )
        four = lax.ppermute(relayed, "angle", second_hop)
        three = sent[2] if direct else lax.ppermute(crossed[0], "angle", middles)
        return (partial, four, three, *([sent[1]] if soon else []))

    def total(partial_ref, four_ref, *fillers):
        direct = sum(widen(ref[...]) for ref in fillers)
        return partial_ref[...] + widen(four_ref[...]) + jnp.where(at_end(), 0.0, direct)

    def mark(array, weight):
        def body(array_ref, out_ref):
            out_ref[...] = jnp.zeros_like(out_ref)

        return kernel_call(body, [f32(8, TILE)], (array,), weight, name="mark", specs=[HELD])[0]

    def finish(pieces, weight=1, after=()):
        def body(*refs):
            refs[-1][...] = total(*refs[: len(pieces)])

        return kernel_call(
            body,
            [f32(*pieces[0].shape)],
            (*pieces, *after),
            pieces[0].size * 2 * weight,
            name="finish",
            specs=[VMEM] * len(pieces) + [HELD] * len(after),
        )[0]

    def store(done, pieces, index, volume=None, weight=1, after=()):
        given = [*done, *pieces]
        held = [*after, *([] if volume is None else [volume])]

        def body(*refs):
            ready, refs = refs[: len(done)], refs[len(done) :]
            volume_ref, total_ref, sem = refs[-3:]

            def copy(i, source):
                at = pl.ds(chunks[i][0], chunks[i][1])
                return pltpu.make_async_copy(source, volume_ref.at[:, at], sem.at[i])

            copies = [copy(i, ref) for i, ref in enumerate(ready)]
            for c in copies:
                c.start()
            total_ref[...] = total(*refs[: len(pieces)])
            copies.append(copy(index, total_ref))
            copies[-1].start()
            for c in copies:
                c.wait()

        size = shard * widths[index]
        return pl.pallas_call(
            body,
            out_shape=f32(shard, cols),
            in_specs=[VMEM] * len(given) + [HELD] * len(held),
            out_specs=HELD,
            input_output_aliases={} if volume is None else {len(given) + len(after): 0},
            scratch_shapes=[
                pltpu.VMEM((shard, widths[index]), jnp.float32),
                pltpu.SemaphoreType.DMA((len(chunks),)),
            ],
            compiler_params=pltpu.CompilerParams(vmem_limit_bytes=VMEM_BYTES),
            cost_estimate=pl.CostEstimate(
                flops=size * 2 * weight, bytes_accessed=size * 4, transcendentals=0
            ),
            name="store",
        )(*given, *held)

    if not quick:
        sums = [
            lax.psum_scatter(project(i)[0], "angle", scatter_dimension=0, tiled=True)
            for i in range(len(chunks))
        ]
        return jnp.concatenate([sums[i] for i in sorted(range(len(chunks)), key=chunks.__getitem__)], 1)

    last = len(chunks) - 1
    *own, far, kept = project(0)
    sent = first_hops(*own)
    done, pieces = [], []
    for j in range(last + 1):
        here = (sent, own, far, kept)
        after = sent[2:] if j == 0 else []
        if j < last:
            earlier = [p[0] for p in pieces[-1:]] if j else [last_out[-1]]
            *own, far, kept = project(j + 1, after=earlier)
            sent = first_hops(*own)
            after = [*after, kept]
            if j:
                done.append(finish(pieces[-1], weight=FINISH_WEIGHTS[j - 1], after=[kept]))
                after.append(done[-1])
        pieces.append(relay(*here, after=after, weight=WEIGHTS[j], soon=SOON[j]))
    swap = [mark(sent[1], MARK)] if SOON[last] else []
    volume = store(done, pieces[last - 1], last - 1, weight=FINISH_WEIGHTS[last - 1], after=swap)
    return store([], pieces[last], last, volume)


def solution(mesh):
    placed = (
        P(("group", "angle"), "slab", "col"),
        P(),
        P(("group", "angle"), "slab"),
        P(("group", "angle"), "slab", None),
        P(("group", "angle"), "slab", None),
    )
    return jax.shard_map(
        on_device,
        mesh=mesh,
        in_specs=placed,
        out_specs=P(("group", "slab", "angle"), "col"),
        check_vma=False,
    )
```

```python
import math

import jax
import jax.numpy as jnp
from jax import lax
from jax.experimental import pallas as pl
from jax.experimental.pallas import tpu as pltpu
from jax.sharding import PartitionSpec as P

BLOCK = 256
TILE = 128
STACK = 8
DIRECT = (False, False, False, True)
SOON = (False, False, False, True)
WEIGHTS = (40000, 28000, 1, 1)
FINISH_WEIGHTS = (1, 1, 10000)
MARK = 1000000000
VMEM_BYTES = 14 * 1024 * 1024
FIRST_VMEM_BYTES = 104 * 512 * 1024
LINE_ORDER = ((3, 2, 1, 0), (0, 2, 3, 1), (3, 1, 0, 2), (0, 1, 2, 3))

VMEM = pl.BlockSpec(memory_space=pltpu.VMEM)
HELD = pl.BlockSpec(memory_space=pltpu.HBM)
SMEM = pl.BlockSpec(memory_space=pltpu.SMEM)


def kernel_call(
    body, out_shape, args, flops, scratch=(), name=None, specs=None, grant=VMEM_BYTES, carried=()
):
    specs = specs or [VMEM] * len(args)
    moved = sum(a.size * a.dtype.itemsize for a in (*args, *out_shape))
    n_in, n_out, n_through = len(args), len(out_shape), len(carried)

    def kernel(*refs):
        ins, refs = refs[:n_in], refs[n_in + n_through :]
        body(*ins, *refs[:n_out], *refs[n_out + n_through :])

    return pl.pallas_call(
        kernel,
        out_shape=[*out_shape, *(jax.ShapeDtypeStruct(c.shape, c.dtype) for c in carried)],
        in_specs=[*specs, *([HELD] * n_through)],
        out_specs=[VMEM] * n_out + [HELD] * n_through,
        input_output_aliases={n_in + i: n_out + i for i in range(n_through)},
        scratch_shapes=list(scratch),
        compiler_params=pltpu.CompilerParams(vmem_limit_bytes=grant),
        cost_estimate=pl.CostEstimate(flops=flops, bytes_accessed=moved, transcendentals=0),
        name=name,
    )(*args, *carried)


def build_band(taps_ref, band_ref):
    count = taps_ref.shape[0]
    steps, tiles = band_ref.shape[1] // TILE, band_ref.shape[0] // TILE
    zero = jnp.zeros((TILE, TILE), jnp.float32)
    ahead = lax.broadcasted_iota(jnp.int32, (TILE, TILE), 1) >= lax.broadcasted_iota(
        jnp.int32, (TILE, TILE), 0
    )
    taps = taps_ref[...].astype(jnp.float32)

    def shifted(d):
        if not 0 <= d < count:
            return zero
        row = jnp.broadcast_to(taps[d : d + 1, :], (TILE, TILE))
        return pltpu.roll(row, 0, 1, stride=1, stride_axis=0)

    before = zero
    for d in range(-(steps - 1), tiles):
        here = shifted(d)
        block = jnp.where(ahead, here, before).T.astype(jnp.bfloat16)
        before = here
        for c in range(steps):
            if 0 <= d + c < tiles:
                band_ref[(d + c) * TILE : (d + c + 1) * TILE, c * TILE : (c + 1) * TILE] = block


def cosine_factor(row_start, col_start, sizes):
    total_rows, total_cols, count = sizes
    distance = jnp.float32(total_cols)
    v = lax.broadcasted_iota(jnp.int32, (count, 1), 0) + row_start
    v = v.astype(jnp.float32) - total_rows / 2 + 0.5
    u = lax.broadcasted_iota(jnp.int32, (1, BLOCK), 1) + col_start
    u = u.astype(jnp.float32) - total_cols / 2 + 0.5
    return distance / jnp.sqrt(distance * distance + u * u + v * v)


def weigh(proj_ref, weighted_ref, half, row_at, row_start, col_start, sizes, c):
    angles, count = proj_ref.shape[0], sizes[2]
    factor = cosine_factor(row_start + row_at, col_start + c, sizes)
    for a in range(angles):
        raw = proj_ref[a, pl.ds(row_at, count), c : c + BLOCK].astype(jnp.float32)
        at = (half * angles + a) * count
        weighted_ref[at : at + count, c : c + BLOCK] = (raw * factor).astype(jnp.bfloat16)


def filter_columns(work, count, band_ref, weighted_at):
    length = band_ref.shape[0]
    reach = (length - BLOCK) // 2
    groups = []
    for half, first, width, out_ref in work:
        starts = range(first, first + width, BLOCK)
        for at in range(0, len(starts), STACK):
            groups.append((half, starts[at : at + STACK], out_ref, at))

    def touch(index):
        if index < len(groups):
            half, starts, _, _ = groups[index]
            for c in range(starts[0] - reach, starts[-1] + BLOCK + reach, BLOCK):
                weighted_at(half, c)

    touch(0)
    for index, (half, starts, out_ref, at) in enumerate(groups):
        touch(index + 1)
        tall = jnp.concatenate(
            [
                jnp.concatenate(
                    [weighted_at(half, c)() for c in range(s - reach, s + BLOCK + reach, BLOCK)],
                    axis=1,
                )
                for s in starts
            ],
            axis=0,
        )
        result = jnp.dot(tall, band_ref[...], preferred_element_type=jnp.float32)
        result = result.astype(jnp.bfloat16)
        for k in range(len(starts)):
            out_ref[:, (at + k) * BLOCK : (at + k + 1) * BLOCK] = result[
                k * count : (k + 1) * count, :
            ]


def bf16(*shape):
    return jax.ShapeDtypeStruct(shape, jnp.bfloat16)


def f32(*shape):
    return jax.ShapeDtypeStruct(shape, jnp.float32)


def chunk_plan(cols, reach):
    assert cols >= 4 * reach and reach % (4 * BLOCK) == 0
    first, second = reach + BLOCK, 2 * reach
    third = second + (cols - 2 * reach) * 3 // 8
    return [(first, second - first), (second, third - second), (third, cols - third), (0, first)]


def on_device(projections, filter_taps, row_first, interp_index, interp_frac):
    angles, rows, cols = projections.shape
    depth = interp_index.shape[2]
    taps = filter_taps.shape[0]
    reach = taps // 2
    length = taps + BLOCK
    margin = rows // 2
    slabs, line, sides = (lax.axis_size(n) for n in ("slab", "angle", "col"))
    scale = math.pi / (angles * line)
    both = slabs == 2
    halos = 1 if both else 2
    quick = line == 4
    shard = depth // line
    order = LINE_ORDER if quick else (tuple(range(line)),) * line
    total_rows, total_cols = rows * slabs, cols * sides
    chunks = chunk_plan(cols, reach)
    widths = [w for _, w in chunks]
    part = angles * margin
    sizes = (total_rows, total_cols, margin)

    def half_rows(slab):
        if both:
            return jnp.where(slab == 0, margin, 0), jnp.where(slab == 0, 0, margin)
        return margin, 0

    def aligned(row):
        return row if isinstance(row, int) else pl.multiple_of(row, margin)

    start, width = chunks[0]
    window_at, window = start - reach, width + 2 * reach
    early = halos

    def window_kernel(proj_ref, weighted_ref, edge_ref, raw_ref, factor_ref, sem):
        slab = lax.axis_index("slab")
        col = lax.axis_index("col")
        starts = [aligned(r) for r in half_rows(slab)][:early]
        copies = [
            pltpu.make_async_copy(
                proj_ref.at[a, pl.ds(r, margin), pl.ds(window_at, window)],
                raw_ref.at[a, pl.ds(r, margin), :],
                sem.at[a * 2 + h],
            )
            for a in range(angles)
            for h, r in enumerate(starts)
        ]
        edge_col = pl.multiple_of(jnp.where(col == 0, cols - reach, 0), TILE)
        edge_copy = pltpu.make_async_copy(
            proj_ref.at[:, :, pl.ds(edge_col, reach)], edge_ref, sem.at[2 * angles]
        )
        for copy in copies:
            copy.start()
        edge_copy.start()
        for half, r in enumerate(starts):
            for c in range(0, window, BLOCK):
                factor_ref[half, :, c : c + BLOCK] = cosine_factor(
                    slab * rows + r, col * cols + window_at + c, sizes
                )
        for a in range(angles):
            for half, r in enumerate(starts):
                copies[a * early + half].wait()
                at = (half * angles + a) * margin
                for c in range(0, window, BLOCK):
                    cut = slice(c, c + BLOCK)
                    raw = raw_ref[a, pl.ds(r, margin), cut].astype(jnp.float32)
                    weighted_ref[at : at + margin, cut] = (
                        raw * factor_ref[half, :, cut]
                    ).astype(jnp.bfloat16)
        edge_copy.wait()

    ahead, edge = kernel_call(
        window_kernel,
        [bf16(early * part, window), bf16(angles, rows, reach)],
        (projections,),
        early * part * window * 4,
        scratch=[
            pltpu.VMEM((angles, rows, window), jnp.bfloat16),
            pltpu.VMEM((early, margin, window), jnp.float32),
            pltpu.SemaphoreType.DMA((2 * angles + 1,)),
        ],
        name="first_window",
        specs=[HELD],
        grant=FIRST_VMEM_BYTES,
    )

    def first_kernel(weighted_ref, taps_ref, band_ref, *outs):
        build_band(taps_ref, band_ref)

        def weighted_at(half, c):
            at = c - window_at
            return lambda: weighted_ref[half * part : (half + 1) * part, at : at + BLOCK]

        work = [(h, start, width, out_ref) for h, out_ref in enumerate(outs)]
        filter_columns(work, part, band_ref, weighted_at)

    band, *first_out = kernel_call(
        first_kernel,
        [bf16(length, BLOCK)] + [bf16(part, width)] * early,
        (ahead, filter_taps.reshape(taps // TILE, TILE)),
        2 * early * part * length * width,
        name="first_columns",
    )

    up = [(i, (i + 1) % slabs) for i in range(slabs - 1)]
    down = [(j, i) for i, j in up]

    def exchange(sends):
        if both:
            return [lax.ppermute(sends[0], "slab", up + down)]
        return [lax.ppermute(sends[0], "slab", up), lax.ppermute(sends[1], "slab", down)]

    assert sides == 2
    received = lax.ppermute(edge, "col", [(0, 1), (1, 0)])
    halo_rows = [exchange(first_out)]

    def write_weights(first_ref, index_ref, frac_ref, own_ref, halo_ref):
        slab = lax.axis_index("slab")
        angle = lax.axis_index("angle")
        if both:
            bases = [jnp.where(slab == 0, rows, rows - margin)]
        else:
            bases = [slab * rows - margin, (slab + 1) * rows]

        def weights(a, base):
            slot = lax.broadcasted_iota(jnp.int32, (margin, depth), 0) + base
            position = index_ref[a] + first_ref[a]
            frac = frac_ref[a]
            high = frac.astype(jnp.bfloat16).astype(jnp.float32)
            low = (1.0 - frac).astype(jnp.bfloat16).astype(jnp.float32)
            return jnp.where(slot == position, low, 0.0) + jnp.where(slot == position + 1, high, 0.0)

        here = [slab * rows + r for r in half_rows(slab)]
        for starts, ref in ((here, own_ref), (bases, halo_ref)):
            table = jnp.concatenate([weights(a, b) for b in starts for a in range(angles)], axis=0)
            turned = table.T.astype(jnp.bfloat16)
            for s in range(line):
                if quick:
                    places = [o.index(s) for o in order]
                    place = places[line - 1]
                    for i in range(line - 1):
                        place = jnp.where(angle == i, places[i], place)
                    at = pl.multiple_of(place * shard, shard)
                else:
                    at = s * shard
                ref[pl.ds(at, shard), :] = turned[s * shard : (s + 1) * shard, :]

    def filter_here(refs, work, band_ref):
        proj_ref, received_ref, weighted_ref, halo_cols_ref = refs
        slab = lax.axis_index("slab")
        col = lax.axis_index("col")
        starts = [aligned(r) for r in half_rows(slab)]
        lower = col == 0
        from_col = jnp.where(lower, cols, col * cols - reach)
        none = jnp.zeros((part, BLOCK), jnp.bfloat16)
        known = set()

        def weighted_at(half, c):
            inside = 0 <= c < cols
            source, into = (proj_ref, weighted_ref) if inside else (received_ref, halo_cols_ref)
            first_col = col * cols if inside else from_col
            at = c if inside else c % reach
            if (half, at, inside) not in known:
                known.add((half, at, inside))
                weigh(source, into, half, starts[half], slab * rows, first_col, sizes, at)

            def load():
                block = into[half * part : (half + 1) * part, at : at + BLOCK]
                if c < 0:
                    block = jnp.where(lower, none, block)
                elif c >= cols:
                    block = jnp.where(lower, block, none)
                return block

            return load

        filter_columns(work, part, band_ref, weighted_at)

    scratch = [pltpu.VMEM((2 * part, n), jnp.bfloat16) for n in (cols, reach)]

    work = [(1, *chunks[0])][: 2 - early]
    work += [(half, *chunk) for chunk in chunks[1:-1] for half in (0, 1)]

    def second_kernel(proj_ref, received_ref, band_ref, first_ref, index_ref, frac_ref,
                      own_ref, halo_ref, *rest):
        outs = [(*w, ref) for w, ref in zip(work, rest)]
        filter_here((proj_ref, received_ref, *rest[-2:]), outs, band_ref)
        write_weights(first_ref, index_ref, frac_ref, own_ref, halo_ref)

    own_weight, halo_weight, *second_out = kernel_call(
        second_kernel,
        [bf16(depth, 2 * part), bf16(depth, halos * part)] + [bf16(part, w[2]) for w in work],
        (projections, received, band, row_first[:, 0], interp_index, interp_frac),
        2 * part * length * sum(w[2] for w in work),
        scratch=scratch,
        name="other_columns",
        specs=[VMEM, VMEM, VMEM, SMEM, VMEM, VMEM],
    )

    def last_kernel(proj_ref, received_ref, taps_ref, *rest):
        *outs, band_ref, weighted_ref, halo_cols_ref = rest
        build_band(taps_ref, band_ref)
        filter_here(
            (proj_ref, received_ref, weighted_ref, halo_cols_ref),
            [(half, *chunks[-1], ref) for half, ref in enumerate(outs)],
            band_ref,
        )

    before = second_out[-2:]
    *last_out, before[0] = kernel_call(
        last_kernel,
        [bf16(part, widths[-1])] * 2,
        (projections, received, filter_taps.reshape(taps // TILE, TILE)),
        4 * part * length * widths[-1],
        scratch=[pltpu.VMEM((length, BLOCK), jnp.bfloat16)] + scratch,
        name="last_columns",
        carried=before[:1],
    )
    second_out = [*second_out[:-2], *before, *last_out]
    filtered = [(*first_out, *second_out[: 2 - early])]
    for at in range(2 - early, len(second_out), 2):
        filtered.append(second_out[at : at + 2])
        halo_rows.append(exchange(second_out[at : at + halos]))

    def project(index, after=()):
        width = widths[index]

        def body(own_ref, halo_ref, *rest):
            sources, outs = rest[: 2 + halos], rest[2 + halos + len(after) :]
            for c in range(0, width, BLOCK):
                cut = slice(c, c + BLOCK)
                own = jnp.concatenate([ref[:, cut] for ref in sources[:2]], axis=0)
                other = [ref[:, cut] for ref in sources[2:]]
                other = other[0] if len(other) == 1 else jnp.concatenate(other, axis=0)
                total = jnp.dot(own_ref[...], own, preferred_element_type=jnp.float32)
                total += jnp.dot(halo_ref[...], other, preferred_element_type=jnp.float32)
                total = total * scale
                at = 0
                for out in outs:
                    out[:, cut] = total[at : at + out.shape[0], :].astype(out.dtype)
                    at += out.shape[0]

        if quick:
            first = [bf16(shard, width)] * 2 if DIRECT[index] else [bf16(2 * shard, width)]
            shapes = [*first, bf16(shard, width), f32(shard, width)]
        else:
            shapes = [f32(depth, width)]
        return kernel_call(
            body,
            shapes,
            (own_weight, halo_weight, *filtered[index], *halo_rows[index], *after),
            2 * depth * (2 + halos) * part * width,
            name="interpolate",
            specs=[VMEM] * (4 + halos) + [HELD] * len(after),
        )

    def widen(x):
        return x.astype(jnp.float32)

    def at_end():
        angle = lax.axis_index("angle")
        return (angle == 0) | (angle == line - 1)

    neighbours = [(0, 1), (1, 0), (2, 3), (3, 2)]
    middles = [(1, 2), (2, 1), (0, 0), (3, 3)]
    second_hop = [(0, 1), (1, 3), (2, 0), (3, 2)]
    straight = [(0, 2), (3, 1), (1, 0), (2, 3)]

    def first_hops(*parts):
        if len(parts) == 1:
            return [lax.ppermute(parts[0], "angle", neighbours)]
        near, middle = parts
        two = lax.ppermute(middle, "angle", straight)
        three = lax.ppermute(middle, "angle", middles)
        one = lax.ppermute(near, "angle", neighbours)
        return [one, three, two]

    def relay(sent, own, far, kept, after=(), weight=1, soon=False):
        direct = len(sent) == 3
        arrived = sent[: 1 if soon else 2] if direct else [sent[0], own[0]]
        extra = len(arrived) - 1

        def body(one_ref, *rest):
            other_ref = rest[0]
            far_ref, kept_ref = rest[extra : extra + 2]
            outs = rest[extra + 2 + len(after) :]
            end = at_end()
            near = widen(one_ref[:shard, :])
            relayed = widen(far_ref[...]) + jnp.where(end, 0.0, near)
            outs[0][...] = relayed.astype(jnp.bfloat16)
            if soon:
                outs[1][...] = kept_ref[...] + jnp.where(end, near, 0.0)
            elif direct:
                outs[1][...] = kept_ref[...] + jnp.where(end, near, widen(other_ref[...]))
            else:
                outs[1][...] = kept_ref[...] + jnp.where(end, near, 0.0)
                crossed = widen(one_ref[shard:, :]) + widen(other_ref[shard:, :])
                outs[2][...] = crossed.astype(jnp.bfloat16)

        relayed, partial, *crossed = kernel_call(
            body,
            [bf16(*far.shape), f32(*kept.shape)] + [bf16(*far.shape)] * (not direct),
            (*arrived, far, kept, *after),
            far.size * 2 * weight,
            name="relay",
            specs=[VMEM] * (3 + extra) + [HELD] * len(after),
        )
        four = lax.ppermute(relayed, "angle", second_hop)
        three = sent[2] if direct else lax.ppermute(crossed[0], "angle", middles)
        return (partial, four, three, *([sent[1]] if soon else []))

    def total(partial_ref, four_ref, *fillers):
        direct = sum(widen(ref[...]) for ref in fillers)
        return partial_ref[...] + widen(four_ref[...]) + jnp.where(at_end(), 0.0, direct)

    def mark(array, weight):
        def body(array_ref, out_ref):
            out_ref[...] = jnp.zeros_like(out_ref)

        return kernel_call(body, [f32(8, TILE)], (array,), weight, name="mark", specs=[HELD])[0]

    def finish(pieces, weight=1, after=()):
        def body(*refs):
            refs[-1][...] = total(*refs[: len(pieces)])

        return kernel_call(
            body,
            [f32(*pieces[0].shape)],
            (*pieces, *after),
            pieces[0].size * 2 * weight,
            name="finish",
            specs=[VMEM] * len(pieces) + [HELD] * len(after),
        )[0]

    def store(done, pieces, index, volume=None, weight=1, after=()):
        given = [*done, *pieces]
        held = [*after, *([] if volume is None else [volume])]

        def body(*refs):
            ready, refs = refs[: len(done)], refs[len(done) :]
            volume_ref, total_ref, sem = refs[-3:]

            def copy(i, source):
                at = pl.ds(chunks[i][0], chunks[i][1])
                return pltpu.make_async_copy(source, volume_ref.at[:, at], sem.at[i])

            copies = [copy(i, ref) for i, ref in enumerate(ready)]
            for c in copies:
                c.start()
            total_ref[...] = total(*refs[: len(pieces)])
            copies.append(copy(index, total_ref))
            copies[-1].start()
            for c in copies:
                c.wait()

        size = shard * widths[index]
        return pl.pallas_call(
            body,
            out_shape=f32(shard, cols),
            in_specs=[VMEM] * len(given) + [HELD] * len(held),
            out_specs=HELD,
            input_output_aliases={} if volume is None else {len(given) + len(after): 0},
            scratch_shapes=[
                pltpu.VMEM((shard, widths[index]), jnp.float32),
                pltpu.SemaphoreType.DMA((len(chunks),)),
            ],
            compiler_params=pltpu.CompilerParams(vmem_limit_bytes=VMEM_BYTES),
            cost_estimate=pl.CostEstimate(
                flops=size * 2 * weight, bytes_accessed=size * 4, transcendentals=0
            ),
            name="store",
        )(*given, *held)

    if not quick:
        sums = [
            lax.psum_scatter(project(i)[0], "angle", scatter_dimension=0, tiled=True)
            for i in range(len(chunks))
        ]
        return jnp.concatenate([sums[i] for i in sorted(range(len(chunks)), key=chunks.__getitem__)], 1)

    last = len(chunks) - 1
    *own, far, kept = project(0)
    sent = first_hops(*own)
    done, pieces = [], []
    for j in range(last + 1):
        here = (sent, own, far, kept)
        after = sent[2:] if j == 0 else []
        if j < last:
            earlier = [p[0] for p in pieces[-1:]] if j else [last_out[-1]]
            *own, far, kept = project(j + 1, after=earlier)
            sent = first_hops(*own)
            after = [*after, kept]
            if j:
                done.append(finish(pieces[-1], weight=FINISH_WEIGHTS[j - 1], after=[kept]))
                after.append(done[-1])
        pieces.append(relay(*here, after=after, weight=WEIGHTS[j], soon=SOON[j]))
    swap = [mark(sent[1], MARK)] if SOON[last] else []
    volume = store(done, pieces[last - 1], last - 1, weight=FINISH_WEIGHTS[last - 1], after=swap)
    return store([], pieces[last], last, volume)


def solution(mesh):
    placed = (
        P(("group", "angle"), "slab", "col"),
        P(),
        P(("group", "angle"), "slab"),
        P(("group", "angle"), "slab", None),
        P(("group", "angle"), "slab", None),
    )
    return jax.shard_map(
        on_device,
        mesh=mesh,
        in_specs=placed,
        out_specs=P(("group", "slab", "angle"), "col"),
        check_vma=False,
    )
```

```python
import math

import jax
import jax.numpy as jnp
from jax import lax
from jax.experimental import pallas as pl
from jax.experimental.pallas import tpu as pltpu
from jax.sharding import PartitionSpec as P

BLOCK = 256
TILE = 128
STACK = 8
DIRECT = (False, False, False, True)
SOON = (False, False, False, True)
WEIGHTS = (40000, 28000, 1, 1)
FINISH_WEIGHTS = (1, 1, 10000)
MARK = 1000000000
VMEM_BYTES = 14 * 1024 * 1024
FIRST_VMEM_BYTES = 104 * 512 * 1024
LINE_ORDER = ((3, 2, 1, 0), (0, 2, 3, 1), (3, 1, 0, 2), (0, 1, 2, 3))

VMEM = pl.BlockSpec(memory_space=pltpu.VMEM)
HELD = pl.BlockSpec(memory_space=pltpu.HBM)
SMEM = pl.BlockSpec(memory_space=pltpu.SMEM)


def kernel_call(
    body, out_shape, args, flops, scratch=(), name=None, specs=None, grant=VMEM_BYTES, carried=()
):
    specs = specs or [VMEM] * len(args)
    moved = sum(a.size * a.dtype.itemsize for a in (*args, *out_shape))
    n_in, n_out, n_through = len(args), len(out_shape), len(carried)

    def kernel(*refs):
        ins, refs = refs[:n_in], refs[n_in + n_through :]
        body(*ins, *refs[:n_out], *refs[n_out + n_through :])

    return pl.pallas_call(
        kernel,
        out_shape=[*out_shape, *(jax.ShapeDtypeStruct(c.shape, c.dtype) for c in carried)],
        in_specs=[*specs, *([HELD] * n_through)],
        out_specs=[VMEM] * n_out + [HELD] * n_through,
        input_output_aliases={n_in + i: n_out + i for i in range(n_through)},
        scratch_shapes=list(scratch),
        compiler_params=pltpu.CompilerParams(vmem_limit_bytes=grant),
        cost_estimate=pl.CostEstimate(flops=flops, bytes_accessed=moved, transcendentals=0),
        name=name,
    )(*args, *carried)


def build_band(taps_ref, band_ref):
    count = taps_ref.shape[0]
    steps, tiles = band_ref.shape[1] // TILE, band_ref.shape[0] // TILE
    zero = jnp.zeros((TILE, TILE), jnp.float32)
    ahead = lax.broadcasted_iota(jnp.int32, (TILE, TILE), 1) >= lax.broadcasted_iota(
        jnp.int32, (TILE, TILE), 0
    )
    taps = taps_ref[...].astype(jnp.float32)

    def shifted(d):
        if not 0 <= d < count:
            return zero
        row = jnp.broadcast_to(taps[d : d + 1, :], (TILE, TILE))
        return pltpu.roll(row, 0, 1, stride=1, stride_axis=0)

    before = zero
    for d in range(-(steps - 1), tiles):
        here = shifted(d)
        block = jnp.where(ahead, here, before).T.astype(jnp.bfloat16)
        before = here
        for c in range(steps):
            if 0 <= d + c < tiles:
                band_ref[(d + c) * TILE : (d + c + 1) * TILE, c * TILE : (c + 1) * TILE] = block


def cosine_factor(row_start, col_start, sizes):
    total_rows, total_cols, count = sizes
    distance = jnp.float32(total_cols)
    v = lax.broadcasted_iota(jnp.int32, (count, 1), 0) + row_start
    v = v.astype(jnp.float32) - total_rows / 2 + 0.5
    u = lax.broadcasted_iota(jnp.int32, (1, BLOCK), 1) + col_start
    u = u.astype(jnp.float32) - total_cols / 2 + 0.5
    return distance / jnp.sqrt(distance * distance + u * u + v * v)


def weigh(proj_ref, weighted_ref, half, row_at, row_start, col_start, sizes, c):
    angles, count = proj_ref.shape[0], sizes[2]
    factor = cosine_factor(row_start + row_at, col_start + c, sizes)
    for a in range(angles):
        raw = proj_ref[a, pl.ds(row_at, count), c : c + BLOCK].astype(jnp.float32)
        at = (half * angles + a) * count
        weighted_ref[at : at + count, c : c + BLOCK] = (raw * factor).astype(jnp.bfloat16)


def filter_columns(work, count, band_ref, weighted_at):
    length = band_ref.shape[0]
    reach = (length - BLOCK) // 2
    groups = []
    for half, first, width, out_ref in work:
        starts = range(first, first + width, BLOCK)
        for at in range(0, len(starts), STACK):
            groups.append((half, starts[at : at + STACK], out_ref, at))

    def touch(index):
        if index < len(groups):
            half, starts, _, _ = groups[index]
            for c in range(starts[0] - reach, starts[-1] + BLOCK + reach, BLOCK):
                weighted_at(half, c)

    touch(0)
    for index, (half, starts, out_ref, at) in enumerate(groups):
        touch(index + 1)
        tall = jnp.concatenate(
            [
                jnp.concatenate(
                    [weighted_at(half, c)() for c in range(s - reach, s + BLOCK + reach, BLOCK)],
                    axis=1,
                )
                for s in starts
            ],
            axis=0,
        )
        result = jnp.dot(tall, band_ref[...], preferred_element_type=jnp.float32)
        result = result.astype(jnp.bfloat16)
        for k in range(len(starts)):
            out_ref[:, (at + k) * BLOCK : (at + k + 1) * BLOCK] = result[
                k * count : (k + 1) * count, :
            ]


def bf16(*shape):
    return jax.ShapeDtypeStruct(shape, jnp.bfloat16)


def f32(*shape):
    return jax.ShapeDtypeStruct(shape, jnp.float32)


def chunk_plan(cols, reach):
    assert cols >= 4 * reach and reach % (4 * BLOCK) == 0
    first, second = reach + BLOCK, 2 * reach
    third = second + (cols - 2 * reach) * 3 // 8
    return [(first, second - first), (second, third - second), (third, cols - third), (0, first)]


def on_device(projections, filter_taps, row_first, interp_index, interp_frac):
    angles, rows, cols = projections.shape
    depth = interp_index.shape[2]
    taps = filter_taps.shape[0]
    reach = taps // 2
    length = taps + BLOCK
    margin = rows // 2
    slabs, line, sides = (lax.axis_size(n) for n in ("slab", "angle", "col"))
    scale = math.pi / (angles * line)
    both = slabs == 2
    halos = 1 if both else 2
    quick = line == 4
    shard = depth // line
    order = LINE_ORDER if quick else (tuple(range(line)),) * line
    total_rows, total_cols = rows * slabs, cols * sides
    chunks = chunk_plan(cols, reach)
    widths = [w for _, w in chunks]
    part = angles * margin
    sizes = (total_rows, total_cols, margin)

    def half_rows(slab):
        if both:
            return jnp.where(slab == 0, margin, 0), jnp.where(slab == 0, 0, margin)
        return margin, 0

    def aligned(row):
        return row if isinstance(row, int) else pl.multiple_of(row, margin)

    start, width = chunks[0]
    window_at, window = start - reach, width + 2 * reach
    early = halos

    def window_kernel(proj_ref, weighted_ref, edge_ref, raw_ref, factor_ref, sem):
        slab = lax.axis_index("slab")
        col = lax.axis_index("col")
        starts = [aligned(r) for r in half_rows(slab)][:early]
        copies = [
            pltpu.make_async_copy(
                proj_ref.at[a, pl.ds(r, margin), pl.ds(window_at, window)],
                raw_ref.at[a, pl.ds(r, margin), :],
                sem.at[a * 2 + h],
            )
            for a in range(angles)
            for h, r in enumerate(starts)
        ]
        edge_col = pl.multiple_of(jnp.where(col == 0, cols - reach, 0), TILE)
        edge_copy = pltpu.make_async_copy(
            proj_ref.at[:, :, pl.ds(edge_col, reach)], edge_ref, sem.at[2 * angles]
        )
        for copy in copies:
            copy.start()
        edge_copy.start()
        for half, r in enumerate(starts):
            for c in range(0, window, BLOCK):
                factor_ref[half, :, c : c + BLOCK] = cosine_factor(
                    slab * rows + r, col * cols + window_at + c, sizes
                )
        for a in range(angles):
            for half, r in enumerate(starts):
                copies[a * early + half].wait()
                at = (half * angles + a) * margin
                for c in range(0, window, BLOCK):
                    cut = slice(c, c + BLOCK)
                    raw = raw_ref[a, pl.ds(r, margin), cut].astype(jnp.float32)
                    weighted_ref[at : at + margin, cut] = (
                        raw * factor_ref[half, :, cut]
                    ).astype(jnp.bfloat16)
        edge_copy.wait()

    ahead, edge = kernel_call(
        window_kernel,
        [bf16(early * part, window), bf16(angles, rows, reach)],
        (projections,),
        early * part * window * 4,
        scratch=[
            pltpu.VMEM((angles, rows, window), jnp.bfloat16),
            pltpu.VMEM((early, margin, window), jnp.float32),
            pltpu.SemaphoreType.DMA((2 * angles + 1,)),
        ],
        name="first_window",
        specs=[HELD],
        grant=FIRST_VMEM_BYTES,
    )

    def first_kernel(weighted_ref, taps_ref, band_ref, *outs):
        build_band(taps_ref, band_ref)

        def weighted_at(half, c):
            at = c - window_at
            return lambda: weighted_ref[half * part : (half + 1) * part, at : at + BLOCK]

        work = [(h, start, width, out_ref) for h, out_ref in enumerate(outs)]
        filter_columns(work, part, band_ref, weighted_at)

    band, *first_out = kernel_call(
        first_kernel,
        [bf16(length, BLOCK)] + [bf16(part, width)] * early,
        (ahead, filter_taps.reshape(taps // TILE, TILE)),
        2 * early * part * length * width,
        name="first_columns",
    )

    up = [(i, (i + 1) % slabs) for i in range(slabs - 1)]
    down = [(j, i) for i, j in up]

    def exchange(sends):
        if both:
            return [lax.ppermute(sends[0], "slab", up + down)]
        return [lax.ppermute(sends[0], "slab", up), lax.ppermute(sends[1], "slab", down)]

    assert sides == 2
    received = lax.ppermute(edge, "col", [(0, 1), (1, 0)])
    halo_rows = [exchange(first_out)]

    def write_weights(first_ref, index_ref, frac_ref, own_ref, halo_ref):
        slab = lax.axis_index("slab")
        angle = lax.axis_index("angle")
        if both:
            bases = [jnp.where(slab == 0, rows, rows - margin)]
        else:
            bases = [slab * rows - margin, (slab + 1) * rows]

        def weights(a, base):
            slot = lax.broadcasted_iota(jnp.int32, (margin, depth), 0) + base
            position = index_ref[a] + first_ref[a]
            frac = frac_ref[a]
            high = frac.astype(jnp.bfloat16).astype(jnp.float32)
            low = (1.0 - frac).astype(jnp.bfloat16).astype(jnp.float32)
            return jnp.where(slot == position, low, 0.0) + jnp.where(slot == position + 1, high, 0.0)

        here = [slab * rows + r for r in half_rows(slab)]
        for starts, ref in ((here, own_ref), (bases, halo_ref)):
            table = jnp.concatenate([weights(a, b) for b in starts for a in range(angles)], axis=0)
            turned = table.T.astype(jnp.bfloat16)
            for s in range(line):
                if quick:
                    places = [o.index(s) for o in order]
                    place = places[line - 1]
                    for i in range(line - 1):
                        place = jnp.where(angle == i, places[i], place)
                    at = pl.multiple_of(place * shard, shard)
                else:
                    at = s * shard
                ref[pl.ds(at, shard), :] = turned[s * shard : (s + 1) * shard, :]

    def filter_here(refs, work, band_ref):
        proj_ref, received_ref, weighted_ref, halo_cols_ref = refs
        slab = lax.axis_index("slab")
        col = lax.axis_index("col")
        starts = [aligned(r) for r in half_rows(slab)]
        lower = col == 0
        from_col = jnp.where(lower, cols, col * cols - reach)
        none = jnp.zeros((part, BLOCK), jnp.bfloat16)
        known = set()

        def weighted_at(half, c):
            inside = 0 <= c < cols
            source, into = (proj_ref, weighted_ref) if inside else (received_ref, halo_cols_ref)
            first_col = col * cols if inside else from_col
            at = c if inside else c % reach
            if (half, at, inside) not in known:
                known.add((half, at, inside))
                weigh(source, into, half, starts[half], slab * rows, first_col, sizes, at)

            def load():
                block = into[half * part : (half + 1) * part, at : at + BLOCK]
                if c < 0:
                    block = jnp.where(lower, none, block)
                elif c >= cols:
                    block = jnp.where(lower, block, none)
                return block

            return load

        filter_columns(work, part, band_ref, weighted_at)

    scratch = [pltpu.VMEM((2 * part, n), jnp.bfloat16) for n in (cols, reach)]

    work = [(1, *chunks[0])][: 2 - early]
    work += [(half, *chunk) for chunk in chunks[1:-1] for half in (0, 1)]

    def second_kernel(proj_ref, received_ref, band_ref, first_ref, index_ref, frac_ref,
                      own_ref, halo_ref, *rest):
        outs = [(*w, ref) for w, ref in zip(work, rest)]
        filter_here((proj_ref, received_ref, *rest[-2:]), outs, band_ref)
        write_weights(first_ref, index_ref, frac_ref, own_ref, halo_ref)

    own_weight, halo_weight, *second_out = kernel_call(
        second_kernel,
        [bf16(depth, 2 * part), bf16(depth, halos * part)] + [bf16(part, w[2]) for w in work],
        (projections, received, band, row_first[:, 0], interp_index, interp_frac),
        2 * part * length * sum(w[2] for w in work),
        scratch=scratch,
        name="other_columns",
        specs=[VMEM, VMEM, VMEM, SMEM, VMEM, VMEM],
    )

    def last_kernel(proj_ref, received_ref, taps_ref, *rest):
        *outs, band_ref, weighted_ref, halo_cols_ref = rest
        build_band(taps_ref, band_ref)
        filter_here(
            (proj_ref, received_ref, weighted_ref, halo_cols_ref),
            [(half, *chunks[-1], ref) for half, ref in enumerate(outs)],
            band_ref,
        )

    before = second_out[-2:]
    *last_out, before[0] = kernel_call(
        last_kernel,
        [bf16(part, widths[-1])] * 2,
        (projections, received, filter_taps.reshape(taps // TILE, TILE)),
        4 * part * length * widths[-1],
        scratch=[pltpu.VMEM((length, BLOCK), jnp.bfloat16)] + scratch,
        name="last_columns",
        carried=before[:1],
    )
    second_out = [*second_out[:-2], *before, *last_out]
    filtered = [(*first_out, *second_out[: 2 - early])]
    for at in range(2 - early, len(second_out), 2):
        filtered.append(second_out[at : at + 2])
        halo_rows.append(exchange(second_out[at : at + halos]))

    def project(index, after=()):
        width = widths[index]

        def body(own_ref, halo_ref, *rest):
            sources, outs = rest[: 2 + halos], rest[2 + halos + len(after) :]
            for c in range(0, width, BLOCK):
                cut = slice(c, c + BLOCK)
                own = jnp.concatenate([ref[:, cut] for ref in sources[:2]], axis=0)
                other = [ref[:, cut] for ref in sources[2:]]
                other = other[0] if len(other) == 1 else jnp.concatenate(other, axis=0)
                total = jnp.dot(own_ref[...], own, preferred_element_type=jnp.float32)
                total += jnp.dot(halo_ref[...], other, preferred_element_type=jnp.float32)
                total = total * scale
                at = 0
                for i, out in enumerate(outs):
                    if len(outs) == 5 and i == 2:
                        at -= out.shape[0]
                    out[:, cut] = total[at : at + out.shape[0], :].astype(out.dtype)
                    at += out.shape[0]

        if quick:
            first = [bf16(shard, width)] * 2 if DIRECT[index] else [bf16(2 * shard, width)]
            again = [bf16(shard, width)] * SOON[index]
            shapes = [*first, *again, bf16(shard, width), f32(shard, width)]
        else:
            shapes = [f32(depth, width)]
        return kernel_call(
            body,
            shapes,
            (own_weight, halo_weight, *filtered[index], *halo_rows[index], *after),
            2 * depth * (2 + halos) * part * width,
            name="interpolate",
            specs=[VMEM] * (4 + halos) + [HELD] * len(after),
        )

    def widen(x):
        return x.astype(jnp.float32)

    def at_end():
        angle = lax.axis_index("angle")
        return (angle == 0) | (angle == line - 1)

    neighbours = [(0, 1), (1, 0), (2, 3), (3, 2)]
    middles = [(1, 2), (2, 1), (0, 0), (3, 3)]
    second_hop = [(0, 1), (1, 3), (2, 0), (3, 2)]
    straight = [(0, 2), (3, 1), (1, 0), (2, 3)]

    def first_hops(*parts):
        if len(parts) == 1:
            return [lax.ppermute(parts[0], "angle", neighbours)]
        near, middle, *later = parts
        two = [] if later else [lax.ppermute(middle, "angle", straight)]
        three = lax.ppermute(middle, "angle", middles)
        one = lax.ppermute(near, "angle", neighbours)
        return [one, three, *two]

    def relay(sent, own, far, kept, after=(), weight=1, soon=False):
        direct = len(sent) > 1
        arrived = sent[: 1 if soon else 2] if direct else [sent[0], own[0]]
        later = own[2:]
        extra = len(arrived) - 1

        def body(one_ref, *rest):
            other_ref = rest[0]
            far_ref, kept_ref = rest[extra : extra + 2]
            outs = rest[extra + 2 + len(after) :]
            end = at_end()
            near = widen(one_ref[:shard, :])
            relayed = widen(far_ref[...]) + jnp.where(end, 0.0, near)
            outs[0][...] = relayed.astype(jnp.bfloat16)
            if soon:
                outs[1][...] = kept_ref[...] + jnp.where(end, near, 0.0)
            elif direct:
                outs[1][...] = kept_ref[...] + jnp.where(end, near, widen(other_ref[...]))
            else:
                outs[1][...] = kept_ref[...] + jnp.where(end, near, 0.0)
                crossed = widen(one_ref[shard:, :]) + widen(other_ref[shard:, :])
                outs[2][...] = crossed.astype(jnp.bfloat16)

        relayed, partial, *others = kernel_call(
            body,
            [bf16(*far.shape), f32(*kept.shape)] + [bf16(*far.shape)] * (not direct),
            (*arrived, far, kept, *after),
            far.size * 2 * weight,
            name="relay",
            specs=[VMEM] * (3 + extra) + [HELD] * len(after),
            carried=later,
        )
        four = lax.ppermute(relayed, "angle", second_hop)
        if not direct:
            return partial, four, lax.ppermute(others[0], "angle", middles)
        two = lax.ppermute(others[0], "angle", straight[:2]) if later else sent[2]
        return (partial, four, two, *([sent[1]] if soon else []))

    def total(partial_ref, four_ref, *fillers):
        direct = sum(widen(ref[...]) for ref in fillers)
        return partial_ref[...] + widen(four_ref[...]) + jnp.where(at_end(), 0.0, direct)

    def mark(array, weight):
        def body(array_ref, out_ref):
            out_ref[...] = jnp.zeros_like(out_ref)

        return kernel_call(body, [f32(8, TILE)], (array,), weight, name="mark", specs=[HELD])[0]

    def finish(pieces, weight=1, after=()):
        def body(*refs):
            refs[-1][...] = total(*refs[: len(pieces)])

        return kernel_call(
            body,
            [f32(*pieces[0].shape)],
            (*pieces, *after),
            pieces[0].size * 2 * weight,
            name="finish",
            specs=[VMEM] * len(pieces) + [HELD] * len(after),
        )[0]

    def store(done, pieces, index, volume=None, weight=1, after=()):
        given = [*done, *pieces]
        held = [*after, *([] if volume is None else [volume])]

        def body(*refs):
            ready, refs = refs[: len(done)], refs[len(done) :]
            volume_ref, total_ref, sem = refs[-3:]

            def copy(i, source):
                at = pl.ds(chunks[i][0], chunks[i][1])
                return pltpu.make_async_copy(source, volume_ref.at[:, at], sem.at[i])

            copies = [copy(i, ref) for i, ref in enumerate(ready)]
            for c in copies:
                c.start()
            total_ref[...] = total(*refs[: len(pieces)])
            copies.append(copy(index, total_ref))
            copies[-1].start()
            for c in copies:
                c.wait()

        size = shard * widths[index]
        return pl.pallas_call(
            body,
            out_shape=f32(shard, cols),
            in_specs=[VMEM] * len(given) + [HELD] * len(held),
            out_specs=HELD,
            input_output_aliases={} if volume is None else {len(given) + len(after): 0},
            scratch_shapes=[
                pltpu.VMEM((shard, widths[index]), jnp.float32),
                pltpu.SemaphoreType.DMA((len(chunks),)),
            ],
            compiler_params=pltpu.CompilerParams(vmem_limit_bytes=VMEM_BYTES),
            cost_estimate=pl.CostEstimate(
                flops=size * 2 * weight, bytes_accessed=size * 4, transcendentals=0
            ),
            name="store",
        )(*given, *held)

    if not quick:
        sums = [
            lax.psum_scatter(project(i)[0], "angle", scatter_dimension=0, tiled=True)
            for i in range(len(chunks))
        ]
        return jnp.concatenate([sums[i] for i in sorted(range(len(chunks)), key=chunks.__getitem__)], 1)

    last = len(chunks) - 1
    *own, far, kept = project(0)
    sent = first_hops(*own)
    done, pieces = [], []
    for j in range(last + 1):
        here = (sent, own, far, kept)
        after = sent[2:] if j == 0 else []
        if j < last:
            earlier = [p[0] for p in pieces[-1:]] if j else [last_out[-1]]
            *own, far, kept = project(j + 1, after=earlier)
            sent = first_hops(*own)
            after = [*after, kept]
            if j:
                done.append(finish(pieces[-1], weight=FINISH_WEIGHTS[j - 1], after=[kept]))
                after.append(done[-1])
        pieces.append(relay(*here, after=after, weight=WEIGHTS[j], soon=SOON[j]))
    swap = [mark(sent[1], MARK)] if SOON[last] else []
    volume = store(done, pieces[last - 1], last - 1, weight=FINISH_WEIGHTS[last - 1], after=swap)
    return store([], pieces[last], last, volume)


def solution(mesh):
    placed = (
        P(("group", "angle"), "slab", "col"),
        P(),
        P(("group", "angle"), "slab"),
        P(("group", "angle"), "slab", None),
        P(("group", "angle"), "slab", None),
    )
    return jax.shard_map(
        on_device,
        mesh=mesh,
        in_specs=placed,
        out_specs=P(("group", "slab", "angle"), "col"),
        check_vma=False,
    )
```

```python
import math

import jax
import jax.numpy as jnp
from jax import lax
from jax.experimental import pallas as pl
from jax.experimental.pallas import tpu as pltpu
from jax.sharding import PartitionSpec as P

BLOCK = 256
TILE = 128
STACK = 8
DIRECT = (False, False, False, True)
SOON = (False, False, False, True)
WEIGHTS = (40000, 28000, 1, 1)
FINISH_WEIGHTS = (1, 1, 10000)
MARK = 1000000000
VMEM_BYTES = 14 * 1024 * 1024
FIRST_VMEM_BYTES = 104 * 512 * 1024
SECOND_VMEM_BYTES = 102 * 512 * 1024
LINE_ORDER = ((3, 2, 1, 0), (0, 2, 3, 1), (3, 1, 0, 2), (0, 1, 2, 3))

VMEM = pl.BlockSpec(memory_space=pltpu.VMEM)
HELD = pl.BlockSpec(memory_space=pltpu.HBM)
SMEM = pl.BlockSpec(memory_space=pltpu.SMEM)


def kernel_call(
    body, out_shape, args, flops, scratch=(), name=None, specs=None, grant=VMEM_BYTES, carried=()
):
    specs = specs or [VMEM] * len(args)
    moved = sum(a.size * a.dtype.itemsize for a in (*args, *out_shape))
    n_in, n_out, n_through = len(args), len(out_shape), len(carried)

    def kernel(*refs):
        ins, refs = refs[:n_in], refs[n_in + n_through :]
        body(*ins, *refs[:n_out], *refs[n_out + n_through :])

    return pl.pallas_call(
        kernel,
        out_shape=[*out_shape, *(jax.ShapeDtypeStruct(c.shape, c.dtype) for c in carried)],
        in_specs=[*specs, *([HELD] * n_through)],
        out_specs=[VMEM] * n_out + [HELD] * n_through,
        input_output_aliases={n_in + i: n_out + i for i in range(n_through)},
        scratch_shapes=list(scratch),
        compiler_params=pltpu.CompilerParams(vmem_limit_bytes=grant),
        cost_estimate=pl.CostEstimate(flops=flops, bytes_accessed=moved, transcendentals=0),
        name=name,
    )(*args, *carried)


def build_band(taps_ref, band_ref):
    count = taps_ref.shape[0]
    steps, tiles = band_ref.shape[1] // TILE, band_ref.shape[0] // TILE
    zero = jnp.zeros((TILE, TILE), jnp.float32)
    ahead = lax.broadcasted_iota(jnp.int32, (TILE, TILE), 1) >= lax.broadcasted_iota(
        jnp.int32, (TILE, TILE), 0
    )
    taps = taps_ref[...].astype(jnp.float32)

    def shifted(d):
        if not 0 <= d < count:
            return zero
        row = jnp.broadcast_to(taps[d : d + 1, :], (TILE, TILE))
        return pltpu.roll(row, 0, 1, stride=1, stride_axis=0)

    before = zero
    for d in range(-(steps - 1), tiles):
        here = shifted(d)
        block = jnp.where(ahead, here, before).T.astype(jnp.bfloat16)
        before = here
        for c in range(steps):
            if 0 <= d + c < tiles:
                band_ref[(d + c) * TILE : (d + c + 1) * TILE, c * TILE : (c + 1) * TILE] = block


def cosine_factor(row_start, col_start, sizes):
    total_rows, total_cols, count = sizes
    distance = jnp.float32(total_cols)
    v = lax.broadcasted_iota(jnp.int32, (count, 1), 0) + row_start
    v = v.astype(jnp.float32) - total_rows / 2 + 0.5
    u = lax.broadcasted_iota(jnp.int32, (1, BLOCK), 1) + col_start
    u = u.astype(jnp.float32) - total_cols / 2 + 0.5
    return distance / jnp.sqrt(distance * distance + u * u + v * v)


def weigh(proj_ref, weighted_ref, half, row_at, row_start, col_start, sizes, c):
    angles, count = proj_ref.shape[0], sizes[2]
    factor = cosine_factor(row_start + row_at, col_start + c, sizes)
    for a in range(angles):
        raw = proj_ref[a, pl.ds(row_at, count), c : c + BLOCK].astype(jnp.float32)
        at = (half * angles + a) * count
        weighted_ref[at : at + count, c : c + BLOCK] = (raw * factor).astype(jnp.bfloat16)


def filter_columns(work, count, band_ref, weighted_at):
    length = band_ref.shape[0]
    reach = (length - BLOCK) // 2
    groups = []
    for half, first, width, out_ref in work:
        starts = range(first, first + width, BLOCK)
        for at in range(0, len(starts), STACK):
            groups.append((half, starts[at : at + STACK], out_ref, at))

    def touch(index):
        if index < len(groups):
            half, starts, _, _ = groups[index]
            for c in range(starts[0] - reach, starts[-1] + BLOCK + reach, BLOCK):
                weighted_at(half, c)

    touch(0)
    for index, (half, starts, out_ref, at) in enumerate(groups):
        touch(index + 1)
        tall = jnp.concatenate(
            [
                jnp.concatenate(
                    [weighted_at(half, c)() for c in range(s - reach, s + BLOCK + reach, BLOCK)],
                    axis=1,
                )
                for s in starts
            ],
            axis=0,
        )
        result = jnp.dot(tall, band_ref[...], preferred_element_type=jnp.float32)
        result = result.astype(jnp.bfloat16)
        for k in range(len(starts)):
            out_ref[:, (at + k) * BLOCK : (at + k + 1) * BLOCK] = result[
                k * count : (k + 1) * count, :
            ]


def bf16(*shape):
    return jax.ShapeDtypeStruct(shape, jnp.bfloat16)


def f32(*shape):
    return jax.ShapeDtypeStruct(shape, jnp.float32)


def chunk_plan(cols, reach):
    assert cols >= 4 * reach and reach % (4 * BLOCK) == 0
    first, second = reach + BLOCK, 2 * reach
    third = second + (cols - 2 * reach) * 3 // 8
    return [(first, second - first), (second, third - second), (third, cols - third), (0, first)]


def on_device(projections, filter_taps, row_first, interp_index, interp_frac):
    angles, rows, cols = projections.shape
    depth = interp_index.shape[2]
    taps = filter_taps.shape[0]
    reach = taps // 2
    length = taps + BLOCK
    margin = rows // 2
    slabs, line, sides = (lax.axis_size(n) for n in ("slab", "angle", "col"))
    scale = math.pi / (angles * line)
    both = slabs == 2
    halos = 1 if both else 2
    quick = line == 4
    shard = depth // line
    order = LINE_ORDER if quick else (tuple(range(line)),) * line
    total_rows, total_cols = rows * slabs, cols * sides
    chunks = chunk_plan(cols, reach)
    widths = [w for _, w in chunks]
    part = angles * margin
    sizes = (total_rows, total_cols, margin)

    def half_rows(slab):
        if both:
            return jnp.where(slab == 0, margin, 0), jnp.where(slab == 0, 0, margin)
        return margin, 0

    def aligned(row):
        return row if isinstance(row, int) else pl.multiple_of(row, margin)

    start, width = chunks[0]
    window_at, window = start - reach, width + 2 * reach
    early = halos

    def window_kernel(proj_ref, weighted_ref, raw_ref, factor_ref, sem):
        slab = lax.axis_index("slab")
        col = lax.axis_index("col")
        starts = [aligned(r) for r in half_rows(slab)][:early]
        copies = [
            pltpu.make_async_copy(
                proj_ref.at[a, pl.ds(r, margin), pl.ds(window_at, window)],
                raw_ref.at[a, pl.ds(r, margin), :],
                sem.at[a * 2 + h],
            )
            for a in range(angles)
            for h, r in enumerate(starts)
        ]
        for copy in copies:
            copy.start()
        for half, r in enumerate(starts):
            for c in range(0, window, BLOCK):
                factor_ref[half, :, c : c + BLOCK] = cosine_factor(
                    slab * rows + r, col * cols + window_at + c, sizes
                )
        for a in range(angles):
            for half, r in enumerate(starts):
                copies[a * early + half].wait()
                at = (half * angles + a) * margin
                for c in range(0, window, BLOCK):
                    cut = slice(c, c + BLOCK)
                    raw = raw_ref[a, pl.ds(r, margin), cut].astype(jnp.float32)
                    weighted_ref[at : at + margin, cut] = (
                        raw * factor_ref[half, :, cut]
                    ).astype(jnp.bfloat16)

    (ahead,) = kernel_call(
        window_kernel,
        [bf16(early * part, window)],
        (projections,),
        early * part * window * 4,
        scratch=[
            pltpu.VMEM((angles, rows, window), jnp.bfloat16),
            pltpu.VMEM((early, margin, window), jnp.float32),
            pltpu.SemaphoreType.DMA((2 * angles,)),
        ],
        name="first_window",
        specs=[HELD],
        grant=FIRST_VMEM_BYTES,
    )

    def first_kernel(proj_ref, weighted_ref, taps_ref, band_ref, edge_ref, *rest):
        *outs, sem = rest
        col = lax.axis_index("col")
        edge_col = pl.multiple_of(jnp.where(col == 0, cols - reach, 0), TILE)
        edge_copy = pltpu.make_async_copy(
            proj_ref.at[:, :, pl.ds(edge_col, reach)], edge_ref, sem.at[0]
        )
        edge_copy.start()
        build_band(taps_ref, band_ref)

        def weighted_at(half, c):
            at = c - window_at
            return lambda: weighted_ref[half * part : (half + 1) * part, at : at + BLOCK]

        work = [(h, start, width, out_ref) for h, out_ref in enumerate(outs)]
        filter_columns(work, part, band_ref, weighted_at)
        edge_copy.wait()

    band, edge, *first_out = kernel_call(
        first_kernel,
        [bf16(length, BLOCK), bf16(angles, rows, reach)] + [bf16(part, width)] * early,
        (projections, ahead, filter_taps.reshape(taps // TILE, TILE)),
        2 * early * part * length * width,
        scratch=[pltpu.SemaphoreType.DMA((1,))],
        name="first_columns",
        specs=[HELD, VMEM, VMEM],
        grant=SECOND_VMEM_BYTES,
    )

    up = [(i, (i + 1) % slabs) for i in range(slabs - 1)]
    down = [(j, i) for i, j in up]

    def exchange(sends):
        if both:
            return [lax.ppermute(sends[0], "slab", up + down)]
        return [lax.ppermute(sends[0], "slab", up), lax.ppermute(sends[1], "slab", down)]

    assert sides == 2
    received = lax.ppermute(edge, "col", [(0, 1), (1, 0)])
    halo_rows = [exchange(first_out)]

    def write_weights(first_ref, index_ref, frac_ref, own_ref, halo_ref):
        slab = lax.axis_index("slab")
        angle = lax.axis_index("angle")
        if both:
            bases = [jnp.where(slab == 0, rows, rows - margin)]
        else:
            bases = [slab * rows - margin, (slab + 1) * rows]

        def weights(a, base):
            slot = lax.broadcasted_iota(jnp.int32, (margin, depth), 0) + base
            position = index_ref[a] + first_ref[a]
            frac = frac_ref[a]
            high = frac.astype(jnp.bfloat16).astype(jnp.float32)
            low = (1.0 - frac).astype(jnp.bfloat16).astype(jnp.float32)
            return jnp.where(slot == position, low, 0.0) + jnp.where(slot == position + 1, high, 0.0)

        here = [slab * rows + r for r in half_rows(slab)]
        for starts, ref in ((here, own_ref), (bases, halo_ref)):
            table = jnp.concatenate([weights(a, b) for b in starts for a in range(angles)], axis=0)
            turned = table.T.astype(jnp.bfloat16)
            for s in range(line):
                if quick:
                    places = [o.index(s) for o in order]
                    place = places[line - 1]
                    for i in range(line - 1):
                        place = jnp.where(angle == i, places[i], place)
                    at = pl.multiple_of(place * shard, shard)
                else:
                    at = s * shard
                ref[pl.ds(at, shard), :] = turned[s * shard : (s + 1) * shard, :]

    def filter_here(refs, work, band_ref):
        proj_ref, received_ref, weighted_ref, halo_cols_ref = refs
        slab = lax.axis_index("slab")
        col = lax.axis_index("col")
        starts = [aligned(r) for r in half_rows(slab)]
        lower = col == 0
        from_col = jnp.where(lower, cols, col * cols - reach)
        none = jnp.zeros((part, BLOCK), jnp.bfloat16)
        known = set()

        def weighted_at(half, c):
            inside = 0 <= c < cols
            source, into = (proj_ref, weighted_ref) if inside else (received_ref, halo_cols_ref)
            first_col = col * cols if inside else from_col
            at = c if inside else c % reach
            if (half, at, inside) not in known:
                known.add((half, at, inside))
                weigh(source, into, half, starts[half], slab * rows, first_col, sizes, at)

            def load():
                block = into[half * part : (half + 1) * part, at : at + BLOCK]
                if c < 0:
                    block = jnp.where(lower, none, block)
                elif c >= cols:
                    block = jnp.where(lower, block, none)
                return block

            return load

        filter_columns(work, part, band_ref, weighted_at)

    scratch = [pltpu.VMEM((2 * part, n), jnp.bfloat16) for n in (cols, reach)]

    work = [(1, *chunks[0])][: 2 - early]
    work += [(half, *chunk) for chunk in chunks[1:-1] for half in (0, 1)]

    def second_kernel(proj_ref, received_ref, band_ref, first_ref, index_ref, frac_ref,
                      own_ref, halo_ref, *rest):
        outs = [(*w, ref) for w, ref in zip(work, rest)]
        filter_here((proj_ref, received_ref, *rest[-2:]), outs, band_ref)
        write_weights(first_ref, index_ref, frac_ref, own_ref, halo_ref)

    own_weight, halo_weight, *second_out = kernel_call(
        second_kernel,
        [bf16(depth, 2 * part), bf16(depth, halos * part)] + [bf16(part, w[2]) for w in work],
        (projections, received, band, row_first[:, 0], interp_index, interp_frac),
        2 * part * length * sum(w[2] for w in work),
        scratch=scratch,
        name="other_columns",
        specs=[VMEM, VMEM, VMEM, SMEM, VMEM, VMEM],
    )

    def last_kernel(proj_ref, received_ref, taps_ref, *rest):
        *outs, band_ref, weighted_ref, halo_cols_ref = rest
        build_band(taps_ref, band_ref)
        filter_here(
            (proj_ref, received_ref, weighted_ref, halo_cols_ref),
            [(half, *chunks[-1], ref) for half, ref in enumerate(outs)],
            band_ref,
        )

    before = second_out[-2:]
    *last_out, before[0] = kernel_call(
        last_kernel,
        [bf16(part, widths[-1])] * 2,
        (projections, received, filter_taps.reshape(taps // TILE, TILE)),
        4 * part * length * widths[-1],
        scratch=[pltpu.VMEM((length, BLOCK), jnp.bfloat16)] + scratch,
        name="last_columns",
        carried=before[:1],
    )
    second_out = [*second_out[:-2], *before, *last_out]
    filtered = [(*first_out, *second_out[: 2 - early])]
    for at in range(2 - early, len(second_out), 2):
        filtered.append(second_out[at : at + 2])
        halo_rows.append(exchange(second_out[at : at + halos]))

    def project(index, after=()):
        width = widths[index]

        def body(own_ref, halo_ref, *rest):
            sources, outs = rest[: 2 + halos], rest[2 + halos + len(after) :]
            for c in range(0, width, BLOCK):
                cut = slice(c, c + BLOCK)
                own = jnp.concatenate([ref[:, cut] for ref in sources[:2]], axis=0)
                other = [ref[:, cut] for ref in sources[2:]]
                other = other[0] if len(other) == 1 else jnp.concatenate(other, axis=0)
                total = jnp.dot(own_ref[...], own, preferred_element_type=jnp.float32)
                total += jnp.dot(halo_ref[...], other, preferred_element_type=jnp.float32)
                total = total * scale
                at = 0
                for i, out in enumerate(outs):
                    if len(outs) == 5 and i == 2:
                        at -= out.shape[0]
                    out[:, cut] = total[at : at + out.shape[0], :].astype(out.dtype)
                    at += out.shape[0]

        if quick:
            first = [bf16(shard, width)] * 2 if DIRECT[index] else [bf16(2 * shard, width)]
            again = [bf16(shard, width)] * SOON[index]
            shapes = [*first, *again, bf16(shard, width), f32(shard, width)]
        else:
            shapes = [f32(depth, width)]
        return kernel_call(
            body,
            shapes,
            (own_weight, halo_weight, *filtered[index], *halo_rows[index], *after),
            2 * depth * (2 + halos) * part * width,
            name="interpolate",
            specs=[VMEM] * (4 + halos) + [HELD] * len(after),
        )

    def widen(x):
        return x.astype(jnp.float32)

    def at_end():
        angle = lax.axis_index("angle")
        return (angle == 0) | (angle == line - 1)

    neighbours = [(0, 1), (1, 0), (2, 3), (3, 2)]
    middles = [(1, 2), (2, 1), (0, 0), (3, 3)]
    second_hop = [(0, 1), (1, 3), (2, 0), (3, 2)]
    straight = [(0, 2), (3, 1), (1, 0), (2, 3)]

    def first_hops(*parts):
        if len(parts) == 1:
            return [lax.ppermute(parts[0], "angle", neighbours)]
        near, middle, *later = parts
        two = [] if later else [lax.ppermute(middle, "angle", straight)]
        three = lax.ppermute(middle, "angle", middles)
        one = lax.ppermute(near, "angle", neighbours)
        return [one, three, *two]

    def relay(sent, own, far, kept, after=(), weight=1, soon=False):
        direct = len(sent) > 1
        arrived = sent[: 1 if soon else 2] if direct else [sent[0], own[0]]
        later = own[2:]
        extra = len(arrived) - 1

        def body(one_ref, *rest):
            other_ref = rest[0]
            far_ref, kept_ref = rest[extra : extra + 2]
            outs = rest[extra + 2 + len(after) :]
            end = at_end()
            near = widen(one_ref[:shard, :])
            relayed = widen(far_ref[...]) + jnp.where(end, 0.0, near)
            outs[0][...] = relayed.astype(jnp.bfloat16)
            if soon:
                outs[1][...] = kept_ref[...] + jnp.where(end, near, 0.0)
            elif direct:
                outs[1][...] = kept_ref[...] + jnp.where(end, near, widen(other_ref[...]))
            else:
                outs[1][...] = kept_ref[...] + jnp.where(end, near, 0.0)
                crossed = widen(one_ref[shard:, :]) + widen(other_ref[shard:, :])
                outs[2][...] = crossed.astype(jnp.bfloat16)

        relayed, partial, *others = kernel_call(
            body,
            [bf16(*far.shape), f32(*kept.shape)] + [bf16(*far.shape)] * (not direct),
            (*arrived, far, kept, *after),
            far.size * 2 * weight,
            name="relay",
            specs=[VMEM] * (3 + extra) + [HELD] * len(after),
            carried=later,
        )
        four = lax.ppermute(relayed, "angle", second_hop)
        if not direct:
            return partial, four, lax.ppermute(others[0], "angle", middles)
        two = lax.ppermute(others[0], "angle", straight[:2]) if later else sent[2]
        return (partial, four, two, *([sent[1]] if soon else []))

    def total(partial_ref, four_ref, *fillers):
        direct = sum(widen(ref[...]) for ref in fillers)
        return partial_ref[...] + widen(four_ref[...]) + jnp.where(at_end(), 0.0, direct)

    def mark(array, weight):
        def body(array_ref, out_ref):
            out_ref[...] = jnp.zeros_like(out_ref)

        return kernel_call(body, [f32(8, TILE)], (array,), weight, name="mark", specs=[HELD])[0]

    def finish(pieces, weight=1, after=()):
        def body(*refs):
            refs[-1][...] = total(*refs[: len(pieces)])

        return kernel_call(
            body,
            [f32(*pieces[0].shape)],
            (*pieces, *after),
            pieces[0].size * 2 * weight,
            name="finish",
            specs=[VMEM] * len(pieces) + [HELD] * len(after),
        )[0]

    def store(done, pieces, index, volume=None, weight=1, after=()):
        given = [*done, *pieces]
        held = [*after, *([] if volume is None else [volume])]

        def body(*refs):
            ready, refs = refs[: len(done)], refs[len(done) :]
            volume_ref, total_ref, sem = refs[-3:]

            def copy(i, source):
                at = pl.ds(chunks[i][0], chunks[i][1])
                return pltpu.make_async_copy(source, volume_ref.at[:, at], sem.at[i])

            copies = [copy(i, ref) for i, ref in enumerate(ready)]
            for c in copies:
                c.start()
            total_ref[...] = total(*refs[: len(pieces)])
            copies.append(copy(index, total_ref))
            copies[-1].start()
            for c in copies:
                c.wait()

        size = shard * widths[index]
        return pl.pallas_call(
            body,
            out_shape=f32(shard, cols),
            in_specs=[VMEM] * len(given) + [HELD] * len(held),
            out_specs=HELD,
            input_output_aliases={} if volume is None else {len(given) + len(after): 0},
            scratch_shapes=[
                pltpu.VMEM((shard, widths[index]), jnp.float32),
                pltpu.SemaphoreType.DMA((len(chunks),)),
            ],
            compiler_params=pltpu.CompilerParams(vmem_limit_bytes=VMEM_BYTES),
            cost_estimate=pl.CostEstimate(
                flops=size * 2 * weight, bytes_accessed=size * 4, transcendentals=0
            ),
            name="store",
        )(*given, *held)

    if not quick:
        sums = [
            lax.psum_scatter(project(i)[0], "angle", scatter_dimension=0, tiled=True)
            for i in range(len(chunks))
        ]
        return jnp.concatenate([sums[i] for i in sorted(range(len(chunks)), key=chunks.__getitem__)], 1)

    last = len(chunks) - 1
    *own, far, kept = project(0)
    sent = first_hops(*own)
    done, pieces = [], []
    for j in range(last + 1):
        here = (sent, own, far, kept)
        after = sent[2:] if j == 0 else []
        if j < last:
            earlier = [p[0] for p in pieces[-1:]] if j else [last_out[-1]]
            *own, far, kept = project(j + 1, after=earlier)
            sent = first_hops(*own)
            after = [*after, kept]
            if j:
                done.append(finish(pieces[-1], weight=FINISH_WEIGHTS[j - 1], after=[kept]))
                after.append(done[-1])
        pieces.append(relay(*here, after=after, weight=WEIGHTS[j], soon=SOON[j]))
    swap = [mark(sent[1], MARK)] if SOON[last] else []
    volume = store(done, pieces[last - 1], last - 1, weight=FINISH_WEIGHTS[last - 1], after=swap)
    return store([], pieces[last], last, volume)


def solution(mesh):
    placed = (
        P(("group", "angle"), "slab", "col"),
        P(),
        P(("group", "angle"), "slab"),
        P(("group", "angle"), "slab", None),
        P(("group", "angle"), "slab", None),
    )
    return jax.shard_map(
        on_device,
        mesh=mesh,
        in_specs=placed,
        out_specs=P(("group", "slab", "angle"), "col"),
        check_vma=False,
    )
```

```python
import math

import jax
import jax.numpy as jnp
from jax import lax
from jax.experimental import pallas as pl
from jax.experimental.pallas import tpu as pltpu
from jax.sharding import PartitionSpec as P

BLOCK = 256
TILE = 128
STACK = 8
DIRECT = (False, False, False, True)
SOON = (False, False, False, True)
WEIGHTS = (40000, 28000, 1, 1)
FINISH_WEIGHTS = (1, 1, 10000)
MARK = 1000000000
VMEM_BYTES = 14 * 1024 * 1024
FIRST_VMEM_BYTES = 104 * 512 * 1024
LINE_ORDER = ((3, 2, 1, 0), (0, 2, 3, 1), (3, 1, 0, 2), (0, 1, 2, 3))

VMEM = pl.BlockSpec(memory_space=pltpu.VMEM)
HELD = pl.BlockSpec(memory_space=pltpu.HBM)
SMEM = pl.BlockSpec(memory_space=pltpu.SMEM)


def kernel_call(
    body, out_shape, args, flops, scratch=(), name=None, specs=None, grant=VMEM_BYTES, carried=()
):
    specs = specs or [VMEM] * len(args)
    moved = sum(a.size * a.dtype.itemsize for a in (*args, *out_shape))
    n_in, n_out, n_through = len(args), len(out_shape), len(carried)

    def kernel(*refs):
        ins, refs = refs[:n_in], refs[n_in + n_through :]
        body(*ins, *refs[:n_out], *refs[n_out + n_through :])

    return pl.pallas_call(
        kernel,
        out_shape=[*out_shape, *(jax.ShapeDtypeStruct(c.shape, c.dtype) for c in carried)],
        in_specs=[*specs, *([HELD] * n_through)],
        out_specs=[VMEM] * n_out + [HELD] * n_through,
        input_output_aliases={n_in + i: n_out + i for i in range(n_through)},
        scratch_shapes=list(scratch),
        compiler_params=pltpu.CompilerParams(vmem_limit_bytes=grant),
        cost_estimate=pl.CostEstimate(flops=flops, bytes_accessed=moved, transcendentals=0),
        name=name,
    )(*args, *carried)


def build_band(taps_ref, band_ref):
    count = taps_ref.shape[0]
    steps, tiles = band_ref.shape[1] // TILE, band_ref.shape[0] // TILE
    zero = jnp.zeros((TILE, TILE), jnp.float32)
    ahead = lax.broadcasted_iota(jnp.int32, (TILE, TILE), 1) >= lax.broadcasted_iota(
        jnp.int32, (TILE, TILE), 0
    )
    taps = taps_ref[...].astype(jnp.float32)

    def shifted(d):
        if not 0 <= d < count:
            return zero
        row = jnp.broadcast_to(taps[d : d + 1, :], (TILE, TILE))
        return pltpu.roll(row, 0, 1, stride=1, stride_axis=0)

    before = zero
    for d in range(-(steps - 1), tiles):
        here = shifted(d)
        block = jnp.where(ahead, here, before).T.astype(jnp.bfloat16)
        before = here
        for c in range(steps):
            if 0 <= d + c < tiles:
                band_ref[(d + c) * TILE : (d + c + 1) * TILE, c * TILE : (c + 1) * TILE] = block


def cosine_factor(row_start, col_start, sizes):
    total_rows, total_cols, count = sizes
    distance = jnp.float32(total_cols)
    v = lax.broadcasted_iota(jnp.int32, (count, 1), 0) + row_start
    v = v.astype(jnp.float32) - total_rows / 2 + 0.5
    u = lax.broadcasted_iota(jnp.int32, (1, BLOCK), 1) + col_start
    u = u.astype(jnp.float32) - total_cols / 2 + 0.5
    return distance / jnp.sqrt(distance * distance + u * u + v * v)


def weigh(proj_ref, weighted_ref, half, row_at, row_start, col_start, sizes, c):
    angles, count = proj_ref.shape[0], sizes[2]
    factor = cosine_factor(row_start + row_at, col_start + c, sizes)
    for a in range(angles):
        raw = proj_ref[a, pl.ds(row_at, count), c : c + BLOCK].astype(jnp.float32)
        at = (half * angles + a) * count
        weighted_ref[at : at + count, c : c + BLOCK] = (raw * factor).astype(jnp.bfloat16)


def filter_columns(work, count, band_ref, weighted_at):
    length = band_ref.shape[0]
    reach = (length - BLOCK) // 2
    groups = []
    for half, first, width, out_ref in work:
        starts = range(first, first + width, BLOCK)
        for at in range(0, len(starts), STACK):
            groups.append((half, starts[at : at + STACK], out_ref, at))

    def touch(index):
        if index < len(groups):
            half, starts, _, _ = groups[index]
            for c in range(starts[0] - reach, starts[-1] + BLOCK + reach, BLOCK):
                weighted_at(half, c)

    touch(0)
    for index, (half, starts, out_ref, at) in enumerate(groups):
        touch(index + 1)
        tall = jnp.concatenate(
            [
                jnp.concatenate(
                    [weighted_at(half, c)() for c in range(s - reach, s + BLOCK + reach, BLOCK)],
                    axis=1,
                )
                for s in starts
            ],
            axis=0,
        )
        result = jnp.dot(tall, band_ref[...], preferred_element_type=jnp.float32)
        result = result.astype(jnp.bfloat16)
        for k in range(len(starts)):
            out_ref[:, (at + k) * BLOCK : (at + k + 1) * BLOCK] = result[
                k * count : (k + 1) * count, :
            ]


def bf16(*shape):
    return jax.ShapeDtypeStruct(shape, jnp.bfloat16)


def f32(*shape):
    return jax.ShapeDtypeStruct(shape, jnp.float32)


def chunk_plan(cols, reach):
    assert cols >= 4 * reach and reach % (4 * BLOCK) == 0
    first, second = reach + BLOCK, 2 * reach
    third = second + (cols - 2 * reach) * 3 // 8
    return [(first, second - first), (second, third - second), (third, cols - third), (0, first)]


def on_device(projections, filter_taps, row_first, interp_index, interp_frac):
    angles, rows, cols = projections.shape
    depth = interp_index.shape[2]
    taps = filter_taps.shape[0]
    reach = taps // 2
    length = taps + BLOCK
    margin = rows // 2
    slabs, line, sides = (lax.axis_size(n) for n in ("slab", "angle", "col"))
    scale = math.pi / (angles * line)
    both = slabs == 2
    halos = 1 if both else 2
    quick = line == 4
    shard = depth // line
    order = LINE_ORDER if quick else (tuple(range(line)),) * line
    total_rows, total_cols = rows * slabs, cols * sides
    chunks = chunk_plan(cols, reach)
    widths = [w for _, w in chunks]
    part = angles * margin
    sizes = (total_rows, total_cols, margin)

    def half_rows(slab):
        if both:
            return jnp.where(slab == 0, margin, 0), jnp.where(slab == 0, 0, margin)
        return margin, 0

    def aligned(row):
        return row if isinstance(row, int) else pl.multiple_of(row, margin)

    start, width = chunks[0]
    window_at, window = start - reach, width + 2 * reach
    early = halos

    def window_kernel(proj_ref, weighted_ref, edge_ref, raw_ref, factor_ref, sem):
        slab = lax.axis_index("slab")
        col = lax.axis_index("col")
        starts = [aligned(r) for r in half_rows(slab)][:early]
        copies = [
            pltpu.make_async_copy(
                proj_ref.at[a, pl.ds(r, margin), pl.ds(window_at, window)],
                raw_ref.at[a, pl.ds(r, margin), :],
                sem.at[a * 2 + h],
            )
            for a in range(angles)
            for h, r in enumerate(starts)
        ]
        edge_col = pl.multiple_of(jnp.where(col == 0, cols - reach, 0), TILE)
        edge_copy = pltpu.make_async_copy(
            proj_ref.at[:, :, pl.ds(edge_col, reach)], edge_ref, sem.at[2 * angles]
        )
        for copy in copies:
            copy.start()
        edge_copy.start()
        for half, r in enumerate(starts):
            for c in range(0, window, BLOCK):
                factor_ref[half, :, c : c + BLOCK] = cosine_factor(
                    slab * rows + r, col * cols + window_at + c, sizes
                )
        for a in range(angles):
            for half, r in enumerate(starts):
                copies[a * early + half].wait()
                at = (half * angles + a) * margin
                for c in range(0, window, BLOCK):
                    cut = slice(c, c + BLOCK)
                    raw = raw_ref[a, pl.ds(r, margin), cut].astype(jnp.float32)
                    weighted_ref[at : at + margin, cut] = (
                        raw * factor_ref[half, :, cut]
                    ).astype(jnp.bfloat16)
        edge_copy.wait()

    ahead, edge = kernel_call(
        window_kernel,
        [bf16(early * part, window), bf16(angles, rows, reach)],
        (projections,),
        early * part * window * 4,
        scratch=[
            pltpu.VMEM((angles, rows, window), jnp.bfloat16),
            pltpu.VMEM((early, margin, window), jnp.float32),
            pltpu.SemaphoreType.DMA((2 * angles + 1,)),
        ],
        name="first_window",
        specs=[HELD],
        grant=FIRST_VMEM_BYTES,
    )

    def first_kernel(weighted_ref, taps_ref, band_ref, *outs):
        build_band(taps_ref, band_ref)

        def weighted_at(half, c):
            at = c - window_at
            return lambda: weighted_ref[half * part : (half + 1) * part, at : at + BLOCK]

        work = [(h, start, width, out_ref) for h, out_ref in enumerate(outs)]
        filter_columns(work, part, band_ref, weighted_at)

    band, *first_out = kernel_call(
        first_kernel,
        [bf16(length, BLOCK)] + [bf16(part, width)] * early,
        (ahead, filter_taps.reshape(taps // TILE, TILE)),
        2 * early * part * length * width,
        name="first_columns",
    )

    up = [(i, (i + 1) % slabs) for i in range(slabs - 1)]
    down = [(j, i) for i, j in up]

    def exchange(sends):
        if both:
            return [lax.ppermute(sends[0], "slab", up + down)]
        return [lax.ppermute(sends[0], "slab", up), lax.ppermute(sends[1], "slab", down)]

    assert sides == 2
    received = lax.ppermute(edge, "col", [(0, 1), (1, 0)])
    halo_rows = [exchange(first_out)]

    def write_weights(first_ref, index_ref, frac_ref, own_ref, halo_ref):
        slab = lax.axis_index("slab")
        angle = lax.axis_index("angle")
        if both:
            bases = [jnp.where(slab == 0, rows, rows - margin)]
        else:
            bases = [slab * rows - margin, (slab + 1) * rows]

        def weights(a, base):
            slot = lax.broadcasted_iota(jnp.int32, (margin, depth), 0) + base
            position = index_ref[a] + first_ref[a]
            frac = frac_ref[a]
            high = frac.astype(jnp.bfloat16).astype(jnp.float32)
            low = (1.0 - frac).astype(jnp.bfloat16).astype(jnp.float32)
            return jnp.where(slot == position, low, 0.0) + jnp.where(slot == position + 1, high, 0.0)

        here = [slab * rows + r for r in half_rows(slab)]
        for starts, ref in ((here, own_ref), (bases, halo_ref)):
            table = jnp.concatenate([weights(a, b) for b in starts for a in range(angles)], axis=0)
            turned = table.T.astype(jnp.bfloat16)
            for s in range(line):
                if quick:
                    places = [o.index(s) for o in order]
                    place = places[line - 1]
                    for i in range(line - 1):
                        place = jnp.where(angle == i, places[i], place)
                    at = pl.multiple_of(place * shard, shard)
                else:
                    at = s * shard
                ref[pl.ds(at, shard), :] = turned[s * shard : (s + 1) * shard, :]

    def filter_here(refs, work, band_ref):
        proj_ref, received_ref, weighted_ref, halo_cols_ref = refs
        slab = lax.axis_index("slab")
        col = lax.axis_index("col")
        starts = [aligned(r) for r in half_rows(slab)]
        lower = col == 0
        from_col = jnp.where(lower, cols, col * cols - reach)
        none = jnp.zeros((part, BLOCK), jnp.bfloat16)
        known = set()

        def weighted_at(half, c):
            inside = 0 <= c < cols
            source, into = (proj_ref, weighted_ref) if inside else (received_ref, halo_cols_ref)
            first_col = col * cols if inside else from_col
            at = c if inside else c % reach
            if (half, at, inside) not in known:
                known.add((half, at, inside))
                weigh(source, into, half, starts[half], slab * rows, first_col, sizes, at)

            def load():
                block = into[half * part : (half + 1) * part, at : at + BLOCK]
                if c < 0:
                    block = jnp.where(lower, none, block)
                elif c >= cols:
                    block = jnp.where(lower, block, none)
                return block

            return load

        filter_columns(work, part, band_ref, weighted_at)

    scratch = [pltpu.VMEM((2 * part, n), jnp.bfloat16) for n in (cols, reach)]

    work = [(1, *chunks[0])][: 2 - early]
    work += [(half, *chunk) for chunk in chunks[1:-1] for half in (0, 1)]

    def second_kernel(proj_ref, received_ref, band_ref, first_ref, index_ref, frac_ref,
                      own_ref, halo_ref, *rest):
        outs = [(*w, ref) for w, ref in zip(work, rest)]
        filter_here((proj_ref, received_ref, *rest[-2:]), outs, band_ref)
        write_weights(first_ref, index_ref, frac_ref, own_ref, halo_ref)

    own_weight, halo_weight, *second_out = kernel_call(
        second_kernel,
        [bf16(depth, 2 * part), bf16(depth, halos * part)] + [bf16(part, w[2]) for w in work],
        (projections, received, band, row_first[:, 0], interp_index, interp_frac),
        2 * part * length * sum(w[2] for w in work),
        scratch=scratch,
        name="other_columns",
        specs=[VMEM, VMEM, VMEM, SMEM, VMEM, VMEM],
    )

    def last_kernel(proj_ref, received_ref, taps_ref, *rest):
        *outs, band_ref, weighted_ref, halo_cols_ref = rest
        build_band(taps_ref, band_ref)
        filter_here(
            (proj_ref, received_ref, weighted_ref, halo_cols_ref),
            [(half, *chunks[-1], ref) for half, ref in enumerate(outs)],
            band_ref,
        )

    before = second_out[-2:]
    *last_out, before[0] = kernel_call(
        last_kernel,
        [bf16(part, widths[-1])] * 2,
        (projections, received, filter_taps.reshape(taps // TILE, TILE)),
        4 * part * length * widths[-1],
        scratch=[pltpu.VMEM((length, BLOCK), jnp.bfloat16)] + scratch,
        name="last_columns",
        carried=before[:1],
    )
    second_out = [*second_out[:-2], *before, *last_out]
    filtered = [(*first_out, *second_out[: 2 - early])]
    for at in range(2 - early, len(second_out), 2):
        filtered.append(second_out[at : at + 2])
        halo_rows.append(exchange(second_out[at : at + halos]))

    def project(index, after=()):
        width = widths[index]

        def body(own_ref, halo_ref, *rest):
            sources, outs = rest[: 2 + halos], rest[2 + halos + len(after) :]
            for c in range(0, width, 2 * BLOCK):
                cut = slice(c, min(c + 2 * BLOCK, width))
                own = jnp.concatenate([ref[:, cut] for ref in sources[:2]], axis=0)
                other = [ref[:, cut] for ref in sources[2:]]
                other = other[0] if len(other) == 1 else jnp.concatenate(other, axis=0)
                total = jnp.dot(own_ref[...], own, preferred_element_type=jnp.float32)
                total += jnp.dot(halo_ref[...], other, preferred_element_type=jnp.float32)
                total = total * scale
                at = 0
                for i, out in enumerate(outs):
                    if len(outs) == 5 and i == 2:
                        at -= out.shape[0]
                    out[:, cut] = total[at : at + out.shape[0], :].astype(out.dtype)
                    at += out.shape[0]

        if quick:
            first = [bf16(shard, width)] * 2 if DIRECT[index] else [bf16(2 * shard, width)]
            again = [bf16(shard, width)] * SOON[index]
            shapes = [*first, *again, bf16(shard, width), f32(shard, width)]
        else:
            shapes = [f32(depth, width)]
        return kernel_call(
            body,
            shapes,
            (own_weight, halo_weight, *filtered[index], *halo_rows[index], *after),
            2 * depth * (2 + halos) * part * width,
            name="interpolate",
            specs=[VMEM] * (4 + halos) + [HELD] * len(after),
        )

    def widen(x):
        return x.astype(jnp.float32)

    def at_end():
        angle = lax.axis_index("angle")
        return (angle == 0) | (angle == line - 1)

    neighbours = [(0, 1), (1, 0), (2, 3), (3, 2)]
    middles = [(1, 2), (2, 1), (0, 0), (3, 3)]
    second_hop = [(0, 1), (1, 3), (2, 0), (3, 2)]
    straight = [(0, 2), (3, 1), (1, 0), (2, 3)]

    def first_hops(*parts):
        if len(parts) == 1:
            return [lax.ppermute(parts[0], "angle", neighbours)]
        near, middle, *later = parts
        two = [] if later else [lax.ppermute(middle, "angle", straight)]
        three = lax.ppermute(middle, "angle", middles)
        one = lax.ppermute(near, "angle", neighbours)
        return [one, three, *two]

    def relay(sent, own, far, kept, after=(), weight=1, soon=False):
        direct = len(sent) > 1
        arrived = sent[: 1 if soon else 2] if direct else [sent[0], own[0]]
        later = own[2:]
        extra = len(arrived) - 1

        def body(one_ref, *rest):
            other_ref = rest[0]
            far_ref, kept_ref = rest[extra : extra + 2]
            outs = rest[extra + 2 + len(after) :]
            end = at_end()
            near = widen(one_ref[:shard, :])
            relayed = widen(far_ref[...]) + jnp.where(end, 0.0, near)
            outs[0][...] = relayed.astype(jnp.bfloat16)
            if soon:
                outs[1][...] = kept_ref[...] + jnp.where(end, near, 0.0)
            elif direct:
                outs[1][...] = kept_ref[...] + jnp.where(end, near, widen(other_ref[...]))
            else:
                outs[1][...] = kept_ref[...] + jnp.where(end, near, 0.0)
                crossed = widen(one_ref[shard:, :]) + widen(other_ref[shard:, :])
                outs[2][...] = crossed.astype(jnp.bfloat16)

        relayed, partial, *others = kernel_call(
            body,
            [bf16(*far.shape), f32(*kept.shape)] + [bf16(*far.shape)] * (not direct),
            (*arrived, far, kept, *after),
            far.size * 2 * weight,
            name="relay",
            specs=[VMEM] * (3 + extra) + [HELD] * len(after),
            carried=later,
        )
        four = lax.ppermute(relayed, "angle", second_hop)
        if not direct:
            return partial, four, lax.ppermute(others[0], "angle", middles)
        two = lax.ppermute(others[0], "angle", straight[:2]) if later else sent[2]
        return (partial, four, two, *([sent[1]] if soon else []))

    def total(partial_ref, four_ref, *fillers):
        direct = sum(widen(ref[...]) for ref in fillers)
        return partial_ref[...] + widen(four_ref[...]) + jnp.where(at_end(), 0.0, direct)

    def mark(array, weight):
        def body(array_ref, out_ref):
            out_ref[...] = jnp.zeros_like(out_ref)

        return kernel_call(body, [f32(8, TILE)], (array,), weight, name="mark", specs=[HELD])[0]

    def finish(pieces, weight=1, after=()):
        def body(*refs):
            refs[-1][...] = total(*refs[: len(pieces)])

        return kernel_call(
            body,
            [f32(*pieces[0].shape)],
            (*pieces, *after),
            pieces[0].size * 2 * weight,
            name="finish",
            specs=[VMEM] * len(pieces) + [HELD] * len(after),
        )[0]

    def store(done, pieces, index, volume=None, weight=1, after=()):
        given = [*done, *pieces]
        held = [*after, *([] if volume is None else [volume])]

        def body(*refs):
            ready, refs = refs[: len(done)], refs[len(done) :]
            volume_ref, total_ref, sem = refs[-3:]

            def copy(i, source):
                at = pl.ds(chunks[i][0], chunks[i][1])
                return pltpu.make_async_copy(source, volume_ref.at[:, at], sem.at[i])

            copies = [copy(i, ref) for i, ref in enumerate(ready)]
            for c in copies:
                c.start()
            total_ref[...] = total(*refs[: len(pieces)])
            copies.append(copy(index, total_ref))
            copies[-1].start()
            for c in copies:
                c.wait()

        size = shard * widths[index]
        return pl.pallas_call(
            body,
            out_shape=f32(shard, cols),
            in_specs=[VMEM] * len(given) + [HELD] * len(held),
            out_specs=HELD,
            input_output_aliases={} if volume is None else {len(given) + len(after): 0},
            scratch_shapes=[
                pltpu.VMEM((shard, widths[index]), jnp.float32),
                pltpu.SemaphoreType.DMA((len(chunks),)),
            ],
            compiler_params=pltpu.CompilerParams(vmem_limit_bytes=VMEM_BYTES),
            cost_estimate=pl.CostEstimate(
                flops=size * 2 * weight, bytes_accessed=size * 4, transcendentals=0
            ),
            name="store",
        )(*given, *held)

    if not quick:
        sums = [
            lax.psum_scatter(project(i)[0], "angle", scatter_dimension=0, tiled=True)
            for i in range(len(chunks))
        ]
        return jnp.concatenate([sums[i] for i in sorted(range(len(chunks)), key=chunks.__getitem__)], 1)

    last = len(chunks) - 1
    *own, far, kept = project(0)
    sent = first_hops(*own)
    done, pieces = [], []
    for j in range(last + 1):
        here = (sent, own, far, kept)
        after = sent[2:] if j == 0 else []
        if j < last:
            earlier = [p[0] for p in pieces[-1:]] if j else [last_out[-1]]
            *own, far, kept = project(j + 1, after=earlier)
            sent = first_hops(*own)
            after = [*after, kept]
            if j:
                done.append(finish(pieces[-1], weight=FINISH_WEIGHTS[j - 1], after=[kept]))
                after.append(done[-1])
        pieces.append(relay(*here, after=after, weight=WEIGHTS[j], soon=SOON[j]))
    swap = [mark(sent[1], MARK)] if SOON[last] else []
    volume = store(done, pieces[last - 1], last - 1, weight=FINISH_WEIGHTS[last - 1], after=swap)
    return store([], pieces[last], last, volume)


def solution(mesh):
    placed = (
        P(("group", "angle"), "slab", "col"),
        P(),
        P(("group", "angle"), "slab"),
        P(("group", "angle"), "slab", None),
        P(("group", "angle"), "slab", None),
    )
    return jax.shard_map(
        on_device,
        mesh=mesh,
        in_specs=placed,
        out_specs=P(("group", "slab", "angle"), "col"),
        check_vma=False,
    )
```
